32 devices in a mesh: dp: 1, ctx: 32 (over z, y, x, core).
Axes of the slice: x: 2, y: 2, z: 4, core: 2. Of those that a mesh axis runs over, the one named last changes fastest.
Arguments:
- queries: bfloat16 [1, 4096, 1024], P('dp', 'ctx'), may hold values from -1.75 to 1.75
- keys: bfloat16 [1, 4096, 1024], P('dp', 'ctx'), may hold values from -1.8 to 1.8
- values: bfloat16 [1, 4096, 1024], P('dp', 'ctx'), may hold values from -3 to 3
- out_grad: bfloat16 [1, 4096, 1024], P('dp', 'ctx'), may hold values from -1.5 to 1.5
- layer_grad: bfloat16 [1, 4096, 768], P('dp', 'ctx'), may hold values from -6 to 6
- norm_gain: float32 [1024], replicated, may hold values from 0.1 to 1.9
- decay_rates: float32 [8], replicated, as said below
- doc_lengths: int32 [1, 4], P('dp'), may hold values from 1 to 2048, 4096 in all within a row
Outputs:
- query_grad: bfloat16 [1, 4096, 1024], P('dp', 'ctx')
- key_grad: bfloat16 [1, 4096, 1024], P('dp', 'ctx')
- value_grad: bfloat16 [1, 4096, 1024], P('dp', 'ctx')
- proj_grad: float32 [1024, 768], P(('dp', 'ctx'))
The draws below stay inside these ranges and needn't reach their ends.
Inputs may be any that keep to these rules, and one draw needn't show every extreme that they name: `decay_rates`: positive rates; a head's state is multiplied by exp(-rate) per position. `doc_lengths`: each row sums to 4096; the longest document has exactly 2048 positions.
All inputs are finite; a program needn't handle non-finite values.
Results may differ from the reference program's by a relative error of at most 0.0029.
Values sent between devices are 32-bit elements; how exact they have to be, the bound alone decides.
No kernel may reach another device: no remote copies, remote signals or barrier semaphores. Data moves between devices by JAX's collectives and lax.ppermute only.
A program may use at most 128 MiB of HBM per device.

```python
import math
import jax
import jax.numpy as jnp
import numpy as np
from jax import lax

HEADS = 8
DH = 128
TB = 128
NDOC = 4
BUCKET = 768
LEN = 4096
SEQS = 1
HD = 1024
MOSTLEN = 2048
TOKENS = 4096


def head_rates(key):
    rate_key = jax.random.fold_in(key, 11)
    chooser_key, fast_key, middle_key, slow_key = jax.random.split(rate_key, 4)
    chooser = jax.random.uniform(chooser_key, (HEADS,), jnp.float32)
    fast_rate = jnp.exp(jax.random.uniform(fast_key, (HEADS,), jnp.float32, math.log(1.0 / 50.0), math.log(1.0 / 30.0)))
    middle_rate = jnp.exp(jax.random.uniform(middle_key, (HEADS,), jnp.float32, math.log(0.005), math.log(0.015)))
    slow_rate = jnp.exp(jax.random.uniform(slow_key, (HEADS,), jnp.float32, math.log(0.3 / LEN), math.log(2.3 / LEN)))
    fast_share = 0.25
    middle_share = 0.5
    return jnp.where(chooser < fast_share, fast_rate, jnp.where(chooser < middle_share, middle_rate, slow_rate))


def block_gains(key):
    gain_key = jax.random.fold_in(key, 23)
    levels = jax.random.uniform(gain_key, (SEQS, LEN // TB), jnp.float32, -3.0, 0.0)
    return jnp.repeat(jnp.exp(levels), TB, axis=1)[:, :, None]


def unit_noise(key, shape):
    noise_draw = jax.random.normal(key, shape, jnp.float32)
    return jnp.clip(noise_draw, -6.0, 6.0)


def draw_decay_rates(key, part):
    return head_rates(key)


def draw_keys(key, part):
    noise_draw = unit_noise(jax.random.fold_in(key, 31), (SEQS, LEN, HD))
    return (0.3 * block_gains(key) * noise_draw).astype(jnp.bfloat16)


def draw_values(key, part):
    rates = head_rates(key)
    head_scales = 0.5 * jnp.sqrt(jnp.maximum(rates, 4.0 / LEN) * 30.0)
    feature_scales = jnp.repeat(head_scales, DH)
    noise_draw = unit_noise(jax.random.fold_in(key, 37), (SEQS, LEN, HD))
    return (feature_scales * block_gains(key) * noise_draw).astype(jnp.bfloat16)


def block_scale(own_key, shape, shards, least, high):
    gain, own = 1.0, jax.random.fold_in(own_key, 6)
    for axis_at, shards_of in shards:
        draws = jnp.exp(jax.random.uniform(jax.random.fold_in(own, axis_at), (shards_of,), jnp.float32, least / len(shards), high / len(shards)))
        gain = gain * jnp.repeat(draws, shape[axis_at] // shards_of).reshape([-1 if axis == axis_at else 1 for axis in range(len(shape))])
    return gain


def split_up(count, total, bound, skew):
    loads = [(1 << 20) // math.isqrt(standing ** skew) + 1 for standing in range(2, count + 1)]
    rest, given = total - bound - (count - 1), [1] * (count - 1)
    while rest > 0:
        candidates = [i for i in range(count - 1) if given[i] < bound]
        pool, left = sum([loads[i] for i in candidates]), rest
        for i in candidates:
            more = min(bound - given[i], max(1, left * loads[i] // pool), rest)
            given[i] = given[i] + more
            rest = rest - more
    return np.array([bound] + given)


def ragged(stream_key, number_of, total, limit, slope):
    if number_of == 2:
        one = jax.random.randint(stream_key, (), max(1, total - limit), min(limit, total - 1) + 1)
        return jnp.stack([one, total - one])
    tallies = jnp.asarray(split_up(number_of, total, limit, slope), jnp.int32)
    twos = (number_of - 1) // 2
    giver, receiver = tallies[1:1 + 2 * twos:2], tallies[2:2 + 2 * twos:2]
    margin = jnp.minimum(giver - 1, limit - receiver)
    passed = jax.random.randint(jax.random.fold_in(stream_key, 1), (twos,), 0, 1 << 20) % (margin + 1)
    tallies = tallies.at[1:1 + 2 * twos:2].set(giver - passed).at[2:2 + 2 * twos:2].set(receiver + passed)
    return tallies[jax.random.permutation(jax.random.fold_in(stream_key, 2), number_of)]


def normal_values(rng, extent, scale, limit, cuts=(), kind=jnp.bfloat16):
    result = jax.random.normal(rng, extent, jnp.float32) * scale
    if len(cuts) > 0:
        result = block_scale(rng, extent, cuts, -0.22, 0.18) * result
    return jnp.clip(result, min=-limit, max=limit).astype(kind)


def setup_inputs(seed: int = 0) -> dict:
    seeds = jax.random.split(jax.random.key(seed), 9)
    queries = normal_values(seeds[0], (SEQS, LEN, HD), 0.3, 1.75, ((1, 32),))
    keys = draw_keys(jax.random.fold_in(seeds[8], 71), 0)
    values = draw_values(jax.random.fold_in(seeds[8], 71), 0)
    out_grad = normal_values(seeds[3], (SEQS, LEN, HD), 0.25, 1.5, ((1, 32),))
    layer_grad = normal_values(seeds[4], (SEQS, LEN, BUCKET), 1.0, 6.0, ((1, 32),))
    norm_gain = jnp.clip(1.0 + 0.18 * jax.random.normal(seeds[5], (HD,), jnp.float32), 0.1, 1.9)
    decay_rates = draw_decay_rates(jax.random.fold_in(seeds[8], 71), 0)
    doc_lengths = jax.vmap(lambda own: ragged(own, NDOC, LEN, MOSTLEN, 2))(jax.random.split(seeds[7], SEQS)).reshape((SEQS, NDOC)).astype(jnp.int32)
    return dict(queries=queries, keys=keys, values=values, out_grad=out_grad, layer_grad=layer_grad, norm_gain=norm_gain, decay_rates=decay_rates, doc_lengths=doc_lengths)


highest = lax.Precision.HIGHEST
norm_eps = 1e-06

def doc_index(positions, lengths):
    bounds = jnp.cumsum(lengths).astype(jnp.int32)[:-1]
    return lax.optimization_barrier(jnp.sum((positions[..., None] >= bounds).astype(jnp.int32), axis=-1)).astype(jnp.int32)

def decay_tables(decay_rate, doc_ids, prev_id, last_id):
    length = doc_ids.shape[0]
    offsets = jnp.arange(length, dtype=jnp.float32)
    distance = offsets[:, None] - offsets[None, :]
    same_doc = (doc_ids[:, None] == doc_ids[None, :]) & (distance >= 0.0)
    decay_mask = jnp.where(same_doc[None], jnp.exp(-decay_rate[:, None, None] * jnp.maximum(distance, 0.0)[None]), 0.0)
    entry_decay = jnp.where((doc_ids == prev_id)[None, :], jnp.exp(-decay_rate[:, None] * offsets[None, :]), 0.0)
    exit_decay = jnp.where((doc_ids == last_id)[None, :], jnp.exp(-decay_rate[:, None] * (length - offsets)[None, :]), 0.0)
    carry_all = jnp.where(last_id == prev_id, jnp.exp(-decay_rate * length), 0.0)
    return (decay_mask, entry_decay, exit_decay, carry_all)

def block_summary(query_rows, key_rows, value_rows, grad_rows, tables):
    decay_mask, entry_decay, exit_decay, carry_all = tables
    keys_out = key_rows * exit_decay.T[:, :, None]
    local_state = jnp.einsum('jhd,jhe->hde', keys_out, value_rows, precision=highest)
    queries_in = query_rows * entry_decay.T[:, :, None]
    state_pull = jnp.einsum('ihd,ihe->hde', queries_in, grad_rows, precision=highest)
    return (carry_all, local_state, state_pull)

def block_outputs(query_rows, key_rows, value_rows, grad_rows, tables, state_in, state_grad):
    decay_mask, entry_decay, exit_decay, carry_all = tables
    entry_t = entry_decay.T[:, :, None]
    exit_t = exit_decay.T[:, :, None]
    scores = jnp.einsum('ihd,jhd->hij', query_rows, key_rows, precision=highest) * decay_mask
    attention = jnp.einsum('hij,jhe->ihe', scores, value_rows, precision=highest)
    attention = attention + entry_t * jnp.einsum('ihd,hde->ihe', query_rows, state_in, precision=highest)
    grads = jnp.einsum('ihe,jhe->hij', grad_rows, value_rows, precision=highest) * decay_mask
    query_grad = jnp.einsum('hij,jhd->ihd', grads, key_rows, precision=highest)
    query_grad = query_grad + entry_t * jnp.einsum('ihe,hde->ihd', grad_rows, state_in, precision=highest)
    key_grad = jnp.einsum('hij,ihd->jhd', grads, query_rows, precision=highest)
    key_grad = key_grad + exit_t * jnp.einsum('jhe,hde->jhd', value_rows, state_grad, precision=highest)
    value_grad = jnp.einsum('hij,ihe->jhe', scores, grad_rows, precision=highest)
    value_grad = value_grad + exit_t * jnp.einsum('jhd,hde->jhe', key_rows, state_grad, precision=highest)
    return (attention, query_grad, key_grad, value_grad)

def reference(queries, keys, values, out_grad, layer_grad, norm_gain, decay_rates, doc_lengths):
    block_count = LEN // TB
    grad_scale = 1.0 / math.sqrt(TOKENS)

    def one_sequence(inputs):
        query_seq, key_seq, value_seq, grad_seq, layer_seq, lengths = inputs

        def split_heads(array):
            return array.astype(jnp.float32).reshape(block_count, TB, HEADS, DH)
        query_rows = split_heads(query_seq)
        key_rows = split_heads(key_seq)
        value_rows = split_heads(value_seq)
        grad_rows = split_heads(grad_seq)
        positions = jnp.arange(LEN, dtype=jnp.int32).reshape(block_count, TB)
        doc_ids = doc_index(positions, lengths)
        prev_ids = doc_index(jnp.arange(block_count, dtype=jnp.int32) * TB - 1, lengths)
        last_ids = doc_ids[:, -1]
        tables = jax.vmap(decay_tables, in_axes=(None, 0, 0, 0))(decay_rates, doc_ids, prev_ids, last_ids)
        carry_all, local_state, state_pull = jax.vmap(block_summary)(query_rows, key_rows, value_rows, grad_rows, tables)

        def advance(state_now, element):
            return (element[0][:, None, None] * state_now + element[1], state_now)
        empty = jnp.zeros((HEADS, DH, DH), jnp.float32)
        states_in = lax.scan(advance, empty, (carry_all, local_state))[1]
        state_grads = lax.scan(advance, empty, (carry_all, state_pull), reverse=True)[1]
        attention, query_grad, key_grad, value_grad = jax.vmap(block_outputs)(query_rows, key_rows, value_rows, grad_rows, tables, states_in, state_grads)
        attention = attention.reshape(LEN, HD)
        normed = (attention * lax.rsqrt(lax.optimization_barrier(jnp.mean(attention * attention, axis=-1, keepdims=True)) + norm_eps) * norm_gain).astype(jnp.bfloat16)
        term = jnp.dot(normed.astype(jnp.float32).T, layer_seq.astype(jnp.float32), precision=highest)
        return (term, query_grad.reshape(LEN, HD).astype(jnp.bfloat16), key_grad.reshape(LEN, HD).astype(jnp.bfloat16), value_grad.reshape(LEN, HD).astype(jnp.bfloat16))
    terms, query_grad, key_grad, value_grad = lax.map(one_sequence, (queries, keys, values, out_grad, layer_grad, doc_lengths))
    proj_grad = lax.optimization_barrier(jnp.sum(terms, axis=0)) * grad_scale
    return (query_grad, key_grad, value_grad, proj_grad)
```

```python
import functools
import math

import jax
import jax.numpy as jnp
from jax import lax
from jax.experimental import pallas as pl
from jax.experimental.pallas import tpu as pltpu
from jax.sharding import PartitionSpec as P

norm_eps = 1e-06
f32 = jnp.float32
bf16 = jnp.bfloat16

CORES = 2
CHIPS = 4
PLANE = CORES * CHIPS
LONGEST = 2048

SMEM = pl.BlockSpec(memory_space=pltpu.SMEM)
VMEM = pl.BlockSpec(memory_space=pltpu.VMEM)


def dot(a, b, over_a, over_b):
    return lax.dot_general(a, b, (((over_a,), (over_b,)), ((), ())), preferred_element_type=f32)


def split(x):
    high = x.astype(bf16)
    return high, (x - high.astype(f32)).astype(bf16)


def dot2(a, b, over_a, over_b):
    if a.dtype == f32:
        high, low = split(a)
        return dot(high, b, over_a, over_b) + dot(low, b, over_a, over_b)
    high, low = split(b)
    return dot(a, high, over_a, over_b) + dot(a, low, over_a, over_b)


def doc_of(position, lens):
    bound = lens[0, 0]
    doc = jnp.where(position >= bound, 1, 0)
    for k in range(1, lens.shape[1] - 1):
        bound = bound + lens[0, k]
        doc = doc + jnp.where(position >= bound, 1, 0)
    return doc


def carry(from_edge, to_edge, rate, block, lens):
    same = doc_of(from_edge * block - 1, lens) == doc_of(to_edge * block - 1, lens)
    away = jnp.abs(from_edge - to_edge) * block
    row = jnp.full((1, 128), away.astype(f32) * -rate, f32)
    return jnp.where(same, jnp.exp(row), 0.0)


def entry_exit(here, rate, block, lens, dim, shape):
    offsets = lax.broadcasted_iota(jnp.int32, shape, dim)
    docs = doc_of(here * block + offsets, lens)
    into = jnp.where(docs == doc_of(here * block - 1, lens), jnp.exp(-rate * offsets.astype(f32)), 0.0)
    out = jnp.where(
        docs == doc_of(here * block + block - 1, lens), jnp.exp(-rate * (block - offsets).astype(f32)), 0.0
    )
    return into, out


def head_lanes(head, width):
    return pl.ds(pl.multiple_of(head * width, width), width)


def summary_kernel(here_ref, rates, lens, q, k, v, g, keep, send):
    here = here_ref[0]
    block = q.shape[0]
    half, _, width, _ = keep.shape
    core = lax.rem(here, CORES)
    for t in range(half):
        for side, out in ((core, keep), (1 - core, send)):
            head = side * half + t
            into, past = entry_exit(here, rates[head], block, lens, 0, (block, width))
            lanes = head_lanes(head, width)
            out[t, 0] = dot2(k[:, lanes].astype(f32) * past, v[:, lanes], 0, 0)
            out[t, 1] = dot2(q[:, lanes].astype(f32) * into, g[:, lanes], 0, 0)


def chip_kernel(here_ref, rates, lens, keep, recv, *outs, block):
    here = here_ref[0]
    half = keep.shape[0]
    part = half // CHIPS
    core = lax.rem(here, CORES)
    chip = lax.rem(here // CORES, CHIPS)
    edge = here - core
    first = core == 0
    for d in range(CHIPS):
        for t in range(part):
            row = (chip ^ d) * part + t
            rate = rates[core * half + row]
            late = carry(edge + 1, edge + 2, rate, block, lens)
            early = carry(edge + 1, edge, rate, block, lens)
            own_w, other_w = jnp.where(first, late, 1.0), jnp.where(first, 1.0, late)
            outs[d][t, 0] = own_w * keep[row, 0] + other_w * recv[row, 0]
            own_w, other_w = jnp.where(first, 1.0, early), jnp.where(first, early, 1.0)
            outs[d][t, 1] = own_w * keep[row, 1] + other_w * recv[row, 1]


def plane_kernel(here_ref, rates, lens, *refs, block, heads):
    here = here_ref[0]
    totals, (fwd, bwd) = refs[:CHIPS], refs[CHIPS:]
    part = fwd.shape[0]
    core = lax.rem(here, CORES)
    chip = lax.rem(here // CORES, CHIPS)
    base = here - lax.rem(here, PLANE)
    for t in range(part):
        rate = rates[core * (heads // CORES) + chip * part + t]
        sums = [0.0, 0.0]
        for d in range(CHIPS):
            edge = base + (chip ^ d) * CORES
            sums[0] = sums[0] + carry(edge + CORES, base + PLANE, rate, block, lens) * totals[d][t, 0]
            sums[1] = sums[1] + carry(edge, base, rate, block, lens) * totals[d][t, 1]
        fwd[t], bwd[t] = sums


def entry_kernel(here_ref, rates, lens, *refs, block, heads, reach):
    here = here_ref[0]
    totals, befores, afters = refs[:CHIPS], refs[CHIPS : CHIPS + reach], refs[CHIPS + reach : CHIPS + 2 * reach]
    outs = refs[CHIPS + 2 * reach :]
    part = outs[0].shape[0]
    core = lax.rem(here, CORES)
    chip = lax.rem(here // CORES, CHIPS)
    base = here - lax.rem(here, PLANE)
    for t in range(part):
        rate = rates[core * (heads // CORES) + chip * part + t]
        for to in range(CHIPS):
            at = chip ^ to
            start = base + at * CORES
            end = start + CORES
            sums = [0.0, 0.0]
            for d in range(CHIPS):
                if d == to:
                    continue
                other = chip ^ d
                edge = base + other * CORES
                w = jnp.where(other < at, carry(edge + CORES, start, rate, block, lens), 0.0)
                sums[0] = sums[0] + w * totals[d][t, 0]
                w = jnp.where(other > at, carry(edge, end, rate, block, lens), 0.0)
                sums[1] = sums[1] + w * totals[d][t, 1]
            for k in range(reach):
                sums[0] = sums[0] + carry(base - k * PLANE, start, rate, block, lens) * befores[k][t]
                sums[1] = sums[1] + carry(base + (k + 1) * PLANE, end, rate, block, lens) * afters[k][t]
            outs[to][t, 0], outs[to][t, 1] = sums


def states_kernel(here_ref, rates, lens, keep, recv, *refs, block):
    here = here_ref[0]
    entries, (mine, send) = refs[:CHIPS], refs[CHIPS:]
    half = keep.shape[0]
    part = half // CHIPS
    core = lax.rem(here, CORES)
    chip = lax.rem(here // CORES, CHIPS)
    edge = here - core
    first = core == 0
    for d in range(CHIPS):
        for t in range(part):
            row = (chip ^ d) * part + t
            rate = rates[core * half + row]
            before, after = entries[d][t, 0], entries[d][t, 1]
            state0 = jnp.where(first, keep[row, 0], recv[row, 0])
            pull1 = jnp.where(first, recv[row, 1], keep[row, 1])
            before1 = state0 + carry(edge, edge + 1, rate, block, lens) * before
            after0 = pull1 + carry(edge + 2, edge + 1, rate, block, lens) * after
            mine[row, 0] = jnp.where(first, before, before1)
            mine[row, 1] = jnp.where(first, after0, after)
            send[row, 0] = jnp.where(first, before1, before)
            send[row, 1] = jnp.where(first, after, after0)


def within_kernel(here_ref, rates, lens, gain, q, k, v, g, attn, gain_col, q_grad, k_grad, v_grad):
    here = here_ref[0]
    block, features = q.shape
    heads = rates.shape[0]
    width = features // heads
    shape = (block, block)
    at_j = lax.broadcasted_iota(jnp.int32, shape, 0)
    at_i = lax.broadcasted_iota(jnp.int32, shape, 1)
    docs_j = doc_of(here * block + at_j, lens)
    docs_i = doc_of(here * block + at_i, lens)
    away = jnp.maximum(at_i - at_j, 0).astype(f32)
    reached = (docs_i == docs_j) & (at_i >= at_j)
    for head in range(heads):
        lanes = slice(head * width, (head + 1) * width)
        qh, kh, vh, gh = q[:, lanes], k[:, lanes], v[:, lanes], g[:, lanes]
        decay = jnp.where(reached, jnp.exp(-rates[head] * away), 0.0)
        scores = dot(kh, qh, 1, 1) * decay
        grads = dot(vh, gh, 1, 1) * decay
        attn[lanes, :] = dot2(vh, scores, 0, 0)
        v_grad[:, lanes] = dot2(scores, gh, 1, 0)
        k_grad[:, lanes] = dot2(grads, qh, 1, 0)
        q_grad[:, lanes] = dot2(grads, kh, 0, 0)
        gain_col[lanes, :] = jnp.broadcast_to(gain[:, lanes], (block, width)).T


def norm_kernel(here_ref, rates, lens, q, attn, gain_col, mine, recv, keep, send, total, *, rows):
    here = here_ref[0]
    block, features = q.shape
    half = mine.shape[0]
    heads = 2 * half
    width = features // heads
    core = lax.rem(here, CORES)
    squares = jnp.zeros((width, block), f32)
    for t in range(half):
        for side, states in ((core, mine), (1 - core, recv)):
            head = side * half + t
            lanes = head_lanes(head, width)
            into, _ = entry_exit(here, rates[head], block, lens, 1, (width, block))
            state = states[t, 0]
            at = attn[lanes, :] + into * dot2(q[:, lanes], state, 1, 0).T
            total[lanes, :] = at
            squares = squares + at * at
    mean = jnp.sum(squares, axis=0, keepdims=True) * (1.0 / features)
    factor = lax.rsqrt(mean + norm_eps)
    count = features // rows
    for piece in range(count // CORES):
        chip, plane = piece // (count // PLANE), piece % (count // PLANE)
        for side, out in ((core, keep), (1 - core, send)):
            block_at = plane * PLANE + chip * CORES + side
            at = pl.ds(pl.multiple_of(block_at * rows, rows), rows)
            normed = (total[at, :] * factor * gain_col[at, :]).astype(bf16)
            out[piece * rows : (piece + 1) * rows, :] = normed.astype(f32)


def product_kernel(here_ref, keep, recv, layer, layer_recv, *outs, scale):
    here = here_ref[0]
    chip = lax.rem(here // CORES, CHIPS)
    rows = outs[0].shape[0]
    right = jnp.concatenate([layer[...], layer_recv[...].astype(bf16)], axis=0)
    for d in range(CHIPS):
        at = pl.ds(pl.multiple_of((chip ^ d) * rows, rows), rows)
        left = jnp.concatenate([keep[at, :].astype(bf16), recv[at, :].astype(bf16)], axis=1)
        outs[d][...] = dot(left, right, 1, 0) * scale


def outputs_kernel(here_ref, rates, lens, q, k, v, g, mine, recv, q_in, k_in, v_in, q_grad, k_grad, v_grad):
    here = here_ref[0]
    block, features = q.shape
    half = mine.shape[0]
    heads = 2 * half
    width = features // heads
    core = lax.rem(here, CORES)
    for t in range(half):
        for side, states in ((core, mine), (1 - core, recv)):
            head = side * half + t
            lanes = head_lanes(head, width)
            into, past = entry_exit(here, rates[head], block, lens, 0, (block, width))
            before, after = states[t, 0], states[t, 1]
            q_grad[:, lanes] = (q_in[:, lanes] + into * dot2(g[:, lanes], before, 1, 1)).astype(bf16)
            k_grad[:, lanes] = (k_in[:, lanes] + past * dot2(v[:, lanes], after, 1, 1)).astype(bf16)
            v_grad[:, lanes] = (v_in[:, lanes] + past * dot2(k[:, lanes], after, 1, 0)).astype(bf16)


def for_all_dp(keep, send, core, planes, dps):
    sides = jnp.stack([jnp.where(core == 0, keep, send), jnp.where(core == 0, send, keep)])
    rows = 2 * keep.shape[0] // (planes * PLANE)
    whole = sides.reshape(CORES, CHIPS, planes, rows, -1).transpose(2, 1, 0, 3, 4)
    whole = whole.reshape(dps, planes, CHIPS, CORES, rows // dps, -1).transpose(3, 2, 1, 0, 4, 5)
    sides = whole.reshape(sides.shape)
    return sides[core], sides[1 - core]


def call(kernel, specs, outs, name, scratch=(), flops=0, moved=0, **named):
    return pl.pallas_call(
        functools.partial(kernel, **named) if named else kernel,
        out_shape=[jax.ShapeDtypeStruct(shape, dtype) for shape, dtype in outs],
        in_specs=specs,
        out_specs=[VMEM] * len(outs),
        scratch_shapes=list(scratch),
        cost_estimate=pl.CostEstimate(flops=flops, bytes_accessed=moved, transcendentals=0),
        compiler_params=pltpu.CompilerParams(vmem_limit_bytes=32 * 1024 * 1024),
        name=name,
    )


def on_device(queries, keys, values, out_grad, layer_grad, norm_gain, decay_rates, doc_lengths):
    seqs, block, features = queries.shape
    assert seqs == 1
    heads = decay_rates.shape[0]
    width = features // heads
    columns = layer_grad.shape[2]
    half = heads // CORES
    part = half // CHIPS
    count = lax.axis_size("ctx")
    planes = count // PLANE
    dps = lax.axis_size("dp")
    scale = 1.0 / math.sqrt(seqs * block * dps * count)
    here = lax.axis_index("ctx").astype(jnp.int32).reshape(1)
    facts = (here, decay_rates, doc_lengths)
    q, k, v, g = (x.reshape(block, features) for x in (queries, keys, values, out_grad))
    layer = layer_grad.reshape(block, columns)

    def swap(x, bit):
        return lax.ppermute(x, "ctx", [(i, i ^ bit) for i in range(count)])

    def shift(x, by):
        return lax.ppermute(x, "ctx", [(i, i + by) for i in range(count) if 0 <= i + by < count])

    pair = (half, 2, width, width)
    small = (part, 2, width, width)
    keep, send = call(
        summary_kernel, [SMEM] * 3 + [VMEM] * 4, [(pair, f32)] * 2, "summary", flops=1 << 26, moved=1 << 21
    )(*facts, q, k, v, g)
    recv = swap(send, 1)
    layer_recv = swap(layer.astype(f32), 1)
    totals = call(
        chip_kernel, [SMEM] * 3 + [VMEM] * 2, [(small, f32)] * CHIPS, "chip_total", moved=1 << 20, block=block
    )(*facts, keep, recv)
    totals = [totals[0]] + [swap(totals[d], d * CORES) for d in range(1, CHIPS)]
    attn, gain_col, q_in, k_in, v_in = call(
        within_kernel,
        [SMEM] * 3 + [VMEM] * 5,
        [((features, block), f32)] * 2 + [((block, features), f32)] * 3,
        "within",
        flops=1 << 29,
        moved=1 << 22,
    )(*facts, norm_gain.reshape(1, features), q, k, v, g)
    one = (part, width, width)
    fwd, bwd = call(
        plane_kernel,
        [SMEM] * 3 + [VMEM] * CHIPS,
        [(one, f32)] * 2,
        "plane_total",
        moved=1 << 19,
        block=block,
        heads=heads,
    )(*facts, *totals)
    reach = min(planes - 1, -(-LONGEST // (PLANE * block)))
    befores = [shift(fwd, (far + 1) * PLANE) for far in range(reach)]
    afters = [shift(bwd, -(far + 1) * PLANE) for far in range(reach)]
    entries = call(
        entry_kernel,
        [SMEM] * 3 + [VMEM] * (CHIPS + 2 * reach),
        [(small, f32)] * CHIPS,
        "entries",
        moved=1 << 20,
        block=block,
        heads=heads,
        reach=reach,
    )(*facts, *totals, *befores, *afters)
    entries = [entries[0]] + [swap(entries[d], d * CORES) for d in range(1, CHIPS)]
    mine, others = call(
        states_kernel,
        [SMEM] * 3 + [VMEM] * (2 + CHIPS),
        [(pair, f32)] * 2,
        "states",
        moved=1 << 21,
        block=block,
    )(*facts, keep, recv, *entries)
    theirs = swap(others, 1)

    rows = features // count
    half_rows = ((features // CORES, block), f32)
    norm_keep, norm_send = call(
        norm_kernel,
        [SMEM] * 3 + [VMEM] * 5,
        [half_rows] * 2,
        "norm",
        scratch=[pltpu.VMEM((features, block), f32)],
        flops=1 << 26,
        moved=1 << 21,
        rows=rows,
    )(*facts, q, attn, gain_col, mine, theirs)
    if dps > 1:
        norm_keep, norm_send = for_all_dp(norm_keep, norm_send, here[0] % CORES, planes, dps)
    norm_recv = swap(norm_send, 1)
    pieces = call(
        product_kernel,
        [SMEM] + [VMEM] * 4,
        [((features // PLANE, columns), f32)] * CHIPS,
        "product",
        flops=1 << 28,
        moved=1 << 22,
        scale=scale,
    )(here, norm_keep, norm_recv, layer, layer_recv)
    summed = pieces[0]
    for d in range(1, CHIPS):
        summed = summed + swap(pieces[d], d * CORES)
    q_grad, k_grad, v_grad = call(
        outputs_kernel,
        [SMEM] * 3 + [VMEM] * 9,
        [((block, features), bf16)] * 3,
        "outputs",
        flops=1 << 27,
        moved=1 << 22,
    )(*facts, q, k, v, g, mine, theirs, q_in, k_in, v_in)
    by_plane = summed.reshape(planes, rows, columns)
    plane = here[0] // PLANE
    proj_grad = by_plane[plane]
    for d in range(1, planes):
        proj_grad = proj_grad + swap(by_plane[plane ^ d], d * PLANE)
    if dps > 1:
        proj_grad = lax.psum_scatter(proj_grad, "dp", scatter_dimension=0, tiled=True)
    shape_out = (seqs, block, features)
    return (q_grad.reshape(shape_out), k_grad.reshape(shape_out), v_grad.reshape(shape_out), proj_grad)


def solution(mesh):
    rows = P("dp", "ctx", None)
    return jax.shard_map(
        on_device,
        mesh=mesh,
        in_specs=(rows, rows, rows, rows, rows, P(), P(), P("dp", None)),
        out_specs=(rows, rows, rows, P(("dp", "ctx"), None)),
        check_vma=False,
    )
```

```python
import functools
import math

import jax
import jax.numpy as jnp
from jax import lax
from jax.experimental import pallas as pl
from jax.experimental.pallas import tpu as pltpu
from jax.sharding import PartitionSpec as P

norm_eps = 1e-06
f32 = jnp.float32
bf16 = jnp.bfloat16

CORES = 2
CHIPS = 4
PLANE = CORES * CHIPS

SMEM = pl.BlockSpec(memory_space=pltpu.SMEM)
VMEM = pl.BlockSpec(memory_space=pltpu.VMEM)


def dot(a, b, over_a, over_b):
    return lax.dot_general(a, b, (((over_a,), (over_b,)), ((), ())), preferred_element_type=f32)


def split(x):
    high = x.astype(bf16)
    return high, (x - high.astype(f32)).astype(bf16)


def dot2(a, b, over_a, over_b):
    if a.dtype == f32:
        high, low = split(a)
        return dot(high, b, over_a, over_b) + dot(low, b, over_a, over_b)
    high, low = split(b)
    return dot(a, high, over_a, over_b) + dot(a, low, over_a, over_b)


def doc_of(position, lens):
    bound = lens[0, 0]
    doc = jnp.where(position >= bound, 1, 0)
    for k in range(1, lens.shape[1] - 1):
        bound = bound + lens[0, k]
        doc = doc + jnp.where(position >= bound, 1, 0)
    return doc


def carry(from_edge, to_edge, rate, block, lens):
    same = doc_of(from_edge * block - 1, lens) == doc_of(to_edge * block - 1, lens)
    away = jnp.abs(from_edge - to_edge) * block
    row = jnp.full((1, 128), away.astype(f32) * -rate, f32)
    return jnp.where(same, jnp.exp(row), 0.0)


def entry_exit(here, rate, block, lens, dim, shape):
    offsets = lax.broadcasted_iota(jnp.int32, shape, dim)
    docs = doc_of(here * block + offsets, lens)
    into = jnp.where(docs == doc_of(here * block - 1, lens), jnp.exp(-rate * offsets.astype(f32)), 0.0)
    out = jnp.where(
        docs == doc_of(here * block + block - 1, lens), jnp.exp(-rate * (block - offsets).astype(f32)), 0.0
    )
    return into, out


def head_lanes(head, width):
    return pl.ds(pl.multiple_of(head * width, width), width)


def summary_kernel(here_ref, rates, lens, q, k, v, g, keep, send):
    here = here_ref[0]
    block = q.shape[0]
    half, _, width, _ = keep.shape
    core = lax.rem(here, CORES)
    for t in range(half):
        for side, out in ((core, keep), (1 - core, send)):
            head = side * half + t
            into, past = entry_exit(here, rates[head], block, lens, 0, (block, width))
            lanes = head_lanes(head, width)
            out[t, 0] = dot2(k[:, lanes].astype(f32) * past, v[:, lanes], 0, 0)
            out[t, 1] = dot2(q[:, lanes].astype(f32) * into, g[:, lanes], 0, 0)


def chip_kernel(here_ref, rates, lens, keep, recv, totals, *, block):
    here = here_ref[0]
    half = keep.shape[0]
    part = half // CHIPS
    core = lax.rem(here, CORES)
    edge = here - core
    first = core == 0
    for row in range(half):
        rate = rates[core * half + row]
        late = carry(edge + 1, edge + 2, rate, block, lens)
        early = carry(edge + 1, edge, rate, block, lens)
        own_w, other_w = jnp.where(first, late, 1.0), jnp.where(first, 1.0, late)
        totals[row // part, row % part, 0] = own_w * keep[row, 0] + other_w * recv[row, 0]
        own_w, other_w = jnp.where(first, 1.0, early), jnp.where(first, early, 1.0)
        totals[row // part, row % part, 1] = own_w * keep[row, 1] + other_w * recv[row, 1]


def plane_kernel(here_ref, rates, lens, totals, out, *, block, heads):
    here = here_ref[0]
    planes, part = out.shape[:2]
    core = lax.rem(here, CORES)
    chip = lax.rem(here // CORES, CHIPS)
    plane = here // PLANE
    base = plane * PLANE
    for t in range(part):
        rate = rates[core * (heads // CORES) + chip * part + t]
        fwd, bwd = 0.0, 0.0
        for other in range(CHIPS):
            edge = base + other * CORES
            fwd = fwd + carry(edge + CORES, base + PLANE, rate, block, lens) * totals[other, t, 0]
            bwd = bwd + carry(edge, base, rate, block, lens) * totals[other, t, 1]
        for to in range(planes):
            ahead = jnp.where(to > plane, carry(base + PLANE, to * PLANE, rate, block, lens), 0.0)
            behind = jnp.where(to < plane, carry(base, (to + 1) * PLANE, rate, block, lens), 0.0)
            out[to, t] = ahead * fwd + behind * bwd


def entry_kernel(here_ref, rates, lens, totals, others, out, *, block, heads):
    here = here_ref[0]
    planes, part = others.shape[:2]
    core = lax.rem(here, CORES)
    chip = lax.rem(here // CORES, CHIPS)
    plane = here // PLANE
    base = plane * PLANE
    for t in range(part):
        rate = rates[core * (heads // CORES) + chip * part + t]
        before, after = 0.0, 0.0
        for k in range(planes):
            before = before + jnp.where(k < plane, 1.0, 0.0) * others[k, t]
            after = after + jnp.where(k > plane, 1.0, 0.0) * others[k, t]
        for at in range(CHIPS):
            start = base + at * CORES
            end = start + CORES
            fwd = carry(base, start, rate, block, lens) * before
            bwd = carry(base + PLANE, end, rate, block, lens) * after
            for k in range(CHIPS):
                edge = base + k * CORES
                if k < at:
                    fwd = fwd + carry(edge + CORES, start, rate, block, lens) * totals[k, t, 0]
                elif k > at:
                    bwd = bwd + carry(edge, end, rate, block, lens) * totals[k, t, 1]
            out[at, t, 0], out[at, t, 1] = fwd, bwd


def states_kernel(here_ref, rates, lens, keep, recv, entries, mine, send, *, block):
    here = here_ref[0]
    half = keep.shape[0]
    part = half // CHIPS
    core = lax.rem(here, CORES)
    edge = here - core
    first = core == 0
    for row in range(half):
        rate = rates[core * half + row]
        before, after = entries[row // part, row % part, 0], entries[row // part, row % part, 1]
        state0 = jnp.where(first, keep[row, 0], recv[row, 0])
        pull1 = jnp.where(first, recv[row, 1], keep[row, 1])
        before1 = state0 + carry(edge, edge + 1, rate, block, lens) * before
        after0 = pull1 + carry(edge + 2, edge + 1, rate, block, lens) * after
        mine[row, 0] = jnp.where(first, before, before1)
        mine[row, 1] = jnp.where(first, after0, after)
        send[row, 0] = jnp.where(first, before1, before)
        send[row, 1] = jnp.where(first, after, after0)


def within_kernel(here_ref, rates, lens, gain, q, k, v, g, attn, gain_col, q_grad, k_grad, v_grad):
    here = here_ref[0]
    block, features = q.shape
    heads = rates.shape[0]
    width = features // heads
    shape = (block, block)
    at_j = lax.broadcasted_iota(jnp.int32, shape, 0)
    at_i = lax.broadcasted_iota(jnp.int32, shape, 1)
    docs_j = doc_of(here * block + at_j, lens)
    docs_i = doc_of(here * block + at_i, lens)
    away = jnp.maximum(at_i - at_j, 0).astype(f32)
    reached = (docs_i == docs_j) & (at_i >= at_j)
    for head in range(heads):
        lanes = slice(head * width, (head + 1) * width)
        qh, kh, vh, gh = q[:, lanes], k[:, lanes], v[:, lanes], g[:, lanes]
        decay = jnp.where(reached, jnp.exp(-rates[head] * away), 0.0)
        scores = dot(kh, qh, 1, 1) * decay
        grads = dot(vh, gh, 1, 1) * decay
        attn[lanes, :] = dot2(vh, scores, 0, 0)
        v_grad[:, lanes] = dot2(scores, gh, 1, 0)
        k_grad[:, lanes] = dot2(grads, qh, 1, 0)
        q_grad[:, lanes] = dot2(grads, kh, 0, 0)
        gain_col[lanes, :] = jnp.broadcast_to(gain[:, lanes], (block, width)).T


def norm_kernel(here_ref, rates, lens, q, attn, gain_col, mine, recv, out, total, *, rows):
    here = here_ref[0]
    block, features = q.shape
    half = mine.shape[0]
    heads = 2 * half
    width = features // heads
    core = lax.rem(here, CORES)
    squares = jnp.zeros((width, block), f32)
    for t in range(half):
        for side, states in ((core, mine), (1 - core, recv)):
            head = side * half + t
            lanes = head_lanes(head, width)
            into, _ = entry_exit(here, rates[head], block, lens, 1, (width, block))
            state = states[t, 0]
            at = attn[lanes, :] + into * dot2(q[:, lanes], state, 1, 0).T
            total[lanes, :] = at
            squares = squares + at * at
    mean = jnp.sum(squares, axis=0, keepdims=True) * (1.0 / features)
    factor = lax.rsqrt(mean + norm_eps)
    for k in range(features // rows):
        at = slice(k * rows, (k + 1) * rows)
        normed = (total[at, :] * factor * gain_col[at, :]).astype(bf16)
        plane, spot = k // PLANE, k % PLANE
        out[spot, plane * rows : (plane + 1) * rows, :] = normed.astype(f32)


def layer_kernel(layer, out):
    out[...] = layer[...].astype(bf16)


def product_kernel(normed, layer, out, *, scale):
    left = jnp.concatenate([normed[k].astype(bf16) for k in range(PLANE)], axis=1)
    product = dot(left, layer[...], 1, 0) * scale
    out[...] = product.reshape(out.shape)


def sum_kernel(parts, out):
    total = parts[0]
    for k in range(1, parts.shape[0]):
        total = total + parts[k]
    out[...] = total


def outputs_kernel(here_ref, rates, lens, q, k, v, g, mine, recv, q_in, k_in, v_in, q_grad, k_grad, v_grad):
    here = here_ref[0]
    block, features = q.shape
    half = mine.shape[0]
    heads = 2 * half
    width = features // heads
    core = lax.rem(here, CORES)
    for t in range(half):
        for side, states in ((core, mine), (1 - core, recv)):
            head = side * half + t
            lanes = head_lanes(head, width)
            into, past = entry_exit(here, rates[head], block, lens, 0, (block, width))
            before, after = states[t, 0], states[t, 1]
            q_grad[:, lanes] = (q_in[:, lanes] + into * dot2(g[:, lanes], before, 1, 1)).astype(bf16)
            k_grad[:, lanes] = (k_in[:, lanes] + past * dot2(v[:, lanes], after, 1, 1)).astype(bf16)
            v_grad[:, lanes] = (v_in[:, lanes] + past * dot2(k[:, lanes], after, 1, 0)).astype(bf16)


def for_all_dp(normed, planes, dps):
    spots, rows, block = normed.shape
    rows = rows // planes
    whole = normed.reshape(spots, planes, rows, block).swapaxes(0, 1)
    whole = whole.reshape(dps, planes, spots, rows // dps, block).transpose(2, 1, 0, 3, 4)
    return whole.reshape(normed.shape)


def call(kernel, specs, outs, name, scratch=(), flops=0, moved=0, **named):
    return pl.pallas_call(
        functools.partial(kernel, **named) if named else kernel,
        out_shape=[jax.ShapeDtypeStruct(shape, dtype) for shape, dtype in outs],
        in_specs=specs,
        out_specs=[VMEM] * len(outs),
        scratch_shapes=list(scratch),
        cost_estimate=pl.CostEstimate(flops=flops, bytes_accessed=moved, transcendentals=0),
        compiler_params=pltpu.CompilerParams(vmem_limit_bytes=32 * 1024 * 1024),
        name=name,
    )


def on_device(queries, keys, values, out_grad, layer_grad, norm_gain, decay_rates, doc_lengths):
    seqs, block, features = queries.shape
    assert seqs == 1
    heads = decay_rates.shape[0]
    width = features // heads
    columns = layer_grad.shape[2]
    half = heads // CORES
    part = half // CHIPS
    count = lax.axis_size("ctx")
    planes = count // PLANE
    dps = lax.axis_size("dp")
    scale = 1.0 / math.sqrt(seqs * block * dps * count)
    here = lax.axis_index("ctx").astype(jnp.int32).reshape(1)
    facts = (here, decay_rates, doc_lengths)
    q, k, v, g = (x.reshape(block, features) for x in (queries, keys, values, out_grad))
    layer = layer_grad.reshape(block, columns)

    def in_groups(x, groups):
        return lax.all_to_all(x, "ctx", 0, 0, axis_index_groups=groups, tiled=True)

    pairs = [(i, i ^ 1) for i in range(count)]
    plane_groups = [list(range(at, at + PLANE)) for at in range(0, count, PLANE)]
    chip_groups = [group[core::CORES] for group in plane_groups for core in range(CORES)]
    line_groups = [list(range(at, count, PLANE)) for at in range(PLANE)]

    pair = (half, 2, width, width)
    quarter = (CHIPS, part, 2, width, width)
    layer_all = lax.all_gather(layer.astype(f32), "ctx", axis_index_groups=plane_groups, tiled=True)
    keep, send = call(
        summary_kernel, [SMEM] * 3 + [VMEM] * 4, [(pair, f32)] * 2, "summary", flops=1 << 26, moved=1 << 21
    )(*facts, q, k, v, g)
    recv = lax.ppermute(send, "ctx", pairs)
    (totals,) = call(
        chip_kernel, [SMEM] * 3 + [VMEM] * 2, [(quarter, f32)], "chip_total", moved=1 << 20, block=block
    )(*facts, keep, recv)
    totals = in_groups(totals, chip_groups)
    attn, gain_col, q_in, k_in, v_in = call(
        within_kernel,
        [SMEM] * 3 + [VMEM] * 5,
        [((features, block), f32)] * 2 + [((block, features), f32)] * 3,
        "within",
        flops=1 << 29,
        moved=1 << 22,
    )(*facts, norm_gain.reshape(1, features), q, k, v, g)
    (onward,) = call(
        plane_kernel,
        [SMEM] * 3 + [VMEM],
        [((planes, part, width, width), f32)],
        "plane_total",
        moved=1 << 19,
        block=block,
        heads=heads,
    )(*facts, totals)
    others = in_groups(onward, line_groups)
    (entries,) = call(
        entry_kernel,
        [SMEM] * 3 + [VMEM] * 2,
        [(quarter, f32)],
        "entries",
        moved=1 << 20,
        block=block,
        heads=heads,
    )(*facts, totals, others)
    entries = in_groups(entries, chip_groups)
    mine, send = call(
        states_kernel, [SMEM] * 3 + [VMEM] * 3, [(pair, f32)] * 2, "states", moved=1 << 21, block=block
    )(*facts, keep, recv, entries)
    theirs = lax.ppermute(send, "ctx", pairs)

    rows = features // count
    (layer_all,) = call(layer_kernel, [VMEM], [((PLANE * block, columns), bf16)], "layer", moved=1 << 22)(layer_all)
    (normed,) = call(
        norm_kernel,
        [SMEM] * 3 + [VMEM] * 5,
        [((PLANE, planes * rows, block), f32)],
        "norm",
        scratch=[pltpu.VMEM((features, block), f32)],
        flops=1 << 26,
        moved=1 << 21,
        rows=rows,
    )(*facts, q, attn, gain_col, mine, theirs)
    if dps > 1:
        normed = for_all_dp(normed, planes, dps)
    normed = in_groups(normed, plane_groups)
    (product,) = call(
        product_kernel,
        [VMEM] * 2,
        [((planes, rows, columns), f32)],
        "product",
        flops=1 << 28,
        moved=1 << 22,
        scale=scale,
    )(normed, layer_all)
    parts = in_groups(product, line_groups)
    q_grad, k_grad, v_grad = call(
        outputs_kernel,
        [SMEM] * 3 + [VMEM] * 9,
        [((block, features), bf16)] * 3,
        "outputs",
        flops=1 << 27,
        moved=1 << 22,
    )(*facts, q, k, v, g, mine, theirs, q_in, k_in, v_in)
    (proj_grad,) = call(sum_kernel, [VMEM], [((rows, columns), f32)], "sum", moved=1 << 19)(parts)
    if dps > 1:
        proj_grad = lax.psum_scatter(proj_grad, "dp", scatter_dimension=0, tiled=True)
    shape_out = (seqs, block, features)
    return (q_grad.reshape(shape_out), k_grad.reshape(shape_out), v_grad.reshape(shape_out), proj_grad)


def solution(mesh):
    rows = P("dp", "ctx", None)
    return jax.shard_map(
        on_device,
        mesh=mesh,
        in_specs=(rows, rows, rows, rows, rows, P(), P(), P("dp", None)),
        out_specs=(rows, rows, rows, P(("dp", "ctx"), None)),
        check_vma=False,
    )
```

```python
import functools
import math

import jax
import jax.numpy as jnp
from jax import lax
from jax.experimental import pallas as pl
from jax.experimental.pallas import tpu as pltpu
from jax.sharding import PartitionSpec as P

norm_eps = 1e-06
f32 = jnp.float32
bf16 = jnp.bfloat16

CORES = 2
CHIPS = 4
PLANE = CORES * CHIPS

SMEM = pl.BlockSpec(memory_space=pltpu.SMEM)
VMEM = pl.BlockSpec(memory_space=pltpu.VMEM)
HBM = pl.BlockSpec(memory_space=pltpu.HBM)
LONGEST = 2048


def dot(a, b, over_a, over_b):
    return lax.dot_general(a, b, (((over_a,), (over_b,)), ((), ())), preferred_element_type=f32)


def split(x):
    high = x.astype(bf16)
    return high, (x - high.astype(f32)).astype(bf16)


def dot2(a, b, over_a, over_b):
    if a.dtype == f32:
        high, low = split(a)
        return dot(high, b, over_a, over_b) + dot(low, b, over_a, over_b)
    high, low = split(b)
    return dot(a, high, over_a, over_b) + dot(a, low, over_a, over_b)


def doc_of(position, lens):
    bound = lens[0, 0]
    doc = jnp.where(position >= bound, 1, 0)
    for k in range(1, lens.shape[1] - 1):
        bound = bound + lens[0, k]
        doc = doc + jnp.where(position >= bound, 1, 0)
    return doc


def carry(from_edge, to_edge, rate, block, lens):
    same = doc_of(from_edge * block - 1, lens) == doc_of(to_edge * block - 1, lens)
    away = jnp.abs(from_edge - to_edge) * block
    row = jnp.full((1, 128), away.astype(f32) * -rate, f32)
    return jnp.where(same, jnp.exp(row), 0.0)


def entry_exit(here, rate, block, lens, dim, shape):
    offsets = lax.broadcasted_iota(jnp.int32, shape, dim)
    docs = doc_of(here * block + offsets, lens)
    into = jnp.where(docs == doc_of(here * block - 1, lens), jnp.exp(-rate * offsets.astype(f32)), 0.0)
    out = jnp.where(
        docs == doc_of(here * block + block - 1, lens), jnp.exp(-rate * (block - offsets).astype(f32)), 0.0
    )
    return into, out


def head_lanes(head, width):
    return pl.ds(pl.multiple_of(head * width, width), width)


def fetch(refs, spaces, sems):
    copies = [pltpu.make_async_copy(ref, space, sems.at[i]) for i, (ref, space) in enumerate(zip(refs, spaces))]
    for copy in copies:
        copy.start()
    return copies


def summary_kernel(here_ref, rates_in, lens_in, q_in, k_in, v_in, g_in, keep, send, q, k, v, g, rates, lens, sems):
    copies = fetch((rates_in, lens_in, k_in, v_in, q_in, g_in), (rates, lens, k, v, q, g), sems)
    here = here_ref[0]
    block = q.shape[0]
    half, _, width, _ = keep.shape
    core = lax.rem(here, CORES)
    for copy in copies[:4]:
        copy.wait()
    for t in range(half):
        for side, out in ((1 - core, send), (core, keep)):
            head = side * half + t
            _, past = entry_exit(here, rates[head], block, lens, 0, (block, width))
            lanes = head_lanes(head, width)
            out[t, 0] = dot2(k[:, lanes].astype(f32) * past, v[:, lanes], 0, 0)
    for copy in copies[4:]:
        copy.wait()
    for t in range(half):
        for side, out in ((1 - core, send), (core, keep)):
            head = side * half + t
            into, _ = entry_exit(here, rates[head], block, lens, 0, (block, width))
            lanes = head_lanes(head, width)
            out[t, 1] = dot2(q[:, lanes].astype(f32) * into, g[:, lanes], 0, 0)


def chip_kernel(here_ref, rates, lens, keep, recv, *outs, block):
    here = here_ref[0]
    half = keep.shape[0]
    part = half // CHIPS
    core = lax.rem(here, CORES)
    chip = lax.rem(here // CORES, CHIPS)
    edge = here - core
    first = core == 0
    for d in range(CHIPS):
        for t in range(part):
            row = (chip ^ d) * part + t
            rate = rates[core * half + row]
            late = carry(edge + 1, edge + 2, rate, block, lens)
            early = carry(edge + 1, edge, rate, block, lens)
            own_w, other_w = jnp.where(first, late, 1.0), jnp.where(first, 1.0, late)
            outs[d][t, 0] = own_w * keep[row, 0] + other_w * recv[row, 0]
            own_w, other_w = jnp.where(first, 1.0, early), jnp.where(first, early, 1.0)
            outs[d][t, 1] = own_w * keep[row, 1] + other_w * recv[row, 1]


def plane_kernel(here_ref, rates, lens, *refs, block, heads):
    here = here_ref[0]
    totals, layer_in, outs, (layer, space, sems) = refs[:CHIPS], refs[CHIPS], refs[CHIPS + 1 : -3], refs[-3:]
    (copy,) = fetch([layer_in], [space], sems)
    part = outs[0].shape[0]
    core = lax.rem(here, CORES)
    chip = lax.rem(here // CORES, CHIPS)
    plane = here // PLANE
    base = plane * PLANE
    for t in range(part):
        rate = rates[core * (heads // CORES) + chip * part + t]
        fwd, bwd = 0.0, 0.0
        for d in range(CHIPS):
            edge = base + (chip ^ d) * CORES
            fwd = fwd + carry(edge + CORES, base + PLANE, rate, block, lens) * totals[d][t, 0]
            bwd = bwd + carry(edge, base, rate, block, lens) * totals[d][t, 1]
        for d, out in enumerate(outs, 1):
            to = plane ^ d
            ahead = jnp.where(to > plane, carry(base + PLANE, to * PLANE, rate, block, lens), 0.0)
            behind = jnp.where(to < plane, carry(base, (to + 1) * PLANE, rate, block, lens), 0.0)
            out[t] = ahead * fwd + behind * bwd
    copy.wait()
    layer[...] = space[...].astype(f32)


def entry_kernel(here_ref, rates, lens, *refs, block, heads, lines):
    here = here_ref[0]
    totals, others, outs = refs[:CHIPS], refs[CHIPS : CHIPS + lines], refs[CHIPS + lines :]
    part = outs[0].shape[0]
    core = lax.rem(here, CORES)
    chip = lax.rem(here // CORES, CHIPS)
    plane = here // PLANE
    base = plane * PLANE
    for t in range(part):
        rate = rates[core * (heads // CORES) + chip * part + t]
        before, after = 0.0, 0.0
        for d, other in enumerate(others, 1):
            before = before + jnp.where((plane ^ d) < plane, 1.0, 0.0) * other[t]
            after = after + jnp.where((plane ^ d) > plane, 1.0, 0.0) * other[t]
        for to in range(CHIPS):
            at = chip ^ to
            start = base + at * CORES
            end = start + CORES
            fwd = carry(base, start, rate, block, lens) * before
            bwd = carry(base + PLANE, end, rate, block, lens) * after
            for d in range(CHIPS):
                if d == to:
                    continue
                other = chip ^ d
                edge = base + other * CORES
                w = jnp.where(other < at, carry(edge + CORES, start, rate, block, lens), 0.0)
                fwd = fwd + w * totals[d][t, 0]
                w = jnp.where(other > at, carry(edge, end, rate, block, lens), 0.0)
                bwd = bwd + w * totals[d][t, 1]
            outs[to][t, 0], outs[to][t, 1] = fwd, bwd


def states_kernel(here_ref, rates, lens, keep, recv, *refs, block):
    here = here_ref[0]
    entries, layer_in, (mine, send, layer, space, sems) = refs[:CHIPS], refs[CHIPS], refs[CHIPS + 1 :]
    (copy,) = fetch([layer_in], [space], sems)
    half = keep.shape[0]
    part = half // CHIPS
    core = lax.rem(here, CORES)
    chip = lax.rem(here // CORES, CHIPS)
    edge = here - core
    first = core == 0
    for d in range(CHIPS):
        for t in range(part):
            row = (chip ^ d) * part + t
            rate = rates[core * half + row]
            before, after = entries[d][t, 0], entries[d][t, 1]
            state0 = jnp.where(first, keep[row, 0], recv[row, 0])
            pull1 = jnp.where(first, recv[row, 1], keep[row, 1])
            before1 = state0 + carry(edge, edge + 1, rate, block, lens) * before
            after0 = pull1 + carry(edge + 2, edge + 1, rate, block, lens) * after
            mine[row, 0] = jnp.where(first, before, before1)
            mine[row, 1] = jnp.where(first, after0, after)
            send[row, 0] = jnp.where(first, before1, before)
            send[row, 1] = jnp.where(first, after, after0)
    copy.wait()
    layer[...] = space[...].astype(f32)


def causal(here, block, lens):
    at_j = lax.broadcasted_iota(jnp.int32, (block, block), 0)
    at_i = lax.broadcasted_iota(jnp.int32, (block, block), 1)
    docs_j = doc_of(here * block + at_j, lens)
    docs_i = doc_of(here * block + at_i, lens)
    return (docs_i == docs_j) & (at_i >= at_j), jnp.maximum(at_i - at_j, 0).astype(f32)


def within_kernel(here_ref, rates, lens, gain, q_in, k_in, v_in, attn, gain_col, q, k, v, sems):
    copies = fetch((q_in, k_in, v_in), (q, k, v), sems)
    here = here_ref[0]
    block, features = q.shape
    heads = rates.shape[0]
    width = features // heads
    reached, away = causal(here, block, lens)
    for head in range(heads):
        lanes = slice(head * width, (head + 1) * width)
        gain_col[lanes, :] = jnp.broadcast_to(gain[:, lanes], (block, width)).T
    for copy in copies:
        copy.wait()
    for head in range(heads):
        lanes = slice(head * width, (head + 1) * width)
        decay = jnp.where(reached, jnp.exp(-rates[head] * away), 0.0)
        scores = dot(k[:, lanes], q[:, lanes], 1, 1) * decay
        attn[lanes, :] = dot2(v[:, lanes], scores, 0, 0)


def norm_kernel(here_ref, rates, lens, q_in, attn, gain_col, mine, recv, *refs, rows):
    outs, (total, q, sems) = refs[:CHIPS], refs[CHIPS:]
    (copy,) = fetch([q_in], [q], sems)
    here = here_ref[0]
    block, features = q.shape
    half = mine.shape[0]
    heads = 2 * half
    width = features // heads
    core = lax.rem(here, CORES)
    chip = lax.rem(here // CORES, CHIPS)
    squares = jnp.zeros((width, block), f32)
    copy.wait()
    for t in range(half):
        for side, states in ((core, mine), (1 - core, recv)):
            head = side * half + t
            lanes = head_lanes(head, width)
            into, _ = entry_exit(here, rates[head], block, lens, 1, (width, block))
            state = states[t, 0]
            at = attn[lanes, :] + into * dot2(q[:, lanes], state, 1, 0).T
            total[lanes, :] = at
            squares = squares + at * at
    mean = jnp.sum(squares, axis=0, keepdims=True) * (1.0 / features)
    factor = lax.rsqrt(mean + norm_eps)
    planes = features // (PLANE * rows)
    for d in range(CHIPS):
        for to_core in range(CORES):
            for plane in range(planes):
                block_at = plane * PLANE + (chip ^ d) * CORES + to_core
                at = pl.ds(pl.multiple_of(block_at * rows, rows), rows)
                normed = (total[at, :] * factor * gain_col[at, :]).astype(bf16)
                to = to_core * planes + plane
                outs[d][to * rows : (to + 1) * rows, :] = normed.astype(f32)


def product_kernel(here_ref, *refs, scale, other):
    core = lax.rem(here_ref[0], CORES)
    normed, layers, layer, out = refs[:CHIPS], refs[CHIPS : 2 * CHIPS - 1], refs[2 * CHIPS - 1], refs[-1]
    rows = out.shape[0] * out.shape[1]
    side = 1 - core if other else core
    at = pl.ds(pl.multiple_of(side * rows, rows), rows)
    left = jnp.concatenate([x[at, :].astype(bf16) for x in normed], axis=1)
    right = jnp.concatenate([layer[...]] + [x[...].astype(bf16) for x in layers], axis=0)
    product = (dot(left, right, 1, 0) * scale).reshape(out.shape)
    out[...] = product if other else product + refs[-2][...]


def sum_kernel(here_ref, own, *refs):
    plane = here_ref[0] // PLANE
    total = own[plane]
    for x in refs[:-1]:
        total = total + x[...]
    refs[-1][...] = total


def outputs_kernel(here_ref, rates, lens, q_in, k_in, v_in, g_in, mine, recv, q_out, k_out, v_out, *scratch):
    q, k, v, g, q_grad, k_grad, v_grad, sems = scratch
    copies = fetch((q_in, k_in, v_in, g_in), (q, k, v, g), sems)
    here = here_ref[0]
    block, features = q.shape
    half = mine.shape[0]
    heads = 2 * half
    width = features // heads
    core = lax.rem(here, CORES)
    reached, away = causal(here, block, lens)
    for copy in copies:
        copy.wait()
    for t in range(half):
        for side, states in ((core, mine), (1 - core, recv)):
            head = side * half + t
            lanes = head_lanes(head, width)
            rate = rates[head]
            qh, kh, vh, gh = q[:, lanes], k[:, lanes], v[:, lanes], g[:, lanes]
            decay = jnp.where(reached, jnp.exp(-rate * away), 0.0)
            scores = dot(kh, qh, 1, 1) * decay
            grads = dot(vh, gh, 1, 1) * decay
            into, past = entry_exit(here, rate, block, lens, 0, (block, width))
            before, after = states[t, 0], states[t, 1]
            q_grad[:, lanes] = (dot2(grads, kh, 0, 0) + into * dot2(gh, before, 1, 1)).astype(bf16)
            k_grad[:, lanes] = (dot2(grads, qh, 1, 0) + past * dot2(vh, after, 1, 1)).astype(bf16)
            v_grad[:, lanes] = (dot2(scores, gh, 1, 0) + past * dot2(kh, after, 1, 0)).astype(bf16)
    outs = [pltpu.make_async_copy(x, y, sems.at[i]) for i, (x, y) in enumerate(((q_grad, q_out), (k_grad, k_out), (v_grad, v_out)))]
    for copy in outs:
        copy.start()
    for copy in outs:
        copy.wait()


def for_all_dp(outs, here, planes, dps):
    order = (here // CORES) % CHIPS ^ jnp.arange(CHIPS)
    whole = jnp.stack(outs)[order]
    rows = whole.shape[1] // (CORES * planes)
    whole = whole.reshape(CHIPS, CORES, planes, rows, -1).transpose(2, 0, 1, 3, 4)
    whole = whole.reshape(dps, planes, CHIPS, CORES, rows // dps, -1).transpose(2, 3, 1, 0, 4, 5)
    whole = whole.reshape((CHIPS,) + outs[0].shape)[order]
    return [whole[d] for d in range(CHIPS)]


def call(kernel, specs, outs, name, scratch=(), flops=0, moved=0, out_specs=None, **named):
    return pl.pallas_call(
        functools.partial(kernel, **named) if named else kernel,
        out_shape=[jax.ShapeDtypeStruct(shape, dtype) for shape, dtype in outs],
        in_specs=specs,
        out_specs=out_specs or [VMEM] * len(outs),
        scratch_shapes=list(scratch),
        cost_estimate=pl.CostEstimate(flops=flops, bytes_accessed=moved, transcendentals=0),
        compiler_params=pltpu.CompilerParams(vmem_limit_bytes=16 * 1024 * 1024),
        name=name,
    )


def on_device(queries, keys, values, out_grad, layer_grad, norm_gain, decay_rates, doc_lengths):
    seqs, block, features = queries.shape
    assert seqs == 1
    heads = decay_rates.shape[0]
    width = features // heads
    columns = layer_grad.shape[2]
    half = heads // CORES
    part = half // CHIPS
    count = lax.axis_size("ctx")
    planes = count // PLANE
    dps = lax.axis_size("dp")
    scale = 1.0 / math.sqrt(seqs * block * dps * count)
    here = lax.axis_index("ctx").astype(jnp.int32).reshape(1)
    facts = (here, decay_rates, doc_lengths)
    q, k, v, g = (x.reshape(block, features) for x in (queries, keys, values, out_grad))
    layer = layer_grad.reshape(block, columns)

    def swap(x, bit, near=count):
        pairs = [(i, i ^ bit) for i in range(count) if abs(i // PLANE - (i ^ bit) // PLANE) <= near]
        return lax.ppermute(x, "ctx", pairs)

    def copies(number):
        return pltpu.SemaphoreType.DMA((number,))

    pair = ((half, 2, width, width), f32)
    small = ((part, 2, width, width), f32)
    one = ((part, width, width), f32)
    rows_in = pltpu.VMEM((block, features), bf16)
    layer_in = pltpu.VMEM((block, columns), bf16)
    layer_wide = ((block, columns), f32)
    keep, send = call(
        summary_kernel,
        [SMEM] + [HBM] * 6,
        [pair] * 2,
        "summary",
        scratch=[rows_in] * 4 + [pltpu.SMEM((heads,), f32), pltpu.SMEM(doc_lengths.shape, jnp.int32), copies(6)],
        flops=1 << 26,
        moved=1 << 21,
    )(*facts, q, k, v, g)
    recv = swap(send, 1)
    totals = call(
        chip_kernel, [SMEM] * 3 + [VMEM] * 2, [small] * CHIPS, "chip_total", moved=1 << 20, block=block
    )(*facts, keep, recv)
    totals = [totals[0]] + [swap(totals[d], d * CORES) for d in range(1, CHIPS)]
    near = -(-LONGEST // (PLANE * block))
    *onward, layer_f32 = call(
        plane_kernel,
        [SMEM] * 3 + [VMEM] * CHIPS + [HBM],
        [one] * (planes - 1) + [layer_wide],
        "plane_total",
        scratch=[layer_in, copies(1)],
        moved=1 << 19,
        block=block,
        heads=heads,
    )(*facts, *totals, layer)
    others = [swap(x, d * PLANE, near) for d, x in enumerate(onward, 1)]
    layers = [swap(layer_f32, d * CORES) for d in range(1, CHIPS - 1)]
    entries = call(
        entry_kernel,
        [SMEM] * 3 + [VMEM] * (CHIPS + len(others)),
        [small] * CHIPS,
        "entries",
        moved=1 << 20,
        block=block,
        heads=heads,
        lines=len(others),
    )(*facts, *totals, *others)
    entries = [entries[0]] + [swap(entries[d], d * CORES) for d in range(1, CHIPS)]
    mine, send, layer_f32 = call(
        states_kernel,
        [SMEM] * 3 + [VMEM] * (2 + CHIPS) + [HBM],
        [pair] * 2 + [layer_wide],
        "states",
        scratch=[layer_in, copies(1)],
        moved=1 << 21,
        block=block,
    )(*facts, keep, recv, *entries, layer)
    theirs = swap(send, 1)
    layers.append(swap(layer_f32, (CHIPS - 1) * CORES))
    attn, gain_col = call(
        within_kernel,
        [SMEM] * 3 + [VMEM] + [HBM] * 3,
        [((features, block), f32)] * 2,
        "within",
        scratch=[rows_in] * 3 + [copies(3)],
        flops=1 << 28,
        moved=1 << 22,
    )(*facts, norm_gain.reshape(1, features), q, k, v)

    rows = features // count
    normed = call(
        norm_kernel,
        [SMEM] * 3 + [HBM] + [VMEM] * 4,
        [((features // CHIPS, block), f32)] * CHIPS,
        "norm",
        scratch=[pltpu.VMEM((features, block), f32), rows_in, copies(1)],
        flops=1 << 26,
        moved=1 << 21,
        rows=rows,
    )(*facts, q, attn, gain_col, mine, theirs)
    if dps > 1:
        normed = for_all_dp(normed, here[0], planes, dps)
    normed = [normed[0]] + [swap(normed[d], d * CORES) for d in range(1, CHIPS)]
    by_plane = ((planes, rows, columns), f32)
    operands = (here, *normed, *layers, layer)
    specs = [SMEM] + [VMEM] * (2 * CHIPS)
    named = dict(flops=1 << 27, moved=1 << 22, scale=scale)
    (product,) = call(product_kernel, specs, [by_plane], "product_send", other=True, **named)(*operands)
    product = swap(product, 1)
    (product,) = call(product_kernel, specs + [VMEM], [by_plane], "product", other=False, **named)(*operands, product)
    plane = here[0] // PLANE
    parts = [swap(product[plane ^ d], d * PLANE) for d in range(1, planes)]
    q_grad, k_grad, v_grad = call(
        outputs_kernel,
        [SMEM] * 3 + [HBM] * 4 + [VMEM] * 2,
        [((block, features), bf16)] * 3,
        "outputs",
        scratch=[rows_in] * 7 + [copies(4)],
        out_specs=[HBM] * 3,
        flops=1 << 29,
        moved=1 << 22,
    )(*facts, q, k, v, g, mine, theirs)
    (proj_grad,) = call(
        sum_kernel, [SMEM] + [VMEM] * planes, [((rows, columns), f32)], "sum", moved=1 << 19
    )(here, product, *parts)
    if dps > 1:
        proj_grad = lax.psum_scatter(proj_grad, "dp", scatter_dimension=0, tiled=True)
    shape_out = (seqs, block, features)
    return (q_grad.reshape(shape_out), k_grad.reshape(shape_out), v_grad.reshape(shape_out), proj_grad)


def solution(mesh):
    rows = P("dp", "ctx", None)
    return jax.shard_map(
        on_device,
        mesh=mesh,
        in_specs=(rows, rows, rows, rows, rows, P(), P(), P("dp", None)),
        out_specs=(rows, rows, rows, P(("dp", "ctx"), None)),
        check_vma=False,
    )
```

```python
import functools
import math

import jax
import jax.numpy as jnp
from jax import lax
from jax.experimental import pallas as pl
from jax.experimental.pallas import tpu as pltpu
from jax.sharding import PartitionSpec as P

norm_eps = 1e-06
f32 = jnp.float32
bf16 = jnp.bfloat16

CORES = 2
CHIPS = 4
PLANE = CORES * CHIPS

SMEM = pl.BlockSpec(memory_space=pltpu.SMEM)
VMEM = pl.BlockSpec(memory_space=pltpu.VMEM)
HBM = pl.BlockSpec(memory_space=pltpu.HBM)
LONGEST = 2048


def dot(a, b, over_a, over_b):
    return lax.dot_general(a, b, (((over_a,), (over_b,)), ((), ())), preferred_element_type=f32)


def split(x):
    high = x.astype(bf16)
    return high, (x - high.astype(f32)).astype(bf16)


def dot2(a, b, over_a, over_b):
    if a.dtype == f32:
        high, low = split(a)
        return dot(high, b, over_a, over_b) + dot(low, b, over_a, over_b)
    high, low = split(b)
    return dot(a, high, over_a, over_b) + dot(a, low, over_a, over_b)


def doc_of(position, lens):
    bound = lens[0, 0]
    doc = jnp.where(position >= bound, 1, 0)
    for k in range(1, lens.shape[1] - 1):
        bound = bound + lens[0, k]
        doc = doc + jnp.where(position >= bound, 1, 0)
    return doc


def carry(from_edge, to_edge, rate, block, lens):
    same = doc_of(from_edge * block - 1, lens) == doc_of(to_edge * block - 1, lens)
    away = jnp.abs(from_edge - to_edge) * block
    row = jnp.full((1, 128), away.astype(f32) * -rate, f32)
    return jnp.where(same, jnp.exp(row), 0.0)


def entry_exit(here, rate, block, lens, dim, shape):
    offsets = lax.broadcasted_iota(jnp.int32, shape, dim)
    docs = doc_of(here * block + offsets, lens)
    into = jnp.where(docs == doc_of(here * block - 1, lens), jnp.exp(-rate * offsets.astype(f32)), 0.0)
    out = jnp.where(
        docs == doc_of(here * block + block - 1, lens), jnp.exp(-rate * (block - offsets).astype(f32)), 0.0
    )
    return into, out


def head_lanes(head, width):
    return pl.ds(pl.multiple_of(head * width, width), width)


def fetch(refs, spaces, sems):
    copies = [pltpu.make_async_copy(ref, space, sems.at[i]) for i, (ref, space) in enumerate(zip(refs, spaces))]
    for copy in copies:
        copy.start()
    return copies


def summary_kernel(here_ref, rates_in, lens_in, q_in, k_in, v_in, g_in, keep, send, q, k, v, g, rates, lens, sems):
    copies = fetch((rates_in, lens_in, k_in, v_in, q_in, g_in), (rates, lens, k, v, q, g), sems)
    here = here_ref[0]
    block = q.shape[0]
    half, _, width, _ = keep.shape
    core = lax.rem(here, CORES)
    for copy in copies[:4]:
        copy.wait()
    for t in range(half):
        for side, out in ((1 - core, send), (core, keep)):
            head = side * half + t
            _, past = entry_exit(here, rates[head], block, lens, 0, (block, width))
            lanes = head_lanes(head, width)
            out[t, 0] = dot2(k[:, lanes].astype(f32) * past, v[:, lanes], 0, 0)
    for copy in copies[4:]:
        copy.wait()
    for t in range(half):
        for side, out in ((1 - core, send), (core, keep)):
            head = side * half + t
            into, _ = entry_exit(here, rates[head], block, lens, 0, (block, width))
            lanes = head_lanes(head, width)
            out[t, 1] = dot2(q[:, lanes].astype(f32) * into, g[:, lanes], 0, 0)


def chip_kernel(here_ref, rates, lens, keep, recv, *outs, block):
    here = here_ref[0]
    half = keep.shape[0]
    part = half // CHIPS
    core = lax.rem(here, CORES)
    chip = lax.rem(here // CORES, CHIPS)
    edge = here - core
    first = core == 0
    for d in range(CHIPS):
        for t in range(part):
            row = (chip ^ d) * part + t
            rate = rates[core * half + row]
            late = carry(edge + 1, edge + 2, rate, block, lens)
            early = carry(edge + 1, edge, rate, block, lens)
            own_w, other_w = jnp.where(first, late, 1.0), jnp.where(first, 1.0, late)
            outs[d][t, 0] = own_w * keep[row, 0] + other_w * recv[row, 0]
            own_w, other_w = jnp.where(first, 1.0, early), jnp.where(first, early, 1.0)
            outs[d][t, 1] = own_w * keep[row, 1] + other_w * recv[row, 1]


def plane_kernel(here_ref, rates, lens, *refs, block, heads):
    here = here_ref[0]
    totals, layer_in, outs, (layer, space, sems) = refs[:CHIPS], refs[CHIPS], refs[CHIPS + 1 : -3], refs[-3:]
    (copy,) = fetch([layer_in], [space], sems)
    part = outs[0].shape[0]
    core = lax.rem(here, CORES)
    chip = lax.rem(here // CORES, CHIPS)
    plane = here // PLANE
    base = plane * PLANE
    for t in range(part):
        rate = rates[core * (heads // CORES) + chip * part + t]
        fwd, bwd = 0.0, 0.0
        for d in range(CHIPS):
            edge = base + (chip ^ d) * CORES
            fwd = fwd + carry(edge + CORES, base + PLANE, rate, block, lens) * totals[d][t, 0]
            bwd = bwd + carry(edge, base, rate, block, lens) * totals[d][t, 1]
        for d, out in enumerate(outs, 1):
            to = plane ^ d
            ahead = jnp.where(to > plane, carry(base + PLANE, to * PLANE, rate, block, lens), 0.0)
            behind = jnp.where(to < plane, carry(base, (to + 1) * PLANE, rate, block, lens), 0.0)
            out[t] = ahead * fwd + behind * bwd
    copy.wait()
    layer[...] = space[...].astype(f32)


def entry_kernel(here_ref, rates, lens, *refs, block, heads, lines):
    here = here_ref[0]
    totals, others, outs = refs[:CHIPS], refs[CHIPS : CHIPS + lines], refs[CHIPS + lines :]
    part = outs[0].shape[0]
    core = lax.rem(here, CORES)
    chip = lax.rem(here // CORES, CHIPS)
    plane = here // PLANE
    base = plane * PLANE
    for t in range(part):
        rate = rates[core * (heads // CORES) + chip * part + t]
        before, after = 0.0, 0.0
        for d, other in enumerate(others, 1):
            before = before + jnp.where((plane ^ d) < plane, 1.0, 0.0) * other[t]
            after = after + jnp.where((plane ^ d) > plane, 1.0, 0.0) * other[t]
        for to in range(CHIPS):
            at = chip ^ to
            start = base + at * CORES
            end = start + CORES
            fwd = carry(base, start, rate, block, lens) * before
            bwd = carry(base + PLANE, end, rate, block, lens) * after
            for d in range(CHIPS):
                if d == to:
                    continue
                other = chip ^ d
                edge = base + other * CORES
                w = jnp.where(other < at, carry(edge + CORES, start, rate, block, lens), 0.0)
                fwd = fwd + w * totals[d][t, 0]
                w = jnp.where(other > at, carry(edge, end, rate, block, lens), 0.0)
                bwd = bwd + w * totals[d][t, 1]
            outs[to][t, 0], outs[to][t, 1] = fwd, bwd


def states_kernel(here_ref, rates, lens, keep, recv, *refs, block):
    here = here_ref[0]
    entries, layer_in, (mine, send, layer, space, sems) = refs[:CHIPS], refs[CHIPS], refs[CHIPS + 1 :]
    (copy,) = fetch([layer_in], [space], sems)
    half = keep.shape[0]
    part = half // CHIPS
    core = lax.rem(here, CORES)
    chip = lax.rem(here // CORES, CHIPS)
    edge = here - core
    first = core == 0
    for d in range(CHIPS):
        for t in range(part):
            row = (chip ^ d) * part + t
            rate = rates[core * half + row]
            before, after = entries[d][t, 0], entries[d][t, 1]
            state0 = jnp.where(first, keep[row, 0], recv[row, 0])
            pull1 = jnp.where(first, recv[row, 1], keep[row, 1])
            before1 = state0 + carry(edge, edge + 1, rate, block, lens) * before
            after0 = pull1 + carry(edge + 2, edge + 1, rate, block, lens) * after
            mine[row, 0] = jnp.where(first, before, before1)
            mine[row, 1] = jnp.where(first, after0, after)
            send[row, 0] = jnp.where(first, before1, before)
            send[row, 1] = jnp.where(first, after, after0)
    copy.wait()
    layer[...] = space[...].astype(f32)


def causal(here, block, lens):
    at_j = lax.broadcasted_iota(jnp.int32, (block, block), 0)
    at_i = lax.broadcasted_iota(jnp.int32, (block, block), 1)
    docs_j = doc_of(here * block + at_j, lens)
    docs_i = doc_of(here * block + at_i, lens)
    return (docs_i == docs_j) & (at_i >= at_j), jnp.maximum(at_i - at_j, 0).astype(f32)


def within_kernel(here_ref, rates, lens, gain, q_in, k_in, v_in, attn, gain_col, q, k, v, sems):
    copies = fetch((q_in, k_in, v_in), (q, k, v), sems)
    here = here_ref[0]
    block, features = q.shape
    heads = rates.shape[0]
    width = features // heads
    reached, away = causal(here, block, lens)
    for head in range(heads):
        lanes = slice(head * width, (head + 1) * width)
        gain_col[lanes, :] = jnp.broadcast_to(gain[:, lanes], (block, width)).T
    for copy in copies:
        copy.wait()
    for head in range(heads):
        lanes = slice(head * width, (head + 1) * width)
        decay = jnp.where(reached, jnp.exp(-rates[head] * away), 0.0)
        scores = dot(k[:, lanes], q[:, lanes], 1, 1) * decay
        attn[lanes, :] = dot2(v[:, lanes], scores, 0, 0)


def norm_kernel(here_ref, rates, lens, q_in, attn, gain_col, mine, recv, *refs, rows):
    outs, (total, q, sems) = refs[:CHIPS], refs[CHIPS:]
    (copy,) = fetch([q_in], [q], sems)
    here = here_ref[0]
    block, features = q.shape
    half = mine.shape[0]
    heads = 2 * half
    width = features // heads
    core = lax.rem(here, CORES)
    chip = lax.rem(here // CORES, CHIPS)
    squares = jnp.zeros((width, block), f32)
    copy.wait()
    for t in range(half):
        for side, states in ((core, mine), (1 - core, recv)):
            head = side * half + t
            lanes = head_lanes(head, width)
            into, _ = entry_exit(here, rates[head], block, lens, 1, (width, block))
            state = states[t, 0]
            at = attn[lanes, :] + into * dot2(q[:, lanes], state, 1, 0).T
            total[lanes, :] = at
            squares = squares + at * at
    mean = jnp.sum(squares, axis=0, keepdims=True) * (1.0 / features)
    factor = lax.rsqrt(mean + norm_eps)
    planes = features // (PLANE * rows)
    for d in range(CHIPS):
        for to_core in range(CORES):
            for plane in range(planes):
                block_at = plane * PLANE + (chip ^ d) * CORES + to_core
                at = pl.ds(pl.multiple_of(block_at * rows, rows), rows)
                normed = (total[at, :] * factor * gain_col[at, :]).astype(bf16)
                to = to_core * planes + plane
                outs[d][to * rows : (to + 1) * rows, :] = normed.astype(f32)


def product_send_kernel(here_ref, *refs, scale):
    core = lax.rem(here_ref[0], CORES)
    normed, layers, layer, (out, left, right) = refs[:CHIPS], refs[CHIPS : 2 * CHIPS - 1], refs[-4], refs[-3:]
    rows = left.shape[0]
    block = layer.shape[0]
    mine = pl.ds(pl.multiple_of(core * rows, rows), rows)
    other = pl.ds(pl.multiple_of((1 - core) * rows, rows), rows)
    right[:block, :] = layer[...]
    for d, x in enumerate(layers, 1):
        right[d * block : (d + 1) * block, :] = x[...].astype(bf16)
    for d, x in enumerate(normed):
        left[:, d * block : (d + 1) * block] = x[mine, :].astype(bf16)
    send = jnp.concatenate([x[other, :].astype(bf16) for x in normed], axis=1)
    out[...] = (dot(send, right[...], 1, 0) * scale).reshape(out.shape)


def product_kernel(here_ref, left, right, recv, *refs, scale):
    outs, product = refs[:-1], refs[-1]
    plane = here_ref[0] // PLANE
    product[...] = (dot(left[...], right[...], 1, 0) * scale).reshape(product.shape)
    for d, out in enumerate(outs):
        out[...] = product[plane ^ d] + recv[plane ^ d]


def sum_kernel(*refs):
    total = refs[0][...]
    for x in refs[1:-1]:
        total = total + x[...]
    refs[-1][...] = total


def outputs_kernel(here_ref, rates, lens, q_in, k_in, v_in, g_in, mine, recv, q_out, k_out, v_out, *scratch):
    q, k, v, g, q_grad, k_grad, v_grad, sems = scratch
    copies = fetch((q_in, k_in, v_in, g_in), (q, k, v, g), sems)
    here = here_ref[0]
    block, features = q.shape
    half = mine.shape[0]
    heads = 2 * half
    width = features // heads
    core = lax.rem(here, CORES)
    reached, away = causal(here, block, lens)
    for copy in copies:
        copy.wait()
    for t in range(half):
        for side, states in ((core, mine), (1 - core, recv)):
            head = side * half + t
            lanes = head_lanes(head, width)
            rate = rates[head]
            qh, kh, vh, gh = q[:, lanes], k[:, lanes], v[:, lanes], g[:, lanes]
            decay = jnp.where(reached, jnp.exp(-rate * away), 0.0)
            scores = dot(kh, qh, 1, 1) * decay
            grads = dot(vh, gh, 1, 1) * decay
            into, past = entry_exit(here, rate, block, lens, 0, (block, width))
            before, after = states[t, 0], states[t, 1]
            q_grad[:, lanes] = (dot2(grads, kh, 0, 0) + into * dot2(gh, before, 1, 1)).astype(bf16)
            k_grad[:, lanes] = (dot2(grads, qh, 1, 0) + past * dot2(vh, after, 1, 1)).astype(bf16)
            v_grad[:, lanes] = (dot2(scores, gh, 1, 0) + past * dot2(kh, after, 1, 0)).astype(bf16)
    outs = [pltpu.make_async_copy(x, y, sems.at[i]) for i, (x, y) in enumerate(((q_grad, q_out), (k_grad, k_out), (v_grad, v_out)))]
    for copy in outs:
        copy.start()
    for copy in outs:
        copy.wait()


def for_all_dp(outs, here, planes, dps):
    order = (here // CORES) % CHIPS ^ jnp.arange(CHIPS)
    whole = jnp.stack(outs)[order]
    rows = whole.shape[1] // (CORES * planes)
    whole = whole.reshape(CHIPS, CORES, planes, rows, -1).transpose(2, 0, 1, 3, 4)
    whole = whole.reshape(dps, planes, CHIPS, CORES, rows // dps, -1).transpose(2, 3, 1, 0, 4, 5)
    whole = whole.reshape((CHIPS,) + outs[0].shape)[order]
    return [whole[d] for d in range(CHIPS)]


def call(kernel, specs, outs, name, scratch=(), flops=0, moved=0, out_specs=None, after=(), **named):
    reads = len(specs)

    def body(*refs):
        kernel(*refs[:reads], *refs[reads + len(after) :], **named)

    def run(*operands):
        operands = [
            pltpu.with_memory_space_constraint(x, pltpu.HBM) if spec is HBM else x for x, spec in zip(operands, specs)
        ]
        return pl.pallas_call(
            body,
            out_shape=[jax.ShapeDtypeStruct(shape, dtype) for shape, dtype in outs],
            in_specs=list(specs) + [pl.BlockSpec(memory_space=pl.ANY)] * len(after),
            out_specs=out_specs or [VMEM] * len(outs),
            scratch_shapes=list(scratch),
            cost_estimate=pl.CostEstimate(flops=flops, bytes_accessed=moved, transcendentals=0),
            compiler_params=pltpu.CompilerParams(vmem_limit_bytes=16 * 1024 * 1024),
            name=name,
        )(*operands, *after)

    return run


def on_device(queries, keys, values, out_grad, layer_grad, norm_gain, decay_rates, doc_lengths):
    seqs, block, features = queries.shape
    assert seqs == 1
    heads = decay_rates.shape[0]
    width = features // heads
    columns = layer_grad.shape[2]
    half = heads // CORES
    part = half // CHIPS
    count = lax.axis_size("ctx")
    planes = count // PLANE
    dps = lax.axis_size("dp")
    scale = 1.0 / math.sqrt(seqs * block * dps * count)
    here = lax.axis_index("ctx").astype(jnp.int32).reshape(1)
    facts = (here, decay_rates, doc_lengths)
    q, k, v, g = (x.reshape(block, features) for x in (queries, keys, values, out_grad))
    layer = layer_grad.reshape(block, columns)

    def swap(x, bit, near=count):
        pairs = [(i, i ^ bit) for i in range(count) if abs(i // PLANE - (i ^ bit) // PLANE) <= near]
        return lax.ppermute(x, "ctx", pairs)

    def copies(number):
        return pltpu.SemaphoreType.DMA((number,))

    pair = ((half, 2, width, width), f32)
    small = ((part, 2, width, width), f32)
    one = ((part, width, width), f32)
    rows_in = pltpu.VMEM((block, features), bf16)
    layer_in = pltpu.VMEM((block, columns), bf16)
    layer_wide = ((block, columns), f32)
    keep, send = call(
        summary_kernel,
        [SMEM] + [HBM] * 6,
        [pair] * 2,
        "summary",
        scratch=[rows_in] * 4 + [pltpu.SMEM((heads,), f32), pltpu.SMEM(doc_lengths.shape, jnp.int32), copies(6)],
        flops=1 << 26,
        moved=1 << 21,
    )(*facts, q, k, v, g)
    recv = swap(send, 1)
    totals = call(
        chip_kernel, [SMEM] * 3 + [VMEM] * 2, [small] * CHIPS, "chip_total", moved=1 << 20, block=block
    )(*facts, keep, recv)
    totals = [totals[0]] + [swap(totals[d], d * CORES) for d in range(1, CHIPS)]
    near = -(-LONGEST // (PLANE * block))
    *onward, layer_f32 = call(
        plane_kernel,
        [SMEM] * 3 + [VMEM] * CHIPS + [HBM],
        [one] * (planes - 1) + [layer_wide],
        "plane_total",
        scratch=[layer_in, copies(1)],
        moved=1 << 19,
        block=block,
        heads=heads,
    )(*facts, *totals, layer)
    others = [swap(x, d * PLANE, near) for d, x in enumerate(onward, 1)]
    layers = [swap(layer_f32, d * CORES) for d in range(1, CHIPS - 1)]
    entries = call(
        entry_kernel,
        [SMEM] * 3 + [VMEM] * (CHIPS + len(others)),
        [small] * CHIPS,
        "entries",
        moved=1 << 20,
        block=block,
        heads=heads,
        lines=len(others),
    )(*facts, *totals, *others)
    entries = [entries[0]] + [swap(entries[d], d * CORES) for d in range(1, CHIPS)]
    mine, send, layer_f32 = call(
        states_kernel,
        [SMEM] * 3 + [VMEM] * (2 + CHIPS) + [HBM],
        [pair] * 2 + [layer_wide],
        "states",
        scratch=[layer_in, copies(1)],
        moved=1 << 21,
        after=layers,
        block=block,
    )(*facts, keep, recv, *entries, layer)
    theirs = swap(send, 1)
    layers = layers + [swap(layer_f32, (CHIPS - 1) * CORES)]
    attn, gain_col = call(
        within_kernel,
        [SMEM] * 3 + [VMEM] + [HBM] * 3,
        [((features, block), f32)] * 2,
        "within",
        scratch=[rows_in] * 3 + [copies(3)],
        flops=1 << 28,
        moved=1 << 22,
    )(*facts, norm_gain.reshape(1, features), q, k, v)

    rows = features // count
    normed = call(
        norm_kernel,
        [SMEM] * 3 + [HBM] + [VMEM] * 4,
        [((features // CHIPS, block), f32)] * CHIPS,
        "norm",
        scratch=[pltpu.VMEM((features, block), f32), rows_in, copies(1)],
        flops=1 << 26,
        moved=1 << 21,
        rows=rows,
    )(*facts, q, attn, gain_col, mine, theirs)
    if dps > 1:
        normed = for_all_dp(normed, here[0], planes, dps)
    normed = [normed[0]] + [swap(normed[d], d * CORES) for d in range(1, CHIPS)]
    by_plane = ((planes, rows, columns), f32)
    product, left, right = call(
        product_send_kernel,
        [SMEM] + [VMEM] * (2 * CHIPS),
        [by_plane, ((planes * rows, CHIPS * block), bf16), ((CHIPS * block, columns), bf16)],
        "product_send",
        flops=1 << 27,
        moved=1 << 22,
        scale=scale,
    )(here, *normed, *layers, layer)
    parts = call(
        product_kernel,
        [SMEM] + [VMEM] * 3,
        [((rows, columns), f32)] * planes,
        "product",
        scratch=[pltpu.VMEM(*by_plane)],
        flops=1 << 27,
        moved=1 << 21,
        scale=scale,
    )(here, left, right, swap(product, 1))
    parts = [parts[0]] + [swap(parts[d], d * PLANE) for d in range(1, planes)]
    q_grad, k_grad, v_grad = call(
        outputs_kernel,
        [SMEM] * 3 + [HBM] * 4 + [VMEM] * 2,
        [((block, features), bf16)] * 3,
        "outputs",
        scratch=[rows_in] * 7 + [copies(4)],
        out_specs=[HBM] * 3,
        flops=1 << 29,
        moved=1 << 22,
    )(*facts, q, k, v, g, mine, theirs)
    (proj_grad,) = call(sum_kernel, [VMEM] * planes, [((rows, columns), f32)], "sum", moved=1 << 19)(*parts)
    if dps > 1:
        proj_grad = lax.psum_scatter(proj_grad, "dp", scatter_dimension=0, tiled=True)
    shape_out = (seqs, block, features)
    return (q_grad.reshape(shape_out), k_grad.reshape(shape_out), v_grad.reshape(shape_out), proj_grad)


def solution(mesh):
    rows = P("dp", "ctx", None)
    return jax.shard_map(
        on_device,
        mesh=mesh,
        in_specs=(rows, rows, rows, rows, rows, P(), P(), P("dp", None)),
        out_specs=(rows, rows, rows, P(("dp", "ctx"), None)),
        check_vma=False,
    )
```

```python
import functools
import math

import jax
import jax.numpy as jnp
from jax import lax
from jax.experimental import pallas as pl
from jax.experimental.pallas import tpu as pltpu
from jax.sharding import PartitionSpec as P

norm_eps = 1e-06
f32 = jnp.float32
bf16 = jnp.bfloat16

CORES = 2
CHIPS = 4
PLANE = CORES * CHIPS
ORDER = (0, 3, 1, 2)

SMEM = pl.BlockSpec(memory_space=pltpu.SMEM)
VMEM = pl.BlockSpec(memory_space=pltpu.VMEM)
HBM = pl.BlockSpec(memory_space=pltpu.HBM)
LONGEST = 2048


def dot(a, b, over_a, over_b):
    return lax.dot_general(a, b, (((over_a,), (over_b,)), ((), ())), preferred_element_type=f32)


def split(x):
    high = x.astype(bf16)
    return high, (x - high.astype(f32)).astype(bf16)


def dot2(a, b, over_a, over_b):
    if a.dtype == f32:
        high, low = split(a)
        return dot(high, b, over_a, over_b) + dot(low, b, over_a, over_b)
    high, low = split(b)
    return dot(a, high, over_a, over_b) + dot(a, low, over_a, over_b)


def doc_of(position, lens):
    bound = lens[0, 0]
    doc = jnp.where(position >= bound, 1, 0)
    for k in range(1, lens.shape[1] - 1):
        bound = bound + lens[0, k]
        doc = doc + jnp.where(position >= bound, 1, 0)
    return doc


def carry(from_edge, to_edge, rate, block, lens):
    same = doc_of(from_edge * block - 1, lens) == doc_of(to_edge * block - 1, lens)
    away = jnp.abs(from_edge - to_edge) * block
    row = jnp.full((1, 128), away.astype(f32) * -rate, f32)
    return jnp.where(same, jnp.exp(row), 0.0)


def entry_exit(here, rate, block, lens, dim, shape):
    offsets = lax.broadcasted_iota(jnp.int32, shape, dim)
    docs = doc_of(here * block + offsets, lens)
    into = jnp.where(docs == doc_of(here * block - 1, lens), jnp.exp(-rate * offsets.astype(f32)), 0.0)
    out = jnp.where(
        docs == doc_of(here * block + block - 1, lens), jnp.exp(-rate * (block - offsets).astype(f32)), 0.0
    )
    return into, out


def head_lanes(head, width):
    return pl.ds(pl.multiple_of(head * width, width), width)


def fetch(refs, spaces, sems):
    copies = [pltpu.make_async_copy(ref, space, sems.at[i]) for i, (ref, space) in enumerate(zip(refs, spaces))]
    for copy in copies:
        copy.start()
    return copies


def summary_kernel(
    here_ref, rates_in, lens_in, q_in, k_in, v_in, g_in, layer_in, keep, send, top, bottom, *scratch
):
    q, k, v, g, layer, rates, lens, sems = scratch
    copies = fetch((rates_in, lens_in, k_in, v_in, q_in, g_in, layer_in), (rates, lens, k, v, q, g, layer), sems)
    here = here_ref[0]
    block = q.shape[0]
    half, _, width, _ = keep.shape
    core = lax.rem(here, CORES)
    for copy in copies[:4]:
        copy.wait()
    for t in range(half):
        for side, out in ((1 - core, send), (core, keep)):
            head = side * half + t
            _, past = entry_exit(here, rates[head], block, lens, 0, (block, width))
            lanes = head_lanes(head, width)
            out[t, 0] = dot2(k[:, lanes].astype(f32) * past, v[:, lanes], 0, 0)
    for copy in copies[4:]:
        copy.wait()
    for t in range(half):
        for side, out in ((1 - core, send), (core, keep)):
            head = side * half + t
            into, _ = entry_exit(here, rates[head], block, lens, 0, (block, width))
            lanes = head_lanes(head, width)
            out[t, 1] = dot2(q[:, lanes].astype(f32) * into, g[:, lanes], 0, 0)
    top[...] = layer[: block // 2, :].astype(f32)
    bottom[...] = layer[block // 2 :, :].astype(f32)


def chip_kernel(here_ref, rates, lens, keep, recv, *outs, block):
    here = here_ref[0]
    half = keep.shape[0]
    part = half // CHIPS
    core = lax.rem(here, CORES)
    chip = lax.rem(here // CORES, CHIPS)
    edge = here - core
    first = core == 0
    for out, d in zip(outs, ORDER):
        for t in range(part):
            row = (chip ^ d) * part + t
            rate = rates[core * half + row]
            late = carry(edge + 1, edge + 2, rate, block, lens)
            early = carry(edge + 1, edge, rate, block, lens)
            own_w, other_w = jnp.where(first, late, 1.0), jnp.where(first, 1.0, late)
            out[t, 0] = own_w * keep[row, 0] + other_w * recv[row, 0]
            own_w, other_w = jnp.where(first, 1.0, early), jnp.where(first, early, 1.0)
            out[t, 1] = own_w * keep[row, 1] + other_w * recv[row, 1]


def line_order(planes):
    return [2, 1, 3] + list(range(4, planes)) if planes > 3 else list(range(planes - 1, 0, -1))


def plane_kernel(here_ref, rates, lens, *refs, block, heads):
    here = here_ref[0]
    totals, outs = refs[:CHIPS], refs[CHIPS:]
    part = outs[0].shape[0]
    core = lax.rem(here, CORES)
    chip = lax.rem(here // CORES, CHIPS)
    plane = here // PLANE
    base = plane * PLANE
    for t in range(part):
        rate = rates[core * (heads // CORES) + chip * part + t]
        fwd, bwd = 0.0, 0.0
        for total, d in zip(totals, ORDER):
            edge = base + (chip ^ d) * CORES
            fwd = fwd + carry(edge + CORES, base + PLANE, rate, block, lens) * total[t, 0]
            bwd = bwd + carry(edge, base, rate, block, lens) * total[t, 1]
        for out, d in zip(outs, line_order(len(outs) + 1)):
            to = plane ^ d
            ahead = jnp.where(to > plane, carry(base + PLANE, to * PLANE, rate, block, lens), 0.0)
            behind = jnp.where(to < plane, carry(base, (to + 1) * PLANE, rate, block, lens), 0.0)
            out[t] = ahead * fwd + behind * bwd


def forward_kernel(top, bottom, pass_top, pass_bottom):
    pass_top[...] = top[...]
    pass_bottom[...] = bottom[...]


def entry_kernel(here_ref, rates, lens, *refs, block, heads, lines):
    here = here_ref[0]
    totals, others, outs = refs[:CHIPS], refs[CHIPS : CHIPS + lines], refs[CHIPS + lines :]
    part = outs[0].shape[0]
    core = lax.rem(here, CORES)
    chip = lax.rem(here // CORES, CHIPS)
    plane = here // PLANE
    base = plane * PLANE
    for t in range(part):
        rate = rates[core * (heads // CORES) + chip * part + t]
        before, after = 0.0, 0.0
        for other, d in zip(others, line_order(lines + 1)):
            before = before + jnp.where((plane ^ d) < plane, 1.0, 0.0) * other[t]
            after = after + jnp.where((plane ^ d) > plane, 1.0, 0.0) * other[t]
        for out, to in zip(outs, ORDER):
            at = chip ^ to
            start = base + at * CORES
            end = start + CORES
            fwd = carry(base, start, rate, block, lens) * before
            bwd = carry(base + PLANE, end, rate, block, lens) * after
            for total, d in zip(totals, ORDER):
                if d == to:
                    continue
                other = chip ^ d
                edge = base + other * CORES
                w = jnp.where(other < at, carry(edge + CORES, start, rate, block, lens), 0.0)
                fwd = fwd + w * total[t, 0]
                w = jnp.where(other > at, carry(edge, end, rate, block, lens), 0.0)
                bwd = bwd + w * total[t, 1]
            out[t, 0], out[t, 1] = fwd, bwd


def states_kernel(here_ref, rates, lens, keep, recv, *refs, block):
    here = here_ref[0]
    entries, layer, (mine, send, top, bottom) = refs[:CHIPS], refs[CHIPS], refs[CHIPS + 1 :]
    half = keep.shape[0]
    part = half // CHIPS
    core = lax.rem(here, CORES)
    chip = lax.rem(here // CORES, CHIPS)
    edge = here - core
    first = core == 0
    for entry, d in zip(entries, ORDER):
        for t in range(part):
            row = (chip ^ d) * part + t
            rate = rates[core * half + row]
            before, after = entry[t, 0], entry[t, 1]
            state0 = jnp.where(first, keep[row, 0], recv[row, 0])
            pull1 = jnp.where(first, recv[row, 1], keep[row, 1])
            before1 = state0 + carry(edge, edge + 1, rate, block, lens) * before
            after0 = pull1 + carry(edge + 2, edge + 1, rate, block, lens) * after
            mine[row, 0] = jnp.where(first, before, before1)
            mine[row, 1] = jnp.where(first, after0, after)
            send[row, 0] = jnp.where(first, before1, before)
            send[row, 1] = jnp.where(first, after, after0)
    top[...] = layer[: block // 2, :].astype(f32)
    bottom[...] = layer[block // 2 :, :].astype(f32)


def causal(here, block, lens):
    at_j = lax.broadcasted_iota(jnp.int32, (block, block), 0)
    at_i = lax.broadcasted_iota(jnp.int32, (block, block), 1)
    docs_j = doc_of(here * block + at_j, lens)
    docs_i = doc_of(here * block + at_i, lens)
    return (docs_i == docs_j) & (at_i >= at_j), jnp.maximum(at_i - at_j, 0).astype(f32)


def within_kernel(here_ref, rates, lens, gain, q, k, v, attn, gain_col):
    here = here_ref[0]
    block, features = q.shape
    heads = rates.shape[0]
    width = features // heads
    reached, away = causal(here, block, lens)
    for head in range(heads):
        lanes = slice(head * width, (head + 1) * width)
        gain_col[lanes, :] = jnp.broadcast_to(gain[:, lanes], (block, width)).T
        decay = jnp.where(reached, jnp.exp(-rates[head] * away), 0.0)
        scores = dot(k[:, lanes], q[:, lanes], 1, 1) * decay
        attn[lanes, :] = dot2(v[:, lanes], scores, 0, 0)


def norm_kernel(here_ref, rates, lens, q, attn, gain_col, mine, recv, *refs, rows):
    outs, total = refs[:CHIPS], refs[CHIPS]
    here = here_ref[0]
    block, features = q.shape
    half = mine.shape[0]
    heads = 2 * half
    width = features // heads
    core = lax.rem(here, CORES)
    chip = lax.rem(here // CORES, CHIPS)
    squares = jnp.zeros((width, block), f32)
    for t in range(half):
        for side, states in ((core, mine), (1 - core, recv)):
            head = side * half + t
            lanes = head_lanes(head, width)
            into, _ = entry_exit(here, rates[head], block, lens, 1, (width, block))
            state = states[t, 0]
            at = attn[lanes, :] + into * dot2(q[:, lanes], state, 1, 0).T
            total[lanes, :] = at
            squares = squares + at * at
    mean = jnp.sum(squares, axis=0, keepdims=True) * (1.0 / features)
    factor = lax.rsqrt(mean + norm_eps)
    planes = features // (PLANE * rows)
    for out, d in zip(outs, ORDER):
        for to_core in range(CORES):
            for plane in range(planes):
                block_at = plane * PLANE + (chip ^ d) * CORES + to_core
                at = pl.ds(pl.multiple_of(block_at * rows, rows), rows)
                normed = (total[at, :] * factor * gain_col[at, :]).astype(bf16)
                to = to_core * planes + plane
                out[to * rows : (to + 1) * rows, :] = normed.astype(f32)


def product_send_kernel(here_ref, *refs, scale):
    core = lax.rem(here_ref[0], CORES)
    normed, layers, (layer, out, left, right) = refs[:CHIPS], refs[CHIPS:-4], refs[-4:]
    rows = left.shape[0]
    block = layer.shape[0]
    mine = pl.ds(pl.multiple_of(core * rows, rows), rows)
    other = pl.ds(pl.multiple_of((1 - core) * rows, rows), rows)
    right[:block, :] = layer[...]
    for k, x in enumerate(layers, 2):
        right[k * block // 2 : (k + 1) * block // 2, :] = x[...].astype(bf16)
    for d, x in enumerate(normed):
        left[:, d * block : (d + 1) * block] = x[mine, :].astype(bf16)
    send = jnp.concatenate([x[other, :].astype(bf16) for x in normed], axis=1)
    out[...] = (dot(send, right[...], 1, 0) * scale).reshape(out.shape)


def product_kernel(here_ref, left, right, recv, *refs, scale):
    outs, product = refs[:-1], refs[-1]
    plane = here_ref[0] // PLANE
    product[...] = (dot(left[...], right[...], 1, 0) * scale).reshape(product.shape)
    for out, d in zip(outs, [0] + line_order(len(outs))):
        out[...] = product[plane ^ d] + recv[plane ^ d]


def sum_kernel(*refs):
    total = refs[0][...]
    for x in refs[1:-1]:
        total = total + x[...]
    refs[-1][...] = total


def outputs_kernel(here_ref, rates, lens, q_in, k_in, v_in, g_in, mine, recv, q_out, k_out, v_out, *scratch):
    q, k, v, g, q_grad, k_grad, v_grad, sems = scratch
    copies = fetch((q_in, k_in, v_in, g_in), (q, k, v, g), sems)
    here = here_ref[0]
    block, features = q.shape
    half = mine.shape[0]
    heads = 2 * half
    width = features // heads
    core = lax.rem(here, CORES)
    reached, away = causal(here, block, lens)
    for copy in copies:
        copy.wait()
    for t in range(half):
        for side, states in ((core, mine), (1 - core, recv)):
            head = side * half + t
            lanes = head_lanes(head, width)
            rate = rates[head]
            qh, kh, vh, gh = q[:, lanes], k[:, lanes], v[:, lanes], g[:, lanes]
            decay = jnp.where(reached, jnp.exp(-rate * away), 0.0)
            scores = dot(kh, qh, 1, 1) * decay
            grads = dot(vh, gh, 1, 1) * decay
            into, past = entry_exit(here, rate, block, lens, 0, (block, width))
            before, after = states[t, 0], states[t, 1]
            q_grad[:, lanes] = (dot2(grads, kh, 0, 0) + into * dot2(gh, before, 1, 1)).astype(bf16)
            k_grad[:, lanes] = (dot2(grads, qh, 1, 0) + past * dot2(vh, after, 1, 1)).astype(bf16)
            v_grad[:, lanes] = (dot2(scores, gh, 1, 0) + past * dot2(kh, after, 1, 0)).astype(bf16)
    outs = [pltpu.make_async_copy(x, y, sems.at[i]) for i, (x, y) in enumerate(((q_grad, q_out), (k_grad, k_out), (v_grad, v_out)))]
    for copy in outs:
        copy.start()
    for copy in outs:
        copy.wait()


def for_all_dp(outs, here, planes, dps):
    order = (here // CORES) % CHIPS ^ jnp.array(ORDER)
    whole = jnp.zeros((CHIPS,) + outs[0].shape, f32).at[order].set(jnp.stack(outs))
    rows = whole.shape[1] // (CORES * planes)
    whole = whole.reshape(CHIPS, CORES, planes, rows, -1).transpose(2, 0, 1, 3, 4)
    whole = whole.reshape(dps, planes, CHIPS, CORES, rows // dps, -1).transpose(2, 3, 1, 0, 4, 5)
    whole = whole.reshape((CHIPS,) + outs[0].shape)[order]
    return [whole[d] for d in range(CHIPS)]


def call(kernel, specs, outs, name, scratch=(), flops=0, moved=0, out_specs=None, after=(), **named):
    reads = len(specs)

    def body(*refs):
        kernel(*refs[:reads], *refs[reads + len(after) :], **named)

    def run(*operands):
        operands = [
            pltpu.with_memory_space_constraint(x, pltpu.HBM) if spec is HBM else x for x, spec in zip(operands, specs)
        ]
        return pl.pallas_call(
            body,
            out_shape=[jax.ShapeDtypeStruct(shape, dtype) for shape, dtype in outs],
            in_specs=list(specs) + [pl.BlockSpec(memory_space=pl.ANY)] * len(after),
            out_specs=out_specs or [VMEM] * len(outs),
            scratch_shapes=list(scratch),
            cost_estimate=pl.CostEstimate(flops=flops, bytes_accessed=moved, transcendentals=0),
            compiler_params=pltpu.CompilerParams(vmem_limit_bytes=16 * 1024 * 1024),
            name=name,
        )(*operands, *after)

    return run


def on_device(queries, keys, values, out_grad, layer_grad, norm_gain, decay_rates, doc_lengths):
    seqs, block, features = queries.shape
    assert seqs == 1
    heads = decay_rates.shape[0]
    width = features // heads
    columns = layer_grad.shape[2]
    half = heads // CORES
    part = half // CHIPS
    count = lax.axis_size("ctx")
    planes = count // PLANE
    dps = lax.axis_size("dp")
    scale = 1.0 / math.sqrt(seqs * block * dps * count)
    here = lax.axis_index("ctx").astype(jnp.int32).reshape(1)
    facts = (here, decay_rates, doc_lengths)
    q, k, v, g = (x.reshape(block, features) for x in (queries, keys, values, out_grad))
    layer = layer_grad.reshape(block, columns)

    def swap(x, bit, near=count):
        pairs = [(i, i ^ bit) for i in range(count) if abs(i // PLANE - (i ^ bit) // PLANE) <= near]
        return lax.ppermute(x, "ctx", pairs)

    def in_plane(pieces):
        return [pieces[0]] + [swap(x, d * CORES) for x, d in zip(pieces[1:], ORDER[1:])]

    def in_line(pieces, near=count):
        return [swap(x, d * PLANE, near) for x, d in zip(pieces, line_order(planes))]

    pair = ((half, 2, width, width), f32)
    small = ((part, 2, width, width), f32)
    one = ((part, width, width), f32)
    rows_in = pltpu.VMEM((block, features), bf16)
    half_layer = ((block // 2, columns), f32)
    keep, send, top, bottom = call(
        summary_kernel,
        [SMEM] + [HBM] * 7,
        [pair] * 2 + [half_layer] * 2,
        "summary",
        scratch=[rows_in] * 4
        + [
            pltpu.VMEM((block, columns), bf16),
            pltpu.SMEM((heads,), f32),
            pltpu.SMEM(doc_lengths.shape, jnp.int32),
            pltpu.SemaphoreType.DMA((7,)),
        ],
        flops=1 << 26,
        moved=1 << 21,
    )(*facts, q, k, v, g, layer)
    recv = swap(send, 1)
    x_top, y_bottom = swap(top, CORES), swap(bottom, 2 * CORES)
    totals = call(
        chip_kernel, [SMEM] * 3 + [VMEM] * 2, [small] * CHIPS, "chip_total", moved=1 << 20, block=block
    )(*facts, keep, recv)
    totals = in_plane(totals)
    near = -(-LONGEST // (PLANE * block))
    onward = call(
        plane_kernel,
        [SMEM] * 3 + [VMEM] * CHIPS,
        [one] * (planes - 1),
        "plane_total",
        moved=1 << 19,
        after=[x_top, y_bottom],
        block=block,
        heads=heads,
    )(*facts, *totals)
    others = in_line(onward, near)
    pass_top, pass_bottom = call(
        forward_kernel, [VMEM] * 2, [half_layer] * 2, "forward", moved=1 << 20, after=others[:2][-1:]
    )(x_top, y_bottom)
    xy_top, xy_bottom = swap(pass_top, 2 * CORES), swap(pass_bottom, CORES)
    attn, gain_col = call(
        within_kernel,
        [SMEM] * 3 + [VMEM] * 4,
        [((features, block), f32)] * 2,
        "within",
        flops=1 << 28,
        moved=1 << 22,
    )(*facts, norm_gain.reshape(1, features), q, k, v)
    entries = call(
        entry_kernel,
        [SMEM] * 3 + [VMEM] * (CHIPS + len(others)),
        [small] * CHIPS,
        "entries",
        moved=1 << 20,
        block=block,
        heads=heads,
        lines=len(others),
    )(*facts, *totals, *others)
    entries = in_plane(entries)
    mine, send, top, bottom = call(
        states_kernel,
        [SMEM] * 3 + [VMEM] * (3 + CHIPS),
        [pair] * 2 + [half_layer] * 2,
        "states",
        moved=1 << 21,
        after=[xy_top, xy_bottom, attn],
        block=block,
    )(*facts, keep, recv, *entries, layer)
    theirs = swap(send, 1)
    x_bottom, y_top = swap(bottom, CORES), swap(top, 2 * CORES)

    rows = features // count
    normed = call(
        norm_kernel,
        [SMEM] * 3 + [VMEM] * 5,
        [((features // CHIPS, block), f32)] * CHIPS,
        "norm",
        scratch=[pltpu.VMEM((features, block), f32)],
        flops=1 << 26,
        moved=1 << 21,
        rows=rows,
    )(*facts, q, attn, gain_col, mine, theirs)
    if dps > 1:
        normed = for_all_dp(normed, here[0], planes, dps)
    normed = in_plane(normed)
    layers = [xy_top, xy_bottom, x_top, x_bottom, y_top, y_bottom]
    by_plane = ((planes, rows, columns), f32)
    product, left, right = call(
        product_send_kernel,
        [SMEM] + [VMEM] * (CHIPS + len(layers) + 1),
        [by_plane, ((planes * rows, CHIPS * block), bf16), ((CHIPS * block, columns), bf16)],
        "product_send",
        flops=1 << 27,
        moved=1 << 22,
        scale=scale,
    )(here, *normed, *layers, layer)
    parts = call(
        product_kernel,
        [SMEM] + [VMEM] * 3,
        [((rows, columns), f32)] * planes,
        "product",
        scratch=[pltpu.VMEM(*by_plane)],
        flops=1 << 27,
        moved=1 << 21,
        scale=scale,
    )(here, left, right, swap(product, 1))
    parts = [parts[0]] + in_line(parts[1:])
    q_grad, k_grad, v_grad = call(
        outputs_kernel,
        [SMEM] * 3 + [HBM] * 4 + [VMEM] * 2,
        [((block, features), bf16)] * 3,
        "outputs",
        scratch=[rows_in] * 7 + [pltpu.SemaphoreType.DMA((4,))],
        out_specs=[HBM] * 3,
        flops=1 << 29,
        moved=1 << 22,
    )(*facts, q, k, v, g, mine, theirs)
    (proj_grad,) = call(sum_kernel, [VMEM] * planes, [((rows, columns), f32)], "sum", moved=1 << 19)(*parts)
    if dps > 1:
        proj_grad = lax.psum_scatter(proj_grad, "dp", scatter_dimension=0, tiled=True)
    shape_out = (seqs, block, features)
    return (q_grad.reshape(shape_out), k_grad.reshape(shape_out), v_grad.reshape(shape_out), proj_grad)


def solution(mesh):
    rows = P("dp", "ctx", None)
    return jax.shard_map(
        on_device,
        mesh=mesh,
        in_specs=(rows, rows, rows, rows, rows, P(), P(), P("dp", None)),
        out_specs=(rows, rows, rows, P(("dp", "ctx"), None)),
        check_vma=False,
    )
```

```python
import functools
import math

import jax
import jax.numpy as jnp
from jax import lax
from jax.experimental import pallas as pl
from jax.experimental.pallas import tpu as pltpu
from jax.sharding import PartitionSpec as P

norm_eps = 1e-06
f32 = jnp.float32
bf16 = jnp.bfloat16

CORES = 2
CHIPS = 4
PLANE = CORES * CHIPS
ORDER = (0, 3, 1, 2)

SMEM = pl.BlockSpec(memory_space=pltpu.SMEM)
VMEM = pl.BlockSpec(memory_space=pltpu.VMEM)
HBM = pl.BlockSpec(memory_space=pltpu.HBM)
LONGEST = 2048


def dot(a, b, over_a, over_b):
    return lax.dot_general(a, b, (((over_a,), (over_b,)), ((), ())), preferred_element_type=f32)


def split(x):
    high = x.astype(bf16)
    return high, (x - high.astype(f32)).astype(bf16)


def dot2(a, b, over_a, over_b):
    if a.dtype == f32:
        high, low = split(a)
        return dot(high, b, over_a, over_b) + dot(low, b, over_a, over_b)
    high, low = split(b)
    return dot(a, high, over_a, over_b) + dot(a, low, over_a, over_b)


def doc_of(position, lens):
    bound = lens[0, 0]
    doc = jnp.where(position >= bound, 1, 0)
    for k in range(1, lens.shape[1] - 1):
        bound = bound + lens[0, k]
        doc = doc + jnp.where(position >= bound, 1, 0)
    return doc


def carry(from_edge, to_edge, rate, block, lens):
    same = doc_of(from_edge * block - 1, lens) == doc_of(to_edge * block - 1, lens)
    away = jnp.abs(from_edge - to_edge) * block
    row = jnp.full((1, 128), away.astype(f32) * -rate, f32)
    return jnp.where(same, jnp.exp(row), 0.0)


def entry_exit(here, rate, block, lens, dim, shape):
    offsets = lax.broadcasted_iota(jnp.int32, shape, dim)
    docs = doc_of(here * block + offsets, lens)
    into = jnp.where(docs == doc_of(here * block - 1, lens), jnp.exp(-rate * offsets.astype(f32)), 0.0)
    out = jnp.where(
        docs == doc_of(here * block + block - 1, lens), jnp.exp(-rate * (block - offsets).astype(f32)), 0.0
    )
    return into, out


def head_lanes(head, width):
    return pl.ds(pl.multiple_of(head * width, width), width)


def fetch(refs, spaces, sems):
    copies = [pltpu.make_async_copy(ref, space, sems.at[i]) for i, (ref, space) in enumerate(zip(refs, spaces))]
    for copy in copies:
        copy.start()
    return copies


def summary_kernel(
    here_ref, rates_in, lens_in, q_in, k_in, v_in, g_in, layer_in, keep, send, layer_wide, *scratch
):
    q, k, v, g, layer, rates, lens, sems = scratch
    copies = fetch((rates_in, lens_in, k_in, v_in, q_in, g_in, layer_in), (rates, lens, k, v, q, g, layer), sems)
    here = here_ref[0]
    block = q.shape[0]
    half, _, width, _ = keep.shape
    core = lax.rem(here, CORES)
    for copy in copies[:4]:
        copy.wait()
    for t in range(half):
        for side, out in ((1 - core, send), (core, keep)):
            head = side * half + t
            _, past = entry_exit(here, rates[head], block, lens, 0, (block, width))
            lanes = head_lanes(head, width)
            out[t, 0] = dot2(k[:, lanes].astype(f32) * past, v[:, lanes], 0, 0)
    for copy in copies[4:]:
        copy.wait()
    for t in range(half):
        for side, out in ((1 - core, send), (core, keep)):
            head = side * half + t
            into, _ = entry_exit(here, rates[head], block, lens, 0, (block, width))
            lanes = head_lanes(head, width)
            out[t, 1] = dot2(q[:, lanes].astype(f32) * into, g[:, lanes], 0, 0)
    layer_wide[...] = layer[...].astype(f32)


def chip_kernel(here_ref, rates, lens, keep, recv, *outs, block):
    here = here_ref[0]
    half = keep.shape[0]
    part = half // CHIPS
    core = lax.rem(here, CORES)
    chip = lax.rem(here // CORES, CHIPS)
    edge = here - core
    first = core == 0
    for out, d in zip(outs, ORDER):
        for t in range(part):
            row = (chip ^ d) * part + t
            rate = rates[core * half + row]
            late = carry(edge + 1, edge + 2, rate, block, lens)
            early = carry(edge + 1, edge, rate, block, lens)
            own_w, other_w = jnp.where(first, late, 1.0), jnp.where(first, 1.0, late)
            out[t, 0] = own_w * keep[row, 0] + other_w * recv[row, 0]
            own_w, other_w = jnp.where(first, 1.0, early), jnp.where(first, early, 1.0)
            out[t, 1] = own_w * keep[row, 1] + other_w * recv[row, 1]


def line_order(planes):
    return [2, 1, 3] + list(range(4, planes)) if planes > 3 else list(range(planes - 1, 0, -1))


def plane_kernel(here_ref, rates, lens, *refs, block, heads):
    here = here_ref[0]
    totals, outs = refs[:CHIPS], refs[CHIPS:]
    part = outs[0].shape[0]
    core = lax.rem(here, CORES)
    chip = lax.rem(here // CORES, CHIPS)
    plane = here // PLANE
    base = plane * PLANE
    for t in range(part):
        rate = rates[core * (heads // CORES) + chip * part + t]
        fwd, bwd = 0.0, 0.0
        for total, d in zip(totals, ORDER):
            edge = base + (chip ^ d) * CORES
            fwd = fwd + carry(edge + CORES, base + PLANE, rate, block, lens) * total[t, 0]
            bwd = bwd + carry(edge, base, rate, block, lens) * total[t, 1]
        for out, d in zip(outs, line_order(len(outs) + 1)):
            to = plane ^ d
            ahead = jnp.where(to > plane, carry(base + PLANE, to * PLANE, rate, block, lens), 0.0)
            behind = jnp.where(to < plane, carry(base, (to + 1) * PLANE, rate, block, lens), 0.0)
            out[t] = ahead * fwd + behind * bwd


def forward_kernel(layer_x, layer_y, top, bottom):
    top[...] = layer_x[: top.shape[0], :]
    bottom[...] = layer_y[top.shape[0] :, :]


def entry_kernel(here_ref, rates, lens, *refs, block, heads, lines):
    here = here_ref[0]
    totals, others, outs = refs[:CHIPS], refs[CHIPS : CHIPS + lines], refs[CHIPS + lines :]
    part = outs[0].shape[0]
    core = lax.rem(here, CORES)
    chip = lax.rem(here // CORES, CHIPS)
    plane = here // PLANE
    base = plane * PLANE
    for t in range(part):
        rate = rates[core * (heads // CORES) + chip * part + t]
        before, after = 0.0, 0.0
        for other, d in zip(others, line_order(lines + 1)):
            before = before + jnp.where((plane ^ d) < plane, 1.0, 0.0) * other[t]
            after = after + jnp.where((plane ^ d) > plane, 1.0, 0.0) * other[t]
        for out, to in zip(outs, ORDER):
            at = chip ^ to
            start = base + at * CORES
            end = start + CORES
            fwd = carry(base, start, rate, block, lens) * before
            bwd = carry(base + PLANE, end, rate, block, lens) * after
            for total, d in zip(totals, ORDER):
                if d == to:
                    continue
                other = chip ^ d
                edge = base + other * CORES
                w = jnp.where(other < at, carry(edge + CORES, start, rate, block, lens), 0.0)
                fwd = fwd + w * total[t, 0]
                w = jnp.where(other > at, carry(edge, end, rate, block, lens), 0.0)
                bwd = bwd + w * total[t, 1]
            out[t, 0], out[t, 1] = fwd, bwd


def states_kernel(here_ref, rates, lens, keep, recv, *refs, block):
    here = here_ref[0]
    entries, (mine, send) = refs[:CHIPS], refs[CHIPS:]
    half = keep.shape[0]
    part = half // CHIPS
    core = lax.rem(here, CORES)
    chip = lax.rem(here // CORES, CHIPS)
    edge = here - core
    first = core == 0
    for entry, d in zip(entries, ORDER):
        for t in range(part):
            row = (chip ^ d) * part + t
            rate = rates[core * half + row]
            before, after = entry[t, 0], entry[t, 1]
            state0 = jnp.where(first, keep[row, 0], recv[row, 0])
            pull1 = jnp.where(first, recv[row, 1], keep[row, 1])
            before1 = state0 + carry(edge, edge + 1, rate, block, lens) * before
            after0 = pull1 + carry(edge + 2, edge + 1, rate, block, lens) * after
            mine[row, 0] = jnp.where(first, before, before1)
            mine[row, 1] = jnp.where(first, after0, after)
            send[row, 0] = jnp.where(first, before1, before)
            send[row, 1] = jnp.where(first, after, after0)


def causal(here, block, lens):
    at_j = lax.broadcasted_iota(jnp.int32, (block, block), 0)
    at_i = lax.broadcasted_iota(jnp.int32, (block, block), 1)
    docs_j = doc_of(here * block + at_j, lens)
    docs_i = doc_of(here * block + at_i, lens)
    return (docs_i == docs_j) & (at_i >= at_j), jnp.maximum(at_i - at_j, 0).astype(f32)


def within_kernel(here_ref, rates, lens, gain, q, k, v, attn, gain_col):
    here = here_ref[0]
    block, features = q.shape
    heads = rates.shape[0]
    width = features // heads
    reached, away = causal(here, block, lens)
    for head in range(heads):
        lanes = slice(head * width, (head + 1) * width)
        gain_col[lanes, :] = jnp.broadcast_to(gain[:, lanes], (block, width)).T
        decay = jnp.where(reached, jnp.exp(-rates[head] * away), 0.0)
        scores = dot(k[:, lanes], q[:, lanes], 1, 1) * decay
        attn[lanes, :] = dot2(v[:, lanes], scores, 0, 0)


def norm_kernel(here_ref, rates, lens, q, attn, gain_col, mine, recv, *refs, rows):
    outs, total = refs[:CHIPS], refs[CHIPS]
    here = here_ref[0]
    block, features = q.shape
    half = mine.shape[0]
    heads = 2 * half
    width = features // heads
    core = lax.rem(here, CORES)
    chip = lax.rem(here // CORES, CHIPS)
    squares = jnp.zeros((width, block), f32)
    for t in range(half):
        for side, states in ((core, mine), (1 - core, recv)):
            head = side * half + t
            lanes = head_lanes(head, width)
            into, _ = entry_exit(here, rates[head], block, lens, 1, (width, block))
            state = states[t, 0]
            at = attn[lanes, :] + into * dot2(q[:, lanes], state, 1, 0).T
            total[lanes, :] = at
            squares = squares + at * at
    mean = jnp.sum(squares, axis=0, keepdims=True) * (1.0 / features)
    factor = lax.rsqrt(mean + norm_eps)
    planes = features // (PLANE * rows)
    for out, d in zip(outs, ORDER):
        for to_core in range(CORES):
            for plane in range(planes):
                block_at = plane * PLANE + (chip ^ d) * CORES + to_core
                at = pl.ds(pl.multiple_of(block_at * rows, rows), rows)
                normed = (total[at, :] * factor * gain_col[at, :]).astype(bf16)
                to = to_core * planes + plane
                out[to * rows : (to + 1) * rows, :] = normed.astype(f32)


def product_send_kernel(here_ref, *refs, scale):
    core = lax.rem(here_ref[0], CORES)
    normed, layers, (layer, out, left, right) = refs[:CHIPS], refs[CHIPS:-4], refs[-4:]
    rows = left.shape[0]
    block = layer.shape[0]
    mine = pl.ds(pl.multiple_of(core * rows, rows), rows)
    other = pl.ds(pl.multiple_of((1 - core) * rows, rows), rows)
    right[:block, :] = layer[...]
    at = block
    for x in layers:
        right[at : at + x.shape[0], :] = x[...].astype(bf16)
        at = at + x.shape[0]
    for d, x in enumerate(normed):
        left[:, d * block : (d + 1) * block] = x[mine, :].astype(bf16)
    send = jnp.concatenate([x[other, :].astype(bf16) for x in normed], axis=1)
    out[...] = (dot(send, right[...], 1, 0) * scale).reshape(out.shape)


def product_kernel(here_ref, left, right, recv, *refs, scale):
    outs, product = refs[:-1], refs[-1]
    plane = here_ref[0] // PLANE
    product[...] = (dot(left[...], right[...], 1, 0) * scale).reshape(product.shape)
    for out, d in zip(outs, [0] + line_order(len(outs))):
        out[...] = product[plane ^ d] + recv[plane ^ d]


def sum_kernel(*refs):
    total = refs[0][...]
    for x in refs[1:-1]:
        total = total + x[...]
    refs[-1][...] = total


def outputs_kernel(here_ref, rates, lens, q_in, k_in, v_in, g_in, mine, recv, q_out, k_out, v_out, *scratch):
    q, k, v, g, q_grad, k_grad, v_grad, sems = scratch
    copies = fetch((q_in, k_in, v_in, g_in), (q, k, v, g), sems)
    here = here_ref[0]
    block, features = q.shape
    half = mine.shape[0]
    heads = 2 * half
    width = features // heads
    core = lax.rem(here, CORES)
    reached, away = causal(here, block, lens)
    for copy in copies:
        copy.wait()
    for t in range(half):
        for side, states in ((core, mine), (1 - core, recv)):
            head = side * half + t
            lanes = head_lanes(head, width)
            rate = rates[head]
            qh, kh, vh, gh = q[:, lanes], k[:, lanes], v[:, lanes], g[:, lanes]
            decay = jnp.where(reached, jnp.exp(-rate * away), 0.0)
            scores = dot(kh, qh, 1, 1) * decay
            grads = dot(vh, gh, 1, 1) * decay
            into, past = entry_exit(here, rate, block, lens, 0, (block, width))
            before, after = states[t, 0], states[t, 1]
            q_grad[:, lanes] = (dot2(grads, kh, 0, 0) + into * dot2(gh, before, 1, 1)).astype(bf16)
            k_grad[:, lanes] = (dot2(grads, qh, 1, 0) + past * dot2(vh, after, 1, 1)).astype(bf16)
            v_grad[:, lanes] = (dot2(scores, gh, 1, 0) + past * dot2(kh, after, 1, 0)).astype(bf16)
    outs = [pltpu.make_async_copy(x, y, sems.at[i]) for i, (x, y) in enumerate(((q_grad, q_out), (k_grad, k_out), (v_grad, v_out)))]
    for copy in outs:
        copy.start()
    for copy in outs:
        copy.wait()


def for_all_dp(outs, here, planes, dps):
    order = (here // CORES) % CHIPS ^ jnp.array(ORDER)
    whole = jnp.zeros((CHIPS,) + outs[0].shape, f32).at[order].set(jnp.stack(outs))
    rows = whole.shape[1] // (CORES * planes)
    whole = whole.reshape(CHIPS, CORES, planes, rows, -1).transpose(2, 0, 1, 3, 4)
    whole = whole.reshape(dps, planes, CHIPS, CORES, rows // dps, -1).transpose(2, 3, 1, 0, 4, 5)
    whole = whole.reshape((CHIPS,) + outs[0].shape)[order]
    return [whole[d] for d in range(CHIPS)]


def call(kernel, specs, outs, name, scratch=(), flops=0, moved=0, out_specs=None, after=(), **named):
    reads = len(specs)

    def body(*refs):
        kernel(*refs[:reads], *refs[reads + len(after) :], **named)

    def run(*operands):
        operands = [
            pltpu.with_memory_space_constraint(x, pltpu.HBM) if spec is HBM else x for x, spec in zip(operands, specs)
        ]
        return pl.pallas_call(
            body,
            out_shape=[jax.ShapeDtypeStruct(shape, dtype) for shape, dtype in outs],
            in_specs=list(specs) + [pl.BlockSpec(memory_space=pl.ANY)] * len(after),
            out_specs=out_specs or [VMEM] * len(outs),
            scratch_shapes=list(scratch),
            cost_estimate=pl.CostEstimate(flops=flops, bytes_accessed=moved, transcendentals=0),
            compiler_params=pltpu.CompilerParams(vmem_limit_bytes=16 * 1024 * 1024),
            name=name,
        )(*operands, *after)

    return run


def on_device(queries, keys, values, out_grad, layer_grad, norm_gain, decay_rates, doc_lengths):
    seqs, block, features = queries.shape
    assert seqs == 1
    heads = decay_rates.shape[0]
    width = features // heads
    columns = layer_grad.shape[2]
    half = heads // CORES
    part = half // CHIPS
    count = lax.axis_size("ctx")
    planes = count // PLANE
    dps = lax.axis_size("dp")
    scale = 1.0 / math.sqrt(seqs * block * dps * count)
    here = lax.axis_index("ctx").astype(jnp.int32).reshape(1)
    facts = (here, decay_rates, doc_lengths)
    q, k, v, g = (x.reshape(block, features) for x in (queries, keys, values, out_grad))
    layer = layer_grad.reshape(block, columns)

    def swap(x, bit, near=count):
        pairs = [(i, i ^ bit) for i in range(count) if abs(i // PLANE - (i ^ bit) // PLANE) <= near]
        return lax.ppermute(x, "ctx", pairs)

    def in_plane(pieces):
        return [pieces[0]] + [swap(x, d * CORES) for x, d in zip(pieces[1:], ORDER[1:])]

    def in_line(pieces, near=count):
        return [swap(x, d * PLANE, near) for x, d in zip(pieces, line_order(planes))]

    pair = ((half, 2, width, width), f32)
    small = ((part, 2, width, width), f32)
    one = ((part, width, width), f32)
    rows_in = pltpu.VMEM((block, features), bf16)
    half_layer = ((block // 2, columns), f32)
    keep, send, layer_wide = call(
        summary_kernel,
        [SMEM] + [HBM] * 7,
        [pair] * 2 + [((block, columns), f32)],
        "summary",
        scratch=[rows_in] * 4
        + [
            pltpu.VMEM((block, columns), bf16),
            pltpu.SMEM((heads,), f32),
            pltpu.SMEM(doc_lengths.shape, jnp.int32),
            pltpu.SemaphoreType.DMA((7,)),
        ],
        flops=1 << 26,
        moved=1 << 21,
    )(*facts, q, k, v, g, layer)
    recv = swap(send, 1)
    layer_x, layer_y = swap(layer_wide, CORES), swap(layer_wide, 2 * CORES)
    totals = call(
        chip_kernel, [SMEM] * 3 + [VMEM] * 2, [small] * CHIPS, "chip_total", moved=1 << 20, block=block
    )(*facts, keep, recv)
    totals = in_plane(totals)
    near = -(-LONGEST // (PLANE * block))
    onward = call(
        plane_kernel,
        [SMEM] * 3 + [VMEM] * CHIPS,
        [one] * (planes - 1),
        "plane_total",
        moved=1 << 19,
        after=[layer_x, layer_y],
        block=block,
        heads=heads,
    )(*facts, *totals)
    others = in_line(onward, near)
    top, bottom = call(
        forward_kernel, [VMEM] * 2, [half_layer] * 2, "forward", moved=1 << 20
    )(layer_x, layer_y)
    xy_top, xy_bottom = swap(top, 2 * CORES), swap(bottom, CORES)
    attn, gain_col = call(
        within_kernel,
        [SMEM] * 3 + [VMEM] * 4,
        [((features, block), f32)] * 2,
        "within",
        flops=1 << 28,
        moved=1 << 22,
    )(*facts, norm_gain.reshape(1, features), q, k, v)
    entries = call(
        entry_kernel,
        [SMEM] * 3 + [VMEM] * (CHIPS + len(others)),
        [small] * CHIPS,
        "entries",
        moved=1 << 20,
        block=block,
        heads=heads,
        lines=len(others),
    )(*facts, *totals, *others)
    entries = in_plane(entries)
    mine, send = call(
        states_kernel,
        [SMEM] * 3 + [VMEM] * (2 + CHIPS),
        [pair] * 2,
        "states",
        moved=1 << 21,
        after=[xy_top, xy_bottom, attn],
        block=block,
    )(*facts, keep, recv, *entries)
    theirs = swap(send, 1)

    rows = features // count
    normed = call(
        norm_kernel,
        [SMEM] * 3 + [VMEM] * 5,
        [((features // CHIPS, block), f32)] * CHIPS,
        "norm",
        scratch=[pltpu.VMEM((features, block), f32)],
        flops=1 << 26,
        moved=1 << 21,
        rows=rows,
    )(*facts, q, attn, gain_col, mine, theirs)
    if dps > 1:
        normed = for_all_dp(normed, here[0], planes, dps)
    normed = in_plane(normed)
    layers = [xy_top, xy_bottom, layer_x, layer_y]
    by_plane = ((planes, rows, columns), f32)
    product, left, right = call(
        product_send_kernel,
        [SMEM] + [VMEM] * (CHIPS + len(layers) + 1),
        [by_plane, ((planes * rows, CHIPS * block), bf16), ((CHIPS * block, columns), bf16)],
        "product_send",
        flops=1 << 27,
        moved=1 << 22,
        scale=scale,
    )(here, *normed, *layers, layer)
    parts = call(
        product_kernel,
        [SMEM] + [VMEM] * 3,
        [((rows, columns), f32)] * planes,
        "product",
        scratch=[pltpu.VMEM(*by_plane)],
        flops=1 << 27,
        moved=1 << 21,
        scale=scale,
    )(here, left, right, swap(product, 1))
    parts = [parts[0]] + in_line(parts[1:])
    q_grad, k_grad, v_grad = call(
        outputs_kernel,
        [SMEM] * 3 + [HBM] * 4 + [VMEM] * 2,
        [((block, features), bf16)] * 3,
        "outputs",
        scratch=[rows_in] * 7 + [pltpu.SemaphoreType.DMA((4,))],
        out_specs=[HBM] * 3,
        flops=1 << 29,
        moved=1 << 22,
    )(*facts, q, k, v, g, mine, theirs)
    (proj_grad,) = call(sum_kernel, [VMEM] * planes, [((rows, columns), f32)], "sum", moved=1 << 19)(*parts)
    if dps > 1:
        proj_grad = lax.psum_scatter(proj_grad, "dp", scatter_dimension=0, tiled=True)
    shape_out = (seqs, block, features)
    return (q_grad.reshape(shape_out), k_grad.reshape(shape_out), v_grad.reshape(shape_out), proj_grad)


def solution(mesh):
    rows = P("dp", "ctx", None)
    return jax.shard_map(
        on_device,
        mesh=mesh,
        in_specs=(rows, rows, rows, rows, rows, P(), P(), P("dp", None)),
        out_specs=(rows, rows, rows, P(("dp", "ctx"), None)),
        check_vma=False,
    )
```

```python
import functools
import math

import jax
import jax.numpy as jnp
from jax import lax
from jax.experimental import pallas as pl
from jax.experimental.pallas import tpu as pltpu
from jax.sharding import PartitionSpec as P

norm_eps = 1e-06
f32 = jnp.float32
bf16 = jnp.bfloat16

CORES = 2
CHIPS = 4
PLANE = CORES * CHIPS
ORDER = (0, 1, 2, 3)

SMEM = pl.BlockSpec(memory_space=pltpu.SMEM)
VMEM = pl.BlockSpec(memory_space=pltpu.VMEM)
HBM = pl.BlockSpec(memory_space=pltpu.HBM)
LONGEST = 2048


def dot(a, b, over_a, over_b):
    return lax.dot_general(a, b, (((over_a,), (over_b,)), ((), ())), preferred_element_type=f32)


def split(x):
    high = x.astype(bf16)
    return high, (x - high.astype(f32)).astype(bf16)


def dot2(a, b, over_a, over_b):
    if a.dtype == f32:
        high, low = split(a)
        return dot(high, b, over_a, over_b) + dot(low, b, over_a, over_b)
    high, low = split(b)
    return dot(a, high, over_a, over_b) + dot(a, low, over_a, over_b)


def doc_of(position, lens):
    bound = lens[0, 0]
    doc = jnp.where(position >= bound, 1, 0)
    for k in range(1, lens.shape[1] - 1):
        bound = bound + lens[0, k]
        doc = doc + jnp.where(position >= bound, 1, 0)
    return doc


def carry(from_edge, to_edge, rate, block, lens):
    same = doc_of(from_edge * block - 1, lens) == doc_of(to_edge * block - 1, lens)
    away = jnp.abs(from_edge - to_edge) * block
    row = jnp.full((1, 128), away.astype(f32) * -rate, f32)
    return jnp.where(same, jnp.exp(row), 0.0)


def entry_exit(here, rate, block, lens, dim, shape):
    offsets = lax.broadcasted_iota(jnp.int32, shape, dim)
    docs = doc_of(here * block + offsets, lens)
    into = jnp.where(docs == doc_of(here * block - 1, lens), jnp.exp(-rate * offsets.astype(f32)), 0.0)
    out = jnp.where(
        docs == doc_of(here * block + block - 1, lens), jnp.exp(-rate * (block - offsets).astype(f32)), 0.0
    )
    return into, out


def head_lanes(head, width):
    return pl.ds(pl.multiple_of(head * width, width), width)


def fetch(refs, spaces, sems):
    copies = [pltpu.make_async_copy(ref, space, sems.at[i]) for i, (ref, space) in enumerate(zip(refs, spaces))]
    for copy in copies:
        copy.start()
    return copies


def summary_kernel(
    here_ref, rates_in, lens_in, q_in, k_in, v_in, g_in, layer_in, keep, send, top, bottom, *scratch
):
    q, k, v, g, layer, rates, lens, sems = scratch
    copies = fetch((rates_in, lens_in, k_in, v_in, q_in, g_in, layer_in), (rates, lens, k, v, q, g, layer), sems)
    here = here_ref[0]
    block = q.shape[0]
    half, _, width, _ = keep.shape
    core = lax.rem(here, CORES)
    for copy in copies[:4]:
        copy.wait()
    for t in range(half):
        for side, out in ((1 - core, send), (core, keep)):
            head = side * half + t
            _, past = entry_exit(here, rates[head], block, lens, 0, (block, width))
            lanes = head_lanes(head, width)
            out[t, 0] = dot2(k[:, lanes].astype(f32) * past, v[:, lanes], 0, 0)
    for copy in copies[4:]:
        copy.wait()
    for t in range(half):
        for side, out in ((1 - core, send), (core, keep)):
            head = side * half + t
            into, _ = entry_exit(here, rates[head], block, lens, 0, (block, width))
            lanes = head_lanes(head, width)
            out[t, 1] = dot2(q[:, lanes].astype(f32) * into, g[:, lanes], 0, 0)
    top[...] = layer[: block // 2, :].astype(f32)
    bottom[...] = layer[block // 2 :, :].astype(f32)


def chip_kernel(here_ref, rates, lens, keep, recv, *outs, block):
    here = here_ref[0]
    half = keep.shape[0]
    part = half // CHIPS
    core = lax.rem(here, CORES)
    chip = lax.rem(here // CORES, CHIPS)
    edge = here - core
    first = core == 0
    for out, d in zip(outs, ORDER):
        for t in range(part):
            row = (chip ^ d) * part + t
            rate = rates[core * half + row]
            late = carry(edge + 1, edge + 2, rate, block, lens)
            early = carry(edge + 1, edge, rate, block, lens)
            own_w, other_w = jnp.where(first, late, 1.0), jnp.where(first, 1.0, late)
            out[t, 0] = own_w * keep[row, 0] + other_w * recv[row, 0]
            own_w, other_w = jnp.where(first, 1.0, early), jnp.where(first, early, 1.0)
            out[t, 1] = own_w * keep[row, 1] + other_w * recv[row, 1]


def line_order(planes):
    return [2, 1, 3] + list(range(4, planes)) if planes > 3 else list(range(planes - 1, 0, -1))


def plane_kernel(here_ref, rates, lens, *refs, block, heads):
    here = here_ref[0]
    totals, outs = refs[:CHIPS], refs[CHIPS:]
    part = outs[0].shape[0]
    core = lax.rem(here, CORES)
    chip = lax.rem(here // CORES, CHIPS)
    plane = here // PLANE
    base = plane * PLANE
    for t in range(part):
        rate = rates[core * (heads // CORES) + chip * part + t]
        fwd, bwd = 0.0, 0.0
        for total, d in zip(totals, ORDER):
            edge = base + (chip ^ d) * CORES
            fwd = fwd + carry(edge + CORES, base + PLANE, rate, block, lens) * total[t, 0]
            bwd = bwd + carry(edge, base, rate, block, lens) * total[t, 1]
        for out, d in zip(outs, line_order(len(outs) + 1)):
            to = plane ^ d
            ahead = jnp.where(to > plane, carry(base + PLANE, to * PLANE, rate, block, lens), 0.0)
            behind = jnp.where(to < plane, carry(base, (to + 1) * PLANE, rate, block, lens), 0.0)
            out[t] = ahead * fwd + behind * bwd


def forward_kernel(top, bottom, pass_top, pass_bottom):
    pass_top[...] = top[...]
    pass_bottom[...] = bottom[...]


def entry_kernel(here_ref, rates, lens, *refs, block, heads, lines):
    here = here_ref[0]
    totals, others, outs = refs[:CHIPS], refs[CHIPS : CHIPS + lines], refs[CHIPS + lines :]
    part = outs[0].shape[0]
    core = lax.rem(here, CORES)
    chip = lax.rem(here // CORES, CHIPS)
    plane = here // PLANE
    base = plane * PLANE
    for t in range(part):
        rate = rates[core * (heads // CORES) + chip * part + t]
        before, after = 0.0, 0.0
        for other, d in zip(others, line_order(lines + 1)):
            before = before + jnp.where((plane ^ d) < plane, 1.0, 0.0) * other[t]
            after = after + jnp.where((plane ^ d) > plane, 1.0, 0.0) * other[t]
        for out, to in zip(outs, ORDER):
            at = chip ^ to
            start = base + at * CORES
            end = start + CORES
            fwd = carry(base, start, rate, block, lens) * before
            bwd = carry(base + PLANE, end, rate, block, lens) * after
            for total, d in zip(totals, ORDER):
                if d == to:
                    continue
                other = chip ^ d
                edge = base + other * CORES
                w = jnp.where(other < at, carry(edge + CORES, start, rate, block, lens), 0.0)
                fwd = fwd + w * total[t, 0]
                w = jnp.where(other > at, carry(edge, end, rate, block, lens), 0.0)
                bwd = bwd + w * total[t, 1]
            out[t, 0], out[t, 1] = fwd, bwd


def states_kernel(here_ref, rates, lens, keep, recv, *refs, block):
    here = here_ref[0]
    entries, layer, (mine, send, top, bottom) = refs[:CHIPS], refs[CHIPS], refs[CHIPS + 1 :]
    half = keep.shape[0]
    part = half // CHIPS
    core = lax.rem(here, CORES)
    chip = lax.rem(here // CORES, CHIPS)
    edge = here - core
    first = core == 0
    for entry, d in zip(entries, ORDER):
        for t in range(part):
            row = (chip ^ d) * part + t
            rate = rates[core * half + row]
            before, after = entry[t, 0], entry[t, 1]
            state0 = jnp.where(first, keep[row, 0], recv[row, 0])
            pull1 = jnp.where(first, recv[row, 1], keep[row, 1])
            before1 = state0 + carry(edge, edge + 1, rate, block, lens) * before
            after0 = pull1 + carry(edge + 2, edge + 1, rate, block, lens) * after
            mine[row, 0] = jnp.where(first, before, before1)
            mine[row, 1] = jnp.where(first, after0, after)
            send[row, 0] = jnp.where(first, before1, before)
            send[row, 1] = jnp.where(first, after, after0)
    top[...] = layer[: block // 2, :].astype(f32)
    bottom[...] = layer[block // 2 :, :].astype(f32)


def causal(here, block, lens):
    at_j = lax.broadcasted_iota(jnp.int32, (block, block), 0)
    at_i = lax.broadcasted_iota(jnp.int32, (block, block), 1)
    docs_j = doc_of(here * block + at_j, lens)
    docs_i = doc_of(here * block + at_i, lens)
    return (docs_i == docs_j) & (at_i >= at_j), jnp.maximum(at_i - at_j, 0).astype(f32)


def within_kernel(here_ref, rates, lens, gain, q, k, v, attn, gain_col):
    here = here_ref[0]
    block, features = q.shape
    heads = rates.shape[0]
    width = features // heads
    reached, away = causal(here, block, lens)
    for head in range(heads):
        lanes = slice(head * width, (head + 1) * width)
        gain_col[lanes, :] = jnp.broadcast_to(gain[:, lanes], (block, width)).T
        decay = jnp.where(reached, jnp.exp(-rates[head] * away), 0.0)
        scores = dot(k[:, lanes], q[:, lanes], 1, 1) * decay
        attn[lanes, :] = dot2(v[:, lanes], scores, 0, 0)


def norm_kernel(here_ref, rates, lens, q, attn, gain_col, mine, recv, *refs, rows):
    outs, total = refs[:CHIPS], refs[CHIPS]
    here = here_ref[0]
    block, features = q.shape
    half = mine.shape[0]
    heads = 2 * half
    width = features // heads
    core = lax.rem(here, CORES)
    chip = lax.rem(here // CORES, CHIPS)
    squares = jnp.zeros((width, block), f32)
    for t in range(half):
        for side, states in ((core, mine), (1 - core, recv)):
            head = side * half + t
            lanes = head_lanes(head, width)
            into, _ = entry_exit(here, rates[head], block, lens, 1, (width, block))
            state = states[t, 0]
            at = attn[lanes, :] + into * dot2(q[:, lanes], state, 1, 0).T
            total[lanes, :] = at
            squares = squares + at * at
    mean = jnp.sum(squares, axis=0, keepdims=True) * (1.0 / features)
    factor = lax.rsqrt(mean + norm_eps)
    planes = features // (PLANE * rows)
    for out, d in zip(outs, ORDER):
        for to_core in range(CORES):
            for plane in range(planes):
                block_at = plane * PLANE + (chip ^ d) * CORES + to_core
                at = pl.ds(pl.multiple_of(block_at * rows, rows), rows)
                normed = (total[at, :] * factor * gain_col[at, :]).astype(bf16)
                to = to_core * planes + plane
                out[to * rows : (to + 1) * rows, :] = normed.astype(f32)


def product_send_kernel(here_ref, *refs, scale):
    core = lax.rem(here_ref[0], CORES)
    normed, layers, (layer, out, left, right) = refs[:CHIPS], refs[CHIPS:-4], refs[-4:]
    rows = left.shape[0]
    block = layer.shape[0]
    mine = pl.ds(pl.multiple_of(core * rows, rows), rows)
    other = pl.ds(pl.multiple_of((1 - core) * rows, rows), rows)
    right[:block, :] = layer[...]
    for k, x in enumerate(layers, 2):
        right[k * block // 2 : (k + 1) * block // 2, :] = x[...].astype(bf16)
    for d, x in enumerate(normed):
        left[:, d * block : (d + 1) * block] = x[mine, :].astype(bf16)
    send = jnp.concatenate([x[other, :].astype(bf16) for x in normed], axis=1)
    out[...] = (dot(send, right[...], 1, 0) * scale).reshape(out.shape)


def product_kernel(here_ref, left, right, recv, *refs, scale):
    outs, product = refs[:-1], refs[-1]
    plane = here_ref[0] // PLANE
    product[...] = (dot(left[...], right[...], 1, 0) * scale).reshape(product.shape)
    for out, d in zip(outs, [0] + line_order(len(outs))):
        out[...] = product[plane ^ d] + recv[plane ^ d]


def sum_kernel(*refs):
    total = refs[0][...]
    for x in refs[1:-1]:
        total = total + x[...]
    refs[-1][...] = total


def outputs_kernel(here_ref, rates, lens, q_in, k_in, v_in, g_in, mine, recv, q_out, k_out, v_out, *scratch):
    q, k, v, g, q_grad, k_grad, v_grad, sems = scratch
    copies = fetch((q_in, k_in, v_in, g_in), (q, k, v, g), sems)
    here = here_ref[0]
    block, features = q.shape
    half = mine.shape[0]
    heads = 2 * half
    width = features // heads
    core = lax.rem(here, CORES)
    reached, away = causal(here, block, lens)
    for copy in copies:
        copy.wait()
    for t in range(half):
        for side, states in ((core, mine), (1 - core, recv)):
            head = side * half + t
            lanes = head_lanes(head, width)
            rate = rates[head]
            qh, kh, vh, gh = q[:, lanes], k[:, lanes], v[:, lanes], g[:, lanes]
            decay = jnp.where(reached, jnp.exp(-rate * away), 0.0)
            scores = dot(kh, qh, 1, 1) * decay
            grads = dot(vh, gh, 1, 1) * decay
            into, past = entry_exit(here, rate, block, lens, 0, (block, width))
            before, after = states[t, 0], states[t, 1]
            q_grad[:, lanes] = (dot2(grads, kh, 0, 0) + into * dot2(gh, before, 1, 1)).astype(bf16)
            k_grad[:, lanes] = (dot2(grads, qh, 1, 0) + past * dot2(vh, after, 1, 1)).astype(bf16)
            v_grad[:, lanes] = (dot2(scores, gh, 1, 0) + past * dot2(kh, after, 1, 0)).astype(bf16)
    outs = [pltpu.make_async_copy(x, y, sems.at[i]) for i, (x, y) in enumerate(((q_grad, q_out), (k_grad, k_out), (v_grad, v_out)))]
    for copy in outs:
        copy.start()
    for copy in outs:
        copy.wait()


def for_all_dp(outs, here, planes, dps):
    order = (here // CORES) % CHIPS ^ jnp.array(ORDER)
    whole = jnp.zeros((CHIPS,) + outs[0].shape, f32).at[order].set(jnp.stack(outs))
    rows = whole.shape[1] // (CORES * planes)
    whole = whole.reshape(CHIPS, CORES, planes, rows, -1).transpose(2, 0, 1, 3, 4)
    whole = whole.reshape(dps, planes, CHIPS, CORES, rows // dps, -1).transpose(2, 3, 1, 0, 4, 5)
    whole = whole.reshape((CHIPS,) + outs[0].shape)[order]
    return [whole[d] for d in range(CHIPS)]


def call(kernel, specs, outs, name, scratch=(), flops=0, moved=0, out_specs=None, after=(), **named):
    reads = len(specs)

    def body(*refs):
        kernel(*refs[:reads], *refs[reads + len(after) :], **named)

    def run(*operands):
        operands = [
            pltpu.with_memory_space_constraint(x, pltpu.HBM) if spec is HBM else x for x, spec in zip(operands, specs)
        ]
        return pl.pallas_call(
            body,
            out_shape=[jax.ShapeDtypeStruct(shape, dtype) for shape, dtype in outs],
            in_specs=list(specs) + [pl.BlockSpec(memory_space=pl.ANY)] * len(after),
            out_specs=out_specs or [VMEM] * len(outs),
            scratch_shapes=list(scratch),
            cost_estimate=pl.CostEstimate(flops=flops, bytes_accessed=moved, transcendentals=0),
            compiler_params=pltpu.CompilerParams(vmem_limit_bytes=16 * 1024 * 1024),
            name=name,
        )(*operands, *after)

    return run


def on_device(queries, keys, values, out_grad, layer_grad, norm_gain, decay_rates, doc_lengths):
    seqs, block, features = queries.shape
    assert seqs == 1
    heads = decay_rates.shape[0]
    width = features // heads
    columns = layer_grad.shape[2]
    half = heads // CORES
    part = half // CHIPS
    count = lax.axis_size("ctx")
    planes = count // PLANE
    dps = lax.axis_size("dp")
    scale = 1.0 / math.sqrt(seqs * block * dps * count)
    here = lax.axis_index("ctx").astype(jnp.int32).reshape(1)
    facts = (here, decay_rates, doc_lengths)
    q, k, v, g = (x.reshape(block, features) for x in (queries, keys, values, out_grad))
    layer = layer_grad.reshape(block, columns)

    def swap(x, bit, near=count):
        pairs = [(i, i ^ bit) for i in range(count) if abs(i // PLANE - (i ^ bit) // PLANE) <= near]
        return lax.ppermute(x, "ctx", pairs)

    def in_plane(pieces):
        return [pieces[0]] + [swap(x, d * CORES) for x, d in zip(pieces[1:], ORDER[1:])]

    def in_line(pieces, near=count):
        return [swap(x, d * PLANE, near) for x, d in zip(pieces, line_order(planes))]

    pair = ((half, 2, width, width), f32)
    small = ((part, 2, width, width), f32)
    one = ((part, width, width), f32)
    rows_in = pltpu.VMEM((block, features), bf16)
    half_layer = ((block // 2, columns), f32)
    keep, send, top, bottom = call(
        summary_kernel,
        [SMEM] + [HBM] * 7,
        [pair] * 2 + [half_layer] * 2,
        "summary",
        scratch=[rows_in] * 4
        + [
            pltpu.VMEM((block, columns), bf16),
            pltpu.SMEM((heads,), f32),
            pltpu.SMEM(doc_lengths.shape, jnp.int32),
            pltpu.SemaphoreType.DMA((7,)),
        ],
        flops=1 << 26,
        moved=1 << 21,
    )(*facts, q, k, v, g, layer)
    recv = swap(send, 1)
    x_top, y_bottom = swap(top, CORES), swap(bottom, 2 * CORES)
    totals = call(
        chip_kernel, [SMEM] * 3 + [VMEM] * 2, [small] * CHIPS, "chip_total", moved=1 << 20, block=block
    )(*facts, keep, recv)
    totals = in_plane(totals)
    near = -(-LONGEST // (PLANE * block))
    onward = call(
        plane_kernel,
        [SMEM] * 3 + [VMEM] * CHIPS,
        [one] * (planes - 1),
        "plane_total",
        moved=1 << 19,
        after=[x_top, y_bottom],
        block=block,
        heads=heads,
    )(*facts, *totals)
    others = in_line(onward, near)
    pass_top, pass_bottom = call(
        forward_kernel, [VMEM] * 2, [half_layer] * 2, "forward", moved=1 << 20, after=others[:2][-1:]
    )(x_top, y_bottom)
    xy_top, xy_bottom = swap(pass_top, 2 * CORES), swap(pass_bottom, CORES)
    attn, gain_col = call(
        within_kernel,
        [SMEM] * 3 + [VMEM] * 4,
        [((features, block), f32)] * 2,
        "within",
        flops=1 << 28,
        moved=1 << 22,
    )(*facts, norm_gain.reshape(1, features), q, k, v)
    entries = call(
        entry_kernel,
        [SMEM] * 3 + [VMEM] * (CHIPS + len(others)),
        [small] * CHIPS,
        "entries",
        moved=1 << 20,
        block=block,
        heads=heads,
        lines=len(others),
    )(*facts, *totals, *others)
    entries = in_plane(entries)
    mine, send, top, bottom = call(
        states_kernel,
        [SMEM] * 3 + [VMEM] * (3 + CHIPS),
        [pair] * 2 + [half_layer] * 2,
        "states",
        moved=1 << 21,
        after=[xy_top, xy_bottom, attn],
        block=block,
    )(*facts, keep, recv, *entries, layer)
    theirs = swap(send, 1)
    x_bottom, y_top = swap(bottom, CORES), swap(top, 2 * CORES)

    rows = features // count
    normed = call(
        norm_kernel,
        [SMEM] * 3 + [VMEM] * 5,
        [((features // CHIPS, block), f32)] * CHIPS,
        "norm",
        scratch=[pltpu.VMEM((features, block), f32)],
        flops=1 << 26,
        moved=1 << 21,
        rows=rows,
    )(*facts, q, attn, gain_col, mine, theirs)
    if dps > 1:
        normed = for_all_dp(normed, here[0], planes, dps)
    normed = in_plane(normed)
    layers = [x_top, x_bottom, y_top, y_bottom, xy_top, xy_bottom]
    by_plane = ((planes, rows, columns), f32)
    product, left, right = call(
        product_send_kernel,
        [SMEM] + [VMEM] * (CHIPS + len(layers) + 1),
        [by_plane, ((planes * rows, CHIPS * block), bf16), ((CHIPS * block, columns), bf16)],
        "product_send",
        flops=1 << 27,
        moved=1 << 22,
        scale=scale,
    )(here, *normed, *layers, layer)
    parts = call(
        product_kernel,
        [SMEM] + [VMEM] * 3,
        [((rows, columns), f32)] * planes,
        "product",
        scratch=[pltpu.VMEM(*by_plane)],
        flops=1 << 27,
        moved=1 << 21,
        scale=scale,
    )(here, left, right, swap(product, 1))
    parts = [parts[0]] + in_line(parts[1:])
    q_grad, k_grad, v_grad = call(
        outputs_kernel,
        [SMEM] * 3 + [HBM] * 4 + [VMEM] * 2,
        [((block, features), bf16)] * 3,
        "outputs",
        scratch=[rows_in] * 7 + [pltpu.SemaphoreType.DMA((4,))],
        out_specs=[HBM] * 3,
        flops=1 << 29,
        moved=1 << 22,
    )(*facts, q, k, v, g, mine, theirs)
    (proj_grad,) = call(sum_kernel, [VMEM] * planes, [((rows, columns), f32)], "sum", moved=1 << 19)(*parts)
    if dps > 1:
        proj_grad = lax.psum_scatter(proj_grad, "dp", scatter_dimension=0, tiled=True)
    shape_out = (seqs, block, features)
    return (q_grad.reshape(shape_out), k_grad.reshape(shape_out), v_grad.reshape(shape_out), proj_grad)


def solution(mesh):
    rows = P("dp", "ctx", None)
    return jax.shard_map(
        on_device,
        mesh=mesh,
        in_specs=(rows, rows, rows, rows, rows, P(), P(), P("dp", None)),
        out_specs=(rows, rows, rows, P(("dp", "ctx"), None)),
        check_vma=False,
    )
```

```python
import functools
import math

import jax
import jax.numpy as jnp
from jax import lax
from jax.experimental import pallas as pl
from jax.experimental.pallas import tpu as pltpu
from jax.sharding import PartitionSpec as P

norm_eps = 1e-06
f32 = jnp.float32
bf16 = jnp.bfloat16

CORES = 2
CHIPS = 4
PLANE = CORES * CHIPS
ORDER = (0, 3, 1, 2)

SMEM = pl.BlockSpec(memory_space=pltpu.SMEM)
VMEM = pl.BlockSpec(memory_space=pltpu.VMEM)
HBM = pl.BlockSpec(memory_space=pltpu.HBM)
LONGEST = 2048


def dot(a, b, over_a, over_b):
    return lax.dot_general(a, b, (((over_a,), (over_b,)), ((), ())), preferred_element_type=f32)


def split(x):
    high = x.astype(bf16)
    return high, (x - high.astype(f32)).astype(bf16)


def dot2(a, b, over_a, over_b):
    if a.dtype == f32:
        high, low = split(a)
        return dot(high, b, over_a, over_b) + dot(low, b, over_a, over_b)
    high, low = split(b)
    return dot(a, high, over_a, over_b) + dot(a, low, over_a, over_b)


def doc_of(position, lens):
    bound = lens[0, 0]
    doc = jnp.where(position >= bound, 1, 0)
    for k in range(1, lens.shape[1] - 1):
        bound = bound + lens[0, k]
        doc = doc + jnp.where(position >= bound, 1, 0)
    return doc


def carry(from_edge, to_edge, rate, block, lens):
    same = doc_of(from_edge * block - 1, lens) == doc_of(to_edge * block - 1, lens)
    away = jnp.abs(from_edge - to_edge) * block
    row = jnp.full((1, 128), away.astype(f32) * -rate, f32)
    return jnp.where(same, jnp.exp(row), 0.0)


def entry_exit(here, rate, block, lens, dim, shape):
    offsets = lax.broadcasted_iota(jnp.int32, shape, dim)
    docs = doc_of(here * block + offsets, lens)
    into = jnp.where(docs == doc_of(here * block - 1, lens), jnp.exp(-rate * offsets.astype(f32)), 0.0)
    out = jnp.where(
        docs == doc_of(here * block + block - 1, lens), jnp.exp(-rate * (block - offsets).astype(f32)), 0.0
    )
    return into, out


def head_lanes(head, width):
    return pl.ds(pl.multiple_of(head * width, width), width)


def fetch(refs, spaces, sems):
    copies = [pltpu.make_async_copy(ref, space, sems.at[i]) for i, (ref, space) in enumerate(zip(refs, spaces))]
    for copy in copies:
        copy.start()
    return copies


def half_heads(here, half):
    core = lax.rem(here, CORES)
    chip = lax.rem(here // CORES, CHIPS)
    part = half // CHIPS
    rows = [(i * part + t, (chip ^ d) * part + t) for i, d in enumerate(ORDER) for t in range(part)]
    return [(row, core * half + at, (1 - core) * half + at) for row, at in rows]


def summary_kernel(
    here_ref, rates_in, lens_in, q_in, k_in, v_in, g_in, layer_in, keep, send, top, bottom, chip_w, *scratch
):
    q, k, v, g, layer, rates, lens, sems = scratch
    copies = fetch((rates_in, lens_in, k_in, v_in, q_in, g_in, layer_in), (rates, lens, k, v, q, g, layer), sems)
    here = here_ref[0]
    block = q.shape[0]
    half, _, width, _ = keep.shape
    heads = half_heads(here, half)
    first = lax.rem(here, CORES) == 0
    edge = here - lax.rem(here, CORES)
    for copy in copies[:2]:
        copy.wait()
    for row, head, _ in heads:
        late = carry(edge + 1, edge + 2, rates[head], block, lens)
        early = carry(edge + 1, edge, rates[head], block, lens)
        chip_w[row, 0:1, :] = jnp.where(first, late, 1.0)
        chip_w[row, 1:2, :] = jnp.where(first, 1.0, late)
        chip_w[row, 2:3, :] = jnp.where(first, 1.0, early)
        chip_w[row, 3:4, :] = jnp.where(first, early, 1.0)
    offsets = lax.broadcasted_iota(jnp.int32, (block, width), 0)
    docs = doc_of(here * block + offsets, lens)
    enters = docs == doc_of(here * block - 1, lens)
    leaves = docs == doc_of(here * block + block - 1, lens)
    from_start, to_end = offsets.astype(f32), (block - offsets).astype(f32)
    for copy in copies[2:4]:
        copy.wait()
    for row, *pair in heads:
        for head, out in zip(pair, (keep, send)):
            past = jnp.where(leaves, jnp.exp(-rates[head] * to_end), 0.0)
            lanes = head_lanes(head, width)
            out[row, 0] = dot2(v[:, lanes], k[:, lanes].astype(f32) * past, 0, 0)
    for copy in copies[4:]:
        copy.wait()
    for row, *pair in heads:
        for head, out in zip(pair, (keep, send)):
            into = jnp.where(enters, jnp.exp(-rates[head] * from_start), 0.0)
            lanes = head_lanes(head, width)
            out[row, 1] = dot2(q[:, lanes].astype(f32) * into, g[:, lanes], 0, 0)
    top[...] = layer[: block // 2, :].astype(f32)
    bottom[...] = layer[block // 2 :, :].astype(f32)


def chip_kernel(weights, keep, recv, *outs):
    for i, out in enumerate(outs):
        for t in range(out.shape[0]):
            row = i * out.shape[0] + t
            for k in range(2):
                own, other = weights[row, 2 * k : 2 * k + 1, :], weights[row, 2 * k + 1 : 2 * k + 2, :]
                out[t, k] = own * keep[row, k] + other * recv[row, k]


def line_order(planes):
    return [2, 1, 3] + list(range(4, planes)) if planes > 3 else list(range(planes - 1, 0, -1))


def weights_kernel(here_ref, rates, lens, plane_w, line_w, entry_w, state_w, *, block):
    here = here_ref[0]
    half = state_w.shape[0]
    part, lines = line_w.shape[:2]
    core = lax.rem(here, CORES)
    chip = lax.rem(here // CORES, CHIPS)
    plane = here // PLANE
    base = plane * PLANE
    ones = jnp.ones((1, 128), f32)
    for t in range(part):
        rate = rates[core * half + chip * part + t]

        def take(from_edge, to_edge):
            return carry(from_edge, to_edge, rate, block, lens)

        for j, d in enumerate(line_order(lines + 1)):
            to = plane ^ d
            line_w[t, j, 0:1, :] = jnp.where(to > plane, take(base + PLANE, to * PLANE), 0.0)
            line_w[t, j, 1:2, :] = jnp.where(to < plane, take(base, (to + 1) * PLANE), 0.0)
            line_w[t, j, 2:3, :] = jnp.where(to < plane, ones, 0.0)
            line_w[t, j, 3:4, :] = jnp.where(to > plane, ones, 0.0)
        for i, d in enumerate(ORDER):
            edge = base + (chip ^ d) * CORES
            plane_w[t, i, 0:1, :] = take(edge + CORES, base + PLANE)
            plane_w[t, i, 1:2, :] = take(edge, base)
            entry_w[t, i, CHIPS, 0:1, :] = take(base, edge)
            entry_w[t, i, CHIPS, 1:2, :] = take(base + PLANE, edge + CORES)
            for j, e in enumerate(ORDER):
                other = base + (chip ^ e) * CORES
                entry_w[t, i, j, 0:1, :] = jnp.where(other < edge, take(other + CORES, edge), 0.0)
                entry_w[t, i, j, 1:2, :] = jnp.where(other > edge, take(other, edge + CORES), 0.0)
    edge = here - core
    first = core == 0
    for row, head, _ in half_heads(here, half):
        fwd = carry(edge, edge + 1, rates[head], block, lens)
        bwd = carry(edge + 2, edge + 1, rates[head], block, lens)
        rows = ((0.0, 1.0), (1.0, fwd), (1.0, bwd), (0.0, 1.0))
        for k, (core0, core1) in enumerate(((0, 1), (1, 0), (2, 3), (3, 2))):
            for m in range(2):
                state_w[row, 2 * k + m : 2 * k + m + 1, :] = jnp.where(
                    first, ones * rows[core0][m], ones * rows[core1][m]
                )


def plane_kernel(weights, line_w, *refs):
    totals, outs = refs[:CHIPS], refs[CHIPS:]
    for t in range(outs[0].shape[0]):
        fwd, bwd = 0.0, 0.0
        for i, total in enumerate(totals):
            fwd = fwd + weights[t, i, 0:1, :] * total[t, 0]
            bwd = bwd + weights[t, i, 1:2, :] * total[t, 1]
        for j, out in enumerate(outs):
            out[t] = line_w[t, j, 0:1, :] * fwd + line_w[t, j, 1:2, :] * bwd


def forward_kernel(top, bottom, pass_top, pass_bottom):
    pass_top[...] = top[...]
    pass_bottom[...] = bottom[...]


def entry_kernel(weights, line_w, *refs, lines):
    totals, others, outs = refs[:CHIPS], refs[CHIPS : CHIPS + lines], refs[CHIPS + lines :]
    for t in range(outs[0].shape[0]):
        before, after = 0.0, 0.0
        for j, other in enumerate(others):
            before = before + line_w[t, j, 2:3, :] * other[t]
            after = after + line_w[t, j, 3:4, :] * other[t]
        for i, out in enumerate(outs):
            fwd = weights[t, i, CHIPS, 0:1, :] * before
            bwd = weights[t, i, CHIPS, 1:2, :] * after
            for j, total in enumerate(totals):
                if i != j:
                    fwd = fwd + weights[t, i, j, 0:1, :] * total[t, 0]
                    bwd = bwd + weights[t, i, j, 1:2, :] * total[t, 1]
            out[t, 0], out[t, 1] = fwd, bwd


def states_kernel(weights, keep, recv, *refs, block):
    entries, layer, (mine, send, top, bottom) = refs[:CHIPS], refs[CHIPS], refs[CHIPS + 1 :]
    part = entries[0].shape[0]
    for i, entry in enumerate(entries):
        for t in range(part):
            row = i * part + t
            for k in range(2):
                for m, (own, out) in enumerate(((recv, mine), (keep, send))):
                    at = 4 * k + 2 * m
                    out[row, k] = weights[row, at : at + 1, :] * own[row, k] + weights[row, at + 1 : at + 2, :] * entry[t, k]
    top[...] = layer[: block // 2, :].astype(f32)
    bottom[...] = layer[block // 2 :, :].astype(f32)


def causal(here, block, lens):
    at_j = lax.broadcasted_iota(jnp.int32, (block, block), 0)
    at_i = lax.broadcasted_iota(jnp.int32, (block, block), 1)
    docs_j = doc_of(here * block + at_j, lens)
    docs_i = doc_of(here * block + at_i, lens)
    return (docs_i == docs_j) & (at_i >= at_j), jnp.maximum(at_i - at_j, 0).astype(f32)


def within_kernel(here_ref, rates, lens, gain, q, k, v, attn, gain_col, into_rows):
    here = here_ref[0]
    block, features = q.shape
    heads = rates.shape[0]
    width = features // heads
    reached, away = causal(here, block, lens)
    for head in range(heads):
        lanes = slice(head * width, (head + 1) * width)
        gain_col[lanes, :] = jnp.broadcast_to(gain[:, lanes], (block, width)).T
        decay = jnp.where(reached, jnp.exp(-rates[head] * away), 0.0)
        scores = dot(k[:, lanes], q[:, lanes], 1, 1) * decay
        attn[lanes, :] = dot2(v[:, lanes], scores, 0, 0)
        into_rows[head : head + 1, :], _ = entry_exit(here, rates[head], block, lens, 1, (1, block))


def norm_kernel(here_ref, q, attn, gain_col, into_rows, mine, recv, *refs, rows):
    outs, total = refs[:CHIPS], refs[CHIPS]
    here = here_ref[0]
    block, features = q.shape
    half, _, width, _ = mine.shape
    chip = lax.rem(here // CORES, CHIPS)
    squares = jnp.zeros((width, block), f32)
    for row, *pair in half_heads(here, half):
        for head, states in zip(pair, (mine, recv)):
            lanes = head_lanes(head, width)
            at = attn[lanes, :] + into_rows[pl.ds(head, 1), :] * dot2(states[row, 0], q[:, lanes], 1, 1)
            total[lanes, :] = at
            squares = squares + at * at
    mean = jnp.sum(squares, axis=0, keepdims=True) * (1.0 / features)
    factor = lax.rsqrt(mean + norm_eps)
    planes = features // (PLANE * rows)
    for out, d in zip(outs, ORDER):
        for to_core in range(CORES):
            for plane in range(planes):
                block_at = plane * PLANE + (chip ^ d) * CORES + to_core
                at = pl.ds(pl.multiple_of(block_at * rows, rows), rows)
                normed = (total[at, :] * factor * gain_col[at, :]).astype(bf16)
                to = to_core * planes + plane
                out[to * rows : (to + 1) * rows, :] = normed.astype(f32)


def product_send_kernel(here_ref, *refs, scale):
    core = lax.rem(here_ref[0], CORES)
    normed, layers, (layer, out, left, right) = refs[:CHIPS], refs[CHIPS:-4], refs[-4:]
    rows = left.shape[0]
    block = layer.shape[0]
    mine = pl.ds(pl.multiple_of(core * rows, rows), rows)
    other = pl.ds(pl.multiple_of((1 - core) * rows, rows), rows)
    right[:block, :] = layer[...]
    for k, x in enumerate(layers, 2):
        right[k * block // 2 : (k + 1) * block // 2, :] = x[...].astype(bf16)
    for d, x in enumerate(normed):
        left[:, d * block : (d + 1) * block] = x[mine, :].astype(bf16)
    send = jnp.concatenate([x[other, :].astype(bf16) for x in normed], axis=1)
    out[...] = (dot(send, right[...], 1, 0) * scale).reshape(out.shape)


def product_kernel(here_ref, left, right, recv, *refs, scale):
    outs, product = refs[:-1], refs[-1]
    plane = here_ref[0] // PLANE
    product[...] = (dot(left[...], right[...], 1, 0) * scale).reshape(product.shape)
    for out, d in zip(outs, [0] + line_order(len(outs))):
        out[...] = product[plane ^ d] + recv[plane ^ d]


def sum_kernel(*refs):
    total = refs[0][...]
    for x in refs[1:-1]:
        total = total + x[...]
    refs[-1][...] = total


def outputs_kernel(here_ref, rates, lens, q_in, k_in, v_in, g_in, mine, recv, q_out, k_out, v_out, *scratch):
    q, k, v, g, q_grad, k_grad, v_grad, sems = scratch
    copies = fetch((q_in, k_in, v_in, g_in), (q, k, v, g), sems)
    here = here_ref[0]
    block, features = q.shape
    half, _, width, _ = mine.shape
    reached, away = causal(here, block, lens)
    for copy in copies:
        copy.wait()
    for row, *pair in half_heads(here, half):
        for head, states in zip(pair, (mine, recv)):
            lanes = head_lanes(head, width)
            rate = rates[head]
            qh, kh, vh, gh = q[:, lanes], k[:, lanes], v[:, lanes], g[:, lanes]
            decay = jnp.where(reached, jnp.exp(-rate * away), 0.0)
            scores = dot(kh, qh, 1, 1) * decay
            grads = dot(vh, gh, 1, 1) * decay
            into, past = entry_exit(here, rate, block, lens, 0, (block, width))
            before, after = states[row, 0], states[row, 1]
            q_grad[:, lanes] = (dot2(grads, kh, 0, 0) + into * dot2(gh, before, 1, 0)).astype(bf16)
            k_grad[:, lanes] = (dot2(grads, qh, 1, 0) + past * dot2(vh, after, 1, 1)).astype(bf16)
            v_grad[:, lanes] = (dot2(scores, gh, 1, 0) + past * dot2(kh, after, 1, 0)).astype(bf16)
    outs = [pltpu.make_async_copy(x, y, sems.at[i]) for i, (x, y) in enumerate(((q_grad, q_out), (k_grad, k_out), (v_grad, v_out)))]
    for copy in outs:
        copy.start()
    for copy in outs:
        copy.wait()


def for_all_dp(outs, here, planes, dps):
    order = (here // CORES) % CHIPS ^ jnp.array(ORDER)
    whole = jnp.zeros((CHIPS,) + outs[0].shape, f32).at[order].set(jnp.stack(outs))
    rows = whole.shape[1] // (CORES * planes)
    whole = whole.reshape(CHIPS, CORES, planes, rows, -1).transpose(2, 0, 1, 3, 4)
    whole = whole.reshape(dps, planes, CHIPS, CORES, rows // dps, -1).transpose(2, 3, 1, 0, 4, 5)
    whole = whole.reshape((CHIPS,) + outs[0].shape)[order]
    return [whole[d] for d in range(CHIPS)]


def call(kernel, specs, outs, name, scratch=(), flops=0, moved=0, out_specs=None, after=(), **named):
    reads = len(specs)

    def body(*refs):
        kernel(*refs[:reads], *refs[reads + len(after) :], **named)

    def run(*operands):
        operands = [
            pltpu.with_memory_space_constraint(x, pltpu.HBM) if spec is HBM else x for x, spec in zip(operands, specs)
        ]
        return pl.pallas_call(
            body,
            out_shape=[jax.ShapeDtypeStruct(shape, dtype) for shape, dtype in outs],
            in_specs=list(specs) + [pl.BlockSpec(memory_space=pl.ANY)] * len(after),
            out_specs=out_specs or [VMEM] * len(outs),
            scratch_shapes=list(scratch),
            cost_estimate=pl.CostEstimate(flops=flops, bytes_accessed=moved, transcendentals=0),
            compiler_params=pltpu.CompilerParams(vmem_limit_bytes=16 * 1024 * 1024),
            name=name,
        )(*operands, *after)

    return run


def on_device(queries, keys, values, out_grad, layer_grad, norm_gain, decay_rates, doc_lengths):
    seqs, block, features = queries.shape
    assert seqs == 1
    heads = decay_rates.shape[0]
    width = features // heads
    columns = layer_grad.shape[2]
    half = heads // CORES
    part = half // CHIPS
    count = lax.axis_size("ctx")
    planes = count // PLANE
    dps = lax.axis_size("dp")
    scale = 1.0 / math.sqrt(seqs * block * dps * count)
    here = lax.axis_index("ctx").astype(jnp.int32).reshape(1)
    facts = (here, decay_rates, doc_lengths)
    q, k, v, g = (x.reshape(block, features) for x in (queries, keys, values, out_grad))
    layer = layer_grad.reshape(block, columns)

    def swap(x, bit, near=count):
        pairs = [(i, i ^ bit) for i in range(count) if abs(i // PLANE - (i ^ bit) // PLANE) <= near]
        return lax.ppermute(x, "ctx", pairs)

    def in_plane(pieces):
        return [pieces[0]] + [swap(x, d * CORES) for x, d in zip(pieces[1:], ORDER[1:])]

    def in_line(pieces, near=count):
        return [swap(x, d * PLANE, near) for x, d in zip(pieces, line_order(planes))]

    pair = ((half, 2, width, width), f32)
    small = ((part, 2, width, width), f32)
    one = ((part, width, width), f32)
    rows_in = pltpu.VMEM((block, features), bf16)
    half_layer = ((block // 2, columns), f32)
    keep, send, top, bottom, chip_w = call(
        summary_kernel,
        [SMEM] + [HBM] * 7,
        [pair] * 2 + [half_layer] * 2 + [((half, 4, 128), f32)],
        "summary",
        scratch=[rows_in] * 4
        + [
            pltpu.VMEM((block, columns), bf16),
            pltpu.SMEM((heads,), f32),
            pltpu.SMEM(doc_lengths.shape, jnp.int32),
            pltpu.SemaphoreType.DMA((7,)),
        ],
        flops=1 << 26,
        moved=1 << 21,
    )(*facts, q, k, v, g, layer)
    recv = swap(send, 1)
    x_top, y_bottom = swap(top, CORES), swap(bottom, 2 * CORES)
    totals = call(
        chip_kernel, [VMEM] * 3, [small] * CHIPS, "chip_total", moved=1 << 20
    )(chip_w, keep, recv)
    plane_w, line_w, entry_w, state_w = call(
        weights_kernel,
        [SMEM] * 3,
        [
            ((part, CHIPS, 2, 128), f32),
            ((part, planes - 1, 4, 128), f32),
            ((part, CHIPS, CHIPS + 1, 2, 128), f32),
            ((half, 8, 128), f32),
        ],
        "weights",
        moved=1 << 18,
        after=totals[:1],
        block=block,
    )(*facts)
    totals = in_plane(totals)
    near = -(-LONGEST // (PLANE * block))
    onward = call(
        plane_kernel,
        [VMEM] * (2 + CHIPS),
        [one] * (planes - 1),
        "plane_total",
        moved=1 << 19,
        after=[x_top, y_bottom],
    )(plane_w, line_w, *totals)
    others = in_line(onward, near)
    pass_top, pass_bottom = call(
        forward_kernel, [VMEM] * 2, [half_layer] * 2, "forward", moved=1 << 20
    )(x_top, y_bottom)
    xy_top, xy_bottom = swap(pass_top, 2 * CORES), swap(pass_bottom, CORES)
    attn, gain_col, into_rows = call(
        within_kernel,
        [SMEM] * 3 + [VMEM] * 4,
        [((features, block), f32)] * 2 + [((heads, block), f32)],
        "within",
        flops=1 << 28,
        moved=1 << 22,
    )(*facts, norm_gain.reshape(1, features), q, k, v)
    entries = call(
        entry_kernel,
        [VMEM] * (2 + CHIPS + len(others)),
        [small] * CHIPS,
        "entries",
        moved=1 << 20,
        after=[xy_top, xy_bottom],
        lines=len(others),
    )(entry_w, line_w, *totals, *others)
    entries = in_plane(entries)
    mine, send, top, bottom = call(
        states_kernel,
        [VMEM] * (4 + CHIPS),
        [pair] * 2 + [half_layer] * 2,
        "states",
        moved=1 << 21,
        after=[attn],
        block=block,
    )(state_w, keep, recv, *entries, layer)
    theirs = swap(send, 1)
    x_bottom, y_top = swap(bottom, CORES), swap(top, 2 * CORES)

    rows = features // count
    normed = call(
        norm_kernel,
        [SMEM] + [VMEM] * 6,
        [((features // CHIPS, block), f32)] * CHIPS,
        "norm",
        scratch=[pltpu.VMEM((features, block), f32)],
        flops=1 << 26,
        moved=1 << 21,
        rows=rows,
    )(here, q, attn, gain_col, into_rows, mine, theirs)
    if dps > 1:
        normed = for_all_dp(normed, here[0], planes, dps)
    normed = in_plane(normed)
    layers = [xy_top, xy_bottom, x_top, x_bottom, y_top, y_bottom]
    by_plane = ((planes, rows, columns), f32)
    product, left, right = call(
        product_send_kernel,
        [SMEM] + [VMEM] * (CHIPS + len(layers) + 1),
        [by_plane, ((planes * rows, CHIPS * block), bf16), ((CHIPS * block, columns), bf16)],
        "product_send",
        flops=1 << 27,
        moved=1 << 22,
        scale=scale,
    )(here, *normed, *layers, layer)
    parts = call(
        product_kernel,
        [SMEM] + [VMEM] * 3,
        [((rows, columns), f32)] * planes,
        "product",
        scratch=[pltpu.VMEM(*by_plane)],
        flops=1 << 27,
        moved=1 << 21,
        scale=scale,
    )(here, left, right, swap(product, 1))
    parts = [parts[0]] + in_line(parts[1:])
    q_grad, k_grad, v_grad = call(
        outputs_kernel,
        [SMEM] * 3 + [HBM] * 4 + [VMEM] * 2,
        [((block, features), bf16)] * 3,
        "outputs",
        scratch=[rows_in] * 7 + [pltpu.SemaphoreType.DMA((4,))],
        out_specs=[HBM] * 3,
        flops=1 << 29,
        moved=1 << 22,
    )(*facts, q, k, v, g, mine, theirs)
    (proj_grad,) = call(sum_kernel, [VMEM] * planes, [((rows, columns), f32)], "sum", moved=1 << 19)(*parts)
    if dps > 1:
        proj_grad = lax.psum_scatter(proj_grad, "dp", scatter_dimension=0, tiled=True)
    shape_out = (seqs, block, features)
    return (q_grad.reshape(shape_out), k_grad.reshape(shape_out), v_grad.reshape(shape_out), proj_grad)


def solution(mesh):
    rows = P("dp", "ctx", None)
    return jax.shard_map(
        on_device,
        mesh=mesh,
        in_specs=(rows, rows, rows, rows, rows, P(), P(), P("dp", None)),
        out_specs=(rows, rows, rows, P(("dp", "ctx"), None)),
        check_vma=False,
    )
```

```python
import functools
import math

import jax
import jax.numpy as jnp
from jax import lax
from jax.experimental import pallas as pl
from jax.experimental.pallas import tpu as pltpu
from jax.sharding import PartitionSpec as P

norm_eps = 1e-06
f32 = jnp.float32
bf16 = jnp.bfloat16

CORES = 2
CHIPS = 4
PLANE = CORES * CHIPS
ORDER = (0, 1, 2, 3)

SMEM = pl.BlockSpec(memory_space=pltpu.SMEM)
VMEM = pl.BlockSpec(memory_space=pltpu.VMEM)
HBM = pl.BlockSpec(memory_space=pltpu.HBM)
LONGEST = 2048


def dot(a, b, over_a, over_b):
    return lax.dot_general(a, b, (((over_a,), (over_b,)), ((), ())), preferred_element_type=f32)


def split(x):
    high = x.astype(bf16)
    return high, (x - high.astype(f32)).astype(bf16)


def dot2(a, b, over_a, over_b):
    if a.dtype == f32:
        high, low = split(a)
        return dot(high, b, over_a, over_b) + dot(low, b, over_a, over_b)
    high, low = split(b)
    return dot(a, high, over_a, over_b) + dot(a, low, over_a, over_b)


def doc_of(position, lens):
    bound = lens[0, 0]
    doc = jnp.where(position >= bound, 1, 0)
    for k in range(1, lens.shape[1] - 1):
        bound = bound + lens[0, k]
        doc = doc + jnp.where(position >= bound, 1, 0)
    return doc


def carry(from_edge, to_edge, rate, block, lens):
    same = doc_of(from_edge * block - 1, lens) == doc_of(to_edge * block - 1, lens)
    away = jnp.abs(from_edge - to_edge) * block
    row = jnp.full((1, 128), away.astype(f32) * -rate, f32)
    return jnp.where(same, jnp.exp(row), 0.0)


def entry_exit(here, rate, block, lens, dim, shape):
    offsets = lax.broadcasted_iota(jnp.int32, shape, dim)
    docs = doc_of(here * block + offsets, lens)
    into = jnp.where(docs == doc_of(here * block - 1, lens), jnp.exp(-rate * offsets.astype(f32)), 0.0)
    out = jnp.where(
        docs == doc_of(here * block + block - 1, lens), jnp.exp(-rate * (block - offsets).astype(f32)), 0.0
    )
    return into, out


def head_lanes(head, width):
    return pl.ds(pl.multiple_of(head * width, width), width)


def fetch(refs, spaces, sems):
    copies = [pltpu.make_async_copy(ref, space, sems.at[i]) for i, (ref, space) in enumerate(zip(refs, spaces))]
    for copy in copies:
        copy.start()
    return copies


def half_heads(here, half):
    core = lax.rem(here, CORES)
    chip = lax.rem(here // CORES, CHIPS)
    part = half // CHIPS
    rows = [(i * part + t, (chip ^ d) * part + t) for i, d in enumerate(ORDER) for t in range(part)]
    return [(row, core * half + at, (1 - core) * half + at) for row, at in rows]


def summary_kernel(
    here_ref, rates_in, lens_in, q_in, k_in, v_in, g_in, keep, send, chip_w, q, k, v, g, rates, lens, sems
):
    copies = fetch((rates_in, lens_in, k_in, v_in, q_in, g_in), (rates, lens, k, v, q, g), sems)
    here = here_ref[0]
    block = q.shape[0]
    half, _, width, _ = keep.shape
    heads = half_heads(here, half)
    first = lax.rem(here, CORES) == 0
    edge = here - lax.rem(here, CORES)
    for copy in copies[:2]:
        copy.wait()
    for row, head, _ in heads:
        late = carry(edge + 1, edge + 2, rates[head], block, lens)
        early = carry(edge + 1, edge, rates[head], block, lens)
        chip_w[row, 0:1, :] = jnp.where(first, late, 1.0)
        chip_w[row, 1:2, :] = jnp.where(first, 1.0, late)
        chip_w[row, 2:3, :] = jnp.where(first, 1.0, early)
        chip_w[row, 3:4, :] = jnp.where(first, early, 1.0)
    offsets = lax.broadcasted_iota(jnp.int32, (block, width), 0)
    docs = doc_of(here * block + offsets, lens)
    enters = docs == doc_of(here * block - 1, lens)
    leaves = docs == doc_of(here * block + block - 1, lens)
    from_start, to_end = offsets.astype(f32), (block - offsets).astype(f32)
    for copy in copies[2:4]:
        copy.wait()
    for row, *pair in heads:
        for head, out in zip(pair, (keep, send)):
            past = jnp.where(leaves, jnp.exp(-rates[head] * to_end), 0.0)
            lanes = head_lanes(head, width)
            out[row, 0] = dot2(v[:, lanes], k[:, lanes].astype(f32) * past, 0, 0)
    for copy in copies[4:]:
        copy.wait()
    for row, *pair in heads:
        for head, out in zip(pair, (keep, send)):
            into = jnp.where(enters, jnp.exp(-rates[head] * from_start), 0.0)
            lanes = head_lanes(head, width)
            out[row, 1] = dot2(q[:, lanes].astype(f32) * into, g[:, lanes], 0, 0)


def chip_kernel(weights, keep, recv, *outs):
    for i, out in enumerate(outs):
        for t in range(out.shape[0]):
            row = i * out.shape[0] + t
            for k in range(2):
                own, other = weights[row, 2 * k : 2 * k + 1, :], weights[row, 2 * k + 1 : 2 * k + 2, :]
                out[t, k] = own * keep[row, k] + other * recv[row, k]


def line_order(planes):
    return [2, 1, 3] + list(range(4, planes)) if planes > 3 else list(range(planes - 1, 0, -1))


def weights_kernel(here_ref, rates, lens, plane_w, line_w, entry_w, state_w, *, block):
    here = here_ref[0]
    half = state_w.shape[0]
    part, lines = line_w.shape[:2]
    core = lax.rem(here, CORES)
    chip = lax.rem(here // CORES, CHIPS)
    plane = here // PLANE
    base = plane * PLANE
    ones = jnp.ones((1, 128), f32)
    for t in range(part):
        rate = rates[core * half + chip * part + t]

        def take(from_edge, to_edge):
            return carry(from_edge, to_edge, rate, block, lens)

        for j, d in enumerate(line_order(lines + 1)):
            to = plane ^ d
            line_w[t, j, 0:1, :] = jnp.where(to > plane, take(base + PLANE, to * PLANE), 0.0)
            line_w[t, j, 1:2, :] = jnp.where(to < plane, take(base, (to + 1) * PLANE), 0.0)
            line_w[t, j, 2:3, :] = jnp.where(to < plane, ones, 0.0)
            line_w[t, j, 3:4, :] = jnp.where(to > plane, ones, 0.0)
        for i, d in enumerate(ORDER):
            edge = base + (chip ^ d) * CORES
            plane_w[t, i, 0:1, :] = take(edge + CORES, base + PLANE)
            plane_w[t, i, 1:2, :] = take(edge, base)
            entry_w[t, i, CHIPS, 0:1, :] = take(base, edge)
            entry_w[t, i, CHIPS, 1:2, :] = take(base + PLANE, edge + CORES)
            for j, e in enumerate(ORDER):
                other = base + (chip ^ e) * CORES
                entry_w[t, i, j, 0:1, :] = jnp.where(other < edge, take(other + CORES, edge), 0.0)
                entry_w[t, i, j, 1:2, :] = jnp.where(other > edge, take(other, edge + CORES), 0.0)
    edge = here - core
    first = core == 0
    for row, head, _ in half_heads(here, half):
        fwd = carry(edge, edge + 1, rates[head], block, lens)
        bwd = carry(edge + 2, edge + 1, rates[head], block, lens)
        rows = ((0.0, 1.0), (1.0, fwd), (1.0, bwd), (0.0, 1.0))
        for k, (core0, core1) in enumerate(((0, 1), (1, 0), (2, 3), (3, 2))):
            for m in range(2):
                state_w[row, 2 * k + m : 2 * k + m + 1, :] = jnp.where(
                    first, ones * rows[core0][m], ones * rows[core1][m]
                )


def plane_kernel(weights, line_w, *refs):
    totals, outs = refs[:CHIPS], refs[CHIPS:]
    for t in range(outs[0].shape[0]):
        fwd, bwd = 0.0, 0.0
        for i, total in enumerate(totals):
            fwd = fwd + weights[t, i, 0:1, :] * total[t, 0]
            bwd = bwd + weights[t, i, 1:2, :] * total[t, 1]
        for j, out in enumerate(outs):
            out[t] = line_w[t, j, 0:1, :] * fwd + line_w[t, j, 1:2, :] * bwd


def widen_kernel(layer, out):
    out[...] = layer[...].astype(f32)


def forward_kernel(layer_x, layer_y, top, bottom):
    top[...] = layer_x[: top.shape[0], :]
    bottom[...] = layer_y[top.shape[0] :, :]


def entry_kernel(weights, line_w, *refs, lines):
    totals, others, outs = refs[:CHIPS], refs[CHIPS : CHIPS + lines], refs[CHIPS + lines :]
    for t in range(outs[0].shape[0]):
        before, after = 0.0, 0.0
        for j, other in enumerate(others):
            before = before + line_w[t, j, 2:3, :] * other[t]
            after = after + line_w[t, j, 3:4, :] * other[t]
        for i, out in enumerate(outs):
            fwd = weights[t, i, CHIPS, 0:1, :] * before
            bwd = weights[t, i, CHIPS, 1:2, :] * after
            for j, total in enumerate(totals):
                if i != j:
                    fwd = fwd + weights[t, i, j, 0:1, :] * total[t, 0]
                    bwd = bwd + weights[t, i, j, 1:2, :] * total[t, 1]
            out[t, 0], out[t, 1] = fwd, bwd


def states_kernel(weights, keep, recv, *refs):
    entries, (mine, send) = refs[:CHIPS], refs[CHIPS:]
    part = entries[0].shape[0]
    for i, entry in enumerate(entries):
        for t in range(part):
            row = i * part + t
            for k in range(2):
                for m, (own, out) in enumerate(((recv, mine), (keep, send))):
                    at = 4 * k + 2 * m
                    out[row, k] = weights[row, at : at + 1, :] * own[row, k] + weights[row, at + 1 : at + 2, :] * entry[t, k]


def causal(here, block, lens):
    at_j = lax.broadcasted_iota(jnp.int32, (block, block), 0)
    at_i = lax.broadcasted_iota(jnp.int32, (block, block), 1)
    docs_j = doc_of(here * block + at_j, lens)
    docs_i = doc_of(here * block + at_i, lens)
    return (docs_i == docs_j) & (at_i >= at_j), jnp.maximum(at_i - at_j, 0).astype(f32)


def within_kernel(here_ref, rates, lens, gain, q, k, v, attn, gain_col, into_rows):
    here = here_ref[0]
    block, features = q.shape
    heads = rates.shape[0]
    width = features // heads
    reached, away = causal(here, block, lens)
    for head in range(heads):
        lanes = slice(head * width, (head + 1) * width)
        gain_col[lanes, :] = jnp.broadcast_to(gain[:, lanes], (block, width)).T
        decay = jnp.where(reached, jnp.exp(-rates[head] * away), 0.0)
        scores = dot(k[:, lanes], q[:, lanes], 1, 1) * decay
        attn[lanes, :] = dot2(v[:, lanes], scores, 0, 0)
        into_rows[head : head + 1, :], _ = entry_exit(here, rates[head], block, lens, 1, (1, block))


def norm_kernel(here_ref, q, attn, gain_col, into_rows, mine, recv, *refs, rows):
    outs, total = refs[:CHIPS], refs[CHIPS]
    here = here_ref[0]
    block, features = q.shape
    half, _, width, _ = mine.shape
    chip = lax.rem(here // CORES, CHIPS)
    squares = jnp.zeros((width, block), f32)
    for row, *pair in half_heads(here, half):
        for head, states in zip(pair, (mine, recv)):
            lanes = head_lanes(head, width)
            at = attn[lanes, :] + into_rows[pl.ds(head, 1), :] * dot2(states[row, 0], q[:, lanes], 1, 1)
            total[lanes, :] = at
            squares = squares + at * at
    mean = jnp.sum(squares, axis=0, keepdims=True) * (1.0 / features)
    factor = lax.rsqrt(mean + norm_eps)
    planes = features // (PLANE * rows)
    for out, d in zip(outs, ORDER):
        for to_core in range(CORES):
            for plane in range(planes):
                block_at = plane * PLANE + (chip ^ d) * CORES + to_core
                at = pl.ds(pl.multiple_of(block_at * rows, rows), rows)
                normed = (total[at, :] * factor * gain_col[at, :]).astype(bf16)
                to = to_core * planes + plane
                out[to * rows : (to + 1) * rows, :] = normed.astype(f32)


def product_send_kernel(here_ref, *refs, scale):
    core = lax.rem(here_ref[0], CORES)
    normed, layers, (layer, out, left, right) = refs[:CHIPS], refs[CHIPS:-4], refs[-4:]
    rows = left.shape[0]
    block = layer.shape[0]
    mine = pl.ds(pl.multiple_of(core * rows, rows), rows)
    other = pl.ds(pl.multiple_of((1 - core) * rows, rows), rows)
    right[:block, :] = layer[...]
    at = block
    for x in layers:
        right[at : at + x.shape[0], :] = x[...].astype(bf16)
        at = at + x.shape[0]
    for d, x in enumerate(normed):
        left[:, d * block : (d + 1) * block] = x[mine, :].astype(bf16)
    send = jnp.concatenate([x[other, :].astype(bf16) for x in normed], axis=1)
    out[...] = (dot(send, right[...], 1, 0) * scale).reshape(out.shape)


def halve(total, outs):
    pieces = total.shape[0] // len(outs)
    for side, out in enumerate(outs):
        for j in range(pieces):
            out[j] = total[len(outs) * j + side]


def product_kernel(here_ref, left, right, recv, *refs, scale):
    outs, (product, total) = refs[:-2], refs[-2:]
    plane = here_ref[0] // PLANE
    product[...] = (dot(left[...], right[...], 1, 0) * scale).reshape(product.shape)
    for d in range(product.shape[0]):
        total[d] = product[plane ^ d] + recv[plane ^ d]
    halve(total, outs)


def halving_kernel(own, recv, *outs):
    halve(own[...] + recv[...], outs)


def q_grad_kernel(here_ref, rates, lens, k_in, v_in, g_in, mine, recv, out, k, v, g, q_grad, sems):
    copies = fetch((k_in, v_in, g_in), (k, v, g), sems)
    here = here_ref[0]
    block = k.shape[0]
    half, _, width, _ = mine.shape
    reached, away = causal(here, block, lens)
    for copy in copies:
        copy.wait()
    for row, *pair in half_heads(here, half):
        for head, states in zip(pair, (mine, recv)):
            lanes = head_lanes(head, width)
            rate = rates[head]
            grads = dot(v[:, lanes], g[:, lanes], 1, 1) * jnp.where(reached, jnp.exp(-rate * away), 0.0)
            into, _ = entry_exit(here, rate, block, lens, 0, (block, width))
            q_grad[:, lanes] = (
                dot2(grads, k[:, lanes], 0, 0) + into * dot2(g[:, lanes], states[row, 0], 1, 0)
            ).astype(bf16)
    copy = pltpu.make_async_copy(q_grad, out, sems.at[0])
    copy.start()
    copy.wait()


def kv_grad_kernel(here_ref, rates, lens, q_in, k_in, v_in, g_in, mine, recv, k_out, v_out, *scratch):
    q, k, v, g, k_grad, v_grad, sems = scratch
    copies = fetch((q_in, k_in, v_in, g_in), (q, k, v, g), sems)
    here = here_ref[0]
    block = q.shape[0]
    half, _, width, _ = mine.shape
    reached, away = causal(here, block, lens)
    for copy in copies:
        copy.wait()
    for row, *pair in half_heads(here, half):
        for head, states in zip(pair, (mine, recv)):
            lanes = head_lanes(head, width)
            rate = rates[head]
            qh, kh, vh, gh = q[:, lanes], k[:, lanes], v[:, lanes], g[:, lanes]
            decay = jnp.where(reached, jnp.exp(-rate * away), 0.0)
            scores = dot(kh, qh, 1, 1) * decay
            grads = dot(vh, gh, 1, 1) * decay
            _, past = entry_exit(here, rate, block, lens, 0, (block, width))
            after = states[row, 1]
            k_grad[:, lanes] = (dot2(grads, qh, 1, 0) + past * dot2(vh, after, 1, 1)).astype(bf16)
            v_grad[:, lanes] = (dot2(scores, gh, 1, 0) + past * dot2(kh, after, 1, 0)).astype(bf16)
    outs = [pltpu.make_async_copy(k_grad, k_out, sems.at[0]), pltpu.make_async_copy(v_grad, v_out, sems.at[1])]
    for copy in outs:
        copy.start()
    for copy in outs:
        copy.wait()


def for_all_dp(outs, here, planes, dps):
    order = (here // CORES) % CHIPS ^ jnp.array(ORDER)
    whole = jnp.zeros((CHIPS,) + outs[0].shape, f32).at[order].set(jnp.stack(outs))
    rows = whole.shape[1] // (CORES * planes)
    whole = whole.reshape(CHIPS, CORES, planes, rows, -1).transpose(2, 0, 1, 3, 4)
    whole = whole.reshape(dps, planes, CHIPS, CORES, rows // dps, -1).transpose(2, 3, 1, 0, 4, 5)
    whole = whole.reshape((CHIPS,) + outs[0].shape)[order]
    return [whole[d] for d in range(CHIPS)]


def call(kernel, specs, outs, name, scratch=(), flops=0, moved=0, out_specs=None, after=(), **named):
    reads = len(specs)

    def body(*refs):
        kernel(*refs[:reads], *refs[reads + len(after) :], **named)

    def run(*operands):
        operands = [
            pltpu.with_memory_space_constraint(x, pltpu.HBM) if spec is HBM else x for x, spec in zip(operands, specs)
        ]
        return pl.pallas_call(
            body,
            out_shape=[jax.ShapeDtypeStruct(shape, dtype) for shape, dtype in outs],
            in_specs=list(specs) + [pl.BlockSpec(memory_space=pl.ANY)] * len(after),
            out_specs=out_specs or [VMEM] * len(outs),
            scratch_shapes=list(scratch),
            cost_estimate=pl.CostEstimate(flops=flops, bytes_accessed=moved, transcendentals=0),
            compiler_params=pltpu.CompilerParams(vmem_limit_bytes=16 * 1024 * 1024),
            name=name,
        )(*operands, *after)

    return run


def on_device(queries, keys, values, out_grad, layer_grad, norm_gain, decay_rates, doc_lengths):
    seqs, block, features = queries.shape
    assert seqs == 1
    heads = decay_rates.shape[0]
    width = features // heads
    columns = layer_grad.shape[2]
    half = heads // CORES
    part = half // CHIPS
    count = lax.axis_size("ctx")
    planes = count // PLANE
    dps = lax.axis_size("dp")
    scale = 1.0 / math.sqrt(seqs * block * dps * count)
    here = lax.axis_index("ctx").astype(jnp.int32).reshape(1)
    facts = (here, decay_rates, doc_lengths)
    q, k, v, g = (x.reshape(block, features) for x in (queries, keys, values, out_grad))
    layer = layer_grad.reshape(block, columns)

    def swap(x, bit, near=count):
        pairs = [(i, i ^ bit) for i in range(count) if abs(i // PLANE - (i ^ bit) // PLANE) <= near]
        return lax.ppermute(x, "ctx", pairs)

    def in_plane(pieces):
        return [pieces[0]] + [swap(x, d * CORES) for x, d in zip(pieces[1:], ORDER[1:])]

    def in_line(pieces, near=count):
        return [swap(x, d * PLANE, near) for x, d in zip(pieces, line_order(planes))]

    pair = ((half, 2, width, width), f32)
    small = ((part, 2, width, width), f32)
    one = ((part, width, width), f32)
    rows_in = pltpu.VMEM((block, features), bf16)
    half_layer = ((block // 2, columns), f32)
    keep, send, chip_w = call(
        summary_kernel,
        [SMEM] + [HBM] * 6,
        [pair] * 2 + [((half, 4, 128), f32)],
        "summary",
        scratch=[rows_in] * 4
        + [
            pltpu.SMEM((heads,), f32),
            pltpu.SMEM(doc_lengths.shape, jnp.int32),
            pltpu.SemaphoreType.DMA((6,)),
        ],
        flops=1 << 26,
        moved=1 << 21,
    )(*facts, q, k, v, g)
    recv = swap(send, 1)
    totals = call(
        chip_kernel, [VMEM] * 3, [small] * CHIPS, "chip_total", moved=1 << 20
    )(chip_w, keep, recv)
    plane_w, line_w, entry_w, state_w = call(
        weights_kernel,
        [SMEM] * 3,
        [
            ((part, CHIPS, 2, 128), f32),
            ((part, planes - 1, 4, 128), f32),
            ((part, CHIPS, CHIPS + 1, 2, 128), f32),
            ((half, 8, 128), f32),
        ],
        "weights",
        moved=1 << 18,
        after=totals[:1],
        block=block,
    )(*facts)
    attn, gain_col, into_rows = call(
        within_kernel,
        [SMEM] * 3 + [VMEM] * 4,
        [((features, block), f32)] * 2 + [((heads, block), f32)],
        "within",
        flops=1 << 28,
        moved=1 << 22,
        after=totals[:1],
    )(*facts, norm_gain.reshape(1, features), q, k, v)
    totals = in_plane(totals)
    (layer_wide,) = call(
        widen_kernel, [VMEM], [((block, columns), f32)], "widen", moved=1 << 19, after=[*totals[1:], attn, plane_w]
    )(layer)
    layer_x, layer_y = swap(layer_wide, CORES), swap(layer_wide, 2 * CORES)
    near = -(-LONGEST // (PLANE * block))
    onward = call(
        plane_kernel,
        [VMEM] * (2 + CHIPS),
        [one] * (planes - 1),
        "plane_total",
        moved=1 << 19,
        after=[attn],
    )(plane_w, line_w, *totals)
    others = in_line(onward, near)
    entries = call(
        entry_kernel,
        [VMEM] * (2 + CHIPS + len(others)),
        [small] * CHIPS,
        "entries",
        moved=1 << 20,
        lines=len(others),
    )(entry_w, line_w, *totals, *others)
    entries = in_plane(entries)
    top, bottom = call(forward_kernel, [VMEM] * 2, [half_layer] * 2, "forward", moved=1 << 20)(layer_x, layer_y)
    xy_top, xy_bottom = swap(top, 2 * CORES), swap(bottom, CORES)
    mine, send = call(
        states_kernel, [VMEM] * (3 + CHIPS), [pair] * 2, "states", moved=1 << 21, after=[layer_x, layer_y]
    )(state_w, keep, recv, *entries)
    theirs = swap(send, 1)

    rows = features // count
    normed = call(
        norm_kernel,
        [SMEM] + [VMEM] * 6,
        [((features // CHIPS, block), f32)] * CHIPS,
        "norm",
        scratch=[pltpu.VMEM((features, block), f32)],
        flops=1 << 26,
        moved=1 << 21,
        rows=rows,
    )(here, q, attn, gain_col, into_rows, mine, theirs)
    if dps > 1:
        normed = for_all_dp(normed, here[0], planes, dps)
    normed = in_plane(normed)
    layers = [layer_x, layer_y, xy_top, xy_bottom]
    by_plane = ((planes, rows, columns), f32)
    product, left, right = call(
        product_send_kernel,
        [SMEM] + [VMEM] * (CHIPS + len(layers) + 1),
        [by_plane, ((planes * rows, CHIPS * block), bf16), ((CHIPS * block, columns), bf16)],
        "product_send",
        flops=1 << 27,
        moved=1 << 22,
        scale=scale,
    )(here, *normed, *layers, layer)
    (q_grad,) = call(
        q_grad_kernel,
        [SMEM] * 3 + [HBM] * 3 + [VMEM] * 2,
        [((block, features), bf16)],
        "q_grad",
        scratch=[rows_in] * 4 + [pltpu.SemaphoreType.DMA((3,))],
        out_specs=[HBM],
        flops=1 << 27,
        moved=1 << 21,
    )(*facts, k, v, g, mine, theirs)
    k_grad, v_grad = call(
        kv_grad_kernel,
        [SMEM] * 3 + [HBM] * 4 + [VMEM] * 2,
        [((block, features), bf16)] * 2,
        "kv_grad",
        scratch=[rows_in] * 6 + [pltpu.SemaphoreType.DMA((4,))],
        out_specs=[HBM] * 2,
        flops=1 << 28,
        moved=1 << 21,
    )(*facts, q, k, v, g, mine, theirs)
    pieces = planes
    halved = [((pieces // 2, rows, columns), f32)] * 2 if pieces > 1 else [by_plane]
    parts = call(
        product_kernel,
        [SMEM] + [VMEM] * 3,
        halved,
        "product",
        scratch=[pltpu.VMEM(*by_plane)] * 2,
        flops=1 << 27,
        moved=1 << 21,
        scale=scale,
    )(here, left, right, swap(product, 1))
    bit = PLANE
    while pieces > 1:
        pieces = pieces // 2
        halved = [((pieces // 2, rows, columns), f32)] * 2 if pieces > 1 else [((pieces, rows, columns), f32)]
        parts = call(halving_kernel, [VMEM] * 2, halved, "halving", moved=1 << 20, after=[q_grad])(
            parts[0], swap(parts[1], bit)
        )
        bit = 2 * bit
    proj_grad = parts[0][0]
    if dps > 1:
        proj_grad = lax.psum_scatter(proj_grad, "dp", scatter_dimension=0, tiled=True)
    shape_out = (seqs, block, features)
    return (q_grad.reshape(shape_out), k_grad.reshape(shape_out), v_grad.reshape(shape_out), proj_grad)


def solution(mesh):
    rows = P("dp", "ctx", None)
    return jax.shard_map(
        on_device,
        mesh=mesh,
        in_specs=(rows, rows, rows, rows, rows, P(), P(), P("dp", None)),
        out_specs=(rows, rows, rows, P(("dp", "ctx"), None)),
        check_vma=False,
    )
```

```python
import functools
import math

import jax
import jax.numpy as jnp
from jax import lax
from jax.experimental import pallas as pl
from jax.experimental.pallas import tpu as pltpu
from jax.sharding import PartitionSpec as P

norm_eps = 1e-06
f32 = jnp.float32
bf16 = jnp.bfloat16

CORES = 2
CHIPS = 4
PLANE = CORES * CHIPS
ORDER = (0, 1, 2, 3)

SMEM = pl.BlockSpec(memory_space=pltpu.SMEM)
VMEM = pl.BlockSpec(memory_space=pltpu.VMEM)
HBM = pl.BlockSpec(memory_space=pltpu.HBM)
LONGEST = 2048


def dot(a, b, over_a, over_b):
    return lax.dot_general(a, b, (((over_a,), (over_b,)), ((), ())), preferred_element_type=f32)


def split(x):
    high = x.astype(bf16)
    return high, (x - high.astype(f32)).astype(bf16)


def dot2(a, b, over_a, over_b):
    if a.dtype == f32:
        high, low = split(a)
        return dot(high, b, over_a, over_b) + dot(low, b, over_a, over_b)
    high, low = split(b)
    return dot(a, high, over_a, over_b) + dot(a, low, over_a, over_b)


def doc_of(position, lens):
    bound = lens[0, 0]
    doc = jnp.where(position >= bound, 1, 0)
    for k in range(1, lens.shape[1] - 1):
        bound = bound + lens[0, k]
        doc = doc + jnp.where(position >= bound, 1, 0)
    return doc


def carry(from_edge, to_edge, rate, block, lens):
    same = doc_of(from_edge * block - 1, lens) == doc_of(to_edge * block - 1, lens)
    away = jnp.abs(from_edge - to_edge) * block
    row = jnp.full((1, 128), away.astype(f32) * -rate, f32)
    return jnp.where(same, jnp.exp(row), 0.0)


def entry_exit(here, rate, block, lens, dim, shape):
    offsets = lax.broadcasted_iota(jnp.int32, shape, dim)
    docs = doc_of(here * block + offsets, lens)
    into = jnp.where(docs == doc_of(here * block - 1, lens), jnp.exp(-rate * offsets.astype(f32)), 0.0)
    out = jnp.where(
        docs == doc_of(here * block + block - 1, lens), jnp.exp(-rate * (block - offsets).astype(f32)), 0.0
    )
    return into, out


def head_lanes(head, width):
    return pl.ds(pl.multiple_of(head * width, width), width)


def fetch(refs, spaces, sems):
    copies = [pltpu.make_async_copy(ref, space, sems.at[i]) for i, (ref, space) in enumerate(zip(refs, spaces))]
    for copy in copies:
        copy.start()
    return copies


def half_heads(here, half):
    core = lax.rem(here, CORES)
    chip = lax.rem(here // CORES, CHIPS)
    part = half // CHIPS
    rows = [(i * part + t, (chip ^ d) * part + t) for i, d in enumerate(ORDER) for t in range(part)]
    return [(row, core * half + at, (1 - core) * half + at) for row, at in rows]


def summary_kernel(
    here_ref, rates_in, lens_in, q_in, k_in, v_in, g_in, keep, send, chip_w, q, k, v, g, rates, lens, sems
):
    copies = fetch((rates_in, lens_in, k_in, v_in, q_in, g_in), (rates, lens, k, v, q, g), sems)
    here = here_ref[0]
    block = q.shape[0]
    half, _, width, _ = keep.shape
    heads = half_heads(here, half)
    first = lax.rem(here, CORES) == 0
    edge = here - lax.rem(here, CORES)
    for copy in copies[:2]:
        copy.wait()
    for row, head, _ in heads:
        late = carry(edge + 1, edge + 2, rates[head], block, lens)
        early = carry(edge + 1, edge, rates[head], block, lens)
        chip_w[row, 0:1, :] = jnp.where(first, late, 1.0)
        chip_w[row, 1:2, :] = jnp.where(first, 1.0, late)
        chip_w[row, 2:3, :] = jnp.where(first, 1.0, early)
        chip_w[row, 3:4, :] = jnp.where(first, early, 1.0)
    offsets = lax.broadcasted_iota(jnp.int32, (block, width), 0)
    docs = doc_of(here * block + offsets, lens)
    enters = docs == doc_of(here * block - 1, lens)
    leaves = docs == doc_of(here * block + block - 1, lens)
    from_start, to_end = offsets.astype(f32), (block - offsets).astype(f32)
    for copy in copies[2:4]:
        copy.wait()
    for row, *pair in heads:
        for head, out in zip(pair, (keep, send)):
            past = jnp.where(leaves, jnp.exp(-rates[head] * to_end), 0.0)
            lanes = head_lanes(head, width)
            out[row, 0] = dot2(v[:, lanes], k[:, lanes].astype(f32) * past, 0, 0)
    for copy in copies[4:]:
        copy.wait()
    for row, *pair in heads:
        for head, out in zip(pair, (keep, send)):
            into = jnp.where(enters, jnp.exp(-rates[head] * from_start), 0.0)
            lanes = head_lanes(head, width)
            out[row, 1] = dot2(q[:, lanes].astype(f32) * into, g[:, lanes], 0, 0)


def chip_kernel(weights, keep, recv, *outs):
    for i, out in enumerate(outs):
        for t in range(out.shape[0]):
            row = i * out.shape[0] + t
            for k in range(2):
                own, other = weights[row, 2 * k : 2 * k + 1, :], weights[row, 2 * k + 1 : 2 * k + 2, :]
                out[t, k] = own * keep[row, k] + other * recv[row, k]


def line_order(planes):
    return [2, 1, 3] + list(range(4, planes)) if planes > 3 else list(range(planes - 1, 0, -1))


def weights_kernel(here_ref, rates, lens, plane_w, line_w, entry_w, state_w, *, block):
    here = here_ref[0]
    half = state_w.shape[0]
    part, lines = line_w.shape[:2]
    core = lax.rem(here, CORES)
    chip = lax.rem(here // CORES, CHIPS)
    plane = here // PLANE
    base = plane * PLANE
    ones = jnp.ones((1, 128), f32)
    for t in range(part):
        rate = rates[core * half + chip * part + t]

        def take(from_edge, to_edge):
            return carry(from_edge, to_edge, rate, block, lens)

        for j, d in enumerate(line_order(lines + 1)):
            to = plane ^ d
            line_w[t, j, 0:1, :] = jnp.where(to > plane, take(base + PLANE, to * PLANE), 0.0)
            line_w[t, j, 1:2, :] = jnp.where(to < plane, take(base, (to + 1) * PLANE), 0.0)
            line_w[t, j, 2:3, :] = jnp.where(to < plane, ones, 0.0)
            line_w[t, j, 3:4, :] = jnp.where(to > plane, ones, 0.0)
        for i, d in enumerate(ORDER):
            edge = base + (chip ^ d) * CORES
            plane_w[t, i, 0:1, :] = take(edge + CORES, base + PLANE)
            plane_w[t, i, 1:2, :] = take(edge, base)
            entry_w[t, i, CHIPS, 0:1, :] = take(base, edge)
            entry_w[t, i, CHIPS, 1:2, :] = take(base + PLANE, edge + CORES)
            for j, e in enumerate(ORDER):
                other = base + (chip ^ e) * CORES
                entry_w[t, i, j, 0:1, :] = jnp.where(other < edge, take(other + CORES, edge), 0.0)
                entry_w[t, i, j, 1:2, :] = jnp.where(other > edge, take(other, edge + CORES), 0.0)
    edge = here - core
    first = core == 0
    for row, head, _ in half_heads(here, half):
        fwd = carry(edge, edge + 1, rates[head], block, lens)
        bwd = carry(edge + 2, edge + 1, rates[head], block, lens)
        rows = ((0.0, 1.0), (1.0, fwd), (1.0, bwd), (0.0, 1.0))
        for k, (core0, core1) in enumerate(((0, 1), (1, 0), (2, 3), (3, 2))):
            for m in range(2):
                state_w[row, 2 * k + m : 2 * k + m + 1, :] = jnp.where(
                    first, ones * rows[core0][m], ones * rows[core1][m]
                )


def plane_kernel(weights, line_w, *refs):
    totals, outs = refs[:CHIPS], refs[CHIPS:]
    for t in range(outs[0].shape[0]):
        fwd, bwd = 0.0, 0.0
        for i, total in enumerate(totals):
            fwd = fwd + weights[t, i, 0:1, :] * total[t, 0]
            bwd = bwd + weights[t, i, 1:2, :] * total[t, 1]
        for j, out in enumerate(outs):
            out[t] = line_w[t, j, 0:1, :] * fwd + line_w[t, j, 1:2, :] * bwd


def widen_kernel(layer, out):
    out[...] = layer[...].astype(f32)


def forward_kernel(layer_x, layer_y, top, bottom):
    top[...] = layer_x[: top.shape[0], :]
    bottom[...] = layer_y[top.shape[0] :, :]


def entry_kernel(weights, line_w, *refs, lines):
    totals, others, outs = refs[:CHIPS], refs[CHIPS : CHIPS + lines], refs[CHIPS + lines :]
    for t in range(outs[0].shape[0]):
        before, after = 0.0, 0.0
        for j, other in enumerate(others):
            before = before + line_w[t, j, 2:3, :] * other[t]
            after = after + line_w[t, j, 3:4, :] * other[t]
        for i, out in enumerate(outs):
            fwd = weights[t, i, CHIPS, 0:1, :] * before
            bwd = weights[t, i, CHIPS, 1:2, :] * after
            for j, total in enumerate(totals):
                if i != j:
                    fwd = fwd + weights[t, i, j, 0:1, :] * total[t, 0]
                    bwd = bwd + weights[t, i, j, 1:2, :] * total[t, 1]
            out[t, 0], out[t, 1] = fwd, bwd


def states_kernel(weights, keep, recv, *refs):
    entries, (mine, send) = refs[:CHIPS], refs[CHIPS:]
    part = entries[0].shape[0]
    for i, entry in enumerate(entries):
        for t in range(part):
            row = i * part + t
            for k in range(2):
                for m, (own, out) in enumerate(((recv, mine), (keep, send))):
                    at = 4 * k + 2 * m
                    out[row, k] = weights[row, at : at + 1, :] * own[row, k] + weights[row, at + 1 : at + 2, :] * entry[t, k]


def causal(here, block, lens):
    at_j = lax.broadcasted_iota(jnp.int32, (block, block), 0)
    at_i = lax.broadcasted_iota(jnp.int32, (block, block), 1)
    docs_j = doc_of(here * block + at_j, lens)
    docs_i = doc_of(here * block + at_i, lens)
    return (docs_i == docs_j) & (at_i >= at_j), jnp.maximum(at_i - at_j, 0).astype(f32)


def within_kernel(here_ref, rates, lens, gain, q, k, v, attn, gain_col, into_rows):
    here = here_ref[0]
    block, features = q.shape
    heads = rates.shape[0]
    width = features // heads
    reached, away = causal(here, block, lens)
    for head in range(heads):
        lanes = slice(head * width, (head + 1) * width)
        gain_col[lanes, :] = jnp.broadcast_to(gain[:, lanes], (block, width)).T
        decay = jnp.where(reached, jnp.exp(-rates[head] * away), 0.0)
        scores = dot(k[:, lanes], q[:, lanes], 1, 1) * decay
        attn[lanes, :] = dot2(v[:, lanes], scores, 0, 0)
        into_rows[head : head + 1, :], _ = entry_exit(here, rates[head], block, lens, 1, (1, block))


def norm_kernel(here_ref, q, attn, gain_col, into_rows, mine, recv, *refs, rows):
    outs, total = refs[:CHIPS], refs[CHIPS]
    here = here_ref[0]
    block, features = q.shape
    half, _, width, _ = mine.shape
    chip = lax.rem(here // CORES, CHIPS)
    squares = jnp.zeros((width, block), f32)
    for row, *pair in half_heads(here, half):
        for head, states in zip(pair, (mine, recv)):
            lanes = head_lanes(head, width)
            at = attn[lanes, :] + into_rows[pl.ds(head, 1), :] * dot2(states[row, 0], q[:, lanes], 1, 1)
            total[lanes, :] = at
            squares = squares + at * at
    mean = jnp.sum(squares, axis=0, keepdims=True) * (1.0 / features)
    factor = lax.rsqrt(mean + norm_eps)
    planes = features // (PLANE * rows)
    for out, d in zip(outs, ORDER):
        for to_core in range(CORES):
            for plane in range(planes):
                block_at = plane * PLANE + (chip ^ d) * CORES + to_core
                at = pl.ds(pl.multiple_of(block_at * rows, rows), rows)
                normed = (total[at, :] * factor * gain_col[at, :]).astype(bf16)
                to = to_core * planes + plane
                out[to * rows : (to + 1) * rows, :] = normed.astype(f32)


def product_send_kernel(here_ref, *refs, scale):
    core = lax.rem(here_ref[0], CORES)
    normed, layers, (layer, out, left, right) = refs[:CHIPS], refs[CHIPS:-4], refs[-4:]
    rows = left.shape[0]
    block = layer.shape[0]
    mine = pl.ds(pl.multiple_of(core * rows, rows), rows)
    other = pl.ds(pl.multiple_of((1 - core) * rows, rows), rows)
    right[:block, :] = layer[...]
    at = block
    for x in layers:
        right[at : at + x.shape[0], :] = x[...].astype(bf16)
        at = at + x.shape[0]
    for d, x in enumerate(normed):
        left[:, d * block : (d + 1) * block] = x[mine, :].astype(bf16)
    send = jnp.concatenate([x[other, :].astype(bf16) for x in normed], axis=1)
    out[...] = (dot(send, right[...], 1, 0) * scale).reshape(out.shape)


def halve(total, outs):
    pieces = total.shape[0] // len(outs)
    for side, out in enumerate(outs):
        for j in range(pieces):
            out[j] = total[len(outs) * j + side]


def product_kernel(here_ref, left, right, recv, *refs, scale):
    outs, (product, total) = refs[:-2], refs[-2:]
    plane = here_ref[0] // PLANE
    product[...] = (dot(left[...], right[...], 1, 0) * scale).reshape(product.shape)
    for d in range(product.shape[0]):
        total[d] = product[plane ^ d] + recv[plane ^ d]
    halve(total, outs)


def halving_kernel(own, recv, *outs):
    halve(own[...] + recv[...], outs)


def outputs_kernel(here_ref, rates, lens, q_in, k_in, v_in, g_in, mine, recv, q_out, k_out, v_out, *scratch):
    q, k, v, g, q_grad, k_grad, v_grad, sems = scratch
    copies = fetch((q_in, k_in, v_in, g_in), (q, k, v, g), sems)
    here = here_ref[0]
    block, features = q.shape
    half, _, width, _ = mine.shape
    reached, away = causal(here, block, lens)
    for copy in copies:
        copy.wait()
    for row, *pair in half_heads(here, half):
        for head, states in zip(pair, (mine, recv)):
            lanes = head_lanes(head, width)
            rate = rates[head]
            qh, kh, vh, gh = q[:, lanes], k[:, lanes], v[:, lanes], g[:, lanes]
            decay = jnp.where(reached, jnp.exp(-rate * away), 0.0)
            scores = dot(kh, qh, 1, 1) * decay
            grads = dot(vh, gh, 1, 1) * decay
            into, past = entry_exit(here, rate, block, lens, 0, (block, width))
            before, after = states[row, 0], states[row, 1]
            q_grad[:, lanes] = (dot2(grads, kh, 0, 0) + into * dot2(gh, before, 1, 0)).astype(bf16)
            k_grad[:, lanes] = (dot2(grads, qh, 1, 0) + past * dot2(vh, after, 1, 1)).astype(bf16)
            v_grad[:, lanes] = (dot2(scores, gh, 1, 0) + past * dot2(kh, after, 1, 0)).astype(bf16)
    outs = [pltpu.make_async_copy(x, y, sems.at[i]) for i, (x, y) in enumerate(((q_grad, q_out), (k_grad, k_out), (v_grad, v_out)))]
    for copy in outs:
        copy.start()
    for copy in outs:
        copy.wait()


def for_all_dp(outs, here, planes, dps):
    order = (here // CORES) % CHIPS ^ jnp.array(ORDER)
    whole = jnp.zeros((CHIPS,) + outs[0].shape, f32).at[order].set(jnp.stack(outs))
    rows = whole.shape[1] // (CORES * planes)
    whole = whole.reshape(CHIPS, CORES, planes, rows, -1).transpose(2, 0, 1, 3, 4)
    whole = whole.reshape(dps, planes, CHIPS, CORES, rows // dps, -1).transpose(2, 3, 1, 0, 4, 5)
    whole = whole.reshape((CHIPS,) + outs[0].shape)[order]
    return [whole[d] for d in range(CHIPS)]


def call(kernel, specs, outs, name, scratch=(), flops=0, moved=0, out_specs=None, after=(), **named):
    reads = len(specs)

    def body(*refs):
        kernel(*refs[:reads], *refs[reads + len(after) :], **named)

    def run(*operands):
        operands = [
            pltpu.with_memory_space_constraint(x, pltpu.HBM) if spec is HBM else x for x, spec in zip(operands, specs)
        ]
        return pl.pallas_call(
            body,
            out_shape=[jax.ShapeDtypeStruct(shape, dtype) for shape, dtype in outs],
            in_specs=list(specs) + [pl.BlockSpec(memory_space=pl.ANY)] * len(after),
            out_specs=out_specs or [VMEM] * len(outs),
            scratch_shapes=list(scratch),
            cost_estimate=pl.CostEstimate(flops=flops, bytes_accessed=moved, transcendentals=0),
            compiler_params=pltpu.CompilerParams(vmem_limit_bytes=16 * 1024 * 1024),
            name=name,
        )(*operands, *after)

    return run


def on_device(queries, keys, values, out_grad, layer_grad, norm_gain, decay_rates, doc_lengths):
    seqs, block, features = queries.shape
    assert seqs == 1
    heads = decay_rates.shape[0]
    width = features // heads
    columns = layer_grad.shape[2]
    half = heads // CORES
    part = half // CHIPS
    count = lax.axis_size("ctx")
    planes = count // PLANE
    dps = lax.axis_size("dp")
    scale = 1.0 / math.sqrt(seqs * block * dps * count)
    here = lax.axis_index("ctx").astype(jnp.int32).reshape(1)
    facts = (here, decay_rates, doc_lengths)
    q, k, v, g = (x.reshape(block, features) for x in (queries, keys, values, out_grad))
    layer = layer_grad.reshape(block, columns)

    def swap(x, bit, near=count):
        pairs = [(i, i ^ bit) for i in range(count) if abs(i // PLANE - (i ^ bit) // PLANE) <= near]
        return lax.ppermute(x, "ctx", pairs)

    def in_plane(pieces):
        return [pieces[0]] + [swap(x, d * CORES) for x, d in zip(pieces[1:], ORDER[1:])]

    def in_line(pieces, near=count):
        return [swap(x, d * PLANE, near) for x, d in zip(pieces, line_order(planes))]

    pair = ((half, 2, width, width), f32)
    small = ((part, 2, width, width), f32)
    one = ((part, width, width), f32)
    rows_in = pltpu.VMEM((block, features), bf16)
    half_layer = ((block // 2, columns), f32)
    keep, send, chip_w = call(
        summary_kernel,
        [SMEM] + [HBM] * 6,
        [pair] * 2 + [((half, 4, 128), f32)],
        "summary",
        scratch=[rows_in] * 4
        + [
            pltpu.SMEM((heads,), f32),
            pltpu.SMEM(doc_lengths.shape, jnp.int32),
            pltpu.SemaphoreType.DMA((6,)),
        ],
        flops=1 << 26,
        moved=1 << 21,
    )(*facts, q, k, v, g)
    recv = swap(send, 1)
    totals = call(
        chip_kernel, [VMEM] * 3, [small] * CHIPS, "chip_total", moved=1 << 20
    )(chip_w, keep, recv)
    plane_w, line_w, entry_w, state_w = call(
        weights_kernel,
        [SMEM] * 3,
        [
            ((part, CHIPS, 2, 128), f32),
            ((part, planes - 1, 4, 128), f32),
            ((part, CHIPS, CHIPS + 1, 2, 128), f32),
            ((half, 8, 128), f32),
        ],
        "weights",
        moved=1 << 18,
        after=totals[:1],
        block=block,
    )(*facts)
    attn, gain_col, into_rows = call(
        within_kernel,
        [SMEM] * 3 + [VMEM] * 4,
        [((features, block), f32)] * 2 + [((heads, block), f32)],
        "within",
        flops=1 << 28,
        moved=1 << 22,
        after=totals[:1],
    )(*facts, norm_gain.reshape(1, features), q, k, v)
    totals = in_plane(totals)
    (layer_wide,) = call(
        widen_kernel, [VMEM], [((block, columns), f32)], "widen", moved=1 << 19, after=[*totals[1:], attn, plane_w]
    )(layer)
    layer_x, layer_y = swap(layer_wide, CORES), swap(layer_wide, 2 * CORES)
    near = -(-LONGEST // (PLANE * block))
    onward = call(
        plane_kernel,
        [VMEM] * (2 + CHIPS),
        [one] * (planes - 1),
        "plane_total",
        moved=1 << 19,
        after=[attn],
    )(plane_w, line_w, *totals)
    others = in_line(onward, near)
    entries = call(
        entry_kernel,
        [VMEM] * (2 + CHIPS + len(others)),
        [small] * CHIPS,
        "entries",
        moved=1 << 20,
        lines=len(others),
    )(entry_w, line_w, *totals, *others)
    entries = in_plane(entries)
    top, bottom = call(forward_kernel, [VMEM] * 2, [half_layer] * 2, "forward", moved=1 << 20)(layer_x, layer_y)
    xy_top, xy_bottom = swap(top, 2 * CORES), swap(bottom, CORES)
    mine, send = call(
        states_kernel, [VMEM] * (3 + CHIPS), [pair] * 2, "states", moved=1 << 21, after=[layer_x, layer_y]
    )(state_w, keep, recv, *entries)
    theirs = swap(send, 1)

    rows = features // count
    normed = call(
        norm_kernel,
        [SMEM] + [VMEM] * 6,
        [((features // CHIPS, block), f32)] * CHIPS,
        "norm",
        scratch=[pltpu.VMEM((features, block), f32)],
        flops=1 << 26,
        moved=1 << 21,
        rows=rows,
    )(here, q, attn, gain_col, into_rows, mine, theirs)
    if dps > 1:
        normed = for_all_dp(normed, here[0], planes, dps)
    normed = in_plane(normed)
    layers = [layer_x, layer_y, xy_top, xy_bottom]
    q_grad, k_grad, v_grad = call(
        outputs_kernel,
        [SMEM] * 3 + [HBM] * 4 + [VMEM] * 2,
        [((block, features), bf16)] * 3,
        "outputs",
        scratch=[rows_in] * 7 + [pltpu.SemaphoreType.DMA((4,))],
        out_specs=[HBM] * 3,
        flops=1 << 29,
        moved=1 << 22,
    )(*facts, q, k, v, g, mine, theirs)
    by_plane = ((planes, rows, columns), f32)
    product, left, right = call(
        product_send_kernel,
        [SMEM] + [VMEM] * (CHIPS + len(layers) + 1),
        [by_plane, ((planes * rows, CHIPS * block), bf16), ((CHIPS * block, columns), bf16)],
        "product_send",
        flops=1 << 27,
        moved=1 << 22,
        after=[q_grad],
        scale=scale,
    )(here, *normed, *layers, layer)
    pieces = planes
    halved = [((pieces // 2, rows, columns), f32)] * 2 if pieces > 1 else [by_plane]
    parts = call(
        product_kernel,
        [SMEM] + [VMEM] * 3,
        halved,
        "product",
        scratch=[pltpu.VMEM(*by_plane)] * 2,
        flops=1 << 27,
        moved=1 << 21,
        scale=scale,
    )(here, left, right, swap(product, 1))
    bit = PLANE
    while pieces > 1:
        pieces = pieces // 2
        halved = [((pieces // 2, rows, columns), f32)] * 2 if pieces > 1 else [((pieces, rows, columns), f32)]
        parts = call(halving_kernel, [VMEM] * 2, halved, "halving", moved=1 << 20)(parts[0], swap(parts[1], bit))
        bit = 2 * bit
    proj_grad = parts[0][0]
    if dps > 1:
        proj_grad = lax.psum_scatter(proj_grad, "dp", scatter_dimension=0, tiled=True)
    shape_out = (seqs, block, features)
    return (q_grad.reshape(shape_out), k_grad.reshape(shape_out), v_grad.reshape(shape_out), proj_grad)


def solution(mesh):
    rows = P("dp", "ctx", None)
    return jax.shard_map(
        on_device,
        mesh=mesh,
        in_specs=(rows, rows, rows, rows, rows, P(), P(), P("dp", None)),
        out_specs=(rows, rows, rows, P(("dp", "ctx"), None)),
        check_vma=False,
    )
```

```python
import functools
import math

import jax
import jax.numpy as jnp
from jax import lax
from jax.experimental import pallas as pl
from jax.experimental.pallas import tpu as pltpu
from jax.sharding import PartitionSpec as P

norm_eps = 1e-06
f32 = jnp.float32
bf16 = jnp.bfloat16

CORES = 2
CHIPS = 4
PLANE = CORES * CHIPS
ORDER = (0, 1, 2, 3)

SMEM = pl.BlockSpec(memory_space=pltpu.SMEM)
VMEM = pl.BlockSpec(memory_space=pltpu.VMEM)
HBM = pl.BlockSpec(memory_space=pltpu.HBM)
LONGEST = 2048


def dot(a, b, over_a, over_b):
    return lax.dot_general(a, b, (((over_a,), (over_b,)), ((), ())), preferred_element_type=f32)


def split(x):
    high = x.astype(bf16)
    return high, (x - high.astype(f32)).astype(bf16)


def dot2(a, b, over_a, over_b):
    if a.dtype == f32:
        high, low = split(a)
        return dot(high, b, over_a, over_b) + dot(low, b, over_a, over_b)
    high, low = split(b)
    return dot(a, high, over_a, over_b) + dot(a, low, over_a, over_b)


def doc_of(position, lens):
    bound = lens[0, 0]
    doc = jnp.where(position >= bound, 1, 0)
    for k in range(1, lens.shape[1] - 1):
        bound = bound + lens[0, k]
        doc = doc + jnp.where(position >= bound, 1, 0)
    return doc


def carry(from_edge, to_edge, rate, block, lens):
    same = doc_of(from_edge * block - 1, lens) == doc_of(to_edge * block - 1, lens)
    away = jnp.abs(from_edge - to_edge) * block
    row = jnp.full((1, 128), away.astype(f32) * -rate, f32)
    return jnp.where(same, jnp.exp(row), 0.0)


def entry_exit(here, rate, block, lens, dim, shape):
    offsets = lax.broadcasted_iota(jnp.int32, shape, dim)
    docs = doc_of(here * block + offsets, lens)
    into = jnp.where(docs == doc_of(here * block - 1, lens), jnp.exp(-rate * offsets.astype(f32)), 0.0)
    out = jnp.where(
        docs == doc_of(here * block + block - 1, lens), jnp.exp(-rate * (block - offsets).astype(f32)), 0.0
    )
    return into, out


def head_lanes(head, width):
    return pl.ds(pl.multiple_of(head * width, width), width)


def fetch(refs, spaces, sems):
    copies = [pltpu.make_async_copy(ref, space, sems.at[i]) for i, (ref, space) in enumerate(zip(refs, spaces))]
    for copy in copies:
        copy.start()
    return copies


def half_heads(here, half):
    core = lax.rem(here, CORES)
    chip = lax.rem(here // CORES, CHIPS)
    part = half // CHIPS
    rows = [(i * part + t, (chip ^ d) * part + t) for i, d in enumerate(ORDER) for t in range(part)]
    return [(row, core * half + at, (1 - core) * half + at) for row, at in rows]


def summary_kernel(
    here_ref, rates_in, lens_in, q_in, k_in, v_in, g_in, keep, send, chip_w, q, k, v, g, rates, lens, sems
):
    copies = fetch((rates_in, lens_in, k_in, v_in, q_in, g_in), (rates, lens, k, v, q, g), sems)
    here = here_ref[0]
    block = q.shape[0]
    half, _, width, _ = keep.shape
    heads = half_heads(here, half)
    first = lax.rem(here, CORES) == 0
    edge = here - lax.rem(here, CORES)
    for copy in copies[:2]:
        copy.wait()
    for row, head, _ in heads:
        late = carry(edge + 1, edge + 2, rates[head], block, lens)
        early = carry(edge + 1, edge, rates[head], block, lens)
        chip_w[row, 0:1, :] = jnp.where(first, late, 1.0)
        chip_w[row, 1:2, :] = jnp.where(first, 1.0, late)
        chip_w[row, 2:3, :] = jnp.where(first, 1.0, early)
        chip_w[row, 3:4, :] = jnp.where(first, early, 1.0)
    offsets = lax.broadcasted_iota(jnp.int32, (block, width), 0)
    docs = doc_of(here * block + offsets, lens)
    enters = docs == doc_of(here * block - 1, lens)
    leaves = docs == doc_of(here * block + block - 1, lens)
    from_start, to_end = offsets.astype(f32), (block - offsets).astype(f32)
    for copy in copies[2:4]:
        copy.wait()
    for row, *pair in heads:
        for head, out in zip(pair, (keep, send)):
            past = jnp.where(leaves, jnp.exp(-rates[head] * to_end), 0.0)
            lanes = head_lanes(head, width)
            out[row, 0] = dot2(v[:, lanes], k[:, lanes].astype(f32) * past, 0, 0)
    for copy in copies[4:]:
        copy.wait()
    for row, *pair in heads:
        for head, out in zip(pair, (keep, send)):
            into = jnp.where(enters, jnp.exp(-rates[head] * from_start), 0.0)
            lanes = head_lanes(head, width)
            out[row, 1] = dot2(q[:, lanes].astype(f32) * into, g[:, lanes], 0, 0)


def chip_kernel(weights, keep, recv, *outs):
    for i, out in enumerate(outs):
        for t in range(out.shape[0]):
            row = i * out.shape[0] + t
            for k in range(2):
                own, other = weights[row, 2 * k : 2 * k + 1, :], weights[row, 2 * k + 1 : 2 * k + 2, :]
                out[t, k] = own * keep[row, k] + other * recv[row, k]


def line_order(planes):
    return list(range(planes - 1, 0, -1))


def weights_kernel(here_ref, rates, lens, plane_w, line_w, entry_w, state_w, *, block):
    here = here_ref[0]
    half = state_w.shape[0]
    part, lines = line_w.shape[:2]
    core = lax.rem(here, CORES)
    chip = lax.rem(here // CORES, CHIPS)
    plane = here // PLANE
    base = plane * PLANE
    ones = jnp.ones((1, 128), f32)
    for t in range(part):
        rate = rates[core * half + chip * part + t]

        def take(from_edge, to_edge):
            return carry(from_edge, to_edge, rate, block, lens)

        for j, d in enumerate(line_order(lines + 1)):
            to = plane ^ d
            line_w[t, j, 0:1, :] = jnp.where(to > plane, take(base + PLANE, to * PLANE), 0.0)
            line_w[t, j, 1:2, :] = jnp.where(to < plane, take(base, (to + 1) * PLANE), 0.0)
            line_w[t, j, 2:3, :] = jnp.where(to < plane, ones, 0.0)
            line_w[t, j, 3:4, :] = jnp.where(to > plane, ones, 0.0)
        for i, d in enumerate(ORDER):
            edge = base + (chip ^ d) * CORES
            plane_w[t, i, 0:1, :] = take(edge + CORES, base + PLANE)
            plane_w[t, i, 1:2, :] = take(edge, base)
            entry_w[t, i, CHIPS, 0:1, :] = take(base, edge)
            entry_w[t, i, CHIPS, 1:2, :] = take(base + PLANE, edge + CORES)
            for j, e in enumerate(ORDER):
                other = base + (chip ^ e) * CORES
                entry_w[t, i, j, 0:1, :] = jnp.where(other < edge, take(other + CORES, edge), 0.0)
                entry_w[t, i, j, 1:2, :] = jnp.where(other > edge, take(other, edge + CORES), 0.0)
    edge = here - core
    first = core == 0
    for row, head, _ in half_heads(here, half):
        fwd = carry(edge, edge + 1, rates[head], block, lens)
        bwd = carry(edge + 2, edge + 1, rates[head], block, lens)
        rows = ((0.0, 1.0), (1.0, fwd), (1.0, bwd), (0.0, 1.0))
        for k, (core0, core1) in enumerate(((0, 1), (1, 0), (2, 3), (3, 2))):
            for m in range(2):
                state_w[row, 2 * k + m : 2 * k + m + 1, :] = jnp.where(
                    first, ones * rows[core0][m], ones * rows[core1][m]
                )


def plane_kernel(weights, line_w, *refs):
    totals, outs = refs[:CHIPS], refs[CHIPS:]
    for t in range(outs[0].shape[0]):
        fwd, bwd = 0.0, 0.0
        for i, total in enumerate(totals):
            fwd = fwd + weights[t, i, 0:1, :] * total[t, 0]
            bwd = bwd + weights[t, i, 1:2, :] * total[t, 1]
        for j, out in enumerate(outs):
            out[t] = line_w[t, j, 0:1, :] * fwd + line_w[t, j, 1:2, :] * bwd


def widen_kernel(layer, out):
    out[...] = layer[...].astype(f32)


def forward_kernel(layer_x, layer_y, top, bottom):
    top[...] = layer_x[: top.shape[0], :]
    bottom[...] = layer_y[top.shape[0] :, :]


def entry_kernel(weights, line_w, *refs, lines):
    totals, others, outs = refs[:CHIPS], refs[CHIPS : CHIPS + lines], refs[CHIPS + lines :]
    for t in range(outs[0].shape[0]):
        before, after = 0.0, 0.0
        for j, other in enumerate(others):
            before = before + line_w[t, j, 2:3, :] * other[t]
            after = after + line_w[t, j, 3:4, :] * other[t]
        for i, out in enumerate(outs):
            fwd = weights[t, i, CHIPS, 0:1, :] * before
            bwd = weights[t, i, CHIPS, 1:2, :] * after
            for j, total in enumerate(totals):
                if i != j:
                    fwd = fwd + weights[t, i, j, 0:1, :] * total[t, 0]
                    bwd = bwd + weights[t, i, j, 1:2, :] * total[t, 1]
            out[t, 0], out[t, 1] = fwd, bwd


def states_kernel(weights, keep, recv, *refs):
    entries, (mine, send) = refs[:CHIPS], refs[CHIPS:]
    part = entries[0].shape[0]
    for i, entry in enumerate(entries):
        for t in range(part):
            row = i * part + t
            for k in range(2):
                for m, (own, out) in enumerate(((recv, mine), (keep, send))):
                    at = 4 * k + 2 * m
                    out[row, k] = weights[row, at : at + 1, :] * own[row, k] + weights[row, at + 1 : at + 2, :] * entry[t, k]


def causal(here, block, lens):
    at_j = lax.broadcasted_iota(jnp.int32, (block, block), 0)
    at_i = lax.broadcasted_iota(jnp.int32, (block, block), 1)
    docs_j = doc_of(here * block + at_j, lens)
    docs_i = doc_of(here * block + at_i, lens)
    return (docs_i == docs_j) & (at_i >= at_j), jnp.maximum(at_i - at_j, 0).astype(f32)


def within_kernel(here_ref, rates, lens, gain, q, k, v, attn, gain_col, into_rows):
    here = here_ref[0]
    block, features = q.shape
    heads = rates.shape[0]
    width = features // heads
    reached, away = causal(here, block, lens)
    for head in range(heads):
        lanes = slice(head * width, (head + 1) * width)
        gain_col[lanes, :] = jnp.broadcast_to(gain[:, lanes], (block, width)).T
        decay = jnp.where(reached, jnp.exp(-rates[head] * away), 0.0)
        scores = dot(k[:, lanes], q[:, lanes], 1, 1) * decay
        attn[lanes, :] = dot2(v[:, lanes], scores, 0, 0)
        into_rows[head : head + 1, :], _ = entry_exit(here, rates[head], block, lens, 1, (1, block))


def norm_kernel(here_ref, q, attn, gain_col, into_rows, mine, recv, *refs, rows):
    outs, total = refs[:CHIPS], refs[CHIPS]
    here = here_ref[0]
    block, features = q.shape
    half, _, width, _ = mine.shape
    chip = lax.rem(here // CORES, CHIPS)
    squares = jnp.zeros((width, block), f32)
    for row, *pair in half_heads(here, half):
        for head, states in zip(pair, (mine, recv)):
            lanes = head_lanes(head, width)
            at = attn[lanes, :] + into_rows[pl.ds(head, 1), :] * dot2(states[row, 0], q[:, lanes], 1, 1)
            total[lanes, :] = at
            squares = squares + at * at
    mean = jnp.sum(squares, axis=0, keepdims=True) * (1.0 / features)
    factor = lax.rsqrt(mean + norm_eps)
    planes = features // (PLANE * rows)
    for out, d in zip(outs, ORDER):
        for to_core in range(CORES):
            for plane in range(planes):
                block_at = plane * PLANE + (chip ^ d) * CORES + to_core
                at = pl.ds(pl.multiple_of(block_at * rows, rows), rows)
                normed = (total[at, :] * factor * gain_col[at, :]).astype(bf16)
                to = to_core * planes + plane
                out[to * rows : (to + 1) * rows, :] = normed.astype(f32)


def product_send_kernel(here_ref, *refs, scale):
    core = lax.rem(here_ref[0], CORES)
    normed, layers, (layer, out, left, right) = refs[:CHIPS], refs[CHIPS:-4], refs[-4:]
    rows = left.shape[0]
    block = layer.shape[0]
    mine = pl.ds(pl.multiple_of(core * rows, rows), rows)
    other = pl.ds(pl.multiple_of((1 - core) * rows, rows), rows)
    right[:block, :] = layer[...]
    at = block
    for x in layers:
        right[at : at + x.shape[0], :] = x[...].astype(bf16)
        at = at + x.shape[0]
    for d, x in enumerate(normed):
        left[:, d * block : (d + 1) * block] = x[mine, :].astype(bf16)
    send = jnp.concatenate([x[other, :].astype(bf16) for x in normed], axis=1)
    out[...] = (dot(send, right[...], 1, 0) * scale).reshape(out.shape)


def product_kernel(here_ref, left, right, recv, *refs, scale):
    outs, product = refs[:-1], refs[-1]
    plane = here_ref[0] // PLANE
    product[...] = (dot(left[...], right[...], 1, 0) * scale).reshape(product.shape)
    for out, d in zip(outs, [0] + line_order(len(outs))):
        out[...] = product[plane ^ d] + recv[plane ^ d]


def sum_kernel(*refs):
    total = refs[0][...]
    for x in refs[1:-1]:
        total = total + x[...]
    refs[-1][...] = total


def outputs_kernel(here_ref, rates, lens, q_in, k_in, v_in, g_in, mine, recv, q_out, k_out, v_out, *scratch):
    q, k, v, g, q_grad, k_grad, v_grad, sems = scratch
    copies = fetch((q_in, k_in, v_in, g_in), (q, k, v, g), sems)
    here = here_ref[0]
    block, features = q.shape
    half, _, width, _ = mine.shape
    reached, away = causal(here, block, lens)
    for copy in copies:
        copy.wait()
    for row, *pair in half_heads(here, half):
        for head, states in zip(pair, (mine, recv)):
            lanes = head_lanes(head, width)
            rate = rates[head]
            qh, kh, vh, gh = q[:, lanes], k[:, lanes], v[:, lanes], g[:, lanes]
            decay = jnp.where(reached, jnp.exp(-rate * away), 0.0)
            scores = dot(kh, qh, 1, 1) * decay
            grads = dot(vh, gh, 1, 1) * decay
            into, past = entry_exit(here, rate, block, lens, 0, (block, width))
            before, after = states[row, 0], states[row, 1]
            q_grad[:, lanes] = (dot2(grads, kh, 0, 0) + into * dot2(gh, before, 1, 0)).astype(bf16)
            k_grad[:, lanes] = (dot2(grads, qh, 1, 0) + past * dot2(vh, after, 1, 1)).astype(bf16)
            v_grad[:, lanes] = (dot2(scores, gh, 1, 0) + past * dot2(kh, after, 1, 0)).astype(bf16)
    outs = [pltpu.make_async_copy(x, y, sems.at[i]) for i, (x, y) in enumerate(((q_grad, q_out), (k_grad, k_out), (v_grad, v_out)))]
    for copy in outs:
        copy.start()
    for copy in outs:
        copy.wait()


def for_all_dp(outs, here, planes, dps):
    order = (here // CORES) % CHIPS ^ jnp.array(ORDER)
    whole = jnp.zeros((CHIPS,) + outs[0].shape, f32).at[order].set(jnp.stack(outs))
    rows = whole.shape[1] // (CORES * planes)
    whole = whole.reshape(CHIPS, CORES, planes, rows, -1).transpose(2, 0, 1, 3, 4)
    whole = whole.reshape(dps, planes, CHIPS, CORES, rows // dps, -1).transpose(2, 3, 1, 0, 4, 5)
    whole = whole.reshape((CHIPS,) + outs[0].shape)[order]
    return [whole[d] for d in range(CHIPS)]


def call(kernel, specs, outs, name, scratch=(), flops=0, moved=0, out_specs=None, after=(), **named):
    reads = len(specs)

    def body(*refs):
        kernel(*refs[:reads], *refs[reads + len(after) :], **named)

    def run(*operands):
        operands = [
            pltpu.with_memory_space_constraint(x, pltpu.HBM) if spec is HBM else x for x, spec in zip(operands, specs)
        ]
        return pl.pallas_call(
            body,
            out_shape=[jax.ShapeDtypeStruct(shape, dtype) for shape, dtype in outs],
            in_specs=list(specs) + [pl.BlockSpec(memory_space=pl.ANY)] * len(after),
            out_specs=out_specs or [VMEM] * len(outs),
            scratch_shapes=list(scratch),
            cost_estimate=pl.CostEstimate(flops=flops, bytes_accessed=moved, transcendentals=0),
            compiler_params=pltpu.CompilerParams(vmem_limit_bytes=16 * 1024 * 1024),
            name=name,
        )(*operands, *after)

    return run


def on_device(queries, keys, values, out_grad, layer_grad, norm_gain, decay_rates, doc_lengths):
    seqs, block, features = queries.shape
    assert seqs == 1
    heads = decay_rates.shape[0]
    width = features // heads
    columns = layer_grad.shape[2]
    half = heads // CORES
    part = half // CHIPS
    count = lax.axis_size("ctx")
    planes = count // PLANE
    dps = lax.axis_size("dp")
    scale = 1.0 / math.sqrt(seqs * block * dps * count)
    here = lax.axis_index("ctx").astype(jnp.int32).reshape(1)
    facts = (here, decay_rates, doc_lengths)
    q, k, v, g = (x.reshape(block, features) for x in (queries, keys, values, out_grad))
    layer = layer_grad.reshape(block, columns)

    def swap(x, bit, near=count):
        pairs = [(i, i ^ bit) for i in range(count) if abs(i // PLANE - (i ^ bit) // PLANE) <= near]
        return lax.ppermute(x, "ctx", pairs)

    def in_plane(pieces):
        return [pieces[0]] + [swap(x, d * CORES) for x, d in zip(pieces[1:], ORDER[1:])]

    def in_line(pieces, near=count):
        return [swap(x, d * PLANE, near) for x, d in zip(pieces, line_order(planes))]

    pair = ((half, 2, width, width), f32)
    small = ((part, 2, width, width), f32)
    one = ((part, width, width), f32)
    rows_in = pltpu.VMEM((block, features), bf16)
    half_layer = ((block // 2, columns), f32)
    keep, send, chip_w = call(
        summary_kernel,
        [SMEM] + [HBM] * 6,
        [pair] * 2 + [((half, 4, 128), f32)],
        "summary",
        scratch=[rows_in] * 4
        + [
            pltpu.SMEM((heads,), f32),
            pltpu.SMEM(doc_lengths.shape, jnp.int32),
            pltpu.SemaphoreType.DMA((6,)),
        ],
        flops=1 << 26,
        moved=1 << 21,
    )(*facts, q, k, v, g)
    recv = swap(send, 1)
    totals = call(
        chip_kernel, [VMEM] * 3, [small] * CHIPS, "chip_total", moved=1 << 20
    )(chip_w, keep, recv)
    plane_w, line_w, entry_w, state_w = call(
        weights_kernel,
        [SMEM] * 3,
        [
            ((part, CHIPS, 2, 128), f32),
            ((part, planes - 1, 4, 128), f32),
            ((part, CHIPS, CHIPS + 1, 2, 128), f32),
            ((half, 8, 128), f32),
        ],
        "weights",
        moved=1 << 18,
        after=totals[:1],
        block=block,
    )(*facts)
    attn, gain_col, into_rows = call(
        within_kernel,
        [SMEM] * 3 + [VMEM] * 4,
        [((features, block), f32)] * 2 + [((heads, block), f32)],
        "within",
        flops=1 << 28,
        moved=1 << 22,
        after=totals[:1],
    )(*facts, norm_gain.reshape(1, features), q, k, v)
    totals = in_plane(totals)
    (layer_wide,) = call(
        widen_kernel, [VMEM], [((block, columns), f32)], "widen", moved=1 << 19, after=[*totals[1:], attn, plane_w]
    )(layer)
    layer_x, layer_y = swap(layer_wide, CORES), swap(layer_wide, 2 * CORES)
    near = -(-LONGEST // (PLANE * block))
    onward = call(
        plane_kernel,
        [VMEM] * (2 + CHIPS),
        [one] * (planes - 1),
        "plane_total",
        moved=1 << 19,
        after=[attn],
    )(plane_w, line_w, *totals)
    others = in_line(onward, near)
    entries = call(
        entry_kernel,
        [VMEM] * (2 + CHIPS + len(others)),
        [small] * CHIPS,
        "entries",
        moved=1 << 20,
        lines=len(others),
    )(entry_w, line_w, *totals, *others)
    entries = in_plane(entries)
    top, bottom = call(forward_kernel, [VMEM] * 2, [half_layer] * 2, "forward", moved=1 << 20)(layer_x, layer_y)
    xy_top, xy_bottom = swap(top, 2 * CORES), swap(bottom, CORES)
    mine, send = call(
        states_kernel, [VMEM] * (3 + CHIPS), [pair] * 2, "states", moved=1 << 21, after=[layer_x, layer_y]
    )(state_w, keep, recv, *entries)
    theirs = swap(send, 1)

    rows = features // count
    normed = call(
        norm_kernel,
        [SMEM] + [VMEM] * 6,
        [((features // CHIPS, block), f32)] * CHIPS,
        "norm",
        scratch=[pltpu.VMEM((features, block), f32)],
        flops=1 << 26,
        moved=1 << 21,
        rows=rows,
    )(here, q, attn, gain_col, into_rows, mine, theirs)
    if dps > 1:
        normed = for_all_dp(normed, here[0], planes, dps)
    normed = in_plane(normed)
    layers = [layer_x, layer_y, xy_top, xy_bottom]
    by_plane = ((planes, rows, columns), f32)
    product, left, right = call(
        product_send_kernel,
        [SMEM] + [VMEM] * (CHIPS + len(layers) + 1),
        [by_plane, ((planes * rows, CHIPS * block), bf16), ((CHIPS * block, columns), bf16)],
        "product_send",
        flops=1 << 27,
        moved=1 << 22,
        scale=scale,
    )(here, *normed, *layers, layer)
    parts = call(
        product_kernel,
        [SMEM] + [VMEM] * 3,
        [((rows, columns), f32)] * planes,
        "product",
        scratch=[pltpu.VMEM(*by_plane)],
        flops=1 << 27,
        moved=1 << 21,
        scale=scale,
    )(here, left, right, swap(product, 1))
    parts = [parts[0]] + in_line(parts[1:])
    q_grad, k_grad, v_grad = call(
        outputs_kernel,
        [SMEM] * 3 + [HBM] * 4 + [VMEM] * 2,
        [((block, features), bf16)] * 3,
        "outputs",
        scratch=[rows_in] * 7 + [pltpu.SemaphoreType.DMA((4,))],
        out_specs=[HBM] * 3,
        flops=1 << 29,
        moved=1 << 22,
    )(*facts, q, k, v, g, mine, theirs)
    (proj_grad,) = call(sum_kernel, [VMEM] * planes, [((rows, columns), f32)], "sum", moved=1 << 19)(*parts)
    if dps > 1:
        proj_grad = lax.psum_scatter(proj_grad, "dp", scatter_dimension=0, tiled=True)
    shape_out = (seqs, block, features)
    return (q_grad.reshape(shape_out), k_grad.reshape(shape_out), v_grad.reshape(shape_out), proj_grad)


def solution(mesh):
    rows = P("dp", "ctx", None)
    return jax.shard_map(
        on_device,
        mesh=mesh,
        in_specs=(rows, rows, rows, rows, rows, P(), P(), P("dp", None)),
        out_specs=(rows, rows, rows, P(("dp", "ctx"), None)),
        check_vma=False,
    )
```

```python
import functools
import math

import jax
import jax.numpy as jnp
from jax import lax
from jax.experimental import pallas as pl
from jax.experimental.pallas import tpu as pltpu
from jax.sharding import PartitionSpec as P

norm_eps = 1e-06
f32 = jnp.float32
bf16 = jnp.bfloat16

CORES = 2
CHIPS = 4
PLANE = CORES * CHIPS
ORDER = (0, 1, 2, 3)

SMEM = pl.BlockSpec(memory_space=pltpu.SMEM)
VMEM = pl.BlockSpec(memory_space=pltpu.VMEM)
HBM = pl.BlockSpec(memory_space=pltpu.HBM)
LONGEST = 2048


def dot(a, b, over_a, over_b):
    return lax.dot_general(a, b, (((over_a,), (over_b,)), ((), ())), preferred_element_type=f32)


def split(x):
    high = x.astype(bf16)
    return high, (x - high.astype(f32)).astype(bf16)


def dot2(a, b, over_a, over_b):
    if a.dtype == f32:
        high, low = split(a)
        return dot(high, b, over_a, over_b) + dot(low, b, over_a, over_b)
    high, low = split(b)
    return dot(a, high, over_a, over_b) + dot(a, low, over_a, over_b)


def doc_of(position, lens):
    bound = lens[0, 0]
    doc = jnp.where(position >= bound, 1, 0)
    for k in range(1, lens.shape[1] - 1):
        bound = bound + lens[0, k]
        doc = doc + jnp.where(position >= bound, 1, 0)
    return doc


def carry(from_edge, to_edge, rate, block, lens):
    same = doc_of(from_edge * block - 1, lens) == doc_of(to_edge * block - 1, lens)
    away = jnp.abs(from_edge - to_edge) * block
    row = jnp.full((1, 128), away.astype(f32) * -rate, f32)
    return jnp.where(same, jnp.exp(row), 0.0)


def entry_exit(here, rate, block, lens, dim, shape):
    offsets = lax.broadcasted_iota(jnp.int32, shape, dim)
    docs = doc_of(here * block + offsets, lens)
    into = jnp.where(docs == doc_of(here * block - 1, lens), jnp.exp(-rate * offsets.astype(f32)), 0.0)
    out = jnp.where(
        docs == doc_of(here * block + block - 1, lens), jnp.exp(-rate * (block - offsets).astype(f32)), 0.0
    )
    return into, out


def head_lanes(head, width):
    return pl.ds(pl.multiple_of(head * width, width), width)


def fetch(refs, spaces, sems):
    copies = [pltpu.make_async_copy(ref, space, sems.at[i]) for i, (ref, space) in enumerate(zip(refs, spaces))]
    for copy in copies:
        copy.start()
    return copies


def head_rows(here, heads):
    chip = lax.rem(here // CORES, CHIPS)
    part = heads // CHIPS
    return [(i * part + t, (chip ^ d) * part + t) for i, d in enumerate(ORDER) for t in range(part)]


def summary_kernel(
    here_ref, rates_in, lens_in, q_in, k_in, v_in, g_in, keep, send, chip_w, q, k, v, g, rates, lens, sems
):
    copies = fetch((rates_in, lens_in, k_in, v_in, q_in, g_in), (rates, lens, k, v, q, g), sems)
    here = here_ref[0]
    block = q.shape[0]
    heads, width, _ = keep.shape
    rows = head_rows(here, heads)
    first = lax.rem(here, CORES) == 0
    edge = here - lax.rem(here, CORES)
    for copy in copies[:2]:
        copy.wait()
    for row, head in rows:
        late = carry(edge + 1, edge + 2, rates[head], block, lens)
        early = carry(edge + 1, edge, rates[head], block, lens)
        chip_w[row : row + 1, :] = jnp.where(first, late, early)
    offsets = lax.broadcasted_iota(jnp.int32, (block, width), 0)
    docs = doc_of(here * block + offsets, lens)
    enters = docs == doc_of(here * block - 1, lens)
    leaves = docs == doc_of(here * block + block - 1, lens)
    from_start, to_end = offsets.astype(f32), (block - offsets).astype(f32)
    for copy in copies[2:]:
        copy.wait()
    for row, head in rows:
        lanes = head_lanes(head, width)
        past = jnp.where(leaves, jnp.exp(-rates[head] * to_end), 0.0)
        state = dot2(v[:, lanes], k[:, lanes].astype(f32) * past, 0, 0)
        into = jnp.where(enters, jnp.exp(-rates[head] * from_start), 0.0)
        pull = dot2(q[:, lanes].astype(f32) * into, g[:, lanes], 0, 0)
        keep[row] = jnp.where(first, state, pull)
        send[row] = jnp.where(first, pull, state)


def chip_kernel(weights, keep, recv, *outs):
    for i, out in enumerate(outs):
        part = out.shape[0]
        for t in range(part):
            row = i * part + t
            out[t] = weights[row : row + 1, :] * keep[row] + recv[row]


def line_order(planes):
    return list(range(planes - 1, 0, -1))


def weights_kernel(here_ref, rates, lens, plane_w, line_w, entry_w, state_w, *, block):
    here = here_ref[0]
    heads = state_w.shape[0]
    part, reach = line_w.shape[:2]
    first = lax.rem(here, CORES) == 0
    chip = lax.rem(here // CORES, CHIPS)
    base = here - lax.rem(here, PLANE)
    near, far = jnp.where(first, 0, PLANE), jnp.where(first, PLANE, 0)
    chip_near, chip_far = jnp.where(first, 0, CORES), jnp.where(first, CORES, 0)
    way = jnp.where(first, PLANE, -PLANE)
    for t in range(part):
        rate = rates[chip * part + t]

        def take(from_edge, to_edge):
            return carry(from_edge, to_edge, rate, block, lens)

        for k in range(reach):
            line_w[t, k, 0:1, :] = take(base + far, base + far + k * way)
        for i, d in enumerate(ORDER):
            edge = base + (chip ^ d) * CORES
            plane_w[t, i, 0:1, :] = take(edge + chip_far, base + far)
            entry_w[t, i, CHIPS : CHIPS + 1, :] = take(base + near, edge + chip_near)
            for j, e in enumerate(ORDER):
                other = base + (chip ^ e) * CORES
                ahead = jnp.where(first, other < edge, other > edge)
                entry_w[t, i, j : j + 1, :] = jnp.where(ahead, take(other + chip_far, edge + chip_near), 0.0)
    edge = here - lax.rem(here, CORES)
    for row, head in head_rows(here, heads):
        state_w[row : row + 1, :] = carry(edge + chip_near, edge + 1, rates[head], block, lens)


def plane_kernel(weights, line_w, *refs):
    totals, outs = refs[:CHIPS], refs[CHIPS:]
    for t in range(outs[0].shape[0]):
        total = 0.0
        for i, x in enumerate(totals):
            total = total + weights[t, i, 0:1, :] * x[t]
        for k, out in enumerate(outs):
            out[t] = line_w[t, k, 0:1, :] * total


def widen_kernel(layer, out):
    out[...] = layer[...].astype(f32)


def forward_kernel(layer_x, layer_y, top, bottom):
    top[...] = layer_x[: top.shape[0], :]
    bottom[...] = layer_y[top.shape[0] :, :]


def entry_kernel(weights, *refs, lines):
    totals, others, outs = refs[:CHIPS], refs[CHIPS : CHIPS + lines], refs[CHIPS + lines :]
    for t in range(outs[0].shape[0]):
        outside = 0.0
        for other in others:
            outside = outside + other[t]
        for i, out in enumerate(outs):
            entry = weights[t, i, CHIPS : CHIPS + 1, :] * outside
            for j, total in enumerate(totals):
                if i != j:
                    entry = entry + weights[t, i, j : j + 1, :] * total[t]
            out[t] = entry


def states_kernel(weights, keep, *refs):
    entries, send = refs[:CHIPS], refs[CHIPS]
    for i, entry in enumerate(entries):
        part = entry.shape[0]
        for t in range(part):
            row = i * part + t
            send[row] = keep[row] + weights[row : row + 1, :] * entry[t]


def causal(here, block, lens):
    at_j = lax.broadcasted_iota(jnp.int32, (block, block), 0)
    at_i = lax.broadcasted_iota(jnp.int32, (block, block), 1)
    docs_j = doc_of(here * block + at_j, lens)
    docs_i = doc_of(here * block + at_i, lens)
    return (docs_i == docs_j) & (at_i >= at_j), jnp.maximum(at_i - at_j, 0).astype(f32)


def within_kernel(here_ref, rates, lens, gain, q, k, v, attn, gain_col, into_rows):
    here = here_ref[0]
    block, features = q.shape
    heads = rates.shape[0]
    width = features // heads
    reached, away = causal(here, block, lens)
    for head in range(heads):
        lanes = slice(head * width, (head + 1) * width)
        gain_col[lanes, :] = jnp.broadcast_to(gain[:, lanes], (block, width)).T
        decay = jnp.where(reached, jnp.exp(-rates[head] * away), 0.0)
        scores = dot(k[:, lanes], q[:, lanes], 1, 1) * decay
        attn[lanes, :] = dot2(v[:, lanes], scores, 0, 0)
        into_rows[head : head + 1, :], _ = entry_exit(here, rates[head], block, lens, 1, (1, block))


def norm_kernel(here_ref, q, attn, gain_col, into_rows, recv, *refs, rows):
    entries, outs, total = refs[:CHIPS], refs[CHIPS : 2 * CHIPS], refs[2 * CHIPS]
    here = here_ref[0]
    block, features = q.shape
    heads, width, _ = recv.shape
    part = heads // CHIPS
    first = lax.rem(here, CORES) == 0
    chip = lax.rem(here // CORES, CHIPS)
    squares = jnp.zeros((width, block), f32)
    for row, head in head_rows(here, heads):
        lanes = head_lanes(head, width)
        state = jnp.where(first, entries[row // part][row % part], recv[row])
        at = attn[lanes, :] + into_rows[pl.ds(head, 1), :] * dot2(state, q[:, lanes], 1, 1)
        total[lanes, :] = at
        squares = squares + at * at
    mean = jnp.sum(squares, axis=0, keepdims=True) * (1.0 / features)
    factor = lax.rsqrt(mean + norm_eps)
    planes = features // (PLANE * rows)
    for out, d in zip(outs, ORDER):
        for to_core in range(CORES):
            for plane in range(planes):
                block_at = plane * PLANE + (chip ^ d) * CORES + to_core
                at = pl.ds(pl.multiple_of(block_at * rows, rows), rows)
                normed = (total[at, :] * factor * gain_col[at, :]).astype(bf16)
                to = to_core * planes + plane
                out[to * rows : (to + 1) * rows, :] = normed.astype(f32)


def product_send_kernel(here_ref, *refs, scale):
    core = lax.rem(here_ref[0], CORES)
    normed, layers, (layer, out, left, right) = refs[:CHIPS], refs[CHIPS:-4], refs[-4:]
    rows = left.shape[0]
    block = layer.shape[0]
    mine = pl.ds(pl.multiple_of(core * rows, rows), rows)
    other = pl.ds(pl.multiple_of((1 - core) * rows, rows), rows)
    right[:block, :] = layer[...]
    at = block
    for x in layers:
        right[at : at + x.shape[0], :] = x[...].astype(bf16)
        at = at + x.shape[0]
    for d, x in enumerate(normed):
        left[:, d * block : (d + 1) * block] = x[mine, :].astype(bf16)
    send = jnp.concatenate([x[other, :].astype(bf16) for x in normed], axis=1)
    out[...] = (dot(send, right[...], 1, 0) * scale).reshape(out.shape)


def product_kernel(here_ref, left, right, recv, *refs, scale):
    outs, product = refs[:-1], refs[-1]
    plane = here_ref[0] // PLANE
    product[...] = (dot(left[...], right[...], 1, 0) * scale).reshape(product.shape)
    for out, d in zip(outs, [0] + line_order(len(outs))):
        out[...] = product[plane ^ d] + recv[plane ^ d]


def sum_kernel(*refs):
    total = refs[0][...]
    for x in refs[1:-1]:
        total = total + x[...]
    refs[-1][...] = total


def outputs_kernel(here_ref, rates, lens, q_in, k_in, v_in, g_in, recv, *refs):
    entries, (q_out, k_out, v_out, q, k, v, g, q_grad, k_grad, v_grad, sems) = refs[:CHIPS], refs[CHIPS:]
    copies = fetch((q_in, k_in, v_in, g_in), (q, k, v, g), sems)
    here = here_ref[0]
    block, features = q.shape
    heads, width, _ = recv.shape
    part = heads // CHIPS
    first = lax.rem(here, CORES) == 0
    reached, away = causal(here, block, lens)
    for copy in copies:
        copy.wait()
    for row, head in head_rows(here, heads):
        lanes = head_lanes(head, width)
        rate = rates[head]
        qh, kh, vh, gh = q[:, lanes], k[:, lanes], v[:, lanes], g[:, lanes]
        decay = jnp.where(reached, jnp.exp(-rate * away), 0.0)
        scores = dot(kh, qh, 1, 1) * decay
        grads = dot(vh, gh, 1, 1) * decay
        into, past = entry_exit(here, rate, block, lens, 0, (block, width))
        own, other = entries[row // part][row % part], recv[row]
        before, after = jnp.where(first, own, other), jnp.where(first, other, own)
        q_grad[:, lanes] = (dot2(grads, kh, 0, 0) + into * dot2(gh, before, 1, 0)).astype(bf16)
        k_grad[:, lanes] = (dot2(grads, qh, 1, 0) + past * dot2(vh, after, 1, 1)).astype(bf16)
        v_grad[:, lanes] = (dot2(scores, gh, 1, 0) + past * dot2(kh, after, 1, 0)).astype(bf16)
    outs = [pltpu.make_async_copy(x, y, sems.at[i]) for i, (x, y) in enumerate(((q_grad, q_out), (k_grad, k_out), (v_grad, v_out)))]
    for copy in outs:
        copy.start()
    for copy in outs:
        copy.wait()


def for_all_dp(outs, here, planes, dps):
    order = (here // CORES) % CHIPS ^ jnp.array(ORDER)
    whole = jnp.zeros((CHIPS,) + outs[0].shape, f32).at[order].set(jnp.stack(outs))
    rows = whole.shape[1] // (CORES * planes)
    whole = whole.reshape(CHIPS, CORES, planes, rows, -1).transpose(2, 0, 1, 3, 4)
    whole = whole.reshape(dps, planes, CHIPS, CORES, rows // dps, -1).transpose(2, 3, 1, 0, 4, 5)
    whole = whole.reshape((CHIPS,) + outs[0].shape)[order]
    return [whole[d] for d in range(CHIPS)]


def call(kernel, specs, outs, name, scratch=(), flops=0, moved=0, out_specs=None, after=(), **named):
    reads = len(specs)

    def body(*refs):
        kernel(*refs[:reads], *refs[reads + len(after) :], **named)

    def run(*operands):
        operands = [
            pltpu.with_memory_space_constraint(x, pltpu.HBM) if spec is HBM else x for x, spec in zip(operands, specs)
        ]
        return pl.pallas_call(
            body,
            out_shape=[jax.ShapeDtypeStruct(shape, dtype) for shape, dtype in outs],
            in_specs=list(specs) + [pl.BlockSpec(memory_space=pl.ANY)] * len(after),
            out_specs=out_specs or [VMEM] * len(outs),
            scratch_shapes=list(scratch),
            cost_estimate=pl.CostEstimate(flops=flops, bytes_accessed=moved, transcendentals=0),
            compiler_params=pltpu.CompilerParams(vmem_limit_bytes=16 * 1024 * 1024),
            name=name,
        )(*operands, *after)

    return run


def on_device(queries, keys, values, out_grad, layer_grad, norm_gain, decay_rates, doc_lengths):
    seqs, block, features = queries.shape
    assert seqs == 1
    heads = decay_rates.shape[0]
    width = features // heads
    columns = layer_grad.shape[2]
    part = heads // CHIPS
    count = lax.axis_size("ctx")
    planes = count // PLANE
    dps = lax.axis_size("dp")
    scale = 1.0 / math.sqrt(seqs * block * dps * count)
    here = lax.axis_index("ctx").astype(jnp.int32).reshape(1)
    facts = (here, decay_rates, doc_lengths)
    q, k, v, g = (x.reshape(block, features) for x in (queries, keys, values, out_grad))
    layer = layer_grad.reshape(block, columns)

    def swap(x, bit):
        return lax.ppermute(x, "ctx", [(i, i ^ bit) for i in range(count)])

    def in_plane(pieces):
        return [pieces[0]] + [swap(x, d * CORES) for x, d in zip(pieces[1:], ORDER[1:])]

    def onward(x, far):
        ways = [(i, i + far * (PLANE if i % CORES == 0 else -PLANE)) for i in range(count)]
        return lax.ppermute(x, "ctx", [(i, to) for i, to in ways if 0 <= to < count])

    every = ((heads, width, width), f32)
    some = ((part, width, width), f32)
    rows_in = pltpu.VMEM((block, features), bf16)
    half_layer = ((block // 2, columns), f32)
    keep, send, chip_w = call(
        summary_kernel,
        [SMEM] + [HBM] * 6,
        [every] * 2 + [((heads, 128), f32)],
        "summary",
        scratch=[rows_in] * 4
        + [
            pltpu.SMEM((heads,), f32),
            pltpu.SMEM(doc_lengths.shape, jnp.int32),
            pltpu.SemaphoreType.DMA((6,)),
        ],
        flops=1 << 26,
        moved=1 << 21,
    )(*facts, q, k, v, g)
    recv = swap(send, 1)
    totals = call(
        chip_kernel, [VMEM] * 3, [some] * CHIPS, "chip_total", moved=1 << 20
    )(chip_w, keep, recv)
    reach = min(planes - 1, -(-LONGEST // (PLANE * block)))
    plane_w, line_w, entry_w, state_w = call(
        weights_kernel,
        [SMEM] * 3,
        [
            ((part, CHIPS, 1, 128), f32),
            ((part, reach, 1, 128), f32),
            ((part, CHIPS, CHIPS + 1, 128), f32),
            ((heads, 128), f32),
        ],
        "weights",
        moved=1 << 18,
        after=totals[:1],
        block=block,
    )(*facts)
    attn, gain_col, into_rows = call(
        within_kernel,
        [SMEM] * 3 + [VMEM] * 4,
        [((features, block), f32)] * 2 + [((heads, block), f32)],
        "within",
        flops=1 << 28,
        moved=1 << 22,
        after=totals[:1],
    )(*facts, norm_gain.reshape(1, features), q, k, v)
    totals = in_plane(totals)
    (layer_wide,) = call(
        widen_kernel, [VMEM], [((block, columns), f32)], "widen", moved=1 << 19, after=[*totals[1:], attn, plane_w]
    )(layer)
    layer_x, layer_y = swap(layer_wide, CORES), swap(layer_wide, 2 * CORES)
    others = call(
        plane_kernel,
        [VMEM] * (2 + CHIPS),
        [some] * reach,
        "plane_total",
        moved=1 << 19,
        after=[attn],
    )(plane_w, line_w, *totals)
    others = [onward(others[k], k + 1) for k in reversed(range(reach))]
    entries = call(
        entry_kernel,
        [VMEM] * (1 + CHIPS + reach),
        [some] * CHIPS,
        "entries",
        moved=1 << 20,
        lines=reach,
    )(entry_w, *totals, *others)
    entries = in_plane(entries)
    top, bottom = call(forward_kernel, [VMEM] * 2, [half_layer] * 2, "forward", moved=1 << 20)(layer_x, layer_y)
    xy_top, xy_bottom = swap(top, 2 * CORES), swap(bottom, CORES)
    (send,) = call(
        states_kernel, [VMEM] * (2 + CHIPS), [every], "states", moved=1 << 21, after=[layer_x, layer_y]
    )(state_w, keep, *entries)
    theirs = swap(send, 1)

    rows = features // count
    normed = call(
        norm_kernel,
        [SMEM] + [VMEM] * (5 + CHIPS),
        [((features // CHIPS, block), f32)] * CHIPS,
        "norm",
        scratch=[pltpu.VMEM((features, block), f32)],
        flops=1 << 26,
        moved=1 << 21,
        rows=rows,
    )(here, q, attn, gain_col, into_rows, theirs, *entries)
    if dps > 1:
        normed = for_all_dp(normed, here[0], planes, dps)
    normed = in_plane(normed)
    layers = [layer_x, layer_y, xy_top, xy_bottom]
    by_plane = ((planes, rows, columns), f32)
    product, left, right = call(
        product_send_kernel,
        [SMEM] + [VMEM] * (CHIPS + len(layers) + 1),
        [by_plane, ((planes * rows, CHIPS * block), bf16), ((CHIPS * block, columns), bf16)],
        "product_send",
        flops=1 << 27,
        moved=1 << 22,
        scale=scale,
    )(here, *normed, *layers, layer)
    parts = call(
        product_kernel,
        [SMEM] + [VMEM] * 3,
        [((rows, columns), f32)] * planes,
        "product",
        scratch=[pltpu.VMEM(*by_plane)],
        flops=1 << 27,
        moved=1 << 21,
        scale=scale,
    )(here, left, right, swap(product, 1))
    parts = [parts[0]] + [swap(x, d * PLANE) for x, d in zip(parts[1:], line_order(planes))]
    q_grad, k_grad, v_grad = call(
        outputs_kernel,
        [SMEM] * 3 + [HBM] * 4 + [VMEM] * (1 + CHIPS),
        [((block, features), bf16)] * 3,
        "outputs",
        scratch=[rows_in] * 7 + [pltpu.SemaphoreType.DMA((4,))],
        out_specs=[HBM] * 3,
        flops=1 << 29,
        moved=1 << 22,
    )(*facts, q, k, v, g, theirs, *entries)
    (proj_grad,) = call(sum_kernel, [VMEM] * planes, [((rows, columns), f32)], "sum", moved=1 << 19)(*parts)
    if dps > 1:
        proj_grad = lax.psum_scatter(proj_grad, "dp", scatter_dimension=0, tiled=True)
    shape_out = (seqs, block, features)
    return (q_grad.reshape(shape_out), k_grad.reshape(shape_out), v_grad.reshape(shape_out), proj_grad)


def solution(mesh):
    rows = P("dp", "ctx", None)
    return jax.shard_map(
        on_device,
        mesh=mesh,
        in_specs=(rows, rows, rows, rows, rows, P(), P(), P("dp", None)),
        out_specs=(rows, rows, rows, P(("dp", "ctx"), None)),
        check_vma=False,
    )
```

```python
import functools
import math

import jax
import jax.numpy as jnp
from jax import lax
from jax.experimental import pallas as pl
from jax.experimental.pallas import tpu as pltpu
from jax.sharding import PartitionSpec as P

norm_eps = 1e-06
f32 = jnp.float32
bf16 = jnp.bfloat16

CORES = 2
CHIPS = 4
PLANE = CORES * CHIPS

SMEM = pl.BlockSpec(memory_space=pltpu.SMEM)
VMEM = pl.BlockSpec(memory_space=pltpu.VMEM)
HBM = pl.BlockSpec(memory_space=pltpu.HBM)
LONGEST = 2048


def dot(a, b, over_a, over_b):
    return lax.dot_general(a, b, (((over_a,), (over_b,)), ((), ())), preferred_element_type=f32)


def split(x):
    high = x.astype(bf16)
    return high, (x - high.astype(f32)).astype(bf16)


def dot2(a, b, over_a, over_b):
    if a.dtype == f32:
        high, low = split(a)
        return dot(high, b, over_a, over_b) + dot(low, b, over_a, over_b)
    high, low = split(b)
    return dot(a, high, over_a, over_b) + dot(a, low, over_a, over_b)


def doc_of(position, lens):
    bound = lens[0, 0]
    doc = jnp.where(position >= bound, 1, 0)
    for k in range(1, lens.shape[1] - 1):
        bound = bound + lens[0, k]
        doc = doc + jnp.where(position >= bound, 1, 0)
    return doc


def carry(from_edge, to_edge, rate, block, lens):
    same = doc_of(from_edge * block - 1, lens) == doc_of(to_edge * block - 1, lens)
    away = jnp.abs(from_edge - to_edge) * block
    row = jnp.full((1, 128), away.astype(f32) * -rate, f32)
    return jnp.where(same, jnp.exp(row), 0.0)


def entry_exit(here, rate, block, lens, dim, shape):
    offsets = lax.broadcasted_iota(jnp.int32, shape, dim)
    docs = doc_of(here * block + offsets, lens)
    into = jnp.where(docs == doc_of(here * block - 1, lens), jnp.exp(-rate * offsets.astype(f32)), 0.0)
    out = jnp.where(
        docs == doc_of(here * block + block - 1, lens), jnp.exp(-rate * (block - offsets).astype(f32)), 0.0
    )
    return into, out


def head_lanes(head, width):
    return pl.ds(pl.multiple_of(head * width, width), width)


def fetch(refs, spaces, sems):
    copies = [pltpu.make_async_copy(ref, space, sems.at[i]) for i, (ref, space) in enumerate(zip(refs, spaces))]
    for copy in copies:
        copy.start()
    return copies


def in_order(here):
    core = lax.rem(here, CORES)
    chip = lax.rem(here // CORES, CHIPS)
    return [chip, chip ^ (1 + core), chip ^ (2 - core), chip ^ 3]


def half_heads(here, half):
    core = lax.rem(here, CORES)
    part = half // CHIPS
    both = enumerate(zip(in_order(here), in_order(here ^ 1)))
    return [
        (i * part + t, core * half + own * part + t, (1 - core) * half + other * part + t)
        for i, (own, other) in both
        for t in range(part)
    ]


def summary_kernel(
    here_ref, rates_in, lens_in, q_in, k_in, v_in, g_in, keep, send, chip_w, q, k, v, g, rates, lens, sems
):
    copies = fetch((rates_in, lens_in, k_in, v_in, q_in, g_in), (rates, lens, k, v, q, g), sems)
    here = here_ref[0]
    block = q.shape[0]
    half, _, width, _ = keep.shape
    heads = half_heads(here, half)
    first = lax.rem(here, CORES) == 0
    edge = here - lax.rem(here, CORES)
    for copy in copies[:2]:
        copy.wait()
    for row, head, _ in heads:
        late = carry(edge + 1, edge + 2, rates[head], block, lens)
        early = carry(edge + 1, edge, rates[head], block, lens)
        chip_w[row, 0:1, :] = jnp.where(first, late, 1.0)
        chip_w[row, 1:2, :] = jnp.where(first, 1.0, late)
        chip_w[row, 2:3, :] = jnp.where(first, 1.0, early)
        chip_w[row, 3:4, :] = jnp.where(first, early, 1.0)
    offsets = lax.broadcasted_iota(jnp.int32, (block, width), 0)
    docs = doc_of(here * block + offsets, lens)
    enters = docs == doc_of(here * block - 1, lens)
    leaves = docs == doc_of(here * block + block - 1, lens)
    from_start, to_end = offsets.astype(f32), (block - offsets).astype(f32)
    for copy in copies[2:4]:
        copy.wait()
    for row, *pair in heads:
        for head, out in zip(pair, (keep, send)):
            past = jnp.where(leaves, jnp.exp(-rates[head] * to_end), 0.0)
            lanes = head_lanes(head, width)
            out[row, 0] = dot2(v[:, lanes], k[:, lanes].astype(f32) * past, 0, 0)
    for copy in copies[4:]:
        copy.wait()
    for row, *pair in heads:
        for head, out in zip(pair, (keep, send)):
            into = jnp.where(enters, jnp.exp(-rates[head] * from_start), 0.0)
            lanes = head_lanes(head, width)
            out[row, 1] = dot2(q[:, lanes].astype(f32) * into, g[:, lanes], 0, 0)


def chip_kernel(weights, keep, recv, *outs):
    for i, out in enumerate(outs):
        for t in range(out.shape[0]):
            row = i * out.shape[0] + t
            for k in range(2):
                own, other = weights[row, 2 * k : 2 * k + 1, :], weights[row, 2 * k + 1 : 2 * k + 2, :]
                out[t, k] = own * keep[row, k] + other * recv[row, k]


def line_order(planes):
    return list(range(planes - 1, 0, -1))


def scan_order(planes):
    return [d for d in line_order(planes) if d == 2] + [d for d in range(1, planes) if d != 2]


def weights_kernel(here_ref, rates, lens, plane_w, line_w, entry_w, state_w, *, block):
    here = here_ref[0]
    half = state_w.shape[0]
    part, lines = line_w.shape[:2]
    core = lax.rem(here, CORES)
    chips = in_order(here)
    plane = here // PLANE
    base = plane * PLANE
    ones = jnp.ones((1, 128), f32)
    for t in range(part):
        rate = rates[core * half + chips[0] * part + t]

        def take(from_edge, to_edge):
            return carry(from_edge, to_edge, rate, block, lens)

        for j, d in enumerate(scan_order(lines + 1)):
            to = plane ^ d
            line_w[t, j, 0:1, :] = jnp.where(to > plane, take(base + PLANE, to * PLANE), 0.0)
            line_w[t, j, 1:2, :] = jnp.where(to < plane, take(base, (to + 1) * PLANE), 0.0)
            line_w[t, j, 2:3, :] = jnp.where(to < plane, ones, 0.0)
            line_w[t, j, 3:4, :] = jnp.where(to > plane, ones, 0.0)
        for i, at in enumerate(chips):
            edge = base + at * CORES
            plane_w[t, i, 0:1, :] = take(edge + CORES, base + PLANE)
            plane_w[t, i, 1:2, :] = take(edge, base)
            entry_w[t, i, CHIPS, 0:1, :] = take(base, edge)
            entry_w[t, i, CHIPS, 1:2, :] = take(base + PLANE, edge + CORES)
            for j, at_other in enumerate(chips):
                other = base + at_other * CORES
                entry_w[t, i, j, 0:1, :] = jnp.where(other < edge, take(other + CORES, edge), 0.0)
                entry_w[t, i, j, 1:2, :] = jnp.where(other > edge, take(other, edge + CORES), 0.0)
    edge = here - core
    first = core == 0
    for row, head, _ in half_heads(here, half):
        fwd = carry(edge, edge + 1, rates[head], block, lens)
        bwd = carry(edge + 2, edge + 1, rates[head], block, lens)
        rows = ((0.0, 1.0), (1.0, fwd), (1.0, bwd), (0.0, 1.0))
        for k, (core0, core1) in enumerate(((0, 1), (1, 0), (2, 3), (3, 2))):
            for m in range(2):
                state_w[row, 2 * k + m : 2 * k + m + 1, :] = jnp.where(
                    first, ones * rows[core0][m], ones * rows[core1][m]
                )


def plane_kernel(weights, line_w, *refs):
    totals, outs = refs[:CHIPS], refs[CHIPS:]
    for t in range(outs[0].shape[0]):
        fwd, bwd = 0.0, 0.0
        for i, total in enumerate(totals):
            fwd = fwd + weights[t, i, 0:1, :] * total[t, 0]
            bwd = bwd + weights[t, i, 1:2, :] * total[t, 1]
        for j, out in enumerate(outs):
            out[t] = line_w[t, j, 0:1, :] * fwd + line_w[t, j, 1:2, :] * bwd


def widen_kernel(layer, out):
    out[...] = layer[...].astype(f32)


def forward_kernel(layer_first, layer_second, top, bottom):
    top[...] = layer_first[: top.shape[0], :]
    bottom[...] = layer_second[top.shape[0] :, :]


def entry_kernel(weights, line_w, *refs, lines):
    totals, others, outs = refs[:CHIPS], refs[CHIPS : CHIPS + lines], refs[CHIPS + lines :]
    for t in range(outs[0].shape[0]):
        before, after = 0.0, 0.0
        for j, other in enumerate(others):
            before = before + line_w[t, j, 2:3, :] * other[t]
            after = after + line_w[t, j, 3:4, :] * other[t]
        for i, out in enumerate(outs):
            fwd = weights[t, i, CHIPS, 0:1, :] * before
            bwd = weights[t, i, CHIPS, 1:2, :] * after
            for j, total in enumerate(totals):
                if i != j:
                    fwd = fwd + weights[t, i, j, 0:1, :] * total[t, 0]
                    bwd = bwd + weights[t, i, j, 1:2, :] * total[t, 1]
            out[t, 0], out[t, 1] = fwd, bwd


def states_kernel(weights, keep, recv, *refs):
    entries, (mine, send) = refs[:CHIPS], refs[CHIPS:]
    part = entries[0].shape[0]
    for i, entry in enumerate(entries):
        for t in range(part):
            row = i * part + t
            for k in range(2):
                for m, (own, out) in enumerate(((recv, mine), (keep, send))):
                    at = 4 * k + 2 * m
                    out[row, k] = weights[row, at : at + 1, :] * own[row, k] + weights[row, at + 1 : at + 2, :] * entry[t, k]


def causal(here, block, lens):
    at_j = lax.broadcasted_iota(jnp.int32, (block, block), 0)
    at_i = lax.broadcasted_iota(jnp.int32, (block, block), 1)
    docs_j = doc_of(here * block + at_j, lens)
    docs_i = doc_of(here * block + at_i, lens)
    return (docs_i == docs_j) & (at_i >= at_j), jnp.maximum(at_i - at_j, 0).astype(f32)


def within_kernel(here_ref, rates, lens, gain, q, k, v, attn, gain_col, into_rows):
    here = here_ref[0]
    block, features = q.shape
    heads = rates.shape[0]
    width = features // heads
    reached, away = causal(here, block, lens)
    for head in range(heads):
        lanes = slice(head * width, (head + 1) * width)
        gain_col[lanes, :] = jnp.broadcast_to(gain[:, lanes], (block, width)).T
        decay = jnp.where(reached, jnp.exp(-rates[head] * away), 0.0)
        scores = dot(k[:, lanes], q[:, lanes], 1, 1) * decay
        attn[lanes, :] = dot2(v[:, lanes], scores, 0, 0)
        into_rows[head : head + 1, :], _ = entry_exit(here, rates[head], block, lens, 1, (1, block))


def norm_kernel(here_ref, q, attn, gain_col, into_rows, mine, recv, *refs, rows):
    outs, total = refs[:CHIPS], refs[CHIPS]
    here = here_ref[0]
    block, features = q.shape
    half, _, width, _ = mine.shape
    squares = jnp.zeros((width, block), f32)
    for row, *pair in half_heads(here, half):
        for head, states in zip(pair, (mine, recv)):
            lanes = head_lanes(head, width)
            at = attn[lanes, :] + into_rows[pl.ds(head, 1), :] * dot2(states[row, 0], q[:, lanes], 1, 1)
            total[lanes, :] = at
            squares = squares + at * at
    mean = jnp.sum(squares, axis=0, keepdims=True) * (1.0 / features)
    factor = lax.rsqrt(mean + norm_eps)
    planes = features // (PLANE * rows)
    for out, chip in zip(outs, in_order(here)):
        for to_core in range(CORES):
            for plane in range(planes):
                block_at = plane * PLANE + chip * CORES + to_core
                at = pl.ds(pl.multiple_of(block_at * rows, rows), rows)
                normed = (total[at, :] * factor * gain_col[at, :]).astype(bf16)
                to = to_core * planes + plane
                out[to * rows : (to + 1) * rows, :] = normed.astype(f32)


def product_send_kernel(here_ref, *refs, scale):
    core = lax.rem(here_ref[0], CORES)
    normed, layers, (layer, out, left, right) = refs[:CHIPS], refs[CHIPS:-4], refs[-4:]
    rows = left.shape[0]
    block = layer.shape[0]
    mine = pl.ds(pl.multiple_of(core * rows, rows), rows)
    other = pl.ds(pl.multiple_of((1 - core) * rows, rows), rows)
    right[:block, :] = layer[...]
    at = block
    for x in layers:
        right[at : at + x.shape[0], :] = x[...].astype(bf16)
        at = at + x.shape[0]
    for d, x in enumerate(normed):
        left[:, d * block : (d + 1) * block] = x[mine, :].astype(bf16)
    send = jnp.concatenate([x[other, :].astype(bf16) for x in normed], axis=1)
    out[...] = (dot(send, right[...], 1, 0) * scale).reshape(out.shape)


def product_kernel(here_ref, left, right, recv, *refs, scale):
    outs, product = refs[:-1], refs[-1]
    plane = here_ref[0] // PLANE
    product[...] = (dot(left[...], right[...], 1, 0) * scale).reshape(product.shape)
    for out, d in zip(outs, [0] + line_order(len(outs))):
        out[...] = product[plane ^ d] + recv[plane ^ d]


def sum_kernel(*refs):
    total = refs[0][...]
    for x in refs[1:-1]:
        total = total + x[...]
    refs[-1][...] = total


def outputs_kernel(here_ref, rates, lens, q_in, k_in, v_in, g_in, mine, recv, q_out, k_out, v_out, *scratch):
    q, k, v, g, q_grad, k_grad, v_grad, sems = scratch
    copies = fetch((q_in, k_in, v_in, g_in), (q, k, v, g), sems)
    here = here_ref[0]
    block, features = q.shape
    half, _, width, _ = mine.shape
    reached, away = causal(here, block, lens)
    for copy in copies:
        copy.wait()
    for row, *pair in half_heads(here, half):
        for head, states in zip(pair, (mine, recv)):
            lanes = head_lanes(head, width)
            rate = rates[head]
            qh, kh, vh, gh = q[:, lanes], k[:, lanes], v[:, lanes], g[:, lanes]
            decay = jnp.where(reached, jnp.exp(-rate * away), 0.0)
            scores = dot(kh, qh, 1, 1) * decay
            grads = dot(vh, gh, 1, 1) * decay
            into, past = entry_exit(here, rate, block, lens, 0, (block, width))
            before, after = states[row, 0], states[row, 1]
            q_grad[:, lanes] = (dot2(grads, kh, 0, 0) + into * dot2(gh, before, 1, 0)).astype(bf16)
            k_grad[:, lanes] = (dot2(grads, qh, 1, 0) + past * dot2(vh, after, 1, 1)).astype(bf16)
            v_grad[:, lanes] = (dot2(scores, gh, 1, 0) + past * dot2(kh, after, 1, 0)).astype(bf16)
    outs = [pltpu.make_async_copy(x, y, sems.at[i]) for i, (x, y) in enumerate(((q_grad, q_out), (k_grad, k_out), (v_grad, v_out)))]
    for copy in outs:
        copy.start()
    for copy in outs:
        copy.wait()


def for_all_dp(outs, here, planes, dps):
    order = jnp.stack(in_order(here))
    whole = jnp.zeros((CHIPS,) + outs[0].shape, f32).at[order].set(jnp.stack(outs))
    rows = whole.shape[1] // (CORES * planes)
    whole = whole.reshape(CHIPS, CORES, planes, rows, -1).transpose(2, 0, 1, 3, 4)
    whole = whole.reshape(dps, planes, CHIPS, CORES, rows // dps, -1).transpose(2, 3, 1, 0, 4, 5)
    whole = whole.reshape((CHIPS,) + outs[0].shape)[order]
    return [whole[d] for d in range(CHIPS)]


def call(kernel, specs, outs, name, scratch=(), flops=0, moved=0, out_specs=None, after=(), **named):
    reads = len(specs)

    def body(*refs):
        kernel(*refs[:reads], *refs[reads + len(after) :], **named)

    def run(*operands):
        operands = [
            pltpu.with_memory_space_constraint(x, pltpu.HBM) if spec is HBM else x for x, spec in zip(operands, specs)
        ]
        return pl.pallas_call(
            body,
            out_shape=[jax.ShapeDtypeStruct(shape, dtype) for shape, dtype in outs],
            in_specs=list(specs) + [pl.BlockSpec(memory_space=pl.ANY)] * len(after),
            out_specs=out_specs or [VMEM] * len(outs),
            scratch_shapes=list(scratch),
            cost_estimate=pl.CostEstimate(flops=flops, bytes_accessed=moved, transcendentals=0),
            compiler_params=pltpu.CompilerParams(vmem_limit_bytes=16 * 1024 * 1024),
            name=name,
        )(*operands, *after)

    return run


def on_device(queries, keys, values, out_grad, layer_grad, norm_gain, decay_rates, doc_lengths):
    seqs, block, features = queries.shape
    assert seqs == 1
    heads = decay_rates.shape[0]
    width = features // heads
    columns = layer_grad.shape[2]
    half = heads // CORES
    part = half // CHIPS
    count = lax.axis_size("ctx")
    planes = count // PLANE
    dps = lax.axis_size("dp")
    scale = 1.0 / math.sqrt(seqs * block * dps * count)
    here = lax.axis_index("ctx").astype(jnp.int32).reshape(1)
    facts = (here, decay_rates, doc_lengths)
    q, k, v, g = (x.reshape(block, features) for x in (queries, keys, values, out_grad))
    layer = layer_grad.reshape(block, columns)

    def swap(x, bit, near=count):
        pairs = [(i, i ^ bit) for i in range(count) if abs(i // PLANE - (i ^ bit) // PLANE) <= near]
        return lax.ppermute(x, "ctx", pairs)

    def first_of_plane(x):
        return lax.ppermute(x, "ctx", [(i, i ^ (1 + i % CORES) * CORES) for i in range(count)])

    def second_of_plane(x):
        return lax.ppermute(x, "ctx", [(i, i ^ (2 - i % CORES) * CORES) for i in range(count)])

    def in_plane(pieces):
        own, first, second, diagonal = pieces
        return [own, first_of_plane(first), second_of_plane(second), swap(diagonal, 3 * CORES)]

    def in_line(pieces, order, near=count):
        return [swap(x, d * PLANE, near) for x, d in zip(pieces, order)]

    pair = ((half, 2, width, width), f32)
    small = ((part, 2, width, width), f32)
    one = ((part, width, width), f32)
    rows_in = pltpu.VMEM((block, features), bf16)
    half_layer = ((block // 2, columns), f32)
    keep, send, chip_w = call(
        summary_kernel,
        [SMEM] + [HBM] * 6,
        [pair] * 2 + [((half, 4, 128), f32)],
        "summary",
        scratch=[rows_in] * 4
        + [
            pltpu.SMEM((heads,), f32),
            pltpu.SMEM(doc_lengths.shape, jnp.int32),
            pltpu.SemaphoreType.DMA((6,)),
        ],
        flops=1 << 26,
        moved=1 << 21,
    )(*facts, q, k, v, g)
    recv = swap(send, 1)
    totals = call(
        chip_kernel, [VMEM] * 3, [small] * CHIPS, "chip_total", moved=1 << 20
    )(chip_w, keep, recv)
    plane_w, line_w, entry_w, state_w = call(
        weights_kernel,
        [SMEM] * 3,
        [
            ((part, CHIPS, 2, 128), f32),
            ((part, planes - 1, 4, 128), f32),
            ((part, CHIPS, CHIPS + 1, 2, 128), f32),
            ((half, 8, 128), f32),
        ],
        "weights",
        moved=1 << 18,
        after=totals[:1],
        block=block,
    )(*facts)
    attn, gain_col, into_rows = call(
        within_kernel,
        [SMEM] * 3 + [VMEM] * 4,
        [((features, block), f32)] * 2 + [((heads, block), f32)],
        "within",
        flops=1 << 28,
        moved=1 << 22,
        after=totals[:1],
    )(*facts, norm_gain.reshape(1, features), q, k, v)
    totals = in_plane(totals)
    (layer_wide,) = call(
        widen_kernel, [VMEM], [((block, columns), f32)], "widen", moved=1 << 19, after=[*totals[1:], attn, plane_w]
    )(layer)
    layer_first, layer_second = first_of_plane(layer_wide), second_of_plane(layer_wide)
    near = -(-LONGEST // (PLANE * block))
    onward = call(
        plane_kernel,
        [VMEM] * (2 + CHIPS),
        [one] * (planes - 1),
        "plane_total",
        moved=1 << 19,
        after=[attn],
    )(plane_w, line_w, *totals)
    others = in_line(onward, scan_order(planes), near)
    entries = call(
        entry_kernel,
        [VMEM] * (2 + CHIPS + len(others)),
        [small] * CHIPS,
        "entries",
        moved=1 << 20,
        lines=len(others),
    )(entry_w, line_w, *totals, *others)
    entries = in_plane(entries)
    top, bottom = call(forward_kernel, [VMEM] * 2, [half_layer] * 2, "forward", moved=1 << 20)(layer_first, layer_second)
    far_top, far_bottom = second_of_plane(top), first_of_plane(bottom)
    mine, send = call(
        states_kernel, [VMEM] * (3 + CHIPS), [pair] * 2, "states", moved=1 << 21, after=[layer_first, layer_second]
    )(state_w, keep, recv, *entries)
    theirs = swap(send, 1)

    rows = features // count
    normed = call(
        norm_kernel,
        [SMEM] + [VMEM] * 6,
        [((features // CHIPS, block), f32)] * CHIPS,
        "norm",
        scratch=[pltpu.VMEM((features, block), f32)],
        flops=1 << 26,
        moved=1 << 21,
        rows=rows,
    )(here, q, attn, gain_col, into_rows, mine, theirs)
    if dps > 1:
        normed = for_all_dp(normed, here[0], planes, dps)
    normed = in_plane(normed)
    layers = [layer_first, layer_second, far_top, far_bottom]
    by_plane = ((planes, rows, columns), f32)
    product, left, right = call(
        product_send_kernel,
        [SMEM] + [VMEM] * (CHIPS + len(layers) + 1),
        [by_plane, ((planes * rows, CHIPS * block), bf16), ((CHIPS * block, columns), bf16)],
        "product_send",
        flops=1 << 27,
        moved=1 << 22,
        scale=scale,
    )(here, *normed, *layers, layer)
    parts = call(
        product_kernel,
        [SMEM] + [VMEM] * 3,
        [((rows, columns), f32)] * planes,
        "product",
        scratch=[pltpu.VMEM(*by_plane)],
        flops=1 << 27,
        moved=1 << 21,
        scale=scale,
    )(here, left, right, swap(product, 1))
    parts = [parts[0]] + in_line(parts[1:], line_order(planes))
    q_grad, k_grad, v_grad = call(
        outputs_kernel,
        [SMEM] * 3 + [HBM] * 4 + [VMEM] * 2,
        [((block, features), bf16)] * 3,
        "outputs",
        scratch=[rows_in] * 7 + [pltpu.SemaphoreType.DMA((4,))],
        out_specs=[HBM] * 3,
        flops=1 << 29,
        moved=1 << 22,
    )(*facts, q, k, v, g, mine, theirs)
    (proj_grad,) = call(sum_kernel, [VMEM] * planes, [((rows, columns), f32)], "sum", moved=1 << 19)(*parts)
    if dps > 1:
        proj_grad = lax.psum_scatter(proj_grad, "dp", scatter_dimension=0, tiled=True)
    shape_out = (seqs, block, features)
    return (q_grad.reshape(shape_out), k_grad.reshape(shape_out), v_grad.reshape(shape_out), proj_grad)


def solution(mesh):
    rows = P("dp", "ctx", None)
    return jax.shard_map(
        on_device,
        mesh=mesh,
        in_specs=(rows, rows, rows, rows, rows, P(), P(), P("dp", None)),
        out_specs=(rows, rows, rows, P(("dp", "ctx"), None)),
        check_vma=False,
    )
```

```python
import functools
import math

import jax
import jax.numpy as jnp
from jax import lax
from jax.experimental import pallas as pl
from jax.experimental.pallas import tpu as pltpu
from jax.sharding import PartitionSpec as P

norm_eps = 1e-06
f32 = jnp.float32
bf16 = jnp.bfloat16

CORES = 2
CHIPS = 4
PLANE = CORES * CHIPS

SMEM = pl.BlockSpec(memory_space=pltpu.SMEM)
VMEM = pl.BlockSpec(memory_space=pltpu.VMEM)
HBM = pl.BlockSpec(memory_space=pltpu.HBM)
NEXT_CHIP, NEXT_PLANE = CORES, PLANE
FAR_CHIP, FAR_PLANE = 2 * CORES, 2 * PLANE
LONGEST = 2048


def dot(a, b, over_a, over_b):
    return lax.dot_general(a, b, (((over_a,), (over_b,)), ((), ())), preferred_element_type=f32)


def split(x):
    high = x.astype(bf16)
    return high, (x - high.astype(f32)).astype(bf16)


def dot2(a, b, over_a, over_b):
    if a.dtype == f32:
        high, low = split(a)
        return dot(high, b, over_a, over_b) + dot(low, b, over_a, over_b)
    high, low = split(b)
    return dot(a, high, over_a, over_b) + dot(a, low, over_a, over_b)


def doc_of(position, lens):
    bound = lens[0, 0]
    doc = jnp.where(position >= bound, 1, 0)
    for k in range(1, lens.shape[1] - 1):
        bound = bound + lens[0, k]
        doc = doc + jnp.where(position >= bound, 1, 0)
    return doc


def carry(from_edge, to_edge, rate, block, lens):
    same = doc_of(from_edge * block - 1, lens) == doc_of(to_edge * block - 1, lens)
    away = jnp.abs(from_edge - to_edge) * block
    row = jnp.full((1, 128), away.astype(f32) * -rate, f32)
    return jnp.where(same, jnp.exp(row), 0.0)


def entry_exit(here, rate, block, lens, dim, shape):
    offsets = lax.broadcasted_iota(jnp.int32, shape, dim)
    docs = doc_of(here * block + offsets, lens)
    into = jnp.where(docs == doc_of(here * block - 1, lens), jnp.exp(-rate * offsets.astype(f32)), 0.0)
    out = jnp.where(
        docs == doc_of(here * block + block - 1, lens), jnp.exp(-rate * (block - offsets).astype(f32)), 0.0
    )
    return into, out


def head_lanes(head, width):
    return pl.ds(pl.multiple_of(head * width, width), width)


def fetch(refs, spaces, sems):
    copies = [pltpu.make_async_copy(ref, space, sems.at[i]) for i, (ref, space) in enumerate(zip(refs, spaces))]
    for copy in copies:
        copy.start()
    return copies


def in_order(here):
    core = lax.rem(here, CORES)
    chip = lax.rem(here // CORES, CHIPS)
    return [chip, chip ^ (1 + core), chip ^ (2 - core), chip ^ 3]


def in_group(here):
    core = lax.rem(here, CORES)
    first = jnp.where(core == 0, NEXT_CHIP, NEXT_PLANE)
    return [here, here ^ first, here ^ (NEXT_CHIP + NEXT_PLANE - first), here ^ (NEXT_CHIP + NEXT_PLANE)]


def sum_order(planes):
    return [(chip, pair) for pair in reversed(range(planes // 2)) for chip in (1, 0)][:-1]


def half_heads(here, half):
    core = lax.rem(here, CORES)
    part = half // CHIPS
    both = enumerate(zip(in_order(here), in_order(here ^ 1)))
    return [
        (i * part + t, core * half + own * part + t, (1 - core) * half + other * part + t)
        for i, (own, other) in both
        for t in range(part)
    ]


def summary_kernel(
    here_ref, rates_in, lens_in, q_in, k_in, v_in, g_in, layer_in, keep, send, chip_w, layer_wide, *scratch
):
    q, k, v, g, layer, rates, lens, sems = scratch
    copies = fetch((rates_in, lens_in, k_in, v_in, q_in, g_in, layer_in), (rates, lens, k, v, q, g, layer), sems)
    here = here_ref[0]
    block = q.shape[0]
    half, _, width, _ = keep.shape
    heads = half_heads(here, half)
    first = lax.rem(here, CORES) == 0
    edge = here - lax.rem(here, CORES)
    for copy in copies[:2]:
        copy.wait()
    for row, head, _ in heads:
        late = carry(edge + 1, edge + 2, rates[head], block, lens)
        early = carry(edge + 1, edge, rates[head], block, lens)
        chip_w[row, 0:1, :] = jnp.where(first, late, 1.0)
        chip_w[row, 1:2, :] = jnp.where(first, 1.0, late)
        chip_w[row, 2:3, :] = jnp.where(first, 1.0, early)
        chip_w[row, 3:4, :] = jnp.where(first, early, 1.0)
    offsets = lax.broadcasted_iota(jnp.int32, (block, width), 0)
    docs = doc_of(here * block + offsets, lens)
    enters = docs == doc_of(here * block - 1, lens)
    leaves = docs == doc_of(here * block + block - 1, lens)
    from_start, to_end = offsets.astype(f32), (block - offsets).astype(f32)
    for copy in copies[2:4]:
        copy.wait()
    for row, *pair in heads:
        for head, out in zip(pair, (keep, send)):
            past = jnp.where(leaves, jnp.exp(-rates[head] * to_end), 0.0)
            lanes = head_lanes(head, width)
            out[row, 0] = dot2(v[:, lanes], k[:, lanes].astype(f32) * past, 0, 0)
    for copy in copies[4:]:
        copy.wait()
    for row, *pair in heads:
        for head, out in zip(pair, (keep, send)):
            into = jnp.where(enters, jnp.exp(-rates[head] * from_start), 0.0)
            lanes = head_lanes(head, width)
            out[row, 1] = dot2(q[:, lanes].astype(f32) * into, g[:, lanes], 0, 0)
    layer_wide[...] = layer[...].astype(f32)


def chip_kernel(weights, keep, recv, *outs):
    for i, out in enumerate(outs):
        for t in range(out.shape[0]):
            row = i * out.shape[0] + t
            for k in range(2):
                own, other = weights[row, 2 * k : 2 * k + 1, :], weights[row, 2 * k + 1 : 2 * k + 2, :]
                out[t, k] = own * keep[row, k] + other * recv[row, k]


def line_order(planes):
    return list(range(planes - 1, 0, -1))


def scan_order(planes):
    return [d for d in line_order(planes) if d == 2] + [d for d in range(1, planes) if d != 2]


def weights_kernel(here_ref, rates, lens, plane_w, line_w, entry_w, state_w, *, block):
    here = here_ref[0]
    half = state_w.shape[0]
    part, lines = line_w.shape[:2]
    core = lax.rem(here, CORES)
    chips = in_order(here)
    plane = here // PLANE
    base = plane * PLANE
    ones = jnp.ones((1, 128), f32)
    for t in range(part):
        rate = rates[core * half + chips[0] * part + t]

        def take(from_edge, to_edge):
            return carry(from_edge, to_edge, rate, block, lens)

        for j, d in enumerate(scan_order(lines + 1)):
            to = plane ^ d
            line_w[t, j, 0:1, :] = jnp.where(to > plane, take(base + PLANE, to * PLANE), 0.0)
            line_w[t, j, 1:2, :] = jnp.where(to < plane, take(base, (to + 1) * PLANE), 0.0)
            line_w[t, j, 2:3, :] = jnp.where(to < plane, ones, 0.0)
            line_w[t, j, 3:4, :] = jnp.where(to > plane, ones, 0.0)
        for i, at in enumerate(chips):
            edge = base + at * CORES
            plane_w[t, i, 0:1, :] = take(edge + CORES, base + PLANE)
            plane_w[t, i, 1:2, :] = take(edge, base)
            entry_w[t, i, CHIPS, 0:1, :] = take(base, edge)
            entry_w[t, i, CHIPS, 1:2, :] = take(base + PLANE, edge + CORES)
            for j, at_other in enumerate(chips):
                other = base + at_other * CORES
                entry_w[t, i, j, 0:1, :] = jnp.where(other < edge, take(other + CORES, edge), 0.0)
                entry_w[t, i, j, 1:2, :] = jnp.where(other > edge, take(other, edge + CORES), 0.0)
    edge = here - core
    first = core == 0
    for row, head, _ in half_heads(here, half):
        fwd = carry(edge, edge + 1, rates[head], block, lens)
        bwd = carry(edge + 2, edge + 1, rates[head], block, lens)
        rows = ((0.0, 1.0), (1.0, fwd), (1.0, bwd), (0.0, 1.0))
        for k, (core0, core1) in enumerate(((0, 1), (1, 0), (2, 3), (3, 2))):
            for m in range(2):
                state_w[row, 2 * k + m : 2 * k + m + 1, :] = jnp.where(
                    first, ones * rows[core0][m], ones * rows[core1][m]
                )


def plane_kernel(weights, line_w, *refs):
    totals, outs = refs[:CHIPS], refs[CHIPS:]
    for t in range(outs[0].shape[0]):
        fwd, bwd = 0.0, 0.0
        for i, total in enumerate(totals):
            fwd = fwd + weights[t, i, 0:1, :] * total[t, 0]
            bwd = bwd + weights[t, i, 1:2, :] * total[t, 1]
        for j, out in enumerate(outs):
            out[t] = line_w[t, j, 0:1, :] * fwd + line_w[t, j, 1:2, :] * bwd


def widen_kernel(layer, out):
    out[...] = layer[...].astype(f32)


def narrow_kernel(layer, out):
    out[...] = layer[...].astype(bf16)


def entry_kernel(weights, line_w, *refs, lines):
    totals, others, outs = refs[:CHIPS], refs[CHIPS : CHIPS + lines], refs[CHIPS + lines :]
    for t in range(outs[0].shape[0]):
        before, after = 0.0, 0.0
        for j, other in enumerate(others):
            before = before + line_w[t, j, 2:3, :] * other[t]
            after = after + line_w[t, j, 3:4, :] * other[t]
        for i, out in enumerate(outs):
            fwd = weights[t, i, CHIPS, 0:1, :] * before
            bwd = weights[t, i, CHIPS, 1:2, :] * after
            for j, total in enumerate(totals):
                if i != j:
                    fwd = fwd + weights[t, i, j, 0:1, :] * total[t, 0]
                    bwd = bwd + weights[t, i, j, 1:2, :] * total[t, 1]
            out[t, 0], out[t, 1] = fwd, bwd


def states_kernel(weights, keep, recv, *refs):
    entries, (mine, send) = refs[:CHIPS], refs[CHIPS:]
    part = entries[0].shape[0]
    for i, entry in enumerate(entries):
        for t in range(part):
            row = i * part + t
            for k in range(2):
                for m, (own, out) in enumerate(((recv, mine), (keep, send))):
                    at = 4 * k + 2 * m
                    out[row, k] = weights[row, at : at + 1, :] * own[row, k] + weights[row, at + 1 : at + 2, :] * entry[t, k]


def causal(here, block, lens):
    at_j = lax.broadcasted_iota(jnp.int32, (block, block), 0)
    at_i = lax.broadcasted_iota(jnp.int32, (block, block), 1)
    docs_j = doc_of(here * block + at_j, lens)
    docs_i = doc_of(here * block + at_i, lens)
    return (docs_i == docs_j) & (at_i >= at_j), jnp.maximum(at_i - at_j, 0).astype(f32)


def within_kernel(here_ref, rates, lens, gain, q, k, v, attn, gain_col, into_rows):
    here = here_ref[0]
    block, features = q.shape
    heads = rates.shape[0]
    width = features // heads
    reached, away = causal(here, block, lens)
    for head in range(heads):
        lanes = slice(head * width, (head + 1) * width)
        gain_col[lanes, :] = jnp.broadcast_to(gain[:, lanes], (block, width)).T
        decay = jnp.where(reached, jnp.exp(-rates[head] * away), 0.0)
        scores = dot(k[:, lanes], q[:, lanes], 1, 1) * decay
        attn[lanes, :] = dot2(v[:, lanes], scores, 0, 0)
        into_rows[head : head + 1, :], _ = entry_exit(here, rates[head], block, lens, 1, (1, block))


def prepare_kernel(here_ref, rates, lens, gain, q, k, v, *outs, block):
    within_kernel(here_ref, rates, lens, gain, q, k, v, *outs[:3])
    weights_kernel(here_ref, rates, lens, *outs[3:], block=block)


def norm_kernel(here_ref, q, attn, gain_col, into_rows, mine, recv, *refs, rows):
    outs, total = refs[:CHIPS], refs[CHIPS]
    here = here_ref[0]
    block, features = q.shape
    half, _, width, _ = mine.shape
    squares = jnp.zeros((width, block), f32)
    for row, *pair in half_heads(here, half):
        for head, states in zip(pair, (mine, recv)):
            lanes = head_lanes(head, width)
            at = attn[lanes, :] + into_rows[pl.ds(head, 1), :] * dot2(states[row, 0], q[:, lanes], 1, 1)
            total[lanes, :] = at
            squares = squares + at * at
    mean = jnp.sum(squares, axis=0, keepdims=True) * (1.0 / features)
    factor = lax.rsqrt(mean + norm_eps)
    planes = features // (PLANE * rows)
    for out, device in zip(outs, in_group(here)):
        corner = (lax.rem(device // NEXT_PLANE, 2) * NEXT_PLANE) + lax.rem(device // NEXT_CHIP, 2) * NEXT_CHIP
        to = 0
        for core in range(CORES):
            for chip in range(2):
                for pair in range(planes // 2):
                    block_at = corner + core + chip * FAR_CHIP + pair * FAR_PLANE
                    at = pl.ds(pl.multiple_of(block_at * rows, rows), rows)
                    normed = (total[at, :] * factor * gain_col[at, :]).astype(bf16)
                    out[to : to + rows, :] = normed.astype(f32)
                    to = to + rows


def product_send_kernel(here_ref, own, first, second, both, chip_layer, plane_layer, both_layer, layer, out, left, right, *, scale):
    core = lax.rem(here_ref[0], CORES)
    rows = left.shape[0]
    block = layer.shape[0]
    mine = pl.ds(pl.multiple_of(core * rows, rows), rows)
    other = pl.ds(pl.multiple_of((1 - core) * rows, rows), rows)
    for k, x in enumerate((layer, chip_layer, plane_layer, both_layer)):
        right[k * block : (k + 1) * block, :] = x[...].astype(bf16)

    def gathered(at):
        one, two = first[at, :], second[at, :]
        parts = (own[at, :], jnp.where(core == 0, one, two), jnp.where(core == 0, two, one), both[at, :])
        return jnp.concatenate([x.astype(bf16) for x in parts], axis=1)

    left[...] = gathered(mine)
    out[...] = (dot(gathered(other), right[...], 1, 0) * scale).reshape(out.shape)


def product_kernel(here_ref, left, right, recv, *refs, scale):
    outs, product = refs[:-1], refs[-1]
    chip = lax.rem(here_ref[0] // FAR_CHIP, 2)
    pair = here_ref[0] // FAR_PLANE
    pairs = product.shape[0] // 2
    product[...] = (dot(left[...], right[...], 1, 0) * scale).reshape(product.shape)
    for out, (chip_away, pairs_away) in zip(outs, [(0, 0)] + sum_order(len(outs))):
        at = (chip ^ chip_away) * pairs + (pair ^ pairs_away)
        out[...] = product[at] + recv[at]


def sum_kernel(*refs):
    total = refs[0][...]
    for x in refs[1:-1]:
        total = total + x[...]
    refs[-1][...] = total


def outputs_kernel(here_ref, rates, lens, q_in, k_in, v_in, g_in, mine, recv, q_out, k_out, v_out, *scratch):
    q, k, v, g, q_grad, k_grad, v_grad, sems = scratch
    copies = fetch((q_in, k_in, v_in, g_in), (q, k, v, g), sems)
    here = here_ref[0]
    block, features = q.shape
    half, _, width, _ = mine.shape
    reached, away = causal(here, block, lens)
    for copy in copies:
        copy.wait()
    for row, *pair in half_heads(here, half):
        for head, states in zip(pair, (mine, recv)):
            lanes = head_lanes(head, width)
            rate = rates[head]
            qh, kh, vh, gh = q[:, lanes], k[:, lanes], v[:, lanes], g[:, lanes]
            decay = jnp.where(reached, jnp.exp(-rate * away), 0.0)
            scores = dot(kh, qh, 1, 1) * decay
            grads = dot(vh, gh, 1, 1) * decay
            into, past = entry_exit(here, rate, block, lens, 0, (block, width))
            before, after = states[row, 0], states[row, 1]
            q_grad[:, lanes] = (dot2(grads, kh, 0, 0) + into * dot2(gh, before, 1, 0)).astype(bf16)
            k_grad[:, lanes] = (dot2(grads, qh, 1, 0) + past * dot2(vh, after, 1, 1)).astype(bf16)
            v_grad[:, lanes] = (dot2(scores, gh, 1, 0) + past * dot2(kh, after, 1, 0)).astype(bf16)
    outs = [pltpu.make_async_copy(x, y, sems.at[i]) for i, (x, y) in enumerate(((q_grad, q_out), (k_grad, k_out), (v_grad, v_out)))]
    for copy in outs:
        copy.start()
    for copy in outs:
        copy.wait()


def for_all_dp(outs, here, planes, dps):
    order = jnp.stack([device // NEXT_PLANE % 2 * 2 + device // NEXT_CHIP % 2 for device in in_group(here)])
    whole = jnp.zeros((CHIPS,) + outs[0].shape, f32).at[order].set(jnp.stack(outs))
    whole = whole.reshape(2, 2, CORES, 2, planes // 2, -1, whole.shape[-1]).transpose(4, 0, 3, 1, 2, 5, 6)
    rows = whole.shape[5] // dps
    whole = whole.reshape(dps, planes // 2, 2, 2, 2, CORES, rows, -1).transpose(2, 4, 5, 3, 1, 0, 6, 7)
    whole = whole.reshape((CHIPS,) + outs[0].shape)[order]
    return [whole[d] for d in range(CHIPS)]


def call(kernel, specs, outs, name, scratch=(), flops=0, moved=0, out_specs=None, after=(), **named):
    reads = len(specs)

    def body(*refs):
        kernel(*refs[:reads], *refs[reads + len(after) :], **named)

    def run(*operands):
        operands = [
            pltpu.with_memory_space_constraint(x, pltpu.HBM) if spec is HBM else x for x, spec in zip(operands, specs)
        ]
        return pl.pallas_call(
            body,
            out_shape=[jax.ShapeDtypeStruct(shape, dtype) for shape, dtype in outs],
            in_specs=list(specs) + [pl.BlockSpec(memory_space=pl.ANY)] * len(after),
            out_specs=out_specs or [VMEM] * len(outs),
            scratch_shapes=list(scratch),
            cost_estimate=pl.CostEstimate(flops=flops, bytes_accessed=moved, transcendentals=0),
            compiler_params=pltpu.CompilerParams(vmem_limit_bytes=16 * 1024 * 1024),
            name=name,
        )(*operands, *after)

    return run


def on_device(queries, keys, values, out_grad, layer_grad, norm_gain, decay_rates, doc_lengths):
    seqs, block, features = queries.shape
    assert seqs == 1
    assert lax.axis_size("ctx") % FAR_PLANE == 0
    heads = decay_rates.shape[0]
    width = features // heads
    columns = layer_grad.shape[2]
    half = heads // CORES
    part = half // CHIPS
    count = lax.axis_size("ctx")
    planes = count // PLANE
    dps = lax.axis_size("dp")
    scale = 1.0 / math.sqrt(seqs * block * dps * count)
    here = lax.axis_index("ctx").astype(jnp.int32).reshape(1)
    facts = (here, decay_rates, doc_lengths)
    q, k, v, g = (x.reshape(block, features) for x in (queries, keys, values, out_grad))
    layer = layer_grad.reshape(block, columns)

    def swap(x, bit, near=count):
        pairs = [(i, i ^ bit) for i in range(count) if abs(i // PLANE - (i ^ bit) // PLANE) <= near]
        return lax.ppermute(x, "ctx", pairs)

    def first_of_plane(x):
        return lax.ppermute(x, "ctx", [(i, i ^ (1 + i % CORES) * CORES) for i in range(count)])

    def second_of_plane(x):
        return lax.ppermute(x, "ctx", [(i, i ^ (2 - i % CORES) * CORES) for i in range(count)])

    def in_plane(pieces):
        own, first, second, diagonal = pieces
        return [own, first_of_plane(first), second_of_plane(second), swap(diagonal, 3 * CORES)]

    def in_line(pieces, order, near=count):
        return [swap(x, d * PLANE, near) for x, d in zip(pieces, order)]

    pair = ((half, 2, width, width), f32)
    small = ((part, 2, width, width), f32)
    one = ((part, width, width), f32)
    rows_in = pltpu.VMEM((block, features), bf16)
    half_layer = ((block // 2, columns), f32)
    keep, send, chip_w, layer_wide = call(
        summary_kernel,
        [SMEM] + [HBM] * 7,
        [pair] * 2 + [((half, 4, 128), f32), ((block, columns), f32)],
        "summary",
        scratch=[rows_in] * 4
        + [
            pltpu.VMEM((block, columns), bf16),
            pltpu.SMEM((heads,), f32),
            pltpu.SMEM(doc_lengths.shape, jnp.int32),
            pltpu.SemaphoreType.DMA((7,)),
        ],
        flops=1 << 26,
        moved=1 << 21,
    )(*facts, q, k, v, g, layer)
    recv = swap(send, 1)
    plane_layer = swap(layer_wide, NEXT_PLANE)
    totals = call(
        chip_kernel, [VMEM] * 3, [small] * CHIPS, "chip_total", moved=1 << 20
    )(chip_w, keep, recv)
    attn, gain_col, into_rows, plane_w, line_w, entry_w, state_w = call(
        prepare_kernel,
        [SMEM] * 3 + [VMEM] * 4,
        [
            ((features, block), f32),
            ((features, block), f32),
            ((heads, block), f32),
            ((part, CHIPS, 2, 128), f32),
            ((part, planes - 1, 4, 128), f32),
            ((part, CHIPS, CHIPS + 1, 2, 128), f32),
            ((half, 8, 128), f32),
        ],
        "prepare",
        flops=1 << 28,
        moved=1 << 22,
        after=totals[:1],
        block=block,
    )(*facts, norm_gain.reshape(1, features), q, k, v)
    totals = in_plane(totals)
    narrow = ((block, columns), bf16)
    (plane_layer,) = call(narrow_kernel, [VMEM], [narrow], "plane_layer", flops=1 << 31, moved=1 << 19, after=[attn])(
        plane_layer
    )
    (layer_wide,) = call(
        widen_kernel, [VMEM], [((block, columns), f32)], "widen", moved=1 << 19, after=[*totals[1:], plane_layer]
    )(layer)
    chip_layer = swap(layer_wide, NEXT_CHIP)
    near = -(-LONGEST // (PLANE * block))
    onward = call(
        plane_kernel,
        [VMEM] * (2 + CHIPS),
        [one] * (planes - 1),
        "plane_total",
        moved=1 << 19,
        after=[attn, plane_layer],
    )(plane_w, line_w, *totals)
    others = in_line(onward, scan_order(planes), near)
    entries = call(
        entry_kernel,
        [VMEM] * (2 + CHIPS + len(others)),
        [small] * CHIPS,
        "entries",
        moved=1 << 20,
        after=[chip_layer],
        lines=len(others),
    )(entry_w, line_w, *totals, *others)
    entries = in_plane(entries)
    both_layer = swap(chip_layer, NEXT_PLANE)
    (both_layer,) = call(narrow_kernel, [VMEM], [narrow], "both_layer", flops=1 << 31, moved=1 << 19)(both_layer)
    mine, send = call(
        states_kernel, [VMEM] * (3 + CHIPS), [pair] * 2, "states", moved=1 << 21
    )(state_w, keep, recv, *entries)
    theirs = swap(send, 1)

    rows = features // count
    normed = call(
        norm_kernel,
        [SMEM] + [VMEM] * 6,
        [((features // CHIPS, block), f32)] * CHIPS,
        "norm",
        scratch=[pltpu.VMEM((features, block), f32)],
        flops=1 << 26,
        moved=1 << 21,
        after=[both_layer],
        rows=rows,
    )(here, q, attn, gain_col, into_rows, mine, theirs)
    if dps > 1:
        normed = for_all_dp(normed, here[0], planes, dps)
    own, first, second, both = normed
    first = lax.ppermute(first, "ctx", [(i, i ^ (NEXT_PLANE if i % CORES else NEXT_CHIP)) for i in range(count)])
    second = lax.ppermute(second, "ctx", [(i, i ^ (NEXT_CHIP if i % CORES else NEXT_PLANE)) for i in range(count)])
    normed = [own, first, second, swap(both, NEXT_CHIP + NEXT_PLANE)]
    layers = [chip_layer, plane_layer, both_layer]
    by_plane = ((planes, rows, columns), f32)
    product, left, right = call(
        product_send_kernel,
        [SMEM] + [VMEM] * (CHIPS + len(layers) + 1),
        [by_plane, ((planes * rows, CHIPS * block), bf16), ((CHIPS * block, columns), bf16)],
        "product_send",
        flops=1 << 27,
        moved=1 << 22,
        scale=scale,
    )(here, *normed, *layers, layer)
    parts = call(
        product_kernel,
        [SMEM] + [VMEM] * 3,
        [((rows, columns), f32)] * planes,
        "product",
        scratch=[pltpu.VMEM(*by_plane)],
        flops=1 << 27,
        moved=1 << 21,
        scale=scale,
    )(here, left, right, swap(product, 1))
    parts = [parts[0]] + [
        swap(x, chip * FAR_CHIP + pair * FAR_PLANE) for x, (chip, pair) in zip(parts[1:], sum_order(planes))
    ]
    q_grad, k_grad, v_grad = call(
        outputs_kernel,
        [SMEM] * 3 + [HBM] * 4 + [VMEM] * 2,
        [((block, features), bf16)] * 3,
        "outputs",
        scratch=[rows_in] * 7 + [pltpu.SemaphoreType.DMA((4,))],
        out_specs=[HBM] * 3,
        flops=1 << 29,
        moved=1 << 22,
    )(*facts, q, k, v, g, mine, theirs)
    (proj_grad,) = call(sum_kernel, [VMEM] * planes, [((rows, columns), f32)], "sum", moved=1 << 19)(*parts)
    if dps > 1:
        proj_grad = lax.psum_scatter(proj_grad, "dp", scatter_dimension=0, tiled=True)
    shape_out = (seqs, block, features)
    return (q_grad.reshape(shape_out), k_grad.reshape(shape_out), v_grad.reshape(shape_out), proj_grad)


def solution(mesh):
    rows = P("dp", "ctx", None)
    return jax.shard_map(
        on_device,
        mesh=mesh,
        in_specs=(rows, rows, rows, rows, rows, P(), P(), P("dp", None)),
        out_specs=(rows, rows, rows, P(("dp", "ctx"), None)),
        check_vma=False,
    )
```

```python
import functools
import math

import jax
import jax.numpy as jnp
from jax import lax
from jax.experimental import pallas as pl
from jax.experimental.pallas import tpu as pltpu
from jax.sharding import PartitionSpec as P

norm_eps = 1e-06
f32 = jnp.float32
bf16 = jnp.bfloat16

CORES = 2
CHIPS = 4
PLANE = CORES * CHIPS

SMEM = pl.BlockSpec(memory_space=pltpu.SMEM)
VMEM = pl.BlockSpec(memory_space=pltpu.VMEM)
HBM = pl.BlockSpec(memory_space=pltpu.HBM)
NEXT_CHIP, NEXT_PLANE = CORES, PLANE
FAR_CHIP, FAR_PLANE = 2 * CORES, 2 * PLANE
LONGEST = 2048


def dot(a, b, over_a, over_b):
    return lax.dot_general(a, b, (((over_a,), (over_b,)), ((), ())), preferred_element_type=f32)


def split(x):
    high = x.astype(bf16)
    return high, (x - high.astype(f32)).astype(bf16)


def dot2(a, b, over_a, over_b):
    if a.dtype == f32:
        high, low = split(a)
        return dot(high, b, over_a, over_b) + dot(low, b, over_a, over_b)
    high, low = split(b)
    return dot(a, high, over_a, over_b) + dot(a, low, over_a, over_b)


def doc_of(position, lens):
    bound = lens[0, 0]
    doc = jnp.where(position >= bound, 1, 0)
    for k in range(1, lens.shape[1] - 1):
        bound = bound + lens[0, k]
        doc = doc + jnp.where(position >= bound, 1, 0)
    return doc


def carry(from_edge, to_edge, rate, block, lens):
    same = doc_of(from_edge * block - 1, lens) == doc_of(to_edge * block - 1, lens)
    away = jnp.abs(from_edge - to_edge) * block
    row = jnp.full((1, 128), away.astype(f32) * -rate, f32)
    return jnp.where(same, jnp.exp(row), 0.0)


def entry_exit(here, rate, block, lens, dim, shape):
    offsets = lax.broadcasted_iota(jnp.int32, shape, dim)
    docs = doc_of(here * block + offsets, lens)
    into = jnp.where(docs == doc_of(here * block - 1, lens), jnp.exp(-rate * offsets.astype(f32)), 0.0)
    out = jnp.where(
        docs == doc_of(here * block + block - 1, lens), jnp.exp(-rate * (block - offsets).astype(f32)), 0.0
    )
    return into, out


def head_lanes(head, width):
    return pl.ds(pl.multiple_of(head * width, width), width)


def fetch(refs, spaces, sems):
    copies = [pltpu.make_async_copy(ref, space, sems.at[i]) for i, (ref, space) in enumerate(zip(refs, spaces))]
    for copy in copies:
        copy.start()
    return copies


def in_order(here):
    core = lax.rem(here, CORES)
    chip = lax.rem(here // CORES, CHIPS)
    return [chip, chip ^ (1 + core), chip ^ (2 - core), chip ^ 3]


def in_group(here):
    core = lax.rem(here, CORES)
    first = jnp.where(core == 0, NEXT_CHIP, NEXT_PLANE)
    return [here, here ^ first, here ^ (NEXT_CHIP + NEXT_PLANE - first), here ^ (NEXT_CHIP + NEXT_PLANE)]


def sum_order(planes):
    return [(chip, pair) for pair in reversed(range(planes // 2)) for chip in (1, 0)][:-1]


def half_heads(here, half):
    core = lax.rem(here, CORES)
    part = half // CHIPS
    both = enumerate(zip(in_order(here), in_order(here ^ 1)))
    return [
        (i * part + t, core * half + own * part + t, (1 - core) * half + other * part + t)
        for i, (own, other) in both
        for t in range(part)
    ]


def summary_kernel(
    here_ref, rates_in, lens_in, q_in, k_in, v_in, g_in, layer_in, keep, send, chip_w, layer_wide, *scratch
):
    q, k, v, g, layer, rates, lens, sems = scratch
    copies = fetch((rates_in, lens_in, k_in, v_in, q_in, g_in, layer_in), (rates, lens, k, v, q, g, layer), sems)
    here = here_ref[0]
    block = q.shape[0]
    half, _, width, _ = keep.shape
    heads = half_heads(here, half)
    first = lax.rem(here, CORES) == 0
    edge = here - lax.rem(here, CORES)
    for copy in copies[:2]:
        copy.wait()
    for row, head, _ in heads:
        late = carry(edge + 1, edge + 2, rates[head], block, lens)
        early = carry(edge + 1, edge, rates[head], block, lens)
        chip_w[row, 0:1, :] = jnp.where(first, late, 1.0)
        chip_w[row, 1:2, :] = jnp.where(first, 1.0, late)
        chip_w[row, 2:3, :] = jnp.where(first, 1.0, early)
        chip_w[row, 3:4, :] = jnp.where(first, early, 1.0)
    offsets = lax.broadcasted_iota(jnp.int32, (block, width), 0)
    docs = doc_of(here * block + offsets, lens)
    enters = docs == doc_of(here * block - 1, lens)
    leaves = docs == doc_of(here * block + block - 1, lens)
    from_start, to_end = offsets.astype(f32), (block - offsets).astype(f32)
    for copy in copies[2:4]:
        copy.wait()
    for row, *pair in heads:
        for head, out in zip(pair, (keep, send)):
            past = jnp.where(leaves, jnp.exp(-rates[head] * to_end), 0.0)
            lanes = head_lanes(head, width)
            out[row, 0] = dot2(v[:, lanes], k[:, lanes].astype(f32) * past, 0, 0)
    for copy in copies[4:]:
        copy.wait()
    for row, *pair in heads:
        for head, out in zip(pair, (keep, send)):
            into = jnp.where(enters, jnp.exp(-rates[head] * from_start), 0.0)
            lanes = head_lanes(head, width)
            out[row, 1] = dot2(q[:, lanes].astype(f32) * into, g[:, lanes], 0, 0)
    layer_wide[...] = layer[...].astype(f32)


def chip_kernel(weights, keep, recv, *outs):
    for i, out in enumerate(outs):
        for t in range(out.shape[0]):
            row = i * out.shape[0] + t
            for k in range(2):
                own, other = weights[row, 2 * k : 2 * k + 1, :], weights[row, 2 * k + 1 : 2 * k + 2, :]
                out[t, k] = own * keep[row, k] + other * recv[row, k]


def line_order(planes):
    return list(range(planes - 1, 0, -1))


def scan_order(planes):
    return [d for d in line_order(planes) if d == 2] + [d for d in range(1, planes) if d != 2]


def weights_kernel(here_ref, rates, lens, plane_w, line_w, entry_w, state_w, *, block):
    here = here_ref[0]
    half = state_w.shape[0]
    part, lines = line_w.shape[:2]
    core = lax.rem(here, CORES)
    chips = in_order(here)
    plane = here // PLANE
    base = plane * PLANE
    ones = jnp.ones((1, 128), f32)
    for t in range(part):
        rate = rates[core * half + chips[0] * part + t]

        def take(from_edge, to_edge):
            return carry(from_edge, to_edge, rate, block, lens)

        for j, d in enumerate(scan_order(lines + 1)):
            to = plane ^ d
            line_w[t, j, 0:1, :] = jnp.where(to > plane, take(base + PLANE, to * PLANE), 0.0)
            line_w[t, j, 1:2, :] = jnp.where(to < plane, take(base, (to + 1) * PLANE), 0.0)
            line_w[t, j, 2:3, :] = jnp.where(to < plane, ones, 0.0)
            line_w[t, j, 3:4, :] = jnp.where(to > plane, ones, 0.0)
        for i, at in enumerate(chips):
            edge = base + at * CORES
            plane_w[t, i, 0:1, :] = take(edge + CORES, base + PLANE)
            plane_w[t, i, 1:2, :] = take(edge, base)
            entry_w[t, i, CHIPS, 0:1, :] = take(base, edge)
            entry_w[t, i, CHIPS, 1:2, :] = take(base + PLANE, edge + CORES)
            for j, at_other in enumerate(chips):
                other = base + at_other * CORES
                entry_w[t, i, j, 0:1, :] = jnp.where(other < edge, take(other + CORES, edge), 0.0)
                entry_w[t, i, j, 1:2, :] = jnp.where(other > edge, take(other, edge + CORES), 0.0)
    edge = here - core
    first = core == 0
    for row, head, _ in half_heads(here, half):
        fwd = carry(edge, edge + 1, rates[head], block, lens)
        bwd = carry(edge + 2, edge + 1, rates[head], block, lens)
        rows = ((0.0, 1.0), (1.0, fwd), (1.0, bwd), (0.0, 1.0))
        for k, (core0, core1) in enumerate(((0, 1), (1, 0), (2, 3), (3, 2))):
            for m in range(2):
                state_w[row, 2 * k + m : 2 * k + m + 1, :] = jnp.where(
                    first, ones * rows[core0][m], ones * rows[core1][m]
                )


def plane_kernel(weights, line_w, *refs):
    totals, outs = refs[:CHIPS], refs[CHIPS:]
    for t in range(outs[0].shape[0]):
        fwd, bwd = 0.0, 0.0
        for i, total in enumerate(totals):
            fwd = fwd + weights[t, i, 0:1, :] * total[t, 0]
            bwd = bwd + weights[t, i, 1:2, :] * total[t, 1]
        for j, out in enumerate(outs):
            out[t] = line_w[t, j, 0:1, :] * fwd + line_w[t, j, 1:2, :] * bwd


def widen_kernel(layer, out):
    out[...] = layer[...].astype(f32)


def narrow_kernel(layer, out):
    out[...] = layer[...].astype(bf16)


def entry_kernel(weights, line_w, *refs, lines):
    totals, others, outs = refs[:CHIPS], refs[CHIPS : CHIPS + lines], refs[CHIPS + lines :]
    for t in range(outs[0].shape[0]):
        before, after = 0.0, 0.0
        for j, other in enumerate(others):
            before = before + line_w[t, j, 2:3, :] * other[t]
            after = after + line_w[t, j, 3:4, :] * other[t]
        for i, out in enumerate(outs):
            fwd = weights[t, i, CHIPS, 0:1, :] * before
            bwd = weights[t, i, CHIPS, 1:2, :] * after
            for j, total in enumerate(totals):
                if i != j:
                    fwd = fwd + weights[t, i, j, 0:1, :] * total[t, 0]
                    bwd = bwd + weights[t, i, j, 1:2, :] * total[t, 1]
            out[t, 0], out[t, 1] = fwd, bwd


def states_kernel(weights, keep, recv, *refs):
    entries, (mine, send) = refs[:CHIPS], refs[CHIPS:]
    part = entries[0].shape[0]
    for i, entry in enumerate(entries):
        for t in range(part):
            row = i * part + t
            for k in range(2):
                for m, (own, out) in enumerate(((recv, mine), (keep, send))):
                    at = 4 * k + 2 * m
                    out[row, k] = weights[row, at : at + 1, :] * own[row, k] + weights[row, at + 1 : at + 2, :] * entry[t, k]


def causal(here, block, lens):
    at_j = lax.broadcasted_iota(jnp.int32, (block, block), 0)
    at_i = lax.broadcasted_iota(jnp.int32, (block, block), 1)
    docs_j = doc_of(here * block + at_j, lens)
    docs_i = doc_of(here * block + at_i, lens)
    return (docs_i == docs_j) & (at_i >= at_j), jnp.maximum(at_i - at_j, 0).astype(f32)


def within_kernel(here_ref, rates, lens, gain, q, k, v, attn, gain_col, into_rows):
    here = here_ref[0]
    block, features = q.shape
    heads = rates.shape[0]
    width = features // heads
    reached, away = causal(here, block, lens)
    for head in range(heads):
        lanes = slice(head * width, (head + 1) * width)
        gain_col[lanes, :] = jnp.broadcast_to(gain[:, lanes], (block, width)).T
        decay = jnp.where(reached, jnp.exp(-rates[head] * away), 0.0)
        scores = dot(k[:, lanes], q[:, lanes], 1, 1) * decay
        attn[lanes, :] = dot2(v[:, lanes], scores, 0, 0)
        into_rows[head : head + 1, :], _ = entry_exit(here, rates[head], block, lens, 1, (1, block))


def prepare_kernel(here_ref, rates, lens, gain, q, k, v, *outs, block):
    within_kernel(here_ref, rates, lens, gain, q, k, v, *outs[:3])
    weights_kernel(here_ref, rates, lens, *outs[3:], block=block)


def norm_kernel(here_ref, q, attn, gain_col, into_rows, mine, recv, *refs, rows):
    outs, total = refs[:CHIPS], refs[CHIPS]
    here = here_ref[0]
    block, features = q.shape
    half, _, width, _ = mine.shape
    squares = jnp.zeros((width, block), f32)
    for row, *pair in half_heads(here, half):
        for head, states in zip(pair, (mine, recv)):
            lanes = head_lanes(head, width)
            at = attn[lanes, :] + into_rows[pl.ds(head, 1), :] * dot2(states[row, 0], q[:, lanes], 1, 1)
            total[lanes, :] = at
            squares = squares + at * at
    mean = jnp.sum(squares, axis=0, keepdims=True) * (1.0 / features)
    factor = lax.rsqrt(mean + norm_eps)
    planes = features // (PLANE * rows)
    for out, device in zip(outs, in_group(here)):
        corner = (lax.rem(device // NEXT_PLANE, 2) * NEXT_PLANE) + lax.rem(device // NEXT_CHIP, 2) * NEXT_CHIP
        to = 0
        for core in range(CORES):
            for chip in range(2):
                for pair in range(planes // 2):
                    block_at = corner + core + chip * FAR_CHIP + pair * FAR_PLANE
                    at = pl.ds(pl.multiple_of(block_at * rows, rows), rows)
                    normed = (total[at, :] * factor * gain_col[at, :]).astype(bf16)
                    out[to : to + rows, :] = normed.astype(f32)
                    to = to + rows


def product_send_kernel(here_ref, own, first, second, both, chip_layer, plane_layer, both_layer, layer, out, left, right, *, scale):
    core = lax.rem(here_ref[0], CORES)
    rows = left.shape[0]
    block = layer.shape[0]
    mine = pl.ds(pl.multiple_of(core * rows, rows), rows)
    other = pl.ds(pl.multiple_of((1 - core) * rows, rows), rows)
    for k, x in enumerate((layer, chip_layer, plane_layer, both_layer)):
        right[k * block : (k + 1) * block, :] = x[...].astype(bf16)

    def gathered(at):
        one, two = first[at, :], second[at, :]
        parts = (own[at, :], jnp.where(core == 0, one, two), jnp.where(core == 0, two, one), both[at, :])
        return jnp.concatenate([x.astype(bf16) for x in parts], axis=1)

    left[...] = gathered(mine)
    out[...] = (dot(gathered(other), right[...], 1, 0) * scale).reshape(out.shape)


def product_kernel(here_ref, left, right, recv, *refs, scale):
    outs, product = refs[:-1], refs[-1]
    chip = lax.rem(here_ref[0] // FAR_CHIP, 2)
    pair = here_ref[0] // FAR_PLANE
    pairs = product.shape[0] // 2
    product[...] = (dot(left[...], right[...], 1, 0) * scale).reshape(product.shape)
    for out, (chip_away, pairs_away) in zip(outs, [(0, 0)] + sum_order(len(outs))):
        at = (chip ^ chip_away) * pairs + (pair ^ pairs_away)
        out[...] = product[at] + recv[at]


def sum_kernel(*refs):
    total = refs[0][...]
    for x in refs[1:-1]:
        total = total + x[...]
    refs[-1][...] = total


def outputs_kernel(here_ref, rates, lens, q_in, k_in, v_in, g_in, mine, recv, q_out, k_out, v_out, *scratch):
    q, k, v, g, q_grad, k_grad, v_grad, sems = scratch
    copies = fetch((q_in, k_in, v_in, g_in), (q, k, v, g), sems)
    here = here_ref[0]
    block, features = q.shape
    half, _, width, _ = mine.shape
    reached, away = causal(here, block, lens)
    for copy in copies:
        copy.wait()
    for row, *pair in half_heads(here, half):
        for head, states in zip(pair, (mine, recv)):
            lanes = head_lanes(head, width)
            rate = rates[head]
            qh, kh, vh, gh = q[:, lanes], k[:, lanes], v[:, lanes], g[:, lanes]
            decay = jnp.where(reached, jnp.exp(-rate * away), 0.0)
            scores = dot(kh, qh, 1, 1) * decay
            grads = dot(vh, gh, 1, 1) * decay
            into, past = entry_exit(here, rate, block, lens, 0, (block, width))
            before, after = states[row, 0], states[row, 1]
            q_grad[:, lanes] = (dot2(grads, kh, 0, 0) + into * dot2(gh, before, 1, 0)).astype(bf16)
            k_grad[:, lanes] = (dot2(grads, qh, 1, 0) + past * dot2(vh, after, 1, 1)).astype(bf16)
            v_grad[:, lanes] = (dot2(scores, gh, 1, 0) + past * dot2(kh, after, 1, 0)).astype(bf16)
    outs = [pltpu.make_async_copy(x, y, sems.at[i]) for i, (x, y) in enumerate(((q_grad, q_out), (k_grad, k_out), (v_grad, v_out)))]
    for copy in outs:
        copy.start()
    for copy in outs:
        copy.wait()


def for_all_dp(outs, here, planes, dps):
    order = jnp.stack([device // NEXT_PLANE % 2 * 2 + device // NEXT_CHIP % 2 for device in in_group(here)])
    whole = jnp.zeros((CHIPS,) + outs[0].shape, f32).at[order].set(jnp.stack(outs))
    whole = whole.reshape(2, 2, CORES, 2, planes // 2, -1, whole.shape[-1]).transpose(4, 0, 3, 1, 2, 5, 6)
    rows = whole.shape[5] // dps
    whole = whole.reshape(dps, planes // 2, 2, 2, 2, CORES, rows, -1).transpose(2, 4, 5, 3, 1, 0, 6, 7)
    whole = whole.reshape((CHIPS,) + outs[0].shape)[order]
    return [whole[d] for d in range(CHIPS)]


def call(kernel, specs, outs, name, scratch=(), flops=0, moved=0, out_specs=None, after=(), **named):
    reads = len(specs)

    def body(*refs):
        kernel(*refs[:reads], *refs[reads + len(after) :], **named)

    def run(*operands):
        operands = [
            pltpu.with_memory_space_constraint(x, pltpu.HBM) if spec is HBM else x for x, spec in zip(operands, specs)
        ]
        return pl.pallas_call(
            body,
            out_shape=[jax.ShapeDtypeStruct(shape, dtype) for shape, dtype in outs],
            in_specs=list(specs) + [pl.BlockSpec(memory_space=pl.ANY)] * len(after),
            out_specs=out_specs or [VMEM] * len(outs),
            scratch_shapes=list(scratch),
            cost_estimate=pl.CostEstimate(flops=flops, bytes_accessed=moved, transcendentals=0),
            compiler_params=pltpu.CompilerParams(vmem_limit_bytes=16 * 1024 * 1024),
            name=name,
        )(*operands, *after)

    return run


def on_device(queries, keys, values, out_grad, layer_grad, norm_gain, decay_rates, doc_lengths):
    seqs, block, features = queries.shape
    assert seqs == 1
    assert lax.axis_size("ctx") % FAR_PLANE == 0
    heads = decay_rates.shape[0]
    width = features // heads
    columns = layer_grad.shape[2]
    half = heads // CORES
    part = half // CHIPS
    count = lax.axis_size("ctx")
    planes = count // PLANE
    dps = lax.axis_size("dp")
    scale = 1.0 / math.sqrt(seqs * block * dps * count)
    here = lax.axis_index("ctx").astype(jnp.int32).reshape(1)
    facts = (here, decay_rates, doc_lengths)
    q, k, v, g = (x.reshape(block, features) for x in (queries, keys, values, out_grad))
    layer = layer_grad.reshape(block, columns)

    def swap(x, bit, near=count):
        pairs = [(i, i ^ bit) for i in range(count) if abs(i // PLANE - (i ^ bit) // PLANE) <= near]
        return lax.ppermute(x, "ctx", pairs)

    def first_of_plane(x):
        return lax.ppermute(x, "ctx", [(i, i ^ (1 + i % CORES) * CORES) for i in range(count)])

    def second_of_plane(x):
        return lax.ppermute(x, "ctx", [(i, i ^ (2 - i % CORES) * CORES) for i in range(count)])

    def in_plane(pieces):
        own, first, second, diagonal = pieces
        return [own, first_of_plane(first), second_of_plane(second), swap(diagonal, 3 * CORES)]

    def in_line(pieces, order, near=count):
        return [swap(x, d * PLANE, near) for x, d in zip(pieces, order)]

    pair = ((half, 2, width, width), f32)
    small = ((part, 2, width, width), f32)
    one = ((part, width, width), f32)
    rows_in = pltpu.VMEM((block, features), bf16)
    half_layer = ((block // 2, columns), f32)
    keep, send, chip_w, layer_wide = call(
        summary_kernel,
        [SMEM] + [HBM] * 7,
        [pair] * 2 + [((half, 4, 128), f32), ((block, columns), f32)],
        "summary",
        scratch=[rows_in] * 4
        + [
            pltpu.VMEM((block, columns), bf16),
            pltpu.SMEM((heads,), f32),
            pltpu.SMEM(doc_lengths.shape, jnp.int32),
            pltpu.SemaphoreType.DMA((7,)),
        ],
        flops=1 << 26,
        moved=1 << 21,
    )(*facts, q, k, v, g, layer)
    recv = swap(send, 1)
    plane_layer = swap(layer_wide, NEXT_PLANE)
    totals = call(
        chip_kernel, [VMEM] * 3, [small] * CHIPS, "chip_total", moved=1 << 20
    )(chip_w, keep, recv)
    attn, gain_col, into_rows, plane_w, line_w, entry_w, state_w = call(
        prepare_kernel,
        [SMEM] * 3 + [VMEM] * 4,
        [
            ((features, block), f32),
            ((features, block), f32),
            ((heads, block), f32),
            ((part, CHIPS, 2, 128), f32),
            ((part, planes - 1, 4, 128), f32),
            ((part, CHIPS, CHIPS + 1, 2, 128), f32),
            ((half, 8, 128), f32),
        ],
        "prepare",
        flops=1 << 28,
        moved=1 << 22,
        after=totals[:1],
        block=block,
    )(*facts, norm_gain.reshape(1, features), q, k, v)
    totals = in_plane(totals)
    narrow = ((block, columns), bf16)
    (plane_layer,) = call(narrow_kernel, [VMEM], [narrow], "plane_layer", flops=1 << 31, moved=1 << 19, after=[attn])(
        plane_layer
    )
    (layer_wide,) = call(
        widen_kernel, [VMEM], [((block, columns), f32)], "widen", moved=1 << 19, after=[*totals[1:], plane_layer]
    )(layer_wide)
    chip_layer = swap(layer_wide, NEXT_CHIP)
    near = -(-LONGEST // (PLANE * block))
    onward = call(
        plane_kernel,
        [VMEM] * (2 + CHIPS),
        [one] * (planes - 1),
        "plane_total",
        moved=1 << 19,
        after=[attn, plane_layer],
    )(plane_w, line_w, *totals)
    others = in_line(onward, scan_order(planes), near)
    entries = call(
        entry_kernel,
        [VMEM] * (2 + CHIPS + len(others)),
        [small] * CHIPS,
        "entries",
        moved=1 << 20,
        lines=len(others),
    )(entry_w, line_w, *totals, *others)
    entries = in_plane(entries)
    both_layer = swap(chip_layer, NEXT_PLANE)
    (both_layer,) = call(narrow_kernel, [VMEM], [narrow], "both_layer", flops=1 << 31, moved=1 << 19)(both_layer)
    mine, send = call(
        states_kernel, [VMEM] * (3 + CHIPS), [pair] * 2, "states", moved=1 << 21
    )(state_w, keep, recv, *entries)
    theirs = swap(send, 1)

    rows = features // count
    normed = call(
        norm_kernel,
        [SMEM] + [VMEM] * 6,
        [((features // CHIPS, block), f32)] * CHIPS,
        "norm",
        scratch=[pltpu.VMEM((features, block), f32)],
        flops=1 << 26,
        moved=1 << 21,
        after=[both_layer],
        rows=rows,
    )(here, q, attn, gain_col, into_rows, mine, theirs)
    if dps > 1:
        normed = for_all_dp(normed, here[0], planes, dps)
    own, first, second, both = normed
    first = lax.ppermute(first, "ctx", [(i, i ^ (NEXT_PLANE if i % CORES else NEXT_CHIP)) for i in range(count)])
    second = lax.ppermute(second, "ctx", [(i, i ^ (NEXT_CHIP if i % CORES else NEXT_PLANE)) for i in range(count)])
    normed = [own, first, second, swap(both, NEXT_CHIP + NEXT_PLANE)]
    layers = [chip_layer, plane_layer, both_layer]
    by_plane = ((planes, rows, columns), f32)
    product, left, right = call(
        product_send_kernel,
        [SMEM] + [VMEM] * (CHIPS + len(layers) + 1),
        [by_plane, ((planes * rows, CHIPS * block), bf16), ((CHIPS * block, columns), bf16)],
        "product_send",
        flops=1 << 27,
        moved=1 << 22,
        scale=scale,
    )(here, *normed, *layers, layer)
    parts = call(
        product_kernel,
        [SMEM] + [VMEM] * 3,
        [((rows, columns), f32)] * planes,
        "product",
        scratch=[pltpu.VMEM(*by_plane)],
        flops=1 << 27,
        moved=1 << 21,
        scale=scale,
    )(here, left, right, swap(product, 1))
    parts = [parts[0]] + [
        swap(x, chip * FAR_CHIP + pair * FAR_PLANE) for x, (chip, pair) in zip(parts[1:], sum_order(planes))
    ]
    q_grad, k_grad, v_grad = call(
        outputs_kernel,
        [SMEM] * 3 + [HBM] * 4 + [VMEM] * 2,
        [((block, features), bf16)] * 3,
        "outputs",
        scratch=[rows_in] * 7 + [pltpu.SemaphoreType.DMA((4,))],
        out_specs=[HBM] * 3,
        flops=1 << 29,
        moved=1 << 22,
    )(*facts, q, k, v, g, mine, theirs)
    (proj_grad,) = call(sum_kernel, [VMEM] * planes, [((rows, columns), f32)], "sum", moved=1 << 19)(*parts)
    if dps > 1:
        proj_grad = lax.psum_scatter(proj_grad, "dp", scatter_dimension=0, tiled=True)
    shape_out = (seqs, block, features)
    return (q_grad.reshape(shape_out), k_grad.reshape(shape_out), v_grad.reshape(shape_out), proj_grad)


def solution(mesh):
    rows = P("dp", "ctx", None)
    return jax.shard_map(
        on_device,
        mesh=mesh,
        in_specs=(rows, rows, rows, rows, rows, P(), P(), P("dp", None)),
        out_specs=(rows, rows, rows, P(("dp", "ctx"), None)),
        check_vma=False,
    )
```

```python
import functools
import math

import jax
import jax.numpy as jnp
from jax import lax
from jax.experimental import pallas as pl
from jax.experimental.pallas import tpu as pltpu
from jax.sharding import PartitionSpec as P

norm_eps = 1e-06
f32 = jnp.float32
bf16 = jnp.bfloat16

CORES = 2
CHIPS = 4
PLANE = CORES * CHIPS

SMEM = pl.BlockSpec(memory_space=pltpu.SMEM)
VMEM = pl.BlockSpec(memory_space=pltpu.VMEM)
HBM = pl.BlockSpec(memory_space=pltpu.HBM)
NEXT_CHIP, NEXT_PLANE = CORES, PLANE
FAR_CHIP, FAR_PLANE = 2 * CORES, 2 * PLANE
LONGEST = 2048


def dot(a, b, over_a, over_b):
    return lax.dot_general(a, b, (((over_a,), (over_b,)), ((), ())), preferred_element_type=f32)


def split(x):
    high = x.astype(bf16)
    return high, (x - high.astype(f32)).astype(bf16)


def dot2(a, b, over_a, over_b):
    if a.dtype == f32:
        high, low = split(a)
        return dot(high, b, over_a, over_b) + dot(low, b, over_a, over_b)
    high, low = split(b)
    return dot(a, high, over_a, over_b) + dot(a, low, over_a, over_b)


def doc_of(position, lens):
    bound = lens[0, 0]
    doc = jnp.where(position >= bound, 1, 0)
    for k in range(1, lens.shape[1] - 1):
        bound = bound + lens[0, k]
        doc = doc + jnp.where(position >= bound, 1, 0)
    return doc


def carry(from_edge, to_edge, rate, block, lens):
    same = doc_of(from_edge * block - 1, lens) == doc_of(to_edge * block - 1, lens)
    away = jnp.abs(from_edge - to_edge) * block
    row = jnp.full((1, 128), away.astype(f32) * -rate, f32)
    return jnp.where(same, jnp.exp(row), 0.0)


def entry_exit(here, rate, block, lens, dim, shape):
    offsets = lax.broadcasted_iota(jnp.int32, shape, dim)
    docs = doc_of(here * block + offsets, lens)
    into = jnp.where(docs == doc_of(here * block - 1, lens), jnp.exp(-rate * offsets.astype(f32)), 0.0)
    out = jnp.where(
        docs == doc_of(here * block + block - 1, lens), jnp.exp(-rate * (block - offsets).astype(f32)), 0.0
    )
    return into, out


def head_lanes(head, width):
    return pl.ds(pl.multiple_of(head * width, width), width)


def fetch(refs, spaces, sems):
    copies = [pltpu.make_async_copy(ref, space, sems.at[i]) for i, (ref, space) in enumerate(zip(refs, spaces))]
    for copy in copies:
        copy.start()
    return copies


def in_order(here):
    core = lax.rem(here, CORES)
    chip = lax.rem(here // CORES, CHIPS)
    return [chip, chip ^ (1 + core), chip ^ (2 - core), chip ^ 3]


def in_group(here):
    core = lax.rem(here, CORES)
    first = jnp.where(core == 0, NEXT_CHIP, NEXT_PLANE)
    return [here, here ^ first, here ^ (NEXT_CHIP + NEXT_PLANE - first), here ^ (NEXT_CHIP + NEXT_PLANE)]


def sum_order(planes):
    return [(chip, pair) for pair in reversed(range(1, planes // 2)) for chip in (0, 1)] + [(1, 0)]


def half_heads(here, half):
    core = lax.rem(here, CORES)
    part = half // CHIPS
    both = enumerate(zip(in_order(here), in_order(here ^ 1)))
    return [
        (i * part + t, core * half + own * part + t, (1 - core) * half + other * part + t)
        for i, (own, other) in both
        for t in range(part)
    ]


def summary_kernel(
    here_ref, rates_in, lens_in, q_in, k_in, v_in, g_in, layer_in, keep, send, chip_w, layer_wide, *scratch
):
    q, k, v, g, layer, rates, lens, sems = scratch
    copies = fetch((rates_in, lens_in, k_in, v_in, q_in, g_in, layer_in), (rates, lens, k, v, q, g, layer), sems)
    here = here_ref[0]
    block = q.shape[0]
    half, _, width, _ = keep.shape
    heads = half_heads(here, half)
    first = lax.rem(here, CORES) == 0
    edge = here - lax.rem(here, CORES)
    for copy in copies[:2]:
        copy.wait()
    for row, head, _ in heads:
        late = carry(edge + 1, edge + 2, rates[head], block, lens)
        early = carry(edge + 1, edge, rates[head], block, lens)
        chip_w[row, 0:1, :] = jnp.where(first, late, 1.0)
        chip_w[row, 1:2, :] = jnp.where(first, 1.0, late)
        chip_w[row, 2:3, :] = jnp.where(first, 1.0, early)
        chip_w[row, 3:4, :] = jnp.where(first, early, 1.0)
    offsets = lax.broadcasted_iota(jnp.int32, (block, width), 0)
    docs = doc_of(here * block + offsets, lens)
    enters = docs == doc_of(here * block - 1, lens)
    leaves = docs == doc_of(here * block + block - 1, lens)
    from_start, to_end = offsets.astype(f32), (block - offsets).astype(f32)
    for copy in copies[2:4]:
        copy.wait()
    for row, *pair in heads:
        for head, out in zip(pair, (keep, send)):
            past = jnp.where(leaves, jnp.exp(-rates[head] * to_end), 0.0)
            lanes = head_lanes(head, width)
            out[row, 0] = dot2(v[:, lanes], k[:, lanes].astype(f32) * past, 0, 0)
    for copy in copies[4:]:
        copy.wait()
    for row, *pair in heads:
        for head, out in zip(pair, (keep, send)):
            into = jnp.where(enters, jnp.exp(-rates[head] * from_start), 0.0)
            lanes = head_lanes(head, width)
            out[row, 1] = dot2(q[:, lanes].astype(f32) * into, g[:, lanes], 0, 0)
    layer_wide[...] = layer[...].astype(f32)


def chip_kernel(weights, keep, recv, *outs):
    for i, out in enumerate(outs):
        for t in range(out.shape[0]):
            row = i * out.shape[0] + t
            for k in range(2):
                own, other = weights[row, 2 * k : 2 * k + 1, :], weights[row, 2 * k + 1 : 2 * k + 2, :]
                out[t, k] = own * keep[row, k] + other * recv[row, k]


def line_order(planes):
    return list(range(planes - 1, 0, -1))


def scan_order(planes):
    return [d for d in line_order(planes) if d == 2] + [d for d in range(1, planes) if d != 2]


def weights_kernel(here_ref, rates, lens, plane_w, line_w, entry_w, state_w, *, block):
    here = here_ref[0]
    half = state_w.shape[0]
    part, lines = line_w.shape[:2]
    core = lax.rem(here, CORES)
    chips = in_order(here)
    plane = here // PLANE
    base = plane * PLANE
    ones = jnp.ones((1, 128), f32)
    for t in range(part):
        rate = rates[core * half + chips[0] * part + t]

        def take(from_edge, to_edge):
            return carry(from_edge, to_edge, rate, block, lens)

        for j, d in enumerate(scan_order(lines + 1)):
            to = plane ^ d
            line_w[t, j, 0:1, :] = jnp.where(to > plane, take(base + PLANE, to * PLANE), 0.0)
            line_w[t, j, 1:2, :] = jnp.where(to < plane, take(base, (to + 1) * PLANE), 0.0)
            line_w[t, j, 2:3, :] = jnp.where(to < plane, ones, 0.0)
            line_w[t, j, 3:4, :] = jnp.where(to > plane, ones, 0.0)
        for i, at in enumerate(chips):
            edge = base + at * CORES
            plane_w[t, i, 0:1, :] = take(edge + CORES, base + PLANE)
            plane_w[t, i, 1:2, :] = take(edge, base)
            entry_w[t, i, CHIPS, 0:1, :] = take(base, edge)
            entry_w[t, i, CHIPS, 1:2, :] = take(base + PLANE, edge + CORES)
            for j, at_other in enumerate(chips):
                other = base + at_other * CORES
                entry_w[t, i, j, 0:1, :] = jnp.where(other < edge, take(other + CORES, edge), 0.0)
                entry_w[t, i, j, 1:2, :] = jnp.where(other > edge, take(other, edge + CORES), 0.0)
    edge = here - core
    first = core == 0
    for row, head, _ in half_heads(here, half):
        fwd = carry(edge, edge + 1, rates[head], block, lens)
        bwd = carry(edge + 2, edge + 1, rates[head], block, lens)
        rows = ((0.0, 1.0), (1.0, fwd), (1.0, bwd), (0.0, 1.0))
        for k, (core0, core1) in enumerate(((0, 1), (1, 0), (2, 3), (3, 2))):
            for m in range(2):
                state_w[row, 2 * k + m : 2 * k + m + 1, :] = jnp.where(
                    first, ones * rows[core0][m], ones * rows[core1][m]
                )


def plane_kernel(weights, line_w, *refs):
    totals, outs = refs[:CHIPS], refs[CHIPS:]
    for t in range(outs[0].shape[0]):
        fwd, bwd = 0.0, 0.0
        for i, total in enumerate(totals):
            fwd = fwd + weights[t, i, 0:1, :] * total[t, 0]
            bwd = bwd + weights[t, i, 1:2, :] * total[t, 1]
        for j, out in enumerate(outs):
            out[t] = line_w[t, j, 0:1, :] * fwd + line_w[t, j, 1:2, :] * bwd


def widen_kernel(layer, out):
    out[...] = layer[...].astype(f32)


def narrow_kernel(layer, out):
    out[...] = layer[...].astype(bf16)


def entry_kernel(weights, line_w, *refs, lines):
    totals, others, outs = refs[:CHIPS], refs[CHIPS : CHIPS + lines], refs[CHIPS + lines :]
    for t in range(outs[0].shape[0]):
        before, after = 0.0, 0.0
        for j, other in enumerate(others):
            before = before + line_w[t, j, 2:3, :] * other[t]
            after = after + line_w[t, j, 3:4, :] * other[t]
        for i, out in enumerate(outs):
            fwd = weights[t, i, CHIPS, 0:1, :] * before
            bwd = weights[t, i, CHIPS, 1:2, :] * after
            for j, total in enumerate(totals):
                if i != j:
                    fwd = fwd + weights[t, i, j, 0:1, :] * total[t, 0]
                    bwd = bwd + weights[t, i, j, 1:2, :] * total[t, 1]
            out[t, 0], out[t, 1] = fwd, bwd


def states_kernel(weights, keep, recv, *refs):
    entries, (mine, send) = refs[:CHIPS], refs[CHIPS:]
    part = entries[0].shape[0]
    for i, entry in enumerate(entries):
        for t in range(part):
            row = i * part + t
            for k in range(2):
                for m, (own, out) in enumerate(((recv, mine), (keep, send))):
                    at = 4 * k + 2 * m
                    out[row, k] = weights[row, at : at + 1, :] * own[row, k] + weights[row, at + 1 : at + 2, :] * entry[t, k]


def causal(here, block, lens):
    at_j = lax.broadcasted_iota(jnp.int32, (block, block), 0)
    at_i = lax.broadcasted_iota(jnp.int32, (block, block), 1)
    docs_j = doc_of(here * block + at_j, lens)
    docs_i = doc_of(here * block + at_i, lens)
    return (docs_i == docs_j) & (at_i >= at_j), jnp.maximum(at_i - at_j, 0).astype(f32)


def within_kernel(here_ref, rates, lens, gain, q, k, v, attn, gain_col, into_rows):
    here = here_ref[0]
    block, features = q.shape
    heads = rates.shape[0]
    width = features // heads
    reached, away = causal(here, block, lens)
    for head in range(heads):
        lanes = slice(head * width, (head + 1) * width)
        gain_col[lanes, :] = jnp.broadcast_to(gain[:, lanes], (block, width)).T
        decay = jnp.where(reached, jnp.exp(-rates[head] * away), 0.0)
        scores = dot(k[:, lanes], q[:, lanes], 1, 1) * decay
        attn[lanes, :] = dot2(v[:, lanes], scores, 0, 0)
        into_rows[head : head + 1, :], _ = entry_exit(here, rates[head], block, lens, 1, (1, block))


def prepare_kernel(here_ref, rates, lens, gain, q, k, v, *outs, block):
    within_kernel(here_ref, rates, lens, gain, q, k, v, *outs[:3])
    weights_kernel(here_ref, rates, lens, *outs[3:], block=block)


def norm_kernel(here_ref, q, attn, gain_col, into_rows, mine, recv, *refs, rows):
    outs, total = refs[:CHIPS], refs[CHIPS]
    here = here_ref[0]
    block, features = q.shape
    half, _, width, _ = mine.shape
    squares = jnp.zeros((width, block), f32)
    for row, *pair in half_heads(here, half):
        for head, states in zip(pair, (mine, recv)):
            lanes = head_lanes(head, width)
            at = attn[lanes, :] + into_rows[pl.ds(head, 1), :] * dot2(states[row, 0], q[:, lanes], 1, 1)
            total[lanes, :] = at
            squares = squares + at * at
    mean = jnp.sum(squares, axis=0, keepdims=True) * (1.0 / features)
    factor = lax.rsqrt(mean + norm_eps)
    planes = features // (PLANE * rows)
    for out, device in zip(outs, in_group(here)):
        corner = (lax.rem(device // NEXT_PLANE, 2) * NEXT_PLANE) + lax.rem(device // NEXT_CHIP, 2) * NEXT_CHIP
        to = 0
        for core in range(CORES):
            for chip in range(2):
                for pair in range(planes // 2):
                    block_at = corner + core + chip * FAR_CHIP + pair * FAR_PLANE
                    at = pl.ds(pl.multiple_of(block_at * rows, rows), rows)
                    normed = (total[at, :] * factor * gain_col[at, :]).astype(bf16)
                    out[to : to + rows, :] = normed.astype(f32)
                    to = to + rows


def product_send_kernel(here_ref, own, first, second, both, chip_layer, plane_layer, both_layer, layer, out, left, right, *, scale):
    core = lax.rem(here_ref[0], CORES)
    rows = left.shape[0]
    block = layer.shape[0]
    mine = pl.ds(pl.multiple_of(core * rows, rows), rows)
    other = pl.ds(pl.multiple_of((1 - core) * rows, rows), rows)
    for k, x in enumerate((layer, chip_layer, plane_layer, both_layer)):
        right[k * block : (k + 1) * block, :] = x[...].astype(bf16)

    def gathered(at):
        one, two = first[at, :], second[at, :]
        parts = (own[at, :], jnp.where(core == 0, one, two), jnp.where(core == 0, two, one), both[at, :])
        return jnp.concatenate([x.astype(bf16) for x in parts], axis=1)

    left[...] = gathered(mine)
    out[...] = (dot(gathered(other), right[...], 1, 0) * scale).reshape(out.shape)


def product_kernel(here_ref, left, right, recv, *refs, scale):
    outs, product = refs[:-1], refs[-1]
    chip = lax.rem(here_ref[0] // FAR_CHIP, 2)
    pair = here_ref[0] // FAR_PLANE
    pairs = product.shape[0] // 2
    product[...] = (dot(left[...], right[...], 1, 0) * scale).reshape(product.shape)
    for out, (chip_away, pairs_away) in zip(outs, [(0, 0)] + sum_order(len(outs))):
        at = (chip ^ chip_away) * pairs + (pair ^ pairs_away)
        out[...] = product[at] + recv[at]


def sum_kernel(*refs):
    total = refs[0][...]
    for x in refs[1:-1]:
        total = total + x[...]
    refs[-1][...] = total


def outputs_kernel(here_ref, rates, lens, q_in, k_in, v_in, g_in, mine, recv, q_out, k_out, v_out, *scratch):
    q, k, v, g, q_grad, k_grad, v_grad, sems = scratch
    copies = fetch((q_in, k_in, v_in, g_in), (q, k, v, g), sems)
    here = here_ref[0]
    block, features = q.shape
    half, _, width, _ = mine.shape
    reached, away = causal(here, block, lens)
    for copy in copies:
        copy.wait()
    for row, *pair in half_heads(here, half):
        for head, states in zip(pair, (mine, recv)):
            lanes = head_lanes(head, width)
            rate = rates[head]
            qh, kh, vh, gh = q[:, lanes], k[:, lanes], v[:, lanes], g[:, lanes]
            decay = jnp.where(reached, jnp.exp(-rate * away), 0.0)
            scores = dot(kh, qh, 1, 1) * decay
            grads = dot(vh, gh, 1, 1) * decay
            into, past = entry_exit(here, rate, block, lens, 0, (block, width))
            before, after = states[row, 0], states[row, 1]
            q_grad[:, lanes] = (dot2(grads, kh, 0, 0) + into * dot2(gh, before, 1, 0)).astype(bf16)
            k_grad[:, lanes] = (dot2(grads, qh, 1, 0) + past * dot2(vh, after, 1, 1)).astype(bf16)
            v_grad[:, lanes] = (dot2(scores, gh, 1, 0) + past * dot2(kh, after, 1, 0)).astype(bf16)
    outs = [pltpu.make_async_copy(x, y, sems.at[i]) for i, (x, y) in enumerate(((q_grad, q_out), (k_grad, k_out), (v_grad, v_out)))]
    for copy in outs:
        copy.start()
    for copy in outs:
        copy.wait()


def for_all_dp(outs, here, planes, dps):
    order = jnp.stack([device // NEXT_PLANE % 2 * 2 + device // NEXT_CHIP % 2 for device in in_group(here)])
    whole = jnp.zeros((CHIPS,) + outs[0].shape, f32).at[order].set(jnp.stack(outs))
    whole = whole.reshape(2, 2, CORES, 2, planes // 2, -1, whole.shape[-1]).transpose(4, 0, 3, 1, 2, 5, 6)
    rows = whole.shape[5] // dps
    whole = whole.reshape(dps, planes // 2, 2, 2, 2, CORES, rows, -1).transpose(2, 4, 5, 3, 1, 0, 6, 7)
    whole = whole.reshape((CHIPS,) + outs[0].shape)[order]
    return [whole[d] for d in range(CHIPS)]


def call(kernel, specs, outs, name, scratch=(), flops=0, moved=0, out_specs=None, after=(), **named):
    reads = len(specs)

    def body(*refs):
        kernel(*refs[:reads], *refs[reads + len(after) :], **named)

    def run(*operands):
        operands = [
            pltpu.with_memory_space_constraint(x, pltpu.HBM) if spec is HBM else x for x, spec in zip(operands, specs)
        ]
        return pl.pallas_call(
            body,
            out_shape=[jax.ShapeDtypeStruct(shape, dtype) for shape, dtype in outs],
            in_specs=list(specs) + [pl.BlockSpec(memory_space=pl.ANY)] * len(after),
            out_specs=out_specs or [VMEM] * len(outs),
            scratch_shapes=list(scratch),
            cost_estimate=pl.CostEstimate(flops=flops, bytes_accessed=moved, transcendentals=0),
            compiler_params=pltpu.CompilerParams(vmem_limit_bytes=16 * 1024 * 1024),
            name=name,
        )(*operands, *after)

    return run


def on_device(queries, keys, values, out_grad, layer_grad, norm_gain, decay_rates, doc_lengths):
    seqs, block, features = queries.shape
    assert seqs == 1
    assert lax.axis_size("ctx") % FAR_PLANE == 0
    heads = decay_rates.shape[0]
    width = features // heads
    columns = layer_grad.shape[2]
    half = heads // CORES
    part = half // CHIPS
    count = lax.axis_size("ctx")
    planes = count // PLANE
    dps = lax.axis_size("dp")
    scale = 1.0 / math.sqrt(seqs * block * dps * count)
    here = lax.axis_index("ctx").astype(jnp.int32).reshape(1)
    facts = (here, decay_rates, doc_lengths)
    q, k, v, g = (x.reshape(block, features) for x in (queries, keys, values, out_grad))
    layer = layer_grad.reshape(block, columns)

    def swap(x, bit, near=count):
        pairs = [(i, i ^ bit) for i in range(count) if abs(i // PLANE - (i ^ bit) // PLANE) <= near]
        return lax.ppermute(x, "ctx", pairs)

    def first_of_plane(x):
        return lax.ppermute(x, "ctx", [(i, i ^ (1 + i % CORES) * CORES) for i in range(count)])

    def second_of_plane(x):
        return lax.ppermute(x, "ctx", [(i, i ^ (2 - i % CORES) * CORES) for i in range(count)])

    def in_plane(pieces):
        own, first, second, diagonal = pieces
        return [own, first_of_plane(first), second_of_plane(second), swap(diagonal, 3 * CORES)]

    def in_line(pieces, order, near=count):
        return [swap(x, d * PLANE, near) for x, d in zip(pieces, order)]

    pair = ((half, 2, width, width), f32)
    small = ((part, 2, width, width), f32)
    one = ((part, width, width), f32)
    rows_in = pltpu.VMEM((block, features), bf16)
    half_layer = ((block // 2, columns), f32)
    keep, send, chip_w, layer_wide = call(
        summary_kernel,
        [SMEM] + [HBM] * 7,
        [pair] * 2 + [((half, 4, 128), f32), ((block, columns), f32)],
        "summary",
        scratch=[rows_in] * 4
        + [
            pltpu.VMEM((block, columns), bf16),
            pltpu.SMEM((heads,), f32),
            pltpu.SMEM(doc_lengths.shape, jnp.int32),
            pltpu.SemaphoreType.DMA((7,)),
        ],
        flops=1 << 26,
        moved=1 << 21,
    )(*facts, q, k, v, g, layer)
    recv = swap(send, 1)
    plane_layer = swap(layer_wide, NEXT_PLANE)
    totals = call(
        chip_kernel, [VMEM] * 3, [small] * CHIPS, "chip_total", moved=1 << 20
    )(chip_w, keep, recv)
    attn, gain_col, into_rows, plane_w, line_w, entry_w, state_w = call(
        prepare_kernel,
        [SMEM] * 3 + [VMEM] * 4,
        [
            ((features, block), f32),
            ((features, block), f32),
            ((heads, block), f32),
            ((part, CHIPS, 2, 128), f32),
            ((part, planes - 1, 4, 128), f32),
            ((part, CHIPS, CHIPS + 1, 2, 128), f32),
            ((half, 8, 128), f32),
        ],
        "prepare",
        flops=1 << 28,
        moved=1 << 22,
        after=totals[:1],
        block=block,
    )(*facts, norm_gain.reshape(1, features), q, k, v)
    totals = in_plane(totals)
    narrow = ((block, columns), bf16)
    (plane_layer,) = call(narrow_kernel, [VMEM], [narrow], "plane_layer", flops=1 << 34, moved=1 << 19, after=[attn])(
        plane_layer
    )
    (layer_wide,) = call(
        widen_kernel, [VMEM], [((block, columns), f32)], "widen", moved=1 << 19, after=[attn, totals[1]]
    )(layer_wide)
    chip_layer = swap(layer_wide, NEXT_CHIP)
    near = -(-LONGEST // (PLANE * block))
    onward = call(
        plane_kernel,
        [VMEM] * (2 + CHIPS),
        [one] * (planes - 1),
        "plane_total",
        moved=1 << 19,
        after=[attn, plane_layer],
    )(plane_w, line_w, *totals)
    others = in_line(onward, scan_order(planes), near)
    entries = call(
        entry_kernel,
        [VMEM] * (2 + CHIPS + len(others)),
        [small] * CHIPS,
        "entries",
        moved=1 << 20,
        lines=len(others),
    )(entry_w, line_w, *totals, *others)
    entries = in_plane(entries)
    both_layer = swap(chip_layer, NEXT_PLANE)
    (both_layer,) = call(narrow_kernel, [VMEM], [narrow], "both_layer", flops=1 << 31, moved=1 << 19)(both_layer)
    mine, send = call(
        states_kernel, [VMEM] * (3 + CHIPS), [pair] * 2, "states", moved=1 << 21
    )(state_w, keep, recv, *entries)
    theirs = swap(send, 1)

    rows = features // count
    normed = call(
        norm_kernel,
        [SMEM] + [VMEM] * 6,
        [((features // CHIPS, block), f32)] * CHIPS,
        "norm",
        scratch=[pltpu.VMEM((features, block), f32)],
        flops=1 << 26,
        moved=1 << 21,
        after=[both_layer],
        rows=rows,
    )(here, q, attn, gain_col, into_rows, mine, theirs)
    if dps > 1:
        normed = for_all_dp(normed, here[0], planes, dps)
    own, first, second, both = normed
    first = lax.ppermute(first, "ctx", [(i, i ^ (NEXT_PLANE if i % CORES else NEXT_CHIP)) for i in range(count)])
    second = lax.ppermute(second, "ctx", [(i, i ^ (NEXT_CHIP if i % CORES else NEXT_PLANE)) for i in range(count)])
    normed = [own, first, second, swap(both, NEXT_CHIP + NEXT_PLANE)]
    layers = [chip_layer, plane_layer, both_layer]
    by_plane = ((planes, rows, columns), f32)
    product, left, right = call(
        product_send_kernel,
        [SMEM] + [VMEM] * (CHIPS + len(layers) + 1),
        [by_plane, ((planes * rows, CHIPS * block), bf16), ((CHIPS * block, columns), bf16)],
        "product_send",
        flops=1 << 27,
        moved=1 << 22,
        scale=scale,
    )(here, *normed, *layers, layer)
    parts = call(
        product_kernel,
        [SMEM] + [VMEM] * 3,
        [((rows, columns), f32)] * planes,
        "product",
        scratch=[pltpu.VMEM(*by_plane)],
        flops=1 << 27,
        moved=1 << 21,
        scale=scale,
    )(here, left, right, swap(product, 1))
    parts = [parts[0]] + [
        swap(x, chip * FAR_CHIP + pair * FAR_PLANE) for x, (chip, pair) in zip(parts[1:], sum_order(planes))
    ]
    q_grad, k_grad, v_grad = call(
        outputs_kernel,
        [SMEM] * 3 + [HBM] * 4 + [VMEM] * 2,
        [((block, features), bf16)] * 3,
        "outputs",
        scratch=[rows_in] * 7 + [pltpu.SemaphoreType.DMA((4,))],
        out_specs=[HBM] * 3,
        flops=1 << 29,
        moved=1 << 22,
    )(*facts, q, k, v, g, mine, theirs)
    (proj_grad,) = call(sum_kernel, [VMEM] * planes, [((rows, columns), f32)], "sum", moved=1 << 19)(*parts)
    if dps > 1:
        proj_grad = lax.psum_scatter(proj_grad, "dp", scatter_dimension=0, tiled=True)
    shape_out = (seqs, block, features)
    return (q_grad.reshape(shape_out), k_grad.reshape(shape_out), v_grad.reshape(shape_out), proj_grad)


def solution(mesh):
    rows = P("dp", "ctx", None)
    return jax.shard_map(
        on_device,
        mesh=mesh,
        in_specs=(rows, rows, rows, rows, rows, P(), P(), P("dp", None)),
        out_specs=(rows, rows, rows, P(("dp", "ctx"), None)),
        check_vma=False,
    )
```

```python
import functools
import math

import jax
import jax.numpy as jnp
from jax import lax
from jax.experimental import pallas as pl
from jax.experimental.pallas import tpu as pltpu
from jax.sharding import PartitionSpec as P

norm_eps = 1e-06
f32 = jnp.float32
bf16 = jnp.bfloat16

CORES = 2
CHIPS = 4
PLANE = CORES * CHIPS

SMEM = pl.BlockSpec(memory_space=pltpu.SMEM)
VMEM = pl.BlockSpec(memory_space=pltpu.VMEM)
HBM = pl.BlockSpec(memory_space=pltpu.HBM)
NEXT_CHIP, NEXT_PLANE = CORES, PLANE
FAR_CHIP, FAR_PLANE = 2 * CORES, 2 * PLANE
LONGEST = 2048


def dot(a, b, over_a, over_b):
    return lax.dot_general(a, b, (((over_a,), (over_b,)), ((), ())), preferred_element_type=f32)


def split(x):
    high = x.astype(bf16)
    return high, (x - high.astype(f32)).astype(bf16)


def dot2(a, b, over_a, over_b):
    if a.dtype == f32:
        high, low = split(a)
        return dot(high, b, over_a, over_b) + dot(low, b, over_a, over_b)
    high, low = split(b)
    return dot(a, high, over_a, over_b) + dot(a, low, over_a, over_b)


def doc_of(position, lens):
    bound = lens[0, 0]
    doc = jnp.where(position >= bound, 1, 0)
    for k in range(1, lens.shape[1] - 1):
        bound = bound + lens[0, k]
        doc = doc + jnp.where(position >= bound, 1, 0)
    return doc


def carry(from_edge, to_edge, rate, block, lens):
    same = doc_of(from_edge * block - 1, lens) == doc_of(to_edge * block - 1, lens)
    away = jnp.abs(from_edge - to_edge) * block
    row = jnp.full((1, 128), away.astype(f32) * -rate, f32)
    return jnp.where(same, jnp.exp(row), 0.0)


def entry_exit(here, rate, block, lens, dim, shape):
    offsets = lax.broadcasted_iota(jnp.int32, shape, dim)
    docs = doc_of(here * block + offsets, lens)
    into = jnp.where(docs == doc_of(here * block - 1, lens), jnp.exp(-rate * offsets.astype(f32)), 0.0)
    out = jnp.where(
        docs == doc_of(here * block + block - 1, lens), jnp.exp(-rate * (block - offsets).astype(f32)), 0.0
    )
    return into, out


def head_lanes(head, width):
    return pl.ds(pl.multiple_of(head * width, width), width)


def fetch(refs, spaces, sems):
    copies = [pltpu.make_async_copy(ref, space, sems.at[i]) for i, (ref, space) in enumerate(zip(refs, spaces))]
    for copy in copies:
        copy.start()
    return copies


def in_order(here):
    core = lax.rem(here, CORES)
    chip = lax.rem(here // CORES, CHIPS)
    return [chip, chip ^ (1 + core), chip ^ (2 - core), chip ^ 3]


def in_group(here):
    core = lax.rem(here, CORES)
    first = jnp.where(core == 0, NEXT_CHIP, NEXT_PLANE)
    return [here, here ^ first, here ^ (NEXT_CHIP + NEXT_PLANE - first), here ^ (NEXT_CHIP + NEXT_PLANE)]


def sum_order(planes):
    return [(chip, pair) for pair in reversed(range(1, planes // 2)) for chip in (0, 1)] + [(1, 0)]


def half_heads(here, half):
    core = lax.rem(here, CORES)
    part = half // CHIPS
    both = enumerate(zip(in_order(here), in_order(here ^ 1)))
    return [
        (i * part + t, core * half + own * part + t, (1 - core) * half + other * part + t)
        for i, (own, other) in both
        for t in range(part)
    ]


def summary_kernel(
    here_ref, rates_in, lens_in, q_in, k_in, v_in, g_in, layer_in, keep, send, chip_w, layer_wide, *scratch
):
    q, k, v, g, layer, rates, lens, sems = scratch
    copies = fetch((rates_in, lens_in, k_in, v_in, q_in, g_in, layer_in), (rates, lens, k, v, q, g, layer), sems)
    here = here_ref[0]
    block = q.shape[0]
    half, _, width, _ = keep.shape
    heads = half_heads(here, half)
    first = lax.rem(here, CORES) == 0
    edge = here - lax.rem(here, CORES)
    for copy in copies[:2]:
        copy.wait()
    for row, head, _ in heads:
        late = carry(edge + 1, edge + 2, rates[head], block, lens)
        early = carry(edge + 1, edge, rates[head], block, lens)
        chip_w[row, 0:1, :] = jnp.where(first, late, 1.0)
        chip_w[row, 1:2, :] = jnp.where(first, 1.0, late)
        chip_w[row, 2:3, :] = jnp.where(first, 1.0, early)
        chip_w[row, 3:4, :] = jnp.where(first, early, 1.0)
    offsets = lax.broadcasted_iota(jnp.int32, (block, width), 0)
    docs = doc_of(here * block + offsets, lens)
    enters = docs == doc_of(here * block - 1, lens)
    leaves = docs == doc_of(here * block + block - 1, lens)
    from_start, to_end = offsets.astype(f32), (block - offsets).astype(f32)
    for copy in copies[2:4]:
        copy.wait()
    for row, *pair in heads:
        for head, out in zip(pair, (keep, send)):
            past = jnp.where(leaves, jnp.exp(-rates[head] * to_end), 0.0)
            lanes = head_lanes(head, width)
            out[row, 0] = dot2(v[:, lanes], k[:, lanes].astype(f32) * past, 0, 0)
    for copy in copies[4:]:
        copy.wait()
    for row, *pair in heads:
        for head, out in zip(pair, (keep, send)):
            into = jnp.where(enters, jnp.exp(-rates[head] * from_start), 0.0)
            lanes = head_lanes(head, width)
            out[row, 1] = dot2(q[:, lanes].astype(f32) * into, g[:, lanes], 0, 0)
    layer_wide[...] = layer[...].astype(f32)


def chip_kernel(weights, keep, recv, *outs):
    for i, out in enumerate(outs):
        for t in range(out.shape[0]):
            row = i * out.shape[0] + t
            for k in range(2):
                own, other = weights[row, 2 * k : 2 * k + 1, :], weights[row, 2 * k + 1 : 2 * k + 2, :]
                out[t, k] = own * keep[row, k] + other * recv[row, k]


def line_order(planes):
    return list(range(planes - 1, 0, -1))


def scan_order(planes):
    return [d for d in line_order(planes) if d == 2] + [d for d in range(1, planes) if d != 2]


def weights_kernel(here_ref, rates, lens, plane_w, line_w, entry_w, state_w, *, block):
    here = here_ref[0]
    half = state_w.shape[0]
    part, lines = line_w.shape[:2]
    core = lax.rem(here, CORES)
    chips = in_order(here)
    plane = here // PLANE
    base = plane * PLANE
    ones = jnp.ones((1, 128), f32)
    for t in range(part):
        rate = rates[core * half + chips[0] * part + t]

        def take(from_edge, to_edge):
            return carry(from_edge, to_edge, rate, block, lens)

        for j, d in enumerate(scan_order(lines + 1)):
            to = plane ^ d
            line_w[t, j, 0:1, :] = jnp.where(to > plane, take(base + PLANE, to * PLANE), 0.0)
            line_w[t, j, 1:2, :] = jnp.where(to < plane, take(base, (to + 1) * PLANE), 0.0)
            line_w[t, j, 2:3, :] = jnp.where(to < plane, ones, 0.0)
            line_w[t, j, 3:4, :] = jnp.where(to > plane, ones, 0.0)
        for i, at in enumerate(chips):
            edge = base + at * CORES
            plane_w[t, i, 0:1, :] = take(edge + CORES, base + PLANE)
            plane_w[t, i, 1:2, :] = take(edge, base)
            entry_w[t, i, CHIPS, 0:1, :] = take(base, edge)
            entry_w[t, i, CHIPS, 1:2, :] = take(base + PLANE, edge + CORES)
            for j, at_other in enumerate(chips):
                other = base + at_other * CORES
                entry_w[t, i, j, 0:1, :] = jnp.where(other < edge, take(other + CORES, edge), 0.0)
                entry_w[t, i, j, 1:2, :] = jnp.where(other > edge, take(other, edge + CORES), 0.0)
    edge = here - core
    first = core == 0
    for row, head, _ in half_heads(here, half):
        fwd = carry(edge, edge + 1, rates[head], block, lens)
        bwd = carry(edge + 2, edge + 1, rates[head], block, lens)
        rows = ((0.0, 1.0), (1.0, fwd), (1.0, bwd), (0.0, 1.0))
        for k, (core0, core1) in enumerate(((0, 1), (1, 0), (2, 3), (3, 2))):
            for m in range(2):
                state_w[row, 2 * k + m : 2 * k + m + 1, :] = jnp.where(
                    first, ones * rows[core0][m], ones * rows[core1][m]
                )


def plane_kernel(weights, line_w, *refs):
    totals, outs = refs[:CHIPS], refs[CHIPS:]
    for t in range(outs[0].shape[0]):
        fwd, bwd = 0.0, 0.0
        for i, total in enumerate(totals):
            fwd = fwd + weights[t, i, 0:1, :] * total[t, 0]
            bwd = bwd + weights[t, i, 1:2, :] * total[t, 1]
        for j, out in enumerate(outs):
            out[t] = line_w[t, j, 0:1, :] * fwd + line_w[t, j, 1:2, :] * bwd


def widen_kernel(layer, out):
    out[...] = layer[...].astype(f32)


def narrow_kernel(layer, out):
    out[...] = layer[...].astype(bf16)


def entry_kernel(weights, line_w, *refs, lines):
    totals, others, outs = refs[:CHIPS], refs[CHIPS : CHIPS + lines], refs[CHIPS + lines :]
    for t in range(outs[0].shape[0]):
        before, after = 0.0, 0.0
        for j, other in enumerate(others):
            before = before + line_w[t, j, 2:3, :] * other[t]
            after = after + line_w[t, j, 3:4, :] * other[t]
        for i, out in enumerate(outs):
            fwd = weights[t, i, CHIPS, 0:1, :] * before
            bwd = weights[t, i, CHIPS, 1:2, :] * after
            for j, total in enumerate(totals):
                if i != j:
                    fwd = fwd + weights[t, i, j, 0:1, :] * total[t, 0]
                    bwd = bwd + weights[t, i, j, 1:2, :] * total[t, 1]
            out[t, 0], out[t, 1] = fwd, bwd


def states_kernel(weights, keep, recv, *refs):
    entries, (mine, send) = refs[:CHIPS], refs[CHIPS:]
    part = entries[0].shape[0]
    for i, entry in enumerate(entries):
        for t in range(part):
            row = i * part + t
            for k in range(2):
                for m, (own, out) in enumerate(((recv, mine), (keep, send))):
                    at = 4 * k + 2 * m
                    out[row, k] = weights[row, at : at + 1, :] * own[row, k] + weights[row, at + 1 : at + 2, :] * entry[t, k]


def causal(here, block, lens):
    at_j = lax.broadcasted_iota(jnp.int32, (block, block), 0)
    at_i = lax.broadcasted_iota(jnp.int32, (block, block), 1)
    docs_j = doc_of(here * block + at_j, lens)
    docs_i = doc_of(here * block + at_i, lens)
    return (docs_i == docs_j) & (at_i >= at_j), jnp.maximum(at_i - at_j, 0).astype(f32)


def within_kernel(here_ref, rates, lens, gain, q, k, v, attn, gain_col, into_rows):
    here = here_ref[0]
    block, features = q.shape
    heads = rates.shape[0]
    width = features // heads
    reached, away = causal(here, block, lens)
    for head in range(heads):
        lanes = slice(head * width, (head + 1) * width)
        gain_col[lanes, :] = jnp.broadcast_to(gain[:, lanes], (block, width)).T
        decay = jnp.where(reached, jnp.exp(-rates[head] * away), 0.0)
        scores = dot(k[:, lanes], q[:, lanes], 1, 1) * decay
        attn[lanes, :] = dot2(v[:, lanes], scores, 0, 0)
        into_rows[head : head + 1, :], _ = entry_exit(here, rates[head], block, lens, 1, (1, block))


def prepare_kernel(here_ref, rates, lens, gain, q, k, v, *outs, block):
    within_kernel(here_ref, rates, lens, gain, q, k, v, *outs[:3])
    weights_kernel(here_ref, rates, lens, *outs[3:], block=block)


def norm_kernel(here_ref, q, attn, gain_col, into_rows, mine, recv, *refs, rows):
    outs, total = refs[:CHIPS], refs[CHIPS]
    here = here_ref[0]
    block, features = q.shape
    half, _, width, _ = mine.shape
    squares = jnp.zeros((width, block), f32)
    for row, *pair in half_heads(here, half):
        for head, states in zip(pair, (mine, recv)):
            lanes = head_lanes(head, width)
            at = attn[lanes, :] + into_rows[pl.ds(head, 1), :] * dot2(states[row, 0], q[:, lanes], 1, 1)
            total[lanes, :] = at
            squares = squares + at * at
    mean = jnp.sum(squares, axis=0, keepdims=True) * (1.0 / features)
    factor = lax.rsqrt(mean + norm_eps)
    planes = features // (PLANE * rows)
    for out, device in zip(outs, in_group(here)):
        corner = (lax.rem(device // NEXT_PLANE, 2) * NEXT_PLANE) + lax.rem(device // NEXT_CHIP, 2) * NEXT_CHIP
        to = 0
        for core in range(CORES):
            for chip in range(2):
                for pair in range(planes // 2):
                    block_at = corner + core + chip * FAR_CHIP + pair * FAR_PLANE
                    at = pl.ds(pl.multiple_of(block_at * rows, rows), rows)
                    normed = (total[at, :] * factor * gain_col[at, :]).astype(bf16)
                    out[to : to + rows, :] = normed.astype(f32)
                    to = to + rows


def product_send_kernel(here_ref, own, first, second, both, chip_layer, plane_layer, both_layer, layer, out, left, right, *, scale):
    core = lax.rem(here_ref[0], CORES)
    rows = left.shape[0]
    block = layer.shape[0]
    mine = pl.ds(pl.multiple_of(core * rows, rows), rows)
    other = pl.ds(pl.multiple_of((1 - core) * rows, rows), rows)
    for k, x in enumerate((layer, chip_layer, plane_layer, both_layer)):
        right[k * block : (k + 1) * block, :] = x[...].astype(bf16)

    def gathered(at):
        one, two = first[at, :], second[at, :]
        parts = (own[at, :], jnp.where(core == 0, one, two), jnp.where(core == 0, two, one), both[at, :])
        return jnp.concatenate([x.astype(bf16) for x in parts], axis=1)

    left[...] = gathered(mine)
    out[...] = (dot(gathered(other), right[...], 1, 0) * scale).reshape(out.shape)


def product_kernel(here_ref, left, right, recv, *refs, scale):
    outs, product = refs[:-1], refs[-1]
    chip = lax.rem(here_ref[0] // FAR_CHIP, 2)
    pair = here_ref[0] // FAR_PLANE
    pairs = product.shape[0] // 2
    product[...] = (dot(left[...], right[...], 1, 0) * scale).reshape(product.shape)
    for out, (chip_away, pairs_away) in zip(outs, [(0, 0)] + sum_order(len(outs))):
        at = (chip ^ chip_away) * pairs + (pair ^ pairs_away)
        out[...] = product[at] + recv[at]


def sum_kernel(*refs):
    total = refs[0][...]
    for x in refs[1:-1]:
        total = total + x[...]
    refs[-1][...] = total


def outputs_kernel(here_ref, rates, lens, q_in, k_in, v_in, g_in, mine, recv, q_out, k_out, v_out, *scratch):
    q, k, v, g, q_grad, k_grad, v_grad, sems = scratch
    copies = fetch((q_in, k_in, v_in, g_in), (q, k, v, g), sems)
    here = here_ref[0]
    block, features = q.shape
    half, _, width, _ = mine.shape
    reached, away = causal(here, block, lens)
    for copy in copies:
        copy.wait()
    for row, *pair in half_heads(here, half):
        for head, states in zip(pair, (mine, recv)):
            lanes = head_lanes(head, width)
            rate = rates[head]
            qh, kh, vh, gh = q[:, lanes], k[:, lanes], v[:, lanes], g[:, lanes]
            decay = jnp.where(reached, jnp.exp(-rate * away), 0.0)
            scores = dot(kh, qh, 1, 1) * decay
            grads = dot(vh, gh, 1, 1) * decay
            into, past = entry_exit(here, rate, block, lens, 0, (block, width))
            before, after = states[row, 0], states[row, 1]
            q_grad[:, lanes] = (dot2(grads, kh, 0, 0) + into * dot2(gh, before, 1, 0)).astype(bf16)
            k_grad[:, lanes] = (dot2(grads, qh, 1, 0) + past * dot2(vh, after, 1, 1)).astype(bf16)
            v_grad[:, lanes] = (dot2(scores, gh, 1, 0) + past * dot2(kh, after, 1, 0)).astype(bf16)
    outs = [pltpu.make_async_copy(x, y, sems.at[i]) for i, (x, y) in enumerate(((q_grad, q_out), (k_grad, k_out), (v_grad, v_out)))]
    for copy in outs:
        copy.start()
    for copy in outs:
        copy.wait()


def for_all_dp(outs, here, planes, dps):
    order = jnp.stack([device // NEXT_PLANE % 2 * 2 + device // NEXT_CHIP % 2 for device in in_group(here)])
    whole = jnp.zeros((CHIPS,) + outs[0].shape, f32).at[order].set(jnp.stack(outs))
    whole = whole.reshape(2, 2, CORES, 2, planes // 2, -1, whole.shape[-1]).transpose(4, 0, 3, 1, 2, 5, 6)
    rows = whole.shape[5] // dps
    whole = whole.reshape(dps, planes // 2, 2, 2, 2, CORES, rows, -1).transpose(2, 4, 5, 3, 1, 0, 6, 7)
    whole = whole.reshape((CHIPS,) + outs[0].shape)[order]
    return [whole[d] for d in range(CHIPS)]


def call(kernel, specs, outs, name, scratch=(), flops=0, moved=0, out_specs=None, after=(), **named):
    reads = len(specs)

    def body(*refs):
        kernel(*refs[:reads], *refs[reads + len(after) :], **named)

    def run(*operands):
        operands = [
            pltpu.with_memory_space_constraint(x, pltpu.HBM) if spec is HBM else x for x, spec in zip(operands, specs)
        ]
        return pl.pallas_call(
            body,
            out_shape=[jax.ShapeDtypeStruct(shape, dtype) for shape, dtype in outs],
            in_specs=list(specs) + [pl.BlockSpec(memory_space=pl.ANY)] * len(after),
            out_specs=out_specs or [VMEM] * len(outs),
            scratch_shapes=list(scratch),
            cost_estimate=pl.CostEstimate(flops=flops, bytes_accessed=moved, transcendentals=0),
            compiler_params=pltpu.CompilerParams(vmem_limit_bytes=16 * 1024 * 1024),
            name=name,
        )(*operands, *after)

    return run


def on_device(queries, keys, values, out_grad, layer_grad, norm_gain, decay_rates, doc_lengths):
    seqs, block, features = queries.shape
    assert seqs == 1
    assert lax.axis_size("ctx") % FAR_PLANE == 0
    heads = decay_rates.shape[0]
    width = features // heads
    columns = layer_grad.shape[2]
    half = heads // CORES
    part = half // CHIPS
    count = lax.axis_size("ctx")
    planes = count // PLANE
    dps = lax.axis_size("dp")
    scale = 1.0 / math.sqrt(seqs * block * dps * count)
    here = lax.axis_index("ctx").astype(jnp.int32).reshape(1)
    facts = (here, decay_rates, doc_lengths)
    q, k, v, g = (x.reshape(block, features) for x in (queries, keys, values, out_grad))
    layer = layer_grad.reshape(block, columns)

    def swap(x, bit, near=count):
        pairs = [(i, i ^ bit) for i in range(count) if abs(i // PLANE - (i ^ bit) // PLANE) <= near]
        return lax.ppermute(x, "ctx", pairs)

    def first_of_plane(x):
        return lax.ppermute(x, "ctx", [(i, i ^ (1 + i % CORES) * CORES) for i in range(count)])

    def second_of_plane(x):
        return lax.ppermute(x, "ctx", [(i, i ^ (2 - i % CORES) * CORES) for i in range(count)])

    def in_plane(pieces):
        own, first, second, diagonal = pieces
        return [own, first_of_plane(first), second_of_plane(second), swap(diagonal, 3 * CORES)]

    def in_line(pieces, order, near=count):
        return [swap(x, d * PLANE, near) for x, d in zip(pieces, order)]

    pair = ((half, 2, width, width), f32)
    small = ((part, 2, width, width), f32)
    one = ((part, width, width), f32)
    rows_in = pltpu.VMEM((block, features), bf16)
    half_layer = ((block // 2, columns), f32)
    keep, send, chip_w, layer_wide = call(
        summary_kernel,
        [SMEM] + [HBM] * 7,
        [pair] * 2 + [((half, 4, 128), f32), ((block, columns), f32)],
        "summary",
        scratch=[rows_in] * 4
        + [
            pltpu.VMEM((block, columns), bf16),
            pltpu.SMEM((heads,), f32),
            pltpu.SMEM(doc_lengths.shape, jnp.int32),
            pltpu.SemaphoreType.DMA((7,)),
        ],
        flops=1 << 26,
        moved=1 << 21,
    )(*facts, q, k, v, g, layer)
    recv = swap(send, 1)
    plane_layer = swap(layer_wide, NEXT_PLANE)
    totals = call(
        chip_kernel, [VMEM] * 3, [small] * CHIPS, "chip_total", moved=1 << 20
    )(chip_w, keep, recv)
    attn, gain_col, into_rows, plane_w, line_w, entry_w, state_w = call(
        prepare_kernel,
        [SMEM] * 3 + [VMEM] * 4,
        [
            ((features, block), f32),
            ((features, block), f32),
            ((heads, block), f32),
            ((part, CHIPS, 2, 128), f32),
            ((part, planes - 1, 4, 128), f32),
            ((part, CHIPS, CHIPS + 1, 2, 128), f32),
            ((half, 8, 128), f32),
        ],
        "prepare",
        flops=1 << 28,
        moved=1 << 22,
        after=totals[:1],
        block=block,
    )(*facts, norm_gain.reshape(1, features), q, k, v)
    totals = in_plane(totals)
    narrow = ((block, columns), bf16)
    (plane_layer,) = call(narrow_kernel, [VMEM], [narrow], "plane_layer", flops=1 << 34, moved=1 << 19, after=[attn])(
        plane_layer
    )
    (layer_wide,) = call(
        widen_kernel, [VMEM], [((block, columns), f32)], "widen", moved=1 << 19, after=[attn, totals[1]]
    )(layer_wide)
    chip_layer = swap(layer_wide, NEXT_CHIP)
    near = -(-LONGEST // (PLANE * block))
    onward = call(
        plane_kernel,
        [VMEM] * (2 + CHIPS),
        [one] * (planes - 1),
        "plane_total",
        moved=1 << 19,
        after=[attn, plane_layer],
    )(plane_w, line_w, *totals)
    others = in_line(onward, scan_order(planes), near)
    entries = call(
        entry_kernel,
        [VMEM] * (2 + CHIPS + len(others)),
        [small] * CHIPS,
        "entries",
        moved=1 << 20,
        lines=len(others),
    )(entry_w, line_w, *totals, *others)
    entries = in_plane(entries)
    both_layer = swap(chip_layer, NEXT_PLANE)
    (both_layer,) = call(narrow_kernel, [VMEM], [narrow], "both_layer", flops=6 << 29, moved=1 << 19)(both_layer)
    mine, send = call(
        states_kernel, [VMEM] * (3 + CHIPS), [pair] * 2, "states", moved=1 << 21
    )(state_w, keep, recv, *entries)
    theirs = swap(send, 1)

    rows = features // count
    normed = call(
        norm_kernel,
        [SMEM] + [VMEM] * 6,
        [((features // CHIPS, block), f32)] * CHIPS,
        "norm",
        scratch=[pltpu.VMEM((features, block), f32)],
        flops=1 << 26,
        moved=1 << 21,
        after=[both_layer],
        rows=rows,
    )(here, q, attn, gain_col, into_rows, mine, theirs)
    if dps > 1:
        normed = for_all_dp(normed, here[0], planes, dps)
    own, first, second, both = normed
    first = lax.ppermute(first, "ctx", [(i, i ^ (NEXT_PLANE if i % CORES else NEXT_CHIP)) for i in range(count)])
    second = lax.ppermute(second, "ctx", [(i, i ^ (NEXT_CHIP if i % CORES else NEXT_PLANE)) for i in range(count)])
    normed = [own, first, second, swap(both, NEXT_CHIP + NEXT_PLANE)]
    layers = [chip_layer, plane_layer, both_layer]
    by_plane = ((planes, rows, columns), f32)
    product, left, right = call(
        product_send_kernel,
        [SMEM] + [VMEM] * (CHIPS + len(layers) + 1),
        [by_plane, ((planes * rows, CHIPS * block), bf16), ((CHIPS * block, columns), bf16)],
        "product_send",
        flops=1 << 27,
        moved=1 << 22,
        scale=scale,
    )(here, *normed, *layers, layer)
    parts = call(
        product_kernel,
        [SMEM] + [VMEM] * 3,
        [((rows, columns), f32)] * planes,
        "product",
        scratch=[pltpu.VMEM(*by_plane)],
        flops=1 << 27,
        moved=1 << 21,
        scale=scale,
    )(here, left, right, swap(product, 1))
    parts = [parts[0]] + [
        swap(x, chip * FAR_CHIP + pair * FAR_PLANE) for x, (chip, pair) in zip(parts[1:], sum_order(planes))
    ]
    q_grad, k_grad, v_grad = call(
        outputs_kernel,
        [SMEM] * 3 + [HBM] * 4 + [VMEM] * 2,
        [((block, features), bf16)] * 3,
        "outputs",
        scratch=[rows_in] * 7 + [pltpu.SemaphoreType.DMA((4,))],
        out_specs=[HBM] * 3,
        flops=1 << 29,
        moved=1 << 22,
    )(*facts, q, k, v, g, mine, theirs)
    (proj_grad,) = call(sum_kernel, [VMEM] * planes, [((rows, columns), f32)], "sum", moved=1 << 19)(*parts)
    if dps > 1:
        proj_grad = lax.psum_scatter(proj_grad, "dp", scatter_dimension=0, tiled=True)
    shape_out = (seqs, block, features)
    return (q_grad.reshape(shape_out), k_grad.reshape(shape_out), v_grad.reshape(shape_out), proj_grad)


def solution(mesh):
    rows = P("dp", "ctx", None)
    return jax.shard_map(
        on_device,
        mesh=mesh,
        in_specs=(rows, rows, rows, rows, rows, P(), P(), P("dp", None)),
        out_specs=(rows, rows, rows, P(("dp", "ctx"), None)),
        check_vma=False,
    )
```

```python
import functools
import math

import jax
import jax.numpy as jnp
from jax import lax
from jax.experimental import pallas as pl
from jax.experimental.pallas import tpu as pltpu
from jax.sharding import PartitionSpec as P

norm_eps = 1e-06
f32 = jnp.float32
bf16 = jnp.bfloat16

CORES = 2
CHIPS = 4
PLANE = CORES * CHIPS

SMEM = pl.BlockSpec(memory_space=pltpu.SMEM)
VMEM = pl.BlockSpec(memory_space=pltpu.VMEM)
HBM = pl.BlockSpec(memory_space=pltpu.HBM)
NEXT_CHIP, NEXT_PLANE = CORES, PLANE
FAR_CHIP, FAR_PLANE = 2 * CORES, 2 * PLANE
LONGEST = 2048


def dot(a, b, over_a, over_b):
    return lax.dot_general(a, b, (((over_a,), (over_b,)), ((), ())), preferred_element_type=f32)


def split(x):
    high = x.astype(bf16)
    return high, (x - high.astype(f32)).astype(bf16)


def dot2(a, b, over_a, over_b):
    if a.dtype == f32:
        high, low = split(a)
        return dot(high, b, over_a, over_b) + dot(low, b, over_a, over_b)
    high, low = split(b)
    return dot(a, high, over_a, over_b) + dot(a, low, over_a, over_b)


def doc_of(position, lens):
    bound = lens[0, 0]
    doc = jnp.where(position >= bound, 1, 0)
    for k in range(1, lens.shape[1] - 1):
        bound = bound + lens[0, k]
        doc = doc + jnp.where(position >= bound, 1, 0)
    return doc


def carry(from_edge, to_edge, rate, block, lens):
    same = doc_of(from_edge * block - 1, lens) == doc_of(to_edge * block - 1, lens)
    away = jnp.abs(from_edge - to_edge) * block
    row = jnp.full((1, 128), away.astype(f32) * -rate, f32)
    return jnp.where(same, jnp.exp(row), 0.0)


def entry_exit(here, rate, block, lens, dim, shape):
    offsets = lax.broadcasted_iota(jnp.int32, shape, dim)
    docs = doc_of(here * block + offsets, lens)
    into = jnp.where(docs == doc_of(here * block - 1, lens), jnp.exp(-rate * offsets.astype(f32)), 0.0)
    out = jnp.where(
        docs == doc_of(here * block + block - 1, lens), jnp.exp(-rate * (block - offsets).astype(f32)), 0.0
    )
    return into, out


def head_lanes(head, width):
    return pl.ds(pl.multiple_of(head * width, width), width)


def fetch(refs, spaces, sems):
    copies = [pltpu.make_async_copy(ref, space, sems.at[i]) for i, (ref, space) in enumerate(zip(refs, spaces))]
    for copy in copies:
        copy.start()
    return copies


def in_order(here):
    core = lax.rem(here, CORES)
    chip = lax.rem(here // CORES, CHIPS)
    return [chip, chip ^ (1 + core), chip ^ (2 - core), chip ^ 3]


def in_group(here):
    core = lax.rem(here, CORES)
    first = jnp.where(core == 0, NEXT_CHIP, NEXT_PLANE)
    return [here, here ^ first, here ^ (NEXT_CHIP + NEXT_PLANE - first), here ^ (NEXT_CHIP + NEXT_PLANE)]


def sum_order(planes):
    far = [(chip, pair) for pair in reversed(range(1, planes // 2)) for chip in (0, 1)]
    return list(zip(far + [(1, 0)], [(1, 0)] + far))


def half_heads(here, half):
    core = lax.rem(here, CORES)
    part = half // CHIPS
    both = enumerate(zip(in_order(here), in_order(here ^ 1)))
    return [
        (i * part + t, core * half + own * part + t, (1 - core) * half + other * part + t)
        for i, (own, other) in both
        for t in range(part)
    ]


def summary_kernel(
    here_ref, rates_in, lens_in, q_in, k_in, v_in, g_in, layer_in, keep, send, chip_w, layer_wide, *scratch
):
    q, k, v, g, layer, rates, lens, sems = scratch
    copies = fetch((rates_in, lens_in, k_in, v_in, q_in, g_in, layer_in), (rates, lens, k, v, q, g, layer), sems)
    here = here_ref[0]
    block = q.shape[0]
    half, _, width, _ = keep.shape
    heads = half_heads(here, half)
    first = lax.rem(here, CORES) == 0
    edge = here - lax.rem(here, CORES)
    for copy in copies[:2]:
        copy.wait()
    for row, head, _ in heads:
        late = carry(edge + 1, edge + 2, rates[head], block, lens)
        early = carry(edge + 1, edge, rates[head], block, lens)
        chip_w[row, 0:1, :] = jnp.where(first, late, 1.0)
        chip_w[row, 1:2, :] = jnp.where(first, 1.0, late)
        chip_w[row, 2:3, :] = jnp.where(first, 1.0, early)
        chip_w[row, 3:4, :] = jnp.where(first, early, 1.0)
    offsets = lax.broadcasted_iota(jnp.int32, (block, width), 0)
    docs = doc_of(here * block + offsets, lens)
    enters = docs == doc_of(here * block - 1, lens)
    leaves = docs == doc_of(here * block + block - 1, lens)
    from_start, to_end = offsets.astype(f32), (block - offsets).astype(f32)
    for copy in copies[2:4]:
        copy.wait()
    for row, *pair in heads:
        for head, out in zip(pair, (keep, send)):
            past = jnp.where(leaves, jnp.exp(-rates[head] * to_end), 0.0)
            lanes = head_lanes(head, width)
            out[row, 0] = dot2(v[:, lanes], k[:, lanes].astype(f32) * past, 0, 0)
    for copy in copies[4:]:
        copy.wait()
    for row, *pair in heads:
        for head, out in zip(pair, (keep, send)):
            into = jnp.where(enters, jnp.exp(-rates[head] * from_start), 0.0)
            lanes = head_lanes(head, width)
            out[row, 1] = dot2(q[:, lanes].astype(f32) * into, g[:, lanes], 0, 0)
    layer_wide[...] = layer[...].astype(f32)


def chip_kernel(weights, keep, recv, *outs):
    for i, out in enumerate(outs):
        for t in range(out.shape[0]):
            row = i * out.shape[0] + t
            for k in range(2):
                own, other = weights[row, 2 * k : 2 * k + 1, :], weights[row, 2 * k + 1 : 2 * k + 2, :]
                out[t, k] = own * keep[row, k] + other * recv[row, k]


def scan_order(planes):
    order = list(range(1, planes))
    return [(2, 1), (1, 2)] + [(d, d) for d in order[2:]] if planes > 3 else [(d, d) for d in order]


def weights_kernel(here_ref, rates, lens, plane_w, line_w, entry_w, state_w, *, block):
    here = here_ref[0]
    half = state_w.shape[0]
    part, lines = line_w.shape[:2]
    core = lax.rem(here, CORES)
    chips = in_order(here)
    plane = here // PLANE
    base = plane * PLANE
    ones = jnp.ones((1, 128), f32)
    for t in range(part):
        rate = rates[core * half + chips[0] * part + t]

        def take(from_edge, to_edge):
            return carry(from_edge, to_edge, rate, block, lens)

        for j, (d0, d1) in enumerate(scan_order(lines + 1)):
            to = plane ^ jnp.where(core == 0, d0, d1)
            line_w[t, j, 0:1, :] = jnp.where(to > plane, take(base + PLANE, to * PLANE), 0.0)
            line_w[t, j, 1:2, :] = jnp.where(to < plane, take(base, (to + 1) * PLANE), 0.0)
            line_w[t, j, 2:3, :] = jnp.where(to < plane, ones, 0.0)
            line_w[t, j, 3:4, :] = jnp.where(to > plane, ones, 0.0)
        for i, at in enumerate(chips):
            edge = base + at * CORES
            plane_w[t, i, 0:1, :] = take(edge + CORES, base + PLANE)
            plane_w[t, i, 1:2, :] = take(edge, base)
            entry_w[t, i, CHIPS, 0:1, :] = take(base, edge)
            entry_w[t, i, CHIPS, 1:2, :] = take(base + PLANE, edge + CORES)
            for j, at_other in enumerate(chips):
                other = base + at_other * CORES
                entry_w[t, i, j, 0:1, :] = jnp.where(other < edge, take(other + CORES, edge), 0.0)
                entry_w[t, i, j, 1:2, :] = jnp.where(other > edge, take(other, edge + CORES), 0.0)
    edge = here - core
    first = core == 0
    for row, head, _ in half_heads(here, half):
        fwd = carry(edge, edge + 1, rates[head], block, lens)
        bwd = carry(edge + 2, edge + 1, rates[head], block, lens)
        rows = ((0.0, 1.0), (1.0, fwd), (1.0, bwd), (0.0, 1.0))
        for k, (core0, core1) in enumerate(((0, 1), (1, 0), (2, 3), (3, 2))):
            for m in range(2):
                state_w[row, 2 * k + m : 2 * k + m + 1, :] = jnp.where(
                    first, ones * rows[core0][m], ones * rows[core1][m]
                )


def plane_kernel(weights, line_w, *refs):
    totals, outs = refs[:CHIPS], refs[CHIPS:]
    for t in range(outs[0].shape[0]):
        fwd, bwd = 0.0, 0.0
        for i, total in enumerate(totals):
            fwd = fwd + weights[t, i, 0:1, :] * total[t, 0]
            bwd = bwd + weights[t, i, 1:2, :] * total[t, 1]
        for j, out in enumerate(outs):
            out[t] = line_w[t, j, 0:1, :] * fwd + line_w[t, j, 1:2, :] * bwd


def widen_kernel(layer, out):
    out[...] = layer[...].astype(f32)


def narrow_kernel(layer, out):
    out[...] = layer[...].astype(bf16)


def entry_kernel(weights, line_w, *refs, lines):
    totals, others, outs = refs[:CHIPS], refs[CHIPS : CHIPS + lines], refs[CHIPS + lines :]
    for t in range(outs[0].shape[0]):
        before, after = 0.0, 0.0
        for j, other in enumerate(others):
            before = before + line_w[t, j, 2:3, :] * other[t]
            after = after + line_w[t, j, 3:4, :] * other[t]
        for i, out in enumerate(outs):
            fwd = weights[t, i, CHIPS, 0:1, :] * before
            bwd = weights[t, i, CHIPS, 1:2, :] * after
            for j, total in enumerate(totals):
                if i != j:
                    fwd = fwd + weights[t, i, j, 0:1, :] * total[t, 0]
                    bwd = bwd + weights[t, i, j, 1:2, :] * total[t, 1]
            out[t, 0], out[t, 1] = fwd, bwd


def states_kernel(weights, keep, recv, *refs):
    entries, (mine, send) = refs[:CHIPS], refs[CHIPS:]
    part = entries[0].shape[0]
    for i, entry in enumerate(entries):
        for t in range(part):
            row = i * part + t
            for k in range(2):
                for m, (own, out) in enumerate(((recv, mine), (keep, send))):
                    at = 4 * k + 2 * m
                    out[row, k] = weights[row, at : at + 1, :] * own[row, k] + weights[row, at + 1 : at + 2, :] * entry[t, k]


def causal(here, block, lens):
    at_j = lax.broadcasted_iota(jnp.int32, (block, block), 0)
    at_i = lax.broadcasted_iota(jnp.int32, (block, block), 1)
    docs_j = doc_of(here * block + at_j, lens)
    docs_i = doc_of(here * block + at_i, lens)
    return (docs_i == docs_j) & (at_i >= at_j), jnp.maximum(at_i - at_j, 0).astype(f32)


def within_kernel(here_ref, rates, lens, gain, q, k, v, attn, gain_col, into_rows):
    here = here_ref[0]
    block, features = q.shape
    heads = rates.shape[0]
    width = features // heads
    reached, away = causal(here, block, lens)
    for head in range(heads):
        lanes = slice(head * width, (head + 1) * width)
        gain_col[lanes, :] = jnp.broadcast_to(gain[:, lanes], (block, width)).T
        decay = jnp.where(reached, jnp.exp(-rates[head] * away), 0.0)
        scores = dot(k[:, lanes], q[:, lanes], 1, 1) * decay
        attn[lanes, :] = dot2(v[:, lanes], scores, 0, 0)
        into_rows[head : head + 1, :], _ = entry_exit(here, rates[head], block, lens, 1, (1, block))


def prepare_kernel(here_ref, rates, lens, gain, q, k, v, *outs, block):
    within_kernel(here_ref, rates, lens, gain, q, k, v, *outs[:3])
    weights_kernel(here_ref, rates, lens, *outs[3:], block=block)


def norm_kernel(here_ref, q, attn, gain_col, into_rows, mine, recv, *refs, rows):
    outs, total = refs[:CHIPS], refs[CHIPS]
    here = here_ref[0]
    block, features = q.shape
    half, _, width, _ = mine.shape
    squares = jnp.zeros((width, block), f32)
    for row, *pair in half_heads(here, half):
        for head, states in zip(pair, (mine, recv)):
            lanes = head_lanes(head, width)
            at = attn[lanes, :] + into_rows[pl.ds(head, 1), :] * dot2(states[row, 0], q[:, lanes], 1, 1)
            total[lanes, :] = at
            squares = squares + at * at
    mean = jnp.sum(squares, axis=0, keepdims=True) * (1.0 / features)
    factor = lax.rsqrt(mean + norm_eps)
    planes = features // (PLANE * rows)
    for out, device in zip(outs, in_group(here)):
        corner = (lax.rem(device // NEXT_PLANE, 2) * NEXT_PLANE) + lax.rem(device // NEXT_CHIP, 2) * NEXT_CHIP
        to = 0
        for core in range(CORES):
            for chip in range(2):
                for pair in range(planes // 2):
                    block_at = corner + core + chip * FAR_CHIP + pair * FAR_PLANE
                    at = pl.ds(pl.multiple_of(block_at * rows, rows), rows)
                    normed = (total[at, :] * factor * gain_col[at, :]).astype(bf16)
                    out[to : to + rows, :] = normed.astype(f32)
                    to = to + rows


def product_send_kernel(here_ref, own, first, second, both, chip_layer, plane_layer, both_layer, layer, out, left, right, *, scale):
    core = lax.rem(here_ref[0], CORES)
    rows = left.shape[0]
    block = layer.shape[0]
    mine = pl.ds(pl.multiple_of(core * rows, rows), rows)
    other = pl.ds(pl.multiple_of((1 - core) * rows, rows), rows)
    for k, x in enumerate((layer, chip_layer, plane_layer, both_layer)):
        right[k * block : (k + 1) * block, :] = x[...].astype(bf16)

    def gathered(at):
        one, two = first[at, :], second[at, :]
        parts = (own[at, :], jnp.where(core == 0, one, two), jnp.where(core == 0, two, one), both[at, :])
        return jnp.concatenate([x.astype(bf16) for x in parts], axis=1)

    left[...] = gathered(mine)
    out[...] = (dot(gathered(other), right[...], 1, 0) * scale).reshape(out.shape)


def product_kernel(here_ref, left, right, recv, *refs, scale):
    outs, product = refs[:-1], refs[-1]
    chip = lax.rem(here_ref[0] // FAR_CHIP, 2)
    pair = here_ref[0] // FAR_PLANE
    pairs = product.shape[0] // 2
    product[...] = (dot(left[...], right[...], 1, 0) * scale).reshape(product.shape)
    second = lax.rem(here_ref[0], CORES) == 1
    for out, ((chip0, pair0), (chip1, pair1)) in zip(outs, [((0, 0), (0, 0))] + sum_order(len(outs))):
        at = (chip ^ jnp.where(second, chip1, chip0)) * pairs + (pair ^ jnp.where(second, pair1, pair0))
        out[...] = product[at] + recv[at]


def sum_kernel(*refs):
    total = refs[0][...]
    for x in refs[1:-1]:
        total = total + x[...]
    refs[-1][...] = total


def outputs_kernel(here_ref, rates, lens, q_in, k_in, v_in, g_in, mine, recv, q_out, k_out, v_out, *scratch):
    q, k, v, g, q_grad, k_grad, v_grad, sems = scratch
    copies = fetch((q_in, k_in, v_in, g_in), (q, k, v, g), sems)
    here = here_ref[0]
    block, features = q.shape
    half, _, width, _ = mine.shape
    reached, away = causal(here, block, lens)
    for copy in copies:
        copy.wait()
    for row, *pair in half_heads(here, half):
        for head, states in zip(pair, (mine, recv)):
            lanes = head_lanes(head, width)
            rate = rates[head]
            qh, kh, vh, gh = q[:, lanes], k[:, lanes], v[:, lanes], g[:, lanes]
            decay = jnp.where(reached, jnp.exp(-rate * away), 0.0)
            scores = dot(kh, qh, 1, 1) * decay
            grads = dot(vh, gh, 1, 1) * decay
            into, past = entry_exit(here, rate, block, lens, 0, (block, width))
            before, after = states[row, 0], states[row, 1]
            q_grad[:, lanes] = (dot2(grads, kh, 0, 0) + into * dot2(gh, before, 1, 0)).astype(bf16)
            k_grad[:, lanes] = (dot2(grads, qh, 1, 0) + past * dot2(vh, after, 1, 1)).astype(bf16)
            v_grad[:, lanes] = (dot2(scores, gh, 1, 0) + past * dot2(kh, after, 1, 0)).astype(bf16)
    outs = [pltpu.make_async_copy(x, y, sems.at[i]) for i, (x, y) in enumerate(((q_grad, q_out), (k_grad, k_out), (v_grad, v_out)))]
    for copy in outs:
        copy.start()
    for copy in outs:
        copy.wait()


def for_all_dp(outs, here, planes, dps):
    order = jnp.stack([device // NEXT_PLANE % 2 * 2 + device // NEXT_CHIP % 2 for device in in_group(here)])
    whole = jnp.zeros((CHIPS,) + outs[0].shape, f32).at[order].set(jnp.stack(outs))
    whole = whole.reshape(2, 2, CORES, 2, planes // 2, -1, whole.shape[-1]).transpose(4, 0, 3, 1, 2, 5, 6)
    rows = whole.shape[5] // dps
    whole = whole.reshape(dps, planes // 2, 2, 2, 2, CORES, rows, -1).transpose(2, 4, 5, 3, 1, 0, 6, 7)
    whole = whole.reshape((CHIPS,) + outs[0].shape)[order]
    return [whole[d] for d in range(CHIPS)]


def call(kernel, specs, outs, name, scratch=(), flops=0, moved=0, out_specs=None, after=(), **named):
    reads = len(specs)

    def body(*refs):
        kernel(*refs[:reads], *refs[reads + len(after) :], **named)

    def run(*operands):
        operands = [
            pltpu.with_memory_space_constraint(x, pltpu.HBM) if spec is HBM else x for x, spec in zip(operands, specs)
        ]
        return pl.pallas_call(
            body,
            out_shape=[jax.ShapeDtypeStruct(shape, dtype) for shape, dtype in outs],
            in_specs=list(specs) + [pl.BlockSpec(memory_space=pl.ANY)] * len(after),
            out_specs=out_specs or [VMEM] * len(outs),
            scratch_shapes=list(scratch),
            cost_estimate=pl.CostEstimate(flops=flops, bytes_accessed=moved, transcendentals=0),
            compiler_params=pltpu.CompilerParams(vmem_limit_bytes=16 * 1024 * 1024),
            name=name,
        )(*operands, *after)

    return run


def on_device(queries, keys, values, out_grad, layer_grad, norm_gain, decay_rates, doc_lengths):
    seqs, block, features = queries.shape
    assert seqs == 1
    assert lax.axis_size("ctx") % FAR_PLANE == 0
    heads = decay_rates.shape[0]
    width = features // heads
    columns = layer_grad.shape[2]
    half = heads // CORES
    part = half // CHIPS
    count = lax.axis_size("ctx")
    planes = count // PLANE
    dps = lax.axis_size("dp")
    scale = 1.0 / math.sqrt(seqs * block * dps * count)
    here = lax.axis_index("ctx").astype(jnp.int32).reshape(1)
    facts = (here, decay_rates, doc_lengths)
    q, k, v, g = (x.reshape(block, features) for x in (queries, keys, values, out_grad))
    layer = layer_grad.reshape(block, columns)

    def swap(x, bit, near=count):
        pairs = [(i, i ^ bit) for i in range(count) if abs(i // PLANE - (i ^ bit) // PLANE) <= near]
        return lax.ppermute(x, "ctx", pairs)

    def first_of_plane(x):
        return lax.ppermute(x, "ctx", [(i, i ^ (1 + i % CORES) * CORES) for i in range(count)])

    def second_of_plane(x):
        return lax.ppermute(x, "ctx", [(i, i ^ (2 - i % CORES) * CORES) for i in range(count)])

    def in_plane(pieces):
        own, first, second, diagonal = pieces
        return [own, first_of_plane(first), second_of_plane(second), swap(diagonal, 3 * CORES)]

    def by_core(x, bits, near=count):
        pairs = [(i, i ^ bits[i % CORES]) for i in range(count)]
        return lax.ppermute(x, "ctx", [(i, to) for i, to in pairs if abs(i // PLANE - to // PLANE) <= near])

    pair = ((half, 2, width, width), f32)
    small = ((part, 2, width, width), f32)
    one = ((part, width, width), f32)
    rows_in = pltpu.VMEM((block, features), bf16)
    half_layer = ((block // 2, columns), f32)
    keep, send, chip_w, layer_wide = call(
        summary_kernel,
        [SMEM] + [HBM] * 7,
        [pair] * 2 + [((half, 4, 128), f32), ((block, columns), f32)],
        "summary",
        scratch=[rows_in] * 4
        + [
            pltpu.VMEM((block, columns), bf16),
            pltpu.SMEM((heads,), f32),
            pltpu.SMEM(doc_lengths.shape, jnp.int32),
            pltpu.SemaphoreType.DMA((7,)),
        ],
        flops=1 << 26,
        moved=1 << 21,
    )(*facts, q, k, v, g, layer)
    recv = swap(send, 1)
    plane_layer = swap(layer_wide, NEXT_PLANE)
    totals = call(
        chip_kernel, [VMEM] * 3, [small] * CHIPS, "chip_total", moved=1 << 20
    )(chip_w, keep, recv)
    attn, gain_col, into_rows, plane_w, line_w, entry_w, state_w = call(
        prepare_kernel,
        [SMEM] * 3 + [VMEM] * 4,
        [
            ((features, block), f32),
            ((features, block), f32),
            ((heads, block), f32),
            ((part, CHIPS, 2, 128), f32),
            ((part, planes - 1, 4, 128), f32),
            ((part, CHIPS, CHIPS + 1, 2, 128), f32),
            ((half, 8, 128), f32),
        ],
        "prepare",
        flops=1 << 28,
        moved=1 << 22,
        after=totals[:1],
        block=block,
    )(*facts, norm_gain.reshape(1, features), q, k, v)
    totals = in_plane(totals)
    narrow = ((block, columns), bf16)
    (plane_layer,) = call(narrow_kernel, [VMEM], [narrow], "plane_layer", flops=1 << 34, moved=1 << 19, after=[attn])(
        plane_layer
    )
    (layer_wide,) = call(
        widen_kernel, [VMEM], [((block, columns), f32)], "widen", moved=1 << 19, after=[attn, totals[1]]
    )(layer_wide)
    chip_layer = swap(layer_wide, NEXT_CHIP)
    near = -(-LONGEST // (PLANE * block))
    onward = call(
        plane_kernel,
        [VMEM] * (2 + CHIPS),
        [one] * (planes - 1),
        "plane_total",
        moved=1 << 19,
        after=[attn, plane_layer],
    )(plane_w, line_w, *totals)
    others = [by_core(x, (d0 * PLANE, d1 * PLANE), near) for x, (d0, d1) in zip(onward, scan_order(planes))]
    entries = call(
        entry_kernel,
        [VMEM] * (2 + CHIPS + len(others)),
        [small] * CHIPS,
        "entries",
        moved=1 << 20,
        lines=len(others),
    )(entry_w, line_w, *totals, *others)
    entries = in_plane(entries)
    both_layer = swap(chip_layer, NEXT_PLANE)
    (both_layer,) = call(narrow_kernel, [VMEM], [narrow], "both_layer", flops=6 << 29, moved=1 << 19)(both_layer)
    mine, send = call(
        states_kernel, [VMEM] * (3 + CHIPS), [pair] * 2, "states", moved=1 << 21
    )(state_w, keep, recv, *entries)
    theirs = swap(send, 1)

    rows = features // count
    normed = call(
        norm_kernel,
        [SMEM] + [VMEM] * 6,
        [((features // CHIPS, block), f32)] * CHIPS,
        "norm",
        scratch=[pltpu.VMEM((features, block), f32)],
        flops=1 << 26,
        moved=1 << 21,
        after=[both_layer],
        rows=rows,
    )(here, q, attn, gain_col, into_rows, mine, theirs)
    if dps > 1:
        normed = for_all_dp(normed, here[0], planes, dps)
    own, first, second, both = normed
    first = lax.ppermute(first, "ctx", [(i, i ^ (NEXT_PLANE if i % CORES else NEXT_CHIP)) for i in range(count)])
    second = lax.ppermute(second, "ctx", [(i, i ^ (NEXT_CHIP if i % CORES else NEXT_PLANE)) for i in range(count)])
    normed = [own, first, second, swap(both, NEXT_CHIP + NEXT_PLANE)]
    layers = [chip_layer, plane_layer, both_layer]
    by_plane = ((planes, rows, columns), f32)
    product, left, right = call(
        product_send_kernel,
        [SMEM] + [VMEM] * (CHIPS + len(layers) + 1),
        [by_plane, ((planes * rows, CHIPS * block), bf16), ((CHIPS * block, columns), bf16)],
        "product_send",
        flops=1 << 27,
        moved=1 << 22,
        scale=scale,
    )(here, *normed, *layers, layer)
    parts = call(
        product_kernel,
        [SMEM] + [VMEM] * 3,
        [((rows, columns), f32)] * planes,
        "product",
        scratch=[pltpu.VMEM(*by_plane)],
        flops=1 << 27,
        moved=1 << 21,
        scale=scale,
    )(here, left, right, swap(product, 1))
    parts = [parts[0]] + [
        by_core(x, [chip * FAR_CHIP + pair * FAR_PLANE for chip, pair in away])
        for x, away in zip(parts[1:], sum_order(planes))
    ]
    q_grad, k_grad, v_grad = call(
        outputs_kernel,
        [SMEM] * 3 + [HBM] * 4 + [VMEM] * 2,
        [((block, features), bf16)] * 3,
        "outputs",
        scratch=[rows_in] * 7 + [pltpu.SemaphoreType.DMA((4,))],
        out_specs=[HBM] * 3,
        flops=1 << 29,
        moved=1 << 22,
    )(*facts, q, k, v, g, mine, theirs)
    (proj_grad,) = call(sum_kernel, [VMEM] * planes, [((rows, columns), f32)], "sum", moved=1 << 19)(*parts)
    if dps > 1:
        proj_grad = lax.psum_scatter(proj_grad, "dp", scatter_dimension=0, tiled=True)
    shape_out = (seqs, block, features)
    return (q_grad.reshape(shape_out), k_grad.reshape(shape_out), v_grad.reshape(shape_out), proj_grad)


def solution(mesh):
    rows = P("dp", "ctx", None)
    return jax.shard_map(
        on_device,
        mesh=mesh,
        in_specs=(rows, rows, rows, rows, rows, P(), P(), P("dp", None)),
        out_specs=(rows, rows, rows, P(("dp", "ctx"), None)),
        check_vma=False,
    )
```

```python
import functools
import math

import jax
import jax.numpy as jnp
from jax import lax
from jax.experimental import pallas as pl
from jax.experimental.pallas import tpu as pltpu
from jax.sharding import PartitionSpec as P

norm_eps = 1e-06
f32 = jnp.float32
bf16 = jnp.bfloat16

CORES = 2
CHIPS = 4
PLANE = CORES * CHIPS

SMEM = pl.BlockSpec(memory_space=pltpu.SMEM)
VMEM = pl.BlockSpec(memory_space=pltpu.VMEM)
HBM = pl.BlockSpec(memory_space=pltpu.HBM)
NEXT_CHIP, NEXT_PLANE = CORES, PLANE
FAR_CHIP, FAR_PLANE = 2 * CORES, 2 * PLANE
LONGEST = 2048


def dot(a, b, over_a, over_b):
    return lax.dot_general(a, b, (((over_a,), (over_b,)), ((), ())), preferred_element_type=f32)


def split(x):
    high = x.astype(bf16)
    return high, (x - high.astype(f32)).astype(bf16)


def dot2(a, b, over_a, over_b):
    if a.dtype == f32:
        high, low = split(a)
        return dot(high, b, over_a, over_b) + dot(low, b, over_a, over_b)
    high, low = split(b)
    return dot(a, high, over_a, over_b) + dot(a, low, over_a, over_b)


def doc_of(position, lens):
    bound = lens[0, 0]
    doc = jnp.where(position >= bound, 1, 0)
    for k in range(1, lens.shape[1] - 1):
        bound = bound + lens[0, k]
        doc = doc + jnp.where(position >= bound, 1, 0)
    return doc


def carry(from_edge, to_edge, rate, block, lens):
    same = doc_of(from_edge * block - 1, lens) == doc_of(to_edge * block - 1, lens)
    away = jnp.abs(from_edge - to_edge) * block
    row = jnp.full((1, 128), away.astype(f32) * -rate, f32)
    return jnp.where(same, jnp.exp(row), 0.0)


def entry_exit(here, rate, block, lens, dim, shape):
    offsets = lax.broadcasted_iota(jnp.int32, shape, dim)
    docs = doc_of(here * block + offsets, lens)
    into = jnp.where(docs == doc_of(here * block - 1, lens), jnp.exp(-rate * offsets.astype(f32)), 0.0)
    out = jnp.where(
        docs == doc_of(here * block + block - 1, lens), jnp.exp(-rate * (block - offsets).astype(f32)), 0.0
    )
    return into, out


def head_lanes(head, width):
    return pl.ds(pl.multiple_of(head * width, width), width)


def fetch(refs, spaces, sems):
    copies = [pltpu.make_async_copy(ref, space, sems.at[i]) for i, (ref, space) in enumerate(zip(refs, spaces))]
    for copy in copies:
        copy.start()
    return copies


def in_order(here):
    core = lax.rem(here, CORES)
    chip = lax.rem(here // CORES, CHIPS)
    return [chip, chip ^ (1 + core), chip ^ (2 - core), chip ^ 3]


def in_group(here):
    core = lax.rem(here, CORES)
    first = jnp.where(core == 0, NEXT_CHIP, NEXT_PLANE)
    return [here, here ^ first, here ^ (NEXT_CHIP + NEXT_PLANE - first), here ^ (NEXT_CHIP + NEXT_PLANE)]


def sum_order(planes):
    return [(chip, pair) for pair in reversed(range(1, planes // 2)) for chip in (0, 1)] + [(1, 0)]


def half_heads(here, half):
    core = lax.rem(here, CORES)
    part = half // CHIPS
    both = enumerate(zip(in_order(here), in_order(here ^ 1)))
    return [
        (i * part + t, core * half + own * part + t, (1 - core) * half + other * part + t)
        for i, (own, other) in both
        for t in range(part)
    ]


def summary_kernel(
    here_ref, rates_in, lens_in, q_in, k_in, v_in, g_in, layer_in, keep, send, chip_w, layer_wide, *scratch
):
    q, k, v, g, layer, rates, lens, sems = scratch
    copies = fetch((rates_in, lens_in, k_in, v_in, q_in, g_in, layer_in), (rates, lens, k, v, q, g, layer), sems)
    here = here_ref[0]
    block = q.shape[0]
    half, _, width, _ = keep.shape
    heads = half_heads(here, half)
    first = lax.rem(here, CORES) == 0
    edge = here - lax.rem(here, CORES)
    for copy in copies[:2]:
        copy.wait()
    for row, head, _ in heads:
        late = carry(edge + 1, edge + 2, rates[head], block, lens)
        early = carry(edge + 1, edge, rates[head], block, lens)
        chip_w[row, 0:1, :] = jnp.where(first, late, 1.0)
        chip_w[row, 1:2, :] = jnp.where(first, 1.0, late)
        chip_w[row, 2:3, :] = jnp.where(first, 1.0, early)
        chip_w[row, 3:4, :] = jnp.where(first, early, 1.0)
    offsets = lax.broadcasted_iota(jnp.int32, (block, width), 0)
    docs = doc_of(here * block + offsets, lens)
    enters = docs == doc_of(here * block - 1, lens)
    leaves = docs == doc_of(here * block + block - 1, lens)
    from_start, to_end = offsets.astype(f32), (block - offsets).astype(f32)
    for copy in copies[2:4]:
        copy.wait()
    for row, *pair in heads:
        for head, out in zip(pair, (keep, send)):
            past = jnp.where(leaves, jnp.exp(-rates[head] * to_end), 0.0)
            lanes = head_lanes(head, width)
            out[row, 0] = dot2(v[:, lanes], k[:, lanes].astype(f32) * past, 0, 0)
    for copy in copies[4:]:
        copy.wait()
    for row, *pair in heads:
        for head, out in zip(pair, (keep, send)):
            into = jnp.where(enters, jnp.exp(-rates[head] * from_start), 0.0)
            lanes = head_lanes(head, width)
            out[row, 1] = dot2(q[:, lanes].astype(f32) * into, g[:, lanes], 0, 0)
    layer_wide[...] = layer[...].astype(f32)


def chip_kernel(weights, keep, recv, *outs):
    for i, out in enumerate(outs):
        for t in range(out.shape[0]):
            row = i * out.shape[0] + t
            for k in range(2):
                own, other = weights[row, 2 * k : 2 * k + 1, :], weights[row, 2 * k + 1 : 2 * k + 2, :]
                out[t, k] = own * keep[row, k] + other * recv[row, k]


def line_order(planes):
    return list(range(planes - 1, 0, -1))


def scan_order(planes):
    return [d for d in line_order(planes) if d == 2] + [d for d in range(1, planes) if d != 2]


def weights_kernel(here_ref, rates, lens, plane_w, line_w, entry_w, state_w, *, block):
    here = here_ref[0]
    half = state_w.shape[0]
    part, lines = line_w.shape[:2]
    core = lax.rem(here, CORES)
    chips = in_order(here)
    plane = here // PLANE
    base = plane * PLANE
    ones = jnp.ones((1, 128), f32)
    for t in range(part):
        rate = rates[core * half + chips[0] * part + t]

        def take(from_edge, to_edge):
            return carry(from_edge, to_edge, rate, block, lens)

        for j, d in enumerate(scan_order(lines + 1)):
            to = plane ^ d
            line_w[t, j, 0:1, :] = jnp.where(to > plane, take(base + PLANE, to * PLANE), 0.0)
            line_w[t, j, 1:2, :] = jnp.where(to < plane, take(base, (to + 1) * PLANE), 0.0)
            line_w[t, j, 2:3, :] = jnp.where(to < plane, ones, 0.0)
            line_w[t, j, 3:4, :] = jnp.where(to > plane, ones, 0.0)
        for i, at in enumerate(chips):
            edge = base + at * CORES
            plane_w[t, i, 0:1, :] = take(edge + CORES, base + PLANE)
            plane_w[t, i, 1:2, :] = take(edge, base)
            entry_w[t, i, CHIPS, 0:1, :] = take(base, edge)
            entry_w[t, i, CHIPS, 1:2, :] = take(base + PLANE, edge + CORES)
            for j, at_other in enumerate(chips):
                other = base + at_other * CORES
                entry_w[t, i, j, 0:1, :] = jnp.where(other < edge, take(other + CORES, edge), 0.0)
                entry_w[t, i, j, 1:2, :] = jnp.where(other > edge, take(other, edge + CORES), 0.0)
    edge = here - core
    first = core == 0
    for row, head, _ in half_heads(here, half):
        fwd = carry(edge, edge + 1, rates[head], block, lens)
        bwd = carry(edge + 2, edge + 1, rates[head], block, lens)
        rows = ((0.0, 1.0), (1.0, fwd), (1.0, bwd), (0.0, 1.0))
        for k, (core0, core1) in enumerate(((0, 1), (1, 0), (2, 3), (3, 2))):
            for m in range(2):
                state_w[row, 2 * k + m : 2 * k + m + 1, :] = jnp.where(
                    first, ones * rows[core0][m], ones * rows[core1][m]
                )


def plane_kernel(weights, line_w, *refs):
    totals, outs = refs[:CHIPS], refs[CHIPS:]
    for t in range(outs[0].shape[0]):
        fwd, bwd = 0.0, 0.0
        for i, total in enumerate(totals):
            fwd = fwd + weights[t, i, 0:1, :] * total[t, 0]
            bwd = bwd + weights[t, i, 1:2, :] * total[t, 1]
        for j, out in enumerate(outs):
            out[t] = line_w[t, j, 0:1, :] * fwd + line_w[t, j, 1:2, :] * bwd


def widen_kernel(layer, out):
    out[...] = layer[...].astype(f32)


def narrow_kernel(layer, out):
    out[...] = layer[...].astype(bf16)


def entry_kernel(weights, line_w, *refs, lines, way):
    totals, others, outs = refs[:CHIPS], refs[CHIPS : CHIPS + lines], refs[CHIPS + lines :]
    for t in range(outs[0].shape[0]):
        outside = 0.0
        for j, other in enumerate(others):
            outside = outside + line_w[t, j, 2 + way : 3 + way, :] * other[t]
        for i, out in enumerate(outs):
            entry = weights[t, i, CHIPS, way : way + 1, :] * outside
            for j, total in enumerate(totals):
                if i != j:
                    entry = entry + weights[t, i, j, way : way + 1, :] * total[t, way]
            out[t] = entry


def states_kernel(weights, keep, recv, *refs, way):
    entries, (mine, send) = refs[:CHIPS], refs[CHIPS:]
    part = entries[0].shape[0]
    for i, entry in enumerate(entries):
        for t in range(part):
            row = i * part + t
            for m, (own, out) in enumerate(((recv, mine), (keep, send))):
                at = 4 * way + 2 * m
                out[row] = weights[row, at : at + 1, :] * own[row, way] + weights[row, at + 1 : at + 2, :] * entry[t]


def causal(here, block, lens):
    at_j = lax.broadcasted_iota(jnp.int32, (block, block), 0)
    at_i = lax.broadcasted_iota(jnp.int32, (block, block), 1)
    docs_j = doc_of(here * block + at_j, lens)
    docs_i = doc_of(here * block + at_i, lens)
    return (docs_i == docs_j) & (at_i >= at_j), jnp.maximum(at_i - at_j, 0).astype(f32)


def within_kernel(here_ref, rates, lens, gain, q, k, v, attn, gain_col, into_rows):
    here = here_ref[0]
    block, features = q.shape
    heads = rates.shape[0]
    width = features // heads
    reached, away = causal(here, block, lens)
    for head in range(heads):
        lanes = slice(head * width, (head + 1) * width)
        gain_col[lanes, :] = jnp.broadcast_to(gain[:, lanes], (block, width)).T
        decay = jnp.where(reached, jnp.exp(-rates[head] * away), 0.0)
        scores = dot(k[:, lanes], q[:, lanes], 1, 1) * decay
        attn[lanes, :] = dot2(v[:, lanes], scores, 0, 0)
        into_rows[head : head + 1, :], _ = entry_exit(here, rates[head], block, lens, 1, (1, block))


def prepare_kernel(here_ref, rates, lens, gain, q, k, v, *outs, block):
    within_kernel(here_ref, rates, lens, gain, q, k, v, *outs[:3])
    weights_kernel(here_ref, rates, lens, *outs[3:], block=block)


def norm_kernel(here_ref, q, attn, gain_col, into_rows, mine, recv, *refs, rows):
    outs, total = refs[:CHIPS], refs[CHIPS]
    here = here_ref[0]
    block, features = q.shape
    half, width, _ = mine.shape
    squares = jnp.zeros((width, block), f32)
    for row, *pair in half_heads(here, half):
        for head, states in zip(pair, (mine, recv)):
            lanes = head_lanes(head, width)
            at = attn[lanes, :] + into_rows[pl.ds(head, 1), :] * dot2(states[row], q[:, lanes], 1, 1)
            total[lanes, :] = at
            squares = squares + at * at
    mean = jnp.sum(squares, axis=0, keepdims=True) * (1.0 / features)
    factor = lax.rsqrt(mean + norm_eps)
    planes = features // (PLANE * rows)
    for out, device in zip(outs, in_group(here)):
        corner = (lax.rem(device // NEXT_PLANE, 2) * NEXT_PLANE) + lax.rem(device // NEXT_CHIP, 2) * NEXT_CHIP
        to = 0
        for core in range(CORES):
            for chip in range(2):
                for pair in range(planes // 2):
                    block_at = corner + core + chip * FAR_CHIP + pair * FAR_PLANE
                    at = pl.ds(pl.multiple_of(block_at * rows, rows), rows)
                    normed = (total[at, :] * factor * gain_col[at, :]).astype(bf16)
                    out[to : to + rows, :] = normed.astype(f32)
                    to = to + rows


def product_send_kernel(here_ref, own, first, second, both, chip_layer, plane_layer, both_layer, layer, out, left, right, *, scale):
    core = lax.rem(here_ref[0], CORES)
    rows = left.shape[0]
    block = layer.shape[0]
    mine = pl.ds(pl.multiple_of(core * rows, rows), rows)
    other = pl.ds(pl.multiple_of((1 - core) * rows, rows), rows)
    for k, x in enumerate((layer, chip_layer, plane_layer, both_layer)):
        right[k * block : (k + 1) * block, :] = x[...].astype(bf16)

    def gathered(at):
        one, two = first[at, :], second[at, :]
        parts = (own[at, :], jnp.where(core == 0, one, two), jnp.where(core == 0, two, one), both[at, :])
        return jnp.concatenate([x.astype(bf16) for x in parts], axis=1)

    left[...] = gathered(mine)
    out[...] = (dot(gathered(other), right[...], 1, 0) * scale).reshape(out.shape)


def product_kernel(here_ref, left, right, recv, *refs, scale):
    outs, product = refs[:-1], refs[-1]
    chip = lax.rem(here_ref[0] // FAR_CHIP, 2)
    pair = here_ref[0] // FAR_PLANE
    pairs = product.shape[0] // 2
    product[...] = (dot(left[...], right[...], 1, 0) * scale).reshape(product.shape)
    for out, (chip_away, pairs_away) in zip(outs, [(0, 0)] + sum_order(len(outs))):
        at = (chip ^ chip_away) * pairs + (pair ^ pairs_away)
        out[...] = product[at] + recv[at]


def sum_kernel(*refs):
    total = refs[0][...]
    for x in refs[1:-1]:
        total = total + x[...]
    refs[-1][...] = total


def outputs_kernel(
    here_ref, rates, lens, q_in, k_in, v_in, g_in, mine_f, recv_f, mine_b, recv_b, q_out, k_out, v_out, *scratch
):
    q, k, v, g, q_grad, k_grad, v_grad, sems = scratch
    copies = fetch((q_in, k_in, v_in, g_in), (q, k, v, g), sems)
    here = here_ref[0]
    block, features = q.shape
    half, width, _ = mine_f.shape
    reached, away = causal(here, block, lens)
    for copy in copies:
        copy.wait()
    for row, *pair in half_heads(here, half):
        for head, states, pulls in zip(pair, (mine_f, recv_f), (mine_b, recv_b)):
            lanes = head_lanes(head, width)
            rate = rates[head]
            qh, kh, vh, gh = q[:, lanes], k[:, lanes], v[:, lanes], g[:, lanes]
            decay = jnp.where(reached, jnp.exp(-rate * away), 0.0)
            scores = dot(kh, qh, 1, 1) * decay
            grads = dot(vh, gh, 1, 1) * decay
            into, past = entry_exit(here, rate, block, lens, 0, (block, width))
            before, after = states[row], pulls[row]
            q_grad[:, lanes] = (dot2(grads, kh, 0, 0) + into * dot2(gh, before, 1, 0)).astype(bf16)
            k_grad[:, lanes] = (dot2(grads, qh, 1, 0) + past * dot2(vh, after, 1, 1)).astype(bf16)
            v_grad[:, lanes] = (dot2(scores, gh, 1, 0) + past * dot2(kh, after, 1, 0)).astype(bf16)
    outs = [pltpu.make_async_copy(x, y, sems.at[i]) for i, (x, y) in enumerate(((q_grad, q_out), (k_grad, k_out), (v_grad, v_out)))]
    for copy in outs:
        copy.start()
    for copy in outs:
        copy.wait()


def for_all_dp(outs, here, planes, dps):
    order = jnp.stack([device // NEXT_PLANE % 2 * 2 + device // NEXT_CHIP % 2 for device in in_group(here)])
    whole = jnp.zeros((CHIPS,) + outs[0].shape, f32).at[order].set(jnp.stack(outs))
    whole = whole.reshape(2, 2, CORES, 2, planes // 2, -1, whole.shape[-1]).transpose(4, 0, 3, 1, 2, 5, 6)
    rows = whole.shape[5] // dps
    whole = whole.reshape(dps, planes // 2, 2, 2, 2, CORES, rows, -1).transpose(2, 4, 5, 3, 1, 0, 6, 7)
    whole = whole.reshape((CHIPS,) + outs[0].shape)[order]
    return [whole[d] for d in range(CHIPS)]


def call(kernel, specs, outs, name, scratch=(), flops=0, moved=0, out_specs=None, after=(), **named):
    reads = len(specs)

    def body(*refs):
        kernel(*refs[:reads], *refs[reads + len(after) :], **named)

    def run(*operands):
        operands = [
            pltpu.with_memory_space_constraint(x, pltpu.HBM) if spec is HBM else x for x, spec in zip(operands, specs)
        ]
        return pl.pallas_call(
            body,
            out_shape=[jax.ShapeDtypeStruct(shape, dtype) for shape, dtype in outs],
            in_specs=list(specs) + [pl.BlockSpec(memory_space=pl.ANY)] * len(after),
            out_specs=out_specs or [VMEM] * len(outs),
            scratch_shapes=list(scratch),
            cost_estimate=pl.CostEstimate(flops=flops, bytes_accessed=moved, transcendentals=0),
            compiler_params=pltpu.CompilerParams(vmem_limit_bytes=16 * 1024 * 1024),
            name=name,
        )(*operands, *after)

    return run


def on_device(queries, keys, values, out_grad, layer_grad, norm_gain, decay_rates, doc_lengths):
    seqs, block, features = queries.shape
    assert seqs == 1
    assert lax.axis_size("ctx") % FAR_PLANE == 0
    heads = decay_rates.shape[0]
    width = features // heads
    columns = layer_grad.shape[2]
    half = heads // CORES
    part = half // CHIPS
    count = lax.axis_size("ctx")
    planes = count // PLANE
    dps = lax.axis_size("dp")
    scale = 1.0 / math.sqrt(seqs * block * dps * count)
    here = lax.axis_index("ctx").astype(jnp.int32).reshape(1)
    facts = (here, decay_rates, doc_lengths)
    q, k, v, g = (x.reshape(block, features) for x in (queries, keys, values, out_grad))
    layer = layer_grad.reshape(block, columns)

    def swap(x, bit, near=count):
        pairs = [(i, i ^ bit) for i in range(count) if abs(i // PLANE - (i ^ bit) // PLANE) <= near]
        return lax.ppermute(x, "ctx", pairs)

    def first_of_plane(x):
        return lax.ppermute(x, "ctx", [(i, i ^ (1 + i % CORES) * CORES) for i in range(count)])

    def second_of_plane(x):
        return lax.ppermute(x, "ctx", [(i, i ^ (2 - i % CORES) * CORES) for i in range(count)])

    def in_plane(pieces):
        own, first, second, diagonal = pieces
        return [own, first_of_plane(first), second_of_plane(second), swap(diagonal, 3 * CORES)]

    def in_line(pieces, order, near=count):
        return [swap(x, d * PLANE, near) for x, d in zip(pieces, order)]

    pair = ((half, 2, width, width), f32)
    small = ((part, 2, width, width), f32)
    one = ((part, width, width), f32)
    rows_in = pltpu.VMEM((block, features), bf16)
    half_layer = ((block // 2, columns), f32)
    keep, send, chip_w, layer_wide = call(
        summary_kernel,
        [SMEM] + [HBM] * 7,
        [pair] * 2 + [((half, 4, 128), f32), ((block, columns), f32)],
        "summary",
        scratch=[rows_in] * 4
        + [
            pltpu.VMEM((block, columns), bf16),
            pltpu.SMEM((heads,), f32),
            pltpu.SMEM(doc_lengths.shape, jnp.int32),
            pltpu.SemaphoreType.DMA((7,)),
        ],
        flops=1 << 26,
        moved=1 << 21,
    )(*facts, q, k, v, g, layer)
    recv = swap(send, 1)
    plane_layer = swap(layer_wide, NEXT_PLANE)
    totals = call(
        chip_kernel, [VMEM] * 3, [small] * CHIPS, "chip_total", moved=1 << 20
    )(chip_w, keep, recv)
    attn, gain_col, into_rows, plane_w, line_w, entry_w, state_w = call(
        prepare_kernel,
        [SMEM] * 3 + [VMEM] * 4,
        [
            ((features, block), f32),
            ((features, block), f32),
            ((heads, block), f32),
            ((part, CHIPS, 2, 128), f32),
            ((part, planes - 1, 4, 128), f32),
            ((part, CHIPS, CHIPS + 1, 2, 128), f32),
            ((half, 8, 128), f32),
        ],
        "prepare",
        flops=1 << 28,
        moved=1 << 22,
        after=totals[:1],
        block=block,
    )(*facts, norm_gain.reshape(1, features), q, k, v)
    totals = in_plane(totals)
    narrow = ((block, columns), bf16)
    (plane_layer,) = call(narrow_kernel, [VMEM], [narrow], "plane_layer", flops=1 << 34, moved=1 << 19, after=[attn])(
        plane_layer
    )
    (layer_wide,) = call(
        widen_kernel, [VMEM], [((block, columns), f32)], "widen", moved=1 << 19, after=[attn, totals[1]]
    )(layer_wide)
    chip_layer = swap(layer_wide, NEXT_CHIP)
    near = -(-LONGEST // (PLANE * block))
    onward = call(
        plane_kernel,
        [VMEM] * (2 + CHIPS),
        [one] * (planes - 1),
        "plane_total",
        moved=1 << 19,
        after=[attn, plane_layer],
    )(plane_w, line_w, *totals)
    others = in_line(onward, scan_order(planes), near)
    def entries(way, after=()):
        pieces = call(
            entry_kernel,
            [VMEM] * (2 + CHIPS + len(others)),
            [one] * CHIPS,
            ("entries", "entry_gradients")[way],
            moved=1 << 20,
            after=after,
            lines=len(others),
            way=way,
        )(entry_w, line_w, *totals, *others)
        return in_plane(pieces)

    def states(pieces, way):
        mine, send = call(
            states_kernel,
            [VMEM] * (3 + CHIPS),
            [((half, width, width), f32)] * 2,
            ("states", "state_gradients")[way],
            moved=1 << 20,
            way=way,
        )(state_w, keep, recv, *pieces)
        return mine, swap(send, 1)

    forward = entries(0)
    (layer_wide,) = call(
        widen_kernel, [VMEM], [((block, columns), f32)], "gate", moved=1 << 19, after=others
    )(chip_layer)
    both_layer = swap(layer_wide, NEXT_PLANE)
    (both_layer,) = call(narrow_kernel, [VMEM], [narrow], "both_layer", flops=1 << 28, moved=1 << 19)(both_layer)
    forward = states(forward, 0)

    rows = features // count
    normed = call(
        norm_kernel,
        [SMEM] + [VMEM] * 6,
        [((features // CHIPS, block), f32)] * CHIPS,
        "norm",
        scratch=[pltpu.VMEM((features, block), f32)],
        flops=1 << 26,
        moved=1 << 21,
        after=[both_layer],
        rows=rows,
    )(here, q, attn, gain_col, into_rows, *forward)
    if dps > 1:
        normed = for_all_dp(normed, here[0], planes, dps)
    own, first, second, both = normed
    backward = entries(1, after=[own])
    first = lax.ppermute(first, "ctx", [(i, i ^ (NEXT_PLANE if i % CORES else NEXT_CHIP)) for i in range(count)])
    second = lax.ppermute(second, "ctx", [(i, i ^ (NEXT_CHIP if i % CORES else NEXT_PLANE)) for i in range(count)])
    normed = [own, first, second, swap(both, NEXT_CHIP + NEXT_PLANE)]
    layers = [chip_layer, plane_layer, both_layer]
    backward = states(backward, 1)
    by_plane = ((planes, rows, columns), f32)
    product, left, right = call(
        product_send_kernel,
        [SMEM] + [VMEM] * (CHIPS + len(layers) + 1),
        [by_plane, ((planes * rows, CHIPS * block), bf16), ((CHIPS * block, columns), bf16)],
        "product_send",
        after=[backward[0]],
        flops=1 << 27,
        moved=1 << 22,
        scale=scale,
    )(here, *normed, *layers, layer)
    parts = call(
        product_kernel,
        [SMEM] + [VMEM] * 3,
        [((rows, columns), f32)] * planes,
        "product",
        scratch=[pltpu.VMEM(*by_plane)],
        flops=1 << 27,
        moved=1 << 21,
        scale=scale,
    )(here, left, right, swap(product, 1))
    parts = [parts[0]] + [
        swap(x, chip * FAR_CHIP + pair * FAR_PLANE) for x, (chip, pair) in zip(parts[1:], sum_order(planes))
    ]
    q_grad, k_grad, v_grad = call(
        outputs_kernel,
        [SMEM] * 3 + [HBM] * 4 + [VMEM] * 4,
        [((block, features), bf16)] * 3,
        "outputs",
        scratch=[rows_in] * 7 + [pltpu.SemaphoreType.DMA((4,))],
        out_specs=[HBM] * 3,
        flops=1 << 29,
        moved=1 << 22,
    )(*facts, q, k, v, g, *forward, *backward)
    (proj_grad,) = call(sum_kernel, [VMEM] * planes, [((rows, columns), f32)], "sum", moved=1 << 19)(*parts)
    if dps > 1:
        proj_grad = lax.psum_scatter(proj_grad, "dp", scatter_dimension=0, tiled=True)
    shape_out = (seqs, block, features)
    return (q_grad.reshape(shape_out), k_grad.reshape(shape_out), v_grad.reshape(shape_out), proj_grad)


def solution(mesh):
    rows = P("dp", "ctx", None)
    return jax.shard_map(
        on_device,
        mesh=mesh,
        in_specs=(rows, rows, rows, rows, rows, P(), P(), P("dp", None)),
        out_specs=(rows, rows, rows, P(("dp", "ctx"), None)),
        check_vma=False,
    )
```

```python
import functools
import math

import jax
import jax.numpy as jnp
from jax import lax
from jax.experimental import pallas as pl
from jax.experimental.pallas import tpu as pltpu
from jax.sharding import PartitionSpec as P

norm_eps = 1e-06
f32 = jnp.float32
bf16 = jnp.bfloat16

CORES = 2
CHIPS = 4
PLANE = CORES * CHIPS

SMEM = pl.BlockSpec(memory_space=pltpu.SMEM)
VMEM = pl.BlockSpec(memory_space=pltpu.VMEM)
HBM = pl.BlockSpec(memory_space=pltpu.HBM)
NEXT_CHIP, NEXT_PLANE = CORES, PLANE
FAR_CHIP, FAR_PLANE = 2 * CORES, 2 * PLANE
LONGEST = 2048


def dot(a, b, over_a, over_b):
    return lax.dot_general(a, b, (((over_a,), (over_b,)), ((), ())), preferred_element_type=f32)


def split(x):
    high = x.astype(bf16)
    return high, (x - high.astype(f32)).astype(bf16)


def dot2(a, b, over_a, over_b):
    if a.dtype == f32:
        high, low = split(a)
        return dot(high, b, over_a, over_b) + dot(low, b, over_a, over_b)
    high, low = split(b)
    return dot(a, high, over_a, over_b) + dot(a, low, over_a, over_b)


def doc_of(position, lens):
    bound = lens[0, 0]
    doc = jnp.where(position >= bound, 1, 0)
    for k in range(1, lens.shape[1] - 1):
        bound = bound + lens[0, k]
        doc = doc + jnp.where(position >= bound, 1, 0)
    return doc


def carry(from_edge, to_edge, rate, block, lens):
    same = doc_of(from_edge * block - 1, lens) == doc_of(to_edge * block - 1, lens)
    away = jnp.abs(from_edge - to_edge) * block
    row = jnp.full((1, 128), away.astype(f32) * -rate, f32)
    return jnp.where(same, jnp.exp(row), 0.0)


def entry_exit(here, rate, block, lens, dim, shape):
    offsets = lax.broadcasted_iota(jnp.int32, shape, dim)
    docs = doc_of(here * block + offsets, lens)
    into = jnp.where(docs == doc_of(here * block - 1, lens), jnp.exp(-rate * offsets.astype(f32)), 0.0)
    out = jnp.where(
        docs == doc_of(here * block + block - 1, lens), jnp.exp(-rate * (block - offsets).astype(f32)), 0.0
    )
    return into, out


def head_lanes(head, width):
    return pl.ds(pl.multiple_of(head * width, width), width)


def fetch(refs, spaces, sems):
    copies = [pltpu.make_async_copy(ref, space, sems.at[i]) for i, (ref, space) in enumerate(zip(refs, spaces))]
    for copy in copies:
        copy.start()
    return copies


def in_order(here):
    core = lax.rem(here, CORES)
    chip = lax.rem(here // CORES, CHIPS)
    return [chip, chip ^ (1 + core), chip ^ (2 - core), chip ^ 3]


def in_group(here):
    core = lax.rem(here, CORES)
    first = jnp.where(core == 0, NEXT_CHIP, NEXT_PLANE)
    return [here, here ^ first, here ^ (NEXT_CHIP + NEXT_PLANE - first), here ^ (NEXT_CHIP + NEXT_PLANE)]


def sum_order(planes):
    return [(chip, pair) for pair in reversed(range(1, planes // 2)) for chip in (0, 1)] + [(1, 0)]


def half_heads(here, half):
    core = lax.rem(here, CORES)
    part = half // CHIPS
    both = enumerate(zip(in_order(here), in_order(here ^ 1)))
    return [
        (i * part + t, core * half + own * part + t, (1 - core) * half + other * part + t)
        for i, (own, other) in both
        for t in range(part)
    ]


def summary_kernel(
    here_ref, rates_in, lens_in, q_in, k_in, v_in, g_in, layer_in, keep, send, chip_w, layer_wide, *scratch
):
    q, k, v, g, layer, rates, lens, sems = scratch
    copies = fetch((rates_in, lens_in, k_in, v_in, q_in, g_in, layer_in), (rates, lens, k, v, q, g, layer), sems)
    here = here_ref[0]
    block = q.shape[0]
    half, _, width, _ = keep.shape
    heads = half_heads(here, half)
    first = lax.rem(here, CORES) == 0
    edge = here - lax.rem(here, CORES)
    for copy in copies[:2]:
        copy.wait()
    for row, head, _ in heads:
        late = carry(edge + 1, edge + 2, rates[head], block, lens)
        early = carry(edge + 1, edge, rates[head], block, lens)
        chip_w[row, 0:1, :] = jnp.where(first, late, 1.0)
        chip_w[row, 1:2, :] = jnp.where(first, 1.0, late)
        chip_w[row, 2:3, :] = jnp.where(first, 1.0, early)
        chip_w[row, 3:4, :] = jnp.where(first, early, 1.0)
    offsets = lax.broadcasted_iota(jnp.int32, (block, width), 0)
    docs = doc_of(here * block + offsets, lens)
    enters = docs == doc_of(here * block - 1, lens)
    leaves = docs == doc_of(here * block + block - 1, lens)
    from_start, to_end = offsets.astype(f32), (block - offsets).astype(f32)
    for copy in copies[2:4]:
        copy.wait()
    for row, *pair in heads:
        for head, out in zip(pair, (keep, send)):
            past = jnp.where(leaves, jnp.exp(-rates[head] * to_end), 0.0)
            lanes = head_lanes(head, width)
            out[row, 0] = dot2(v[:, lanes], k[:, lanes].astype(f32) * past, 0, 0)
    for copy in copies[4:]:
        copy.wait()
    for row, *pair in heads:
        for head, out in zip(pair, (keep, send)):
            into = jnp.where(enters, jnp.exp(-rates[head] * from_start), 0.0)
            lanes = head_lanes(head, width)
            out[row, 1] = dot2(q[:, lanes].astype(f32) * into, g[:, lanes], 0, 0)
    layer_wide[...] = layer[...].astype(f32)


def chip_kernel(weights, keep, recv, *outs):
    for i, out in enumerate(outs):
        for t in range(out.shape[0]):
            row = i * out.shape[0] + t
            for k in range(2):
                own, other = weights[row, 2 * k : 2 * k + 1, :], weights[row, 2 * k + 1 : 2 * k + 2, :]
                out[t, k] = own * keep[row, k] + other * recv[row, k]


def line_order(planes):
    return list(range(planes - 1, 0, -1))


def scan_order(planes):
    return [d for d in line_order(planes) if d == 2] + [d for d in range(1, planes) if d != 2]


def weights_kernel(here_ref, rates, lens, plane_w, line_w, entry_w, state_w, *, block):
    here = here_ref[0]
    half = state_w.shape[0]
    part, lines = line_w.shape[:2]
    core = lax.rem(here, CORES)
    chips = in_order(here)
    plane = here // PLANE
    base = plane * PLANE
    ones = jnp.ones((1, 128), f32)
    for t in range(part):
        rate = rates[core * half + chips[0] * part + t]

        def take(from_edge, to_edge):
            return carry(from_edge, to_edge, rate, block, lens)

        for j, d in enumerate(scan_order(lines + 1)):
            to = plane ^ d
            line_w[t, j, 0:1, :] = jnp.where(to > plane, take(base + PLANE, to * PLANE), 0.0)
            line_w[t, j, 1:2, :] = jnp.where(to < plane, take(base, (to + 1) * PLANE), 0.0)
            line_w[t, j, 2:3, :] = jnp.where(to < plane, ones, 0.0)
            line_w[t, j, 3:4, :] = jnp.where(to > plane, ones, 0.0)
        for i, at in enumerate(chips):
            edge = base + at * CORES
            plane_w[t, i, 0:1, :] = take(edge + CORES, base + PLANE)
            plane_w[t, i, 1:2, :] = take(edge, base)
            entry_w[t, i, CHIPS, 0:1, :] = take(base, edge)
            entry_w[t, i, CHIPS, 1:2, :] = take(base + PLANE, edge + CORES)
            for j, at_other in enumerate(chips):
                other = base + at_other * CORES
                entry_w[t, i, j, 0:1, :] = jnp.where(other < edge, take(other + CORES, edge), 0.0)
                entry_w[t, i, j, 1:2, :] = jnp.where(other > edge, take(other, edge + CORES), 0.0)
    edge = here - core
    first = core == 0
    for row, head, _ in half_heads(here, half):
        fwd = carry(edge, edge + 1, rates[head], block, lens)
        bwd = carry(edge + 2, edge + 1, rates[head], block, lens)
        rows = ((0.0, 1.0), (1.0, fwd), (1.0, bwd), (0.0, 1.0))
        for k, (core0, core1) in enumerate(((0, 1), (1, 0), (2, 3), (3, 2))):
            for m in range(2):
                state_w[row, 2 * k + m : 2 * k + m + 1, :] = jnp.where(
                    first, ones * rows[core0][m], ones * rows[core1][m]
                )


def plane_kernel(weights, line_w, *refs):
    totals, outs = refs[:CHIPS], refs[CHIPS:]
    for t in range(outs[0].shape[0]):
        fwd, bwd = 0.0, 0.0
        for i, total in enumerate(totals):
            fwd = fwd + weights[t, i, 0:1, :] * total[t, 0]
            bwd = bwd + weights[t, i, 1:2, :] * total[t, 1]
        for j, out in enumerate(outs):
            out[t] = line_w[t, j, 0:1, :] * fwd + line_w[t, j, 1:2, :] * bwd


def widen_kernel(layer, out):
    out[...] = layer[...].astype(f32)


def halves_kernel(layer, top, bottom):
    top[...] = layer[: top.shape[0], :]
    bottom[...] = layer[top.shape[0] :, :]


def narrow_kernel(layer, out):
    out[...] = layer[...].astype(bf16)


def entry_kernel(weights, line_w, *refs, lines):
    totals, others, outs = refs[:CHIPS], refs[CHIPS : CHIPS + lines], refs[CHIPS + lines :]
    for t in range(outs[0].shape[0]):
        before, after = 0.0, 0.0
        for j, other in enumerate(others):
            before = before + line_w[t, j, 2:3, :] * other[t]
            after = after + line_w[t, j, 3:4, :] * other[t]
        for i, out in enumerate(outs):
            fwd = weights[t, i, CHIPS, 0:1, :] * before
            bwd = weights[t, i, CHIPS, 1:2, :] * after
            for j, total in enumerate(totals):
                if i != j:
                    fwd = fwd + weights[t, i, j, 0:1, :] * total[t, 0]
                    bwd = bwd + weights[t, i, j, 1:2, :] * total[t, 1]
            out[t, 0], out[t, 1] = fwd, bwd


def states_kernel(weights, keep, recv, *refs):
    entries, (mine, send) = refs[:CHIPS], refs[CHIPS:]
    part = entries[0].shape[0]
    for i, entry in enumerate(entries):
        for t in range(part):
            row = i * part + t
            for k in range(2):
                for m, (own, out) in enumerate(((recv, mine), (keep, send))):
                    at = 4 * k + 2 * m
                    out[row, k] = weights[row, at : at + 1, :] * own[row, k] + weights[row, at + 1 : at + 2, :] * entry[t, k]


def causal(here, block, lens):
    at_j = lax.broadcasted_iota(jnp.int32, (block, block), 0)
    at_i = lax.broadcasted_iota(jnp.int32, (block, block), 1)
    docs_j = doc_of(here * block + at_j, lens)
    docs_i = doc_of(here * block + at_i, lens)
    return (docs_i == docs_j) & (at_i >= at_j), jnp.maximum(at_i - at_j, 0).astype(f32)


def within_kernel(here_ref, rates, lens, gain, q, k, v, attn, gain_col, into_rows):
    here = here_ref[0]
    block, features = q.shape
    heads = rates.shape[0]
    width = features // heads
    reached, away = causal(here, block, lens)
    for head in range(heads):
        lanes = slice(head * width, (head + 1) * width)
        gain_col[lanes, :] = jnp.broadcast_to(gain[:, lanes], (block, width)).T
        decay = jnp.where(reached, jnp.exp(-rates[head] * away), 0.0)
        scores = dot(k[:, lanes], q[:, lanes], 1, 1) * decay
        attn[lanes, :] = dot2(v[:, lanes], scores, 0, 0)
        into_rows[head : head + 1, :], _ = entry_exit(here, rates[head], block, lens, 1, (1, block))


def prepare_kernel(here_ref, rates, lens, gain, q, k, v, *outs, block):
    within_kernel(here_ref, rates, lens, gain, q, k, v, *outs[:3])
    weights_kernel(here_ref, rates, lens, *outs[3:], block=block)


def norm_kernel(here_ref, q, attn, gain_col, into_rows, mine, recv, *refs, rows):
    outs, total = refs[:CHIPS], refs[CHIPS]
    here = here_ref[0]
    block, features = q.shape
    half, _, width, _ = mine.shape
    squares = jnp.zeros((width, block), f32)
    for row, *pair in half_heads(here, half):
        for head, states in zip(pair, (mine, recv)):
            lanes = head_lanes(head, width)
            at = attn[lanes, :] + into_rows[pl.ds(head, 1), :] * dot2(states[row, 0], q[:, lanes], 1, 1)
            total[lanes, :] = at
            squares = squares + at * at
    mean = jnp.sum(squares, axis=0, keepdims=True) * (1.0 / features)
    factor = lax.rsqrt(mean + norm_eps)
    planes = features // (PLANE * rows)
    for out, device in zip(outs, in_group(here)):
        corner = (lax.rem(device // NEXT_PLANE, 2) * NEXT_PLANE) + lax.rem(device // NEXT_CHIP, 2) * NEXT_CHIP
        to = 0
        for core in range(CORES):
            for chip in range(2):
                for pair in range(planes // 2):
                    block_at = corner + core + chip * FAR_CHIP + pair * FAR_PLANE
                    at = pl.ds(pl.multiple_of(block_at * rows, rows), rows)
                    normed = (total[at, :] * factor * gain_col[at, :]).astype(bf16)
                    out[to : to + rows, :] = normed.astype(f32)
                    to = to + rows


def product_send_kernel(here_ref, own, first, second, both, *refs, scale):
    layers, (layer, out, left, right) = refs[:-4], refs[-4:]
    core = lax.rem(here_ref[0], CORES)
    rows = left.shape[0]
    block = layer.shape[0]
    mine = pl.ds(pl.multiple_of(core * rows, rows), rows)
    other = pl.ds(pl.multiple_of((1 - core) * rows, rows), rows)
    to = 0
    for x in (layer, *layers):
        right[to : to + x.shape[0], :] = x[...].astype(bf16)
        to = to + x.shape[0]

    def gathered(at):
        one, two = first[at, :], second[at, :]
        parts = (own[at, :], jnp.where(core == 0, one, two), jnp.where(core == 0, two, one), both[at, :])
        return jnp.concatenate([x.astype(bf16) for x in parts], axis=1)

    left[...] = gathered(mine)
    out[...] = (dot(gathered(other), right[...], 1, 0) * scale).reshape(out.shape)


def product_kernel(here_ref, left, right, recv, *refs, scale):
    outs, product = refs[:-1], refs[-1]
    chip = lax.rem(here_ref[0] // FAR_CHIP, 2)
    pair = here_ref[0] // FAR_PLANE
    pairs = product.shape[0] // 2
    product[...] = (dot(left[...], right[...], 1, 0) * scale).reshape(product.shape)
    for out, (chip_away, pairs_away) in zip(outs, [(0, 0)] + sum_order(len(outs))):
        at = (chip ^ chip_away) * pairs + (pair ^ pairs_away)
        out[...] = product[at] + recv[at]


def sum_kernel(*refs):
    total = refs[0][...]
    for x in refs[1:-1]:
        total = total + x[...]
    refs[-1][...] = total


def outputs_kernel(here_ref, rates, lens, q_in, k_in, v_in, g_in, mine, recv, q_out, k_out, v_out, *scratch):
    q, k, v, g, q_grad, k_grad, v_grad, sems = scratch
    copies = fetch((q_in, k_in, v_in, g_in), (q, k, v, g), sems)
    here = here_ref[0]
    block, features = q.shape
    half, _, width, _ = mine.shape
    reached, away = causal(here, block, lens)
    for copy in copies:
        copy.wait()
    for row, *pair in half_heads(here, half):
        for head, states in zip(pair, (mine, recv)):
            lanes = head_lanes(head, width)
            rate = rates[head]
            qh, kh, vh, gh = q[:, lanes], k[:, lanes], v[:, lanes], g[:, lanes]
            decay = jnp.where(reached, jnp.exp(-rate * away), 0.0)
            scores = dot(kh, qh, 1, 1) * decay
            grads = dot(vh, gh, 1, 1) * decay
            into, past = entry_exit(here, rate, block, lens, 0, (block, width))
            before, after = states[row, 0], states[row, 1]
            q_grad[:, lanes] = (dot2(grads, kh, 0, 0) + into * dot2(gh, before, 1, 0)).astype(bf16)
            k_grad[:, lanes] = (dot2(grads, qh, 1, 0) + past * dot2(vh, after, 1, 1)).astype(bf16)
            v_grad[:, lanes] = (dot2(scores, gh, 1, 0) + past * dot2(kh, after, 1, 0)).astype(bf16)
    outs = [pltpu.make_async_copy(x, y, sems.at[i]) for i, (x, y) in enumerate(((q_grad, q_out), (k_grad, k_out), (v_grad, v_out)))]
    for copy in outs:
        copy.start()
    for copy in outs:
        copy.wait()


def for_all_dp(outs, here, planes, dps):
    order = jnp.stack([device // NEXT_PLANE % 2 * 2 + device // NEXT_CHIP % 2 for device in in_group(here)])
    whole = jnp.zeros((CHIPS,) + outs[0].shape, f32).at[order].set(jnp.stack(outs))
    whole = whole.reshape(2, 2, CORES, 2, planes // 2, -1, whole.shape[-1]).transpose(4, 0, 3, 1, 2, 5, 6)
    rows = whole.shape[5] // dps
    whole = whole.reshape(dps, planes // 2, 2, 2, 2, CORES, rows, -1).transpose(2, 4, 5, 3, 1, 0, 6, 7)
    whole = whole.reshape((CHIPS,) + outs[0].shape)[order]
    return [whole[d] for d in range(CHIPS)]


def call(kernel, specs, outs, name, scratch=(), flops=0, moved=0, out_specs=None, after=(), **named):
    reads = len(specs)

    def body(*refs):
        kernel(*refs[:reads], *refs[reads + len(after) :], **named)

    def run(*operands):
        operands = [
            pltpu.with_memory_space_constraint(x, pltpu.HBM) if spec is HBM else x for x, spec in zip(operands, specs)
        ]
        return pl.pallas_call(
            body,
            out_shape=[jax.ShapeDtypeStruct(shape, dtype) for shape, dtype in outs],
            in_specs=list(specs) + [pl.BlockSpec(memory_space=pl.ANY)] * len(after),
            out_specs=out_specs or [VMEM] * len(outs),
            scratch_shapes=list(scratch),
            cost_estimate=pl.CostEstimate(flops=flops, bytes_accessed=moved, transcendentals=0),
            compiler_params=pltpu.CompilerParams(vmem_limit_bytes=16 * 1024 * 1024),
            name=name,
        )(*operands, *after)

    return run


def on_device(queries, keys, values, out_grad, layer_grad, norm_gain, decay_rates, doc_lengths):
    seqs, block, features = queries.shape
    assert seqs == 1
    assert lax.axis_size("ctx") % FAR_PLANE == 0
    heads = decay_rates.shape[0]
    width = features // heads
    columns = layer_grad.shape[2]
    half = heads // CORES
    part = half // CHIPS
    count = lax.axis_size("ctx")
    planes = count // PLANE
    dps = lax.axis_size("dp")
    scale = 1.0 / math.sqrt(seqs * block * dps * count)
    here = lax.axis_index("ctx").astype(jnp.int32).reshape(1)
    facts = (here, decay_rates, doc_lengths)
    q, k, v, g = (x.reshape(block, features) for x in (queries, keys, values, out_grad))
    layer = layer_grad.reshape(block, columns)

    def swap(x, bit, near=count):
        pairs = [(i, i ^ bit) for i in range(count) if abs(i // PLANE - (i ^ bit) // PLANE) <= near]
        return lax.ppermute(x, "ctx", pairs)

    def first_of_plane(x):
        return lax.ppermute(x, "ctx", [(i, i ^ (1 + i % CORES) * CORES) for i in range(count)])

    def second_of_plane(x):
        return lax.ppermute(x, "ctx", [(i, i ^ (2 - i % CORES) * CORES) for i in range(count)])

    def in_plane(pieces):
        own, first, second, diagonal = pieces
        return [own, first_of_plane(first), second_of_plane(second), swap(diagonal, 3 * CORES)]

    def in_line(pieces, order, near=count):
        return [swap(x, d * PLANE, near) for x, d in zip(pieces, order)]

    pair = ((half, 2, width, width), f32)
    small = ((part, 2, width, width), f32)
    one = ((part, width, width), f32)
    rows_in = pltpu.VMEM((block, features), bf16)
    half_layer = ((block // 2, columns), f32)
    keep, send, chip_w, layer_wide = call(
        summary_kernel,
        [SMEM] + [HBM] * 7,
        [pair] * 2 + [((half, 4, 128), f32), ((block, columns), f32)],
        "summary",
        scratch=[rows_in] * 4
        + [
            pltpu.VMEM((block, columns), bf16),
            pltpu.SMEM((heads,), f32),
            pltpu.SMEM(doc_lengths.shape, jnp.int32),
            pltpu.SemaphoreType.DMA((7,)),
        ],
        flops=1 << 26,
        moved=1 << 21,
    )(*facts, q, k, v, g, layer)
    recv = swap(send, 1)
    plane_layer = swap(layer_wide, NEXT_PLANE)
    totals = call(
        chip_kernel, [VMEM] * 3, [small] * CHIPS, "chip_total", moved=1 << 20
    )(chip_w, keep, recv)
    attn, gain_col, into_rows, plane_w, line_w, entry_w, state_w = call(
        prepare_kernel,
        [SMEM] * 3 + [VMEM] * 4,
        [
            ((features, block), f32),
            ((features, block), f32),
            ((heads, block), f32),
            ((part, CHIPS, 2, 128), f32),
            ((part, planes - 1, 4, 128), f32),
            ((part, CHIPS, CHIPS + 1, 2, 128), f32),
            ((half, 8, 128), f32),
        ],
        "prepare",
        flops=1 << 28,
        moved=1 << 22,
        after=totals[:1],
        block=block,
    )(*facts, norm_gain.reshape(1, features), q, k, v)
    totals = in_plane(totals)
    narrow = ((block, columns), bf16)
    (plane_layer,) = call(narrow_kernel, [VMEM], [narrow], "plane_layer", flops=1 << 34, moved=1 << 19, after=[attn])(
        plane_layer
    )
    (layer_wide,) = call(
        widen_kernel, [VMEM], [((block, columns), f32)], "widen", moved=1 << 19, after=[attn, totals[1]]
    )(layer_wide)
    chip_layer = swap(layer_wide, NEXT_CHIP)
    near = -(-LONGEST // (PLANE * block))
    onward = call(
        plane_kernel,
        [VMEM] * (2 + CHIPS),
        [one] * (planes - 1),
        "plane_total",
        moved=1 << 19,
        after=[attn, plane_layer],
    )(plane_w, line_w, *totals)
    others = in_line(onward, scan_order(planes), near)
    entries = call(
        entry_kernel,
        [VMEM] * (2 + CHIPS + len(others)),
        [small] * CHIPS,
        "entries",
        moved=1 << 20,
        lines=len(others),
    )(entry_w, line_w, *totals, *others)
    entries = in_plane(entries)
    half_layer = ((block // 2, columns), f32)
    top, bottom = call(halves_kernel, [VMEM], [half_layer] * 2, "halves", moved=1 << 19)(chip_layer)
    both_top, both_bottom = swap(top, NEXT_PLANE), swap(bottom, NEXT_PLANE)
    (both_top,) = call(
        narrow_kernel, [VMEM], [((block // 2, columns), bf16)], "both_top", flops=1 << 32, moved=1 << 18
    )(both_top)
    mine, send = call(
        states_kernel, [VMEM] * (3 + CHIPS), [pair] * 2, "states", moved=1 << 21
    )(state_w, keep, recv, *entries)
    theirs = swap(send, 1)

    rows = features // count
    normed = call(
        norm_kernel,
        [SMEM] + [VMEM] * 6,
        [((features // CHIPS, block), f32)] * CHIPS,
        "norm",
        scratch=[pltpu.VMEM((features, block), f32)],
        flops=1 << 26,
        moved=1 << 21,
        after=[both_top],
        rows=rows,
    )(here, q, attn, gain_col, into_rows, mine, theirs)
    if dps > 1:
        normed = for_all_dp(normed, here[0], planes, dps)
    own, first, second, both = normed
    first = lax.ppermute(first, "ctx", [(i, i ^ (NEXT_PLANE if i % CORES else NEXT_CHIP)) for i in range(count)])
    second = lax.ppermute(second, "ctx", [(i, i ^ (NEXT_CHIP if i % CORES else NEXT_PLANE)) for i in range(count)])
    normed = [own, first, second, swap(both, NEXT_CHIP + NEXT_PLANE)]
    layers = [chip_layer, plane_layer, both_top, both_bottom]
    by_plane = ((planes, rows, columns), f32)
    product, left, right = call(
        product_send_kernel,
        [SMEM] + [VMEM] * (CHIPS + len(layers) + 1),
        [by_plane, ((planes * rows, CHIPS * block), bf16), ((CHIPS * block, columns), bf16)],
        "product_send",
        flops=1 << 27,
        moved=1 << 22,
        scale=scale,
    )(here, *normed, *layers, layer)
    parts = call(
        product_kernel,
        [SMEM] + [VMEM] * 3,
        [((rows, columns), f32)] * planes,
        "product",
        scratch=[pltpu.VMEM(*by_plane)],
        flops=1 << 27,
        moved=1 << 21,
        scale=scale,
    )(here, left, right, swap(product, 1))
    parts = [parts[0]] + [
        swap(x, chip * FAR_CHIP + pair * FAR_PLANE) for x, (chip, pair) in zip(parts[1:], sum_order(planes))
    ]
    q_grad, k_grad, v_grad = call(
        outputs_kernel,
        [SMEM] * 3 + [HBM] * 4 + [VMEM] * 2,
        [((block, features), bf16)] * 3,
        "outputs",
        scratch=[rows_in] * 7 + [pltpu.SemaphoreType.DMA((4,))],
        out_specs=[HBM] * 3,
        flops=1 << 29,
        moved=1 << 22,
    )(*facts, q, k, v, g, mine, theirs)
    (proj_grad,) = call(sum_kernel, [VMEM] * planes, [((rows, columns), f32)], "sum", moved=1 << 19)(*parts)
    if dps > 1:
        proj_grad = lax.psum_scatter(proj_grad, "dp", scatter_dimension=0, tiled=True)
    shape_out = (seqs, block, features)
    return (q_grad.reshape(shape_out), k_grad.reshape(shape_out), v_grad.reshape(shape_out), proj_grad)


def solution(mesh):
    rows = P("dp", "ctx", None)
    return jax.shard_map(
        on_device,
        mesh=mesh,
        in_specs=(rows, rows, rows, rows, rows, P(), P(), P("dp", None)),
        out_specs=(rows, rows, rows, P(("dp", "ctx"), None)),
        check_vma=False,
    )
```

```python
import functools
import math

import jax
import jax.numpy as jnp
from jax import lax
from jax.experimental import pallas as pl
from jax.experimental.pallas import tpu as pltpu
from jax.sharding import PartitionSpec as P

norm_eps = 1e-06
f32 = jnp.float32
bf16 = jnp.bfloat16

CORES = 2
CHIPS = 4
PLANE = CORES * CHIPS

SMEM = pl.BlockSpec(memory_space=pltpu.SMEM)
VMEM = pl.BlockSpec(memory_space=pltpu.VMEM)
HBM = pl.BlockSpec(memory_space=pltpu.HBM)
LONGEST = 2048


def dot(a, b, over_a, over_b):
    return lax.dot_general(a, b, (((over_a,), (over_b,)), ((), ())), preferred_element_type=f32)


def split(x):
    high = x.astype(bf16)
    return high, (x - high.astype(f32)).astype(bf16)


def dot2(a, b, over_a, over_b):
    if a.dtype == f32:
        high, low = split(a)
        return dot(high, b, over_a, over_b) + dot(low, b, over_a, over_b)
    high, low = split(b)
    return dot(a, high, over_a, over_b) + dot(a, low, over_a, over_b)


def doc_of(position, lens):
    bound = lens[0, 0]
    doc = jnp.where(position >= bound, 1, 0)
    for k in range(1, lens.shape[1] - 1):
        bound = bound + lens[0, k]
        doc = doc + jnp.where(position >= bound, 1, 0)
    return doc


def carry(from_edge, to_edge, rate, block, lens):
    same = doc_of(from_edge * block - 1, lens) == doc_of(to_edge * block - 1, lens)
    away = jnp.abs(from_edge - to_edge) * block
    row = jnp.full((1, 128), away.astype(f32) * -rate, f32)
    return jnp.where(same, jnp.exp(row), 0.0)


def entry_exit(here, rate, block, lens, dim, shape):
    offsets = lax.broadcasted_iota(jnp.int32, shape, dim)
    docs = doc_of(here * block + offsets, lens)
    into = jnp.where(docs == doc_of(here * block - 1, lens), jnp.exp(-rate * offsets.astype(f32)), 0.0)
    out = jnp.where(
        docs == doc_of(here * block + block - 1, lens), jnp.exp(-rate * (block - offsets).astype(f32)), 0.0
    )
    return into, out


def head_lanes(head, width):
    return pl.ds(pl.multiple_of(head * width, width), width)


def fetch(refs, spaces, sems):
    copies = [pltpu.make_async_copy(ref, space, sems.at[i]) for i, (ref, space) in enumerate(zip(refs, spaces))]
    for copy in copies:
        copy.start()
    return copies


def in_order(here):
    core = lax.rem(here, CORES)
    chip = lax.rem(here // CORES, CHIPS)
    return [chip, chip ^ (1 + core), chip ^ (2 - core), chip ^ 3]


def half_heads(here, half):
    core = lax.rem(here, CORES)
    part = half // CHIPS
    both = enumerate(zip(in_order(here), in_order(here ^ 1)))
    return [
        (i * part + t, core * half + own * part + t, (1 - core) * half + other * part + t)
        for i, (own, other) in both
        for t in range(part)
    ]


def summary_kernel(
    here_ref, rates_in, lens_in, q_in, k_in, v_in, g_in, keep, send, chip_w, q, k, v, g, rates, lens, sems
):
    copies = fetch((rates_in, lens_in, k_in, v_in, q_in, g_in), (rates, lens, k, v, q, g), sems)
    here = here_ref[0]
    block = q.shape[0]
    half, _, width, _ = keep.shape
    heads = half_heads(here, half)
    first = lax.rem(here, CORES) == 0
    edge = here - lax.rem(here, CORES)
    for copy in copies[:2]:
        copy.wait()
    for row, head, _ in heads:
        late = carry(edge + 1, edge + 2, rates[head], block, lens)
        early = carry(edge + 1, edge, rates[head], block, lens)
        chip_w[row, 0:1, :] = jnp.where(first, late, 1.0)
        chip_w[row, 1:2, :] = jnp.where(first, 1.0, late)
        chip_w[row, 2:3, :] = jnp.where(first, 1.0, early)
        chip_w[row, 3:4, :] = jnp.where(first, early, 1.0)
    offsets = lax.broadcasted_iota(jnp.int32, (block, width), 0)
    docs = doc_of(here * block + offsets, lens)
    enters = docs == doc_of(here * block - 1, lens)
    leaves = docs == doc_of(here * block + block - 1, lens)
    from_start, to_end = offsets.astype(f32), (block - offsets).astype(f32)
    for copy in copies[2:4]:
        copy.wait()
    for row, *pair in heads:
        for head, out in zip(pair, (keep, send)):
            past = jnp.where(leaves, jnp.exp(-rates[head] * to_end), 0.0)
            lanes = head_lanes(head, width)
            out[row, 0] = dot2(v[:, lanes], k[:, lanes].astype(f32) * past, 0, 0)
    for copy in copies[4:]:
        copy.wait()
    for row, *pair in heads:
        for head, out in zip(pair, (keep, send)):
            into = jnp.where(enters, jnp.exp(-rates[head] * from_start), 0.0)
            lanes = head_lanes(head, width)
            out[row, 1] = dot2(q[:, lanes].astype(f32) * into, g[:, lanes], 0, 0)


def chip_kernel(weights, keep, recv, *outs):
    for i, out in enumerate(outs):
        for t in range(out.shape[0]):
            row = i * out.shape[0] + t
            for k in range(2):
                own, other = weights[row, 2 * k : 2 * k + 1, :], weights[row, 2 * k + 1 : 2 * k + 2, :]
                out[t, k] = own * keep[row, k] + other * recv[row, k]


def line_order(planes):
    return list(range(planes - 1, 0, -1))


def scan_order(planes):
    return [d for d in line_order(planes) if d == 2] + [d for d in range(1, planes) if d != 2]


def weights_kernel(here_ref, rates, lens, plane_w, line_w, entry_w, state_w, *, block):
    here = here_ref[0]
    half = state_w.shape[0]
    part, lines = line_w.shape[:2]
    core = lax.rem(here, CORES)
    chips = in_order(here)
    plane = here // PLANE
    base = plane * PLANE
    ones = jnp.ones((1, 128), f32)
    for t in range(part):
        rate = rates[core * half + chips[0] * part + t]

        def take(from_edge, to_edge):
            return carry(from_edge, to_edge, rate, block, lens)

        for j, d in enumerate(scan_order(lines + 1)):
            to = plane ^ d
            line_w[t, j, 0:1, :] = jnp.where(to > plane, take(base + PLANE, to * PLANE), 0.0)
            line_w[t, j, 1:2, :] = jnp.where(to < plane, take(base, (to + 1) * PLANE), 0.0)
            line_w[t, j, 2:3, :] = jnp.where(to < plane, ones, 0.0)
            line_w[t, j, 3:4, :] = jnp.where(to > plane, ones, 0.0)
        for i, at in enumerate(chips):
            edge = base + at * CORES
            plane_w[t, i, 0:1, :] = take(edge + CORES, base + PLANE)
            plane_w[t, i, 1:2, :] = take(edge, base)
            entry_w[t, i, CHIPS, 0:1, :] = take(base, edge)
            entry_w[t, i, CHIPS, 1:2, :] = take(base + PLANE, edge + CORES)
            for j, at_other in enumerate(chips):
                other = base + at_other * CORES
                entry_w[t, i, j, 0:1, :] = jnp.where(other < edge, take(other + CORES, edge), 0.0)
                entry_w[t, i, j, 1:2, :] = jnp.where(other > edge, take(other, edge + CORES), 0.0)
    edge = here - core
    first = core == 0
    for row, head, _ in half_heads(here, half):
        fwd = carry(edge, edge + 1, rates[head], block, lens)
        bwd = carry(edge + 2, edge + 1, rates[head], block, lens)
        rows = ((0.0, 1.0), (1.0, fwd), (1.0, bwd), (0.0, 1.0))
        for k, (core0, core1) in enumerate(((0, 1), (1, 0), (2, 3), (3, 2))):
            for m in range(2):
                state_w[row, 2 * k + m : 2 * k + m + 1, :] = jnp.where(
                    first, ones * rows[core0][m], ones * rows[core1][m]
                )


def plane_kernel(weights, line_w, *refs):
    totals, outs = refs[:CHIPS], refs[CHIPS:]
    for t in range(outs[0].shape[0]):
        fwd, bwd = 0.0, 0.0
        for i, total in enumerate(totals):
            fwd = fwd + weights[t, i, 0:1, :] * total[t, 0]
            bwd = bwd + weights[t, i, 1:2, :] * total[t, 1]
        for j, out in enumerate(outs):
            out[t] = line_w[t, j, 0:1, :] * fwd + line_w[t, j, 1:2, :] * bwd


def narrow_kernel(layer, out):
    out[...] = layer[...].astype(bf16)


def widen_kernel(layer, out):
    out[...] = layer[...].astype(f32)


def forward_kernel(layer_first, layer_second, top, bottom):
    top[...] = layer_first[: top.shape[0], :]
    bottom[...] = layer_second[top.shape[0] :, :]


def entry_kernel(weights, line_w, *refs, lines):
    totals, others, outs = refs[:CHIPS], refs[CHIPS : CHIPS + lines], refs[CHIPS + lines :]
    for t in range(outs[0].shape[0]):
        before, after = 0.0, 0.0
        for j, other in enumerate(others):
            before = before + line_w[t, j, 2:3, :] * other[t]
            after = after + line_w[t, j, 3:4, :] * other[t]
        for i, out in enumerate(outs):
            fwd = weights[t, i, CHIPS, 0:1, :] * before
            bwd = weights[t, i, CHIPS, 1:2, :] * after
            for j, total in enumerate(totals):
                if i != j:
                    fwd = fwd + weights[t, i, j, 0:1, :] * total[t, 0]
                    bwd = bwd + weights[t, i, j, 1:2, :] * total[t, 1]
            out[t, 0], out[t, 1] = fwd, bwd


def states_kernel(weights, keep, recv, *refs):
    entries, (mine, send) = refs[:CHIPS], refs[CHIPS:]
    part = entries[0].shape[0]
    for i, entry in enumerate(entries):
        for t in range(part):
            row = i * part + t
            for k in range(2):
                for m, (own, out) in enumerate(((recv, mine), (keep, send))):
                    at = 4 * k + 2 * m
                    out[row, k] = weights[row, at : at + 1, :] * own[row, k] + weights[row, at + 1 : at + 2, :] * entry[t, k]


def causal(here, block, lens):
    at_j = lax.broadcasted_iota(jnp.int32, (block, block), 0)
    at_i = lax.broadcasted_iota(jnp.int32, (block, block), 1)
    docs_j = doc_of(here * block + at_j, lens)
    docs_i = doc_of(here * block + at_i, lens)
    return (docs_i == docs_j) & (at_i >= at_j), jnp.maximum(at_i - at_j, 0).astype(f32)


def within_kernel(here_ref, rates, lens, gain, q, k, v, attn, gain_col, into_rows):
    here = here_ref[0]
    block, features = q.shape
    heads = rates.shape[0]
    width = features // heads
    reached, away = causal(here, block, lens)
    for head in range(heads):
        lanes = slice(head * width, (head + 1) * width)
        gain_col[lanes, :] = jnp.broadcast_to(gain[:, lanes], (block, width)).T
        decay = jnp.where(reached, jnp.exp(-rates[head] * away), 0.0)
        scores = dot(k[:, lanes], q[:, lanes], 1, 1) * decay
        attn[lanes, :] = dot2(v[:, lanes], scores, 0, 0)
        into_rows[head : head + 1, :], _ = entry_exit(here, rates[head], block, lens, 1, (1, block))


def norm_kernel(here_ref, q, attn, gain_col, into_rows, mine, recv, *refs, rows):
    outs, total = refs[:CHIPS], refs[CHIPS]
    here = here_ref[0]
    block, features = q.shape
    half, _, width, _ = mine.shape
    squares = jnp.zeros((width, block), f32)
    for row, *pair in half_heads(here, half):
        for head, states in zip(pair, (mine, recv)):
            lanes = head_lanes(head, width)
            at = attn[lanes, :] + into_rows[pl.ds(head, 1), :] * dot2(states[row, 0], q[:, lanes], 1, 1)
            total[lanes, :] = at
            squares = squares + at * at
    mean = jnp.sum(squares, axis=0, keepdims=True) * (1.0 / features)
    factor = lax.rsqrt(mean + norm_eps)
    planes = features // (PLANE * rows)
    for out, chip in zip(outs, in_order(here)):
        for to_core in range(CORES):
            for plane in range(planes):
                block_at = plane * PLANE + chip * CORES + to_core
                at = pl.ds(pl.multiple_of(block_at * rows, rows), rows)
                normed = (total[at, :] * factor * gain_col[at, :]).astype(bf16)
                to = to_core * planes + plane
                out[to * rows : (to + 1) * rows, :] = normed.astype(f32)


def product_send_kernel(here_ref, *refs, scale):
    core = lax.rem(here_ref[0], CORES)
    normed, layers, (layer, out, left, right) = refs[:CHIPS], refs[CHIPS:-4], refs[-4:]
    rows = left.shape[0]
    block = layer.shape[0]
    mine = pl.ds(pl.multiple_of(core * rows, rows), rows)
    other = pl.ds(pl.multiple_of((1 - core) * rows, rows), rows)
    right[:block, :] = layer[...]
    at = block
    for x in layers:
        right[at : at + x.shape[0], :] = x[...].astype(bf16)
        at = at + x.shape[0]
    for d, x in enumerate(normed):
        left[:, d * block : (d + 1) * block] = x[mine, :].astype(bf16)
    send = jnp.concatenate([x[other, :].astype(bf16) for x in normed], axis=1)
    out[...] = (dot(send, right[...], 1, 0) * scale).reshape(out.shape)


def product_kernel(here_ref, left, right, recv, *refs, scale):
    outs, product = refs[:-1], refs[-1]
    plane = here_ref[0] // PLANE
    product[...] = (dot(left[...], right[...], 1, 0) * scale).reshape(product.shape)
    for out, d in zip(outs, [0] + line_order(len(outs))):
        out[...] = product[plane ^ d] + recv[plane ^ d]


def sum_kernel(*refs):
    total = refs[0][...]
    for x in refs[1:-1]:
        total = total + x[...]
    refs[-1][...] = total


def outputs_kernel(here_ref, rates, lens, q_in, k_in, v_in, g_in, mine, recv, q_out, k_out, v_out, *scratch):
    q, k, v, g, q_grad, k_grad, v_grad, sems = scratch
    copies = fetch((q_in, k_in, v_in, g_in), (q, k, v, g), sems)
    here = here_ref[0]
    block, features = q.shape
    half, _, width, _ = mine.shape
    reached, away = causal(here, block, lens)
    for copy in copies:
        copy.wait()
    for row, *pair in half_heads(here, half):
        for head, states in zip(pair, (mine, recv)):
            lanes = head_lanes(head, width)
            rate = rates[head]
            qh, kh, vh, gh = q[:, lanes], k[:, lanes], v[:, lanes], g[:, lanes]
            decay = jnp.where(reached, jnp.exp(-rate * away), 0.0)
            scores = dot(kh, qh, 1, 1) * decay
            grads = dot(vh, gh, 1, 1) * decay
            into, past = entry_exit(here, rate, block, lens, 0, (block, width))
            before, after = states[row, 0], states[row, 1]
            q_grad[:, lanes] = (dot2(grads, kh, 0, 0) + into * dot2(gh, before, 1, 0)).astype(bf16)
            k_grad[:, lanes] = (dot2(grads, qh, 1, 0) + past * dot2(vh, after, 1, 1)).astype(bf16)
            v_grad[:, lanes] = (dot2(scores, gh, 1, 0) + past * dot2(kh, after, 1, 0)).astype(bf16)
    outs = [pltpu.make_async_copy(x, y, sems.at[i]) for i, (x, y) in enumerate(((q_grad, q_out), (k_grad, k_out), (v_grad, v_out)))]
    for copy in outs:
        copy.start()
    for copy in outs:
        copy.wait()


def for_all_dp(outs, here, planes, dps):
    order = jnp.stack(in_order(here))
    whole = jnp.zeros((CHIPS,) + outs[0].shape, f32).at[order].set(jnp.stack(outs))
    rows = whole.shape[1] // (CORES * planes)
    whole = whole.reshape(CHIPS, CORES, planes, rows, -1).transpose(2, 0, 1, 3, 4)
    whole = whole.reshape(dps, planes, CHIPS, CORES, rows // dps, -1).transpose(2, 3, 1, 0, 4, 5)
    whole = whole.reshape((CHIPS,) + outs[0].shape)[order]
    return [whole[d] for d in range(CHIPS)]


def call(kernel, specs, outs, name, scratch=(), flops=0, moved=0, out_specs=None, after=(), **named):
    reads = len(specs)

    def body(*refs):
        kernel(*refs[:reads], *refs[reads + len(after) :], **named)

    def run(*operands):
        operands = [
            pltpu.with_memory_space_constraint(x, pltpu.HBM) if spec is HBM else x for x, spec in zip(operands, specs)
        ]
        return pl.pallas_call(
            body,
            out_shape=[jax.ShapeDtypeStruct(shape, dtype) for shape, dtype in outs],
            in_specs=list(specs) + [pl.BlockSpec(memory_space=pl.ANY)] * len(after),
            out_specs=out_specs or [VMEM] * len(outs),
            scratch_shapes=list(scratch),
            cost_estimate=pl.CostEstimate(flops=flops, bytes_accessed=moved, transcendentals=0),
            compiler_params=pltpu.CompilerParams(vmem_limit_bytes=16 * 1024 * 1024),
            name=name,
        )(*operands, *after)

    return run


def on_device(queries, keys, values, out_grad, layer_grad, norm_gain, decay_rates, doc_lengths):
    seqs, block, features = queries.shape
    assert seqs == 1
    heads = decay_rates.shape[0]
    width = features // heads
    columns = layer_grad.shape[2]
    half = heads // CORES
    part = half // CHIPS
    count = lax.axis_size("ctx")
    planes = count // PLANE
    dps = lax.axis_size("dp")
    scale = 1.0 / math.sqrt(seqs * block * dps * count)
    here = lax.axis_index("ctx").astype(jnp.int32).reshape(1)
    facts = (here, decay_rates, doc_lengths)
    q, k, v, g = (x.reshape(block, features) for x in (queries, keys, values, out_grad))
    layer = layer_grad.reshape(block, columns)

    def swap(x, bit, near=count):
        pairs = [(i, i ^ bit) for i in range(count) if abs(i // PLANE - (i ^ bit) // PLANE) <= near]
        return lax.ppermute(x, "ctx", pairs)

    def first_of_plane(x):
        return lax.ppermute(x, "ctx", [(i, i ^ (1 + i % CORES) * CORES) for i in range(count)])

    def second_of_plane(x):
        return lax.ppermute(x, "ctx", [(i, i ^ (2 - i % CORES) * CORES) for i in range(count)])

    def in_plane(pieces):
        own, first, second, diagonal = pieces
        return [own, first_of_plane(first), second_of_plane(second), swap(diagonal, 3 * CORES)]

    def in_line(pieces, order, near=count):
        return [swap(x, d * PLANE, near) for x, d in zip(pieces, order)]

    pair = ((half, 2, width, width), f32)
    small = ((part, 2, width, width), f32)
    one = ((part, width, width), f32)
    rows_in = pltpu.VMEM((block, features), bf16)
    half_layer = ((block // 2, columns), f32)
    keep, send, chip_w = call(
        summary_kernel,
        [SMEM] + [HBM] * 6,
        [pair] * 2 + [((half, 4, 128), f32)],
        "summary",
        scratch=[rows_in] * 4
        + [
            pltpu.SMEM((heads,), f32),
            pltpu.SMEM(doc_lengths.shape, jnp.int32),
            pltpu.SemaphoreType.DMA((6,)),
        ],
        flops=1 << 26,
        moved=1 << 21,
    )(*facts, q, k, v, g)
    recv = swap(send, 1)
    totals = call(
        chip_kernel, [VMEM] * 3, [small] * CHIPS, "chip_total", moved=1 << 20
    )(chip_w, keep, recv)
    attn, gain_col, into_rows = call(
        within_kernel,
        [SMEM] * 3 + [VMEM] * 4,
        [((features, block), f32)] * 2 + [((heads, block), f32)],
        "within",
        flops=1 << 28,
        moved=1 << 22,
        after=totals[:1],
    )(*facts, norm_gain.reshape(1, features), q, k, v)
    totals = in_plane(totals)
    (layer_wide,) = call(
        widen_kernel, [VMEM], [((block, columns), f32)], "widen", moved=1 << 19, after=[attn, totals[1]]
    )(layer)
    plane_w, line_w, entry_w, state_w = call(
        weights_kernel,
        [SMEM] * 3,
        [
            ((part, CHIPS, 2, 128), f32),
            ((part, planes - 1, 4, 128), f32),
            ((part, CHIPS, CHIPS + 1, 2, 128), f32),
            ((half, 8, 128), f32),
        ],
        "weights",
        flops=1 << 34,
        moved=1 << 18,
        after=[layer_wide],
        block=block,
    )(*facts)
    layer_first, layer_second = first_of_plane(layer_wide), second_of_plane(layer_wide)
    near = -(-LONGEST // (PLANE * block))
    onward = call(
        plane_kernel,
        [VMEM] * (2 + CHIPS),
        [one] * (planes - 1),
        "plane_total",
        moved=1 << 19,
        after=[attn],
    )(plane_w, line_w, *totals)
    others = in_line(onward, scan_order(planes), near)
    entries = call(
        entry_kernel,
        [VMEM] * (2 + CHIPS + len(others)),
        [small] * CHIPS,
        "entries",
        moved=1 << 20,
        lines=len(others),
    )(entry_w, line_w, *totals, *others)
    entries = in_plane(entries)
    top, bottom = call(forward_kernel, [VMEM] * 2, [half_layer] * 2, "forward", moved=1 << 20)(layer_first, layer_second)
    far_top, far_bottom = second_of_plane(top), first_of_plane(bottom)
    narrow = ((block // 2, columns), bf16)
    (far_top,) = call(narrow_kernel, [VMEM], [narrow], "far_top", flops=1 << 32, moved=1 << 18)(far_top)
    (far_bottom,) = call(narrow_kernel, [VMEM], [narrow], "far_bottom", flops=1 << 18, moved=1 << 18)(far_bottom)
    mine, send = call(
        states_kernel, [VMEM] * (3 + CHIPS), [pair] * 2, "states", moved=1 << 21
    )(state_w, keep, recv, *entries)
    theirs = swap(send, 1)

    rows = features // count
    normed = call(
        norm_kernel,
        [SMEM] + [VMEM] * 6,
        [((features // CHIPS, block), f32)] * CHIPS,
        "norm",
        scratch=[pltpu.VMEM((features, block), f32)],
        flops=1 << 26,
        moved=1 << 21,
        after=[far_top],
        rows=rows,
    )(here, q, attn, gain_col, into_rows, mine, theirs)
    if dps > 1:
        normed = for_all_dp(normed, here[0], planes, dps)
    normed = in_plane(normed)
    layers = [layer_first, layer_second, far_top, far_bottom]
    by_plane = ((planes, rows, columns), f32)
    product, left, right = call(
        product_send_kernel,
        [SMEM] + [VMEM] * (CHIPS + len(layers) + 1),
        [by_plane, ((planes * rows, CHIPS * block), bf16), ((CHIPS * block, columns), bf16)],
        "product_send",
        flops=1 << 27,
        moved=1 << 22,
        scale=scale,
    )(here, *normed, *layers, layer)
    parts = call(
        product_kernel,
        [SMEM] + [VMEM] * 3,
        [((rows, columns), f32)] * planes,
        "product",
        scratch=[pltpu.VMEM(*by_plane)],
        flops=1 << 27,
        moved=1 << 21,
        scale=scale,
    )(here, left, right, swap(product, 1))
    parts = [parts[0]] + in_line(parts[1:], line_order(planes))
    q_grad, k_grad, v_grad = call(
        outputs_kernel,
        [SMEM] * 3 + [HBM] * 4 + [VMEM] * 2,
        [((block, features), bf16)] * 3,
        "outputs",
        scratch=[rows_in] * 7 + [pltpu.SemaphoreType.DMA((4,))],
        out_specs=[HBM] * 3,
        flops=1 << 29,
        moved=1 << 22,
    )(*facts, q, k, v, g, mine, theirs)
    (proj_grad,) = call(sum_kernel, [VMEM] * planes, [((rows, columns), f32)], "sum", moved=1 << 19)(*parts)
    if dps > 1:
        proj_grad = lax.psum_scatter(proj_grad, "dp", scatter_dimension=0, tiled=True)
    shape_out = (seqs, block, features)
    return (q_grad.reshape(shape_out), k_grad.reshape(shape_out), v_grad.reshape(shape_out), proj_grad)


def solution(mesh):
    rows = P("dp", "ctx", None)
    return jax.shard_map(
        on_device,
        mesh=mesh,
        in_specs=(rows, rows, rows, rows, rows, P(), P(), P("dp", None)),
        out_specs=(rows, rows, rows, P(("dp", "ctx"), None)),
        check_vma=False,
    )
```

```python
import functools
import math

import jax
import jax.numpy as jnp
from jax import lax
from jax.experimental import pallas as pl
from jax.experimental.pallas import tpu as pltpu
from jax.sharding import PartitionSpec as P

norm_eps = 1e-06
f32 = jnp.float32
bf16 = jnp.bfloat16

CORES = 2
CHIPS = 4
PLANE = CORES * CHIPS

SMEM = pl.BlockSpec(memory_space=pltpu.SMEM)
VMEM = pl.BlockSpec(memory_space=pltpu.VMEM)
HBM = pl.BlockSpec(memory_space=pltpu.HBM)
LONGEST = 2048


def dot(a, b, over_a, over_b):
    return lax.dot_general(a, b, (((over_a,), (over_b,)), ((), ())), preferred_element_type=f32)


def split(x):
    high = x.astype(bf16)
    return high, (x - high.astype(f32)).astype(bf16)


def dot2(a, b, over_a, over_b):
    if a.dtype == f32:
        high, low = split(a)
        return dot(high, b, over_a, over_b) + dot(low, b, over_a, over_b)
    high, low = split(b)
    return dot(a, high, over_a, over_b) + dot(a, low, over_a, over_b)


def doc_of(position, lens):
    bound = lens[0, 0]
    doc = jnp.where(position >= bound, 1, 0)
    for k in range(1, lens.shape[1] - 1):
        bound = bound + lens[0, k]
        doc = doc + jnp.where(position >= bound, 1, 0)
    return doc


def carry(from_edge, to_edge, rate, block, lens):
    same = doc_of(from_edge * block - 1, lens) == doc_of(to_edge * block - 1, lens)
    away = jnp.abs(from_edge - to_edge) * block
    row = jnp.full((1, 128), away.astype(f32) * -rate, f32)
    return jnp.where(same, jnp.exp(row), 0.0)


def entry_exit(here, rate, block, lens, dim, shape):
    offsets = lax.broadcasted_iota(jnp.int32, shape, dim)
    docs = doc_of(here * block + offsets, lens)
    into = jnp.where(docs == doc_of(here * block - 1, lens), jnp.exp(-rate * offsets.astype(f32)), 0.0)
    out = jnp.where(
        docs == doc_of(here * block + block - 1, lens), jnp.exp(-rate * (block - offsets).astype(f32)), 0.0
    )
    return into, out


def head_lanes(head, width):
    return pl.ds(pl.multiple_of(head * width, width), width)


def fetch(refs, spaces, sems):
    copies = [pltpu.make_async_copy(ref, space, sems.at[i]) for i, (ref, space) in enumerate(zip(refs, spaces))]
    for copy in copies:
        copy.start()
    return copies


def in_order(here):
    core = lax.rem(here, CORES)
    chip = lax.rem(here // CORES, CHIPS)
    return [chip, chip ^ (1 + core), chip ^ (2 - core), chip ^ 3]


def half_heads(here, half):
    core = lax.rem(here, CORES)
    part = half // CHIPS
    both = enumerate(zip(in_order(here), in_order(here ^ 1)))
    return [
        (i * part + t, core * half + own * part + t, (1 - core) * half + other * part + t)
        for i, (own, other) in both
        for t in range(part)
    ]


def summary_kernel(
    here_ref, rates_in, lens_in, q_in, k_in, v_in, g_in, keep, send, chip_w, q, k, v, g, rates, lens, sems
):
    copies = fetch((rates_in, lens_in, k_in, v_in, q_in, g_in), (rates, lens, k, v, q, g), sems)
    here = here_ref[0]
    block = q.shape[0]
    half, _, width, _ = keep.shape
    heads = half_heads(here, half)
    first = lax.rem(here, CORES) == 0
    edge = here - lax.rem(here, CORES)
    for copy in copies[:2]:
        copy.wait()
    for row, head, _ in heads:
        late = carry(edge + 1, edge + 2, rates[head], block, lens)
        early = carry(edge + 1, edge, rates[head], block, lens)
        chip_w[row, 0:1, :] = jnp.where(first, late, 1.0)
        chip_w[row, 1:2, :] = jnp.where(first, 1.0, late)
        chip_w[row, 2:3, :] = jnp.where(first, 1.0, early)
        chip_w[row, 3:4, :] = jnp.where(first, early, 1.0)
    offsets = lax.broadcasted_iota(jnp.int32, (block, width), 0)
    docs = doc_of(here * block + offsets, lens)
    enters = docs == doc_of(here * block - 1, lens)
    leaves = docs == doc_of(here * block + block - 1, lens)
    from_start, to_end = offsets.astype(f32), (block - offsets).astype(f32)
    for copy in copies[2:4]:
        copy.wait()
    for row, *pair in heads:
        for head, out in zip(pair, (keep, send)):
            past = jnp.where(leaves, jnp.exp(-rates[head] * to_end), 0.0)
            lanes = head_lanes(head, width)
            out[row, 0] = dot2(v[:, lanes], k[:, lanes].astype(f32) * past, 0, 0)
    for copy in copies[4:]:
        copy.wait()
    for row, *pair in heads:
        for head, out in zip(pair, (keep, send)):
            into = jnp.where(enters, jnp.exp(-rates[head] * from_start), 0.0)
            lanes = head_lanes(head, width)
            out[row, 1] = dot2(q[:, lanes].astype(f32) * into, g[:, lanes], 0, 0)


def chip_kernel(weights, keep, recv, *outs):
    for i, out in enumerate(outs):
        for t in range(out.shape[0]):
            row = i * out.shape[0] + t
            for k in range(2):
                own, other = weights[row, 2 * k : 2 * k + 1, :], weights[row, 2 * k + 1 : 2 * k + 2, :]
                out[t, k] = own * keep[row, k] + other * recv[row, k]


def line_order(planes):
    return list(range(planes - 1, 0, -1))


def scan_order(planes):
    return [d for d in line_order(planes) if d == 2] + [d for d in range(1, planes) if d != 2]


def weights_kernel(here_ref, rates, lens, plane_w, line_w, entry_w, state_w, *, block):
    here = here_ref[0]
    half = state_w.shape[0]
    part, lines = line_w.shape[:2]
    core = lax.rem(here, CORES)
    chips = in_order(here)
    plane = here // PLANE
    base = plane * PLANE
    ones = jnp.ones((1, 128), f32)
    for t in range(part):
        rate = rates[core * half + chips[0] * part + t]

        def take(from_edge, to_edge):
            return carry(from_edge, to_edge, rate, block, lens)

        for j, d in enumerate(scan_order(lines + 1)):
            to = plane ^ d
            line_w[t, j, 0:1, :] = jnp.where(to > plane, take(base + PLANE, to * PLANE), 0.0)
            line_w[t, j, 1:2, :] = jnp.where(to < plane, take(base, (to + 1) * PLANE), 0.0)
            line_w[t, j, 2:3, :] = jnp.where(to < plane, ones, 0.0)
            line_w[t, j, 3:4, :] = jnp.where(to > plane, ones, 0.0)
        for i, at in enumerate(chips):
            edge = base + at * CORES
            plane_w[t, i, 0:1, :] = take(edge + CORES, base + PLANE)
            plane_w[t, i, 1:2, :] = take(edge, base)
            entry_w[t, i, CHIPS, 0:1, :] = take(base, edge)
            entry_w[t, i, CHIPS, 1:2, :] = take(base + PLANE, edge + CORES)
            for j, at_other in enumerate(chips):
                other = base + at_other * CORES
                entry_w[t, i, j, 0:1, :] = jnp.where(other < edge, take(other + CORES, edge), 0.0)
                entry_w[t, i, j, 1:2, :] = jnp.where(other > edge, take(other, edge + CORES), 0.0)
    edge = here - core
    first = core == 0
    for row, head, _ in half_heads(here, half):
        fwd = carry(edge, edge + 1, rates[head], block, lens)
        bwd = carry(edge + 2, edge + 1, rates[head], block, lens)
        rows = ((0.0, 1.0), (1.0, fwd), (1.0, bwd), (0.0, 1.0))
        for k, (core0, core1) in enumerate(((0, 1), (1, 0), (2, 3), (3, 2))):
            for m in range(2):
                state_w[row, 2 * k + m : 2 * k + m + 1, :] = jnp.where(
                    first, ones * rows[core0][m], ones * rows[core1][m]
                )


def plane_kernel(weights, line_w, *refs):
    totals, outs = refs[:CHIPS], refs[CHIPS:]
    for t in range(outs[0].shape[0]):
        fwd, bwd = 0.0, 0.0
        for i, total in enumerate(totals):
            fwd = fwd + weights[t, i, 0:1, :] * total[t, 0]
            bwd = bwd + weights[t, i, 1:2, :] * total[t, 1]
        for j, out in enumerate(outs):
            out[t] = line_w[t, j, 0:1, :] * fwd + line_w[t, j, 1:2, :] * bwd


def narrow_kernel(layer, out):
    out[...] = layer[...].astype(bf16)


def widen_kernel(layer, out):
    out[...] = layer[...].astype(f32)


def forward_kernel(layer_first, layer_second, top, bottom):
    top[...] = layer_first[: top.shape[0], :]
    bottom[...] = layer_second[top.shape[0] :, :]


def entry_kernel(weights, line_w, *refs, lines):
    totals, others, outs = refs[:CHIPS], refs[CHIPS : CHIPS + lines], refs[CHIPS + lines :]
    for t in range(outs[0].shape[0]):
        before, after = 0.0, 0.0
        for j, other in enumerate(others):
            before = before + line_w[t, j, 2:3, :] * other[t]
            after = after + line_w[t, j, 3:4, :] * other[t]
        for i, out in enumerate(outs):
            fwd = weights[t, i, CHIPS, 0:1, :] * before
            bwd = weights[t, i, CHIPS, 1:2, :] * after
            for j, total in enumerate(totals):
                if i != j:
                    fwd = fwd + weights[t, i, j, 0:1, :] * total[t, 0]
                    bwd = bwd + weights[t, i, j, 1:2, :] * total[t, 1]
            out[t, 0], out[t, 1] = fwd, bwd


def states_kernel(weights, keep, recv, *refs):
    entries, (mine, send) = refs[:CHIPS], refs[CHIPS:]
    part = entries[0].shape[0]
    for i, entry in enumerate(entries):
        for t in range(part):
            row = i * part + t
            for k in range(2):
                for m, (own, out) in enumerate(((recv, mine), (keep, send))):
                    at = 4 * k + 2 * m
                    out[row, k] = weights[row, at : at + 1, :] * own[row, k] + weights[row, at + 1 : at + 2, :] * entry[t, k]


def causal(here, block, lens):
    at_j = lax.broadcasted_iota(jnp.int32, (block, block), 0)
    at_i = lax.broadcasted_iota(jnp.int32, (block, block), 1)
    docs_j = doc_of(here * block + at_j, lens)
    docs_i = doc_of(here * block + at_i, lens)
    return (docs_i == docs_j) & (at_i >= at_j), jnp.maximum(at_i - at_j, 0).astype(f32)


def within_kernel(here_ref, rates, lens, gain, q, k, v, attn, gain_col, into_rows):
    here = here_ref[0]
    block, features = q.shape
    heads = rates.shape[0]
    width = features // heads
    reached, away = causal(here, block, lens)
    for head in range(heads):
        lanes = slice(head * width, (head + 1) * width)
        gain_col[lanes, :] = jnp.broadcast_to(gain[:, lanes], (block, width)).T
        decay = jnp.where(reached, jnp.exp(-rates[head] * away), 0.0)
        scores = dot(k[:, lanes], q[:, lanes], 1, 1) * decay
        attn[lanes, :] = dot2(v[:, lanes], scores, 0, 0)
        into_rows[head : head + 1, :], _ = entry_exit(here, rates[head], block, lens, 1, (1, block))


def norm_kernel(here_ref, q, attn, gain_col, into_rows, mine, recv, *refs, rows):
    outs, total = refs[:CHIPS], refs[CHIPS]
    here = here_ref[0]
    block, features = q.shape
    half, _, width, _ = mine.shape
    squares = jnp.zeros((width, block), f32)
    for row, *pair in half_heads(here, half):
        for head, states in zip(pair, (mine, recv)):
            lanes = head_lanes(head, width)
            at = attn[lanes, :] + into_rows[pl.ds(head, 1), :] * dot2(states[row, 0], q[:, lanes], 1, 1)
            total[lanes, :] = at
            squares = squares + at * at
    mean = jnp.sum(squares, axis=0, keepdims=True) * (1.0 / features)
    factor = lax.rsqrt(mean + norm_eps)
    planes = features // (PLANE * rows)
    for out, chip in zip(outs, in_order(here)):
        for to_core in range(CORES):
            for plane in range(planes):
                block_at = plane * PLANE + chip * CORES + to_core
                at = pl.ds(pl.multiple_of(block_at * rows, rows), rows)
                normed = (total[at, :] * factor * gain_col[at, :]).astype(bf16)
                to = to_core * planes + plane
                out[to * rows : (to + 1) * rows, :] = normed.astype(f32)


def product_send_kernel(here_ref, *refs, scale):
    core = lax.rem(here_ref[0], CORES)
    normed, layers, (layer, out, left, right) = refs[:CHIPS], refs[CHIPS:-4], refs[-4:]
    rows = left.shape[0]
    block = layer.shape[0]
    mine = pl.ds(pl.multiple_of(core * rows, rows), rows)
    other = pl.ds(pl.multiple_of((1 - core) * rows, rows), rows)
    right[:block, :] = layer[...]
    at = block
    for x in layers:
        right[at : at + x.shape[0], :] = x[...].astype(bf16)
        at = at + x.shape[0]
    for d, x in enumerate(normed):
        left[:, d * block : (d + 1) * block] = x[mine, :].astype(bf16)
    send = jnp.concatenate([x[other, :].astype(bf16) for x in normed], axis=1)
    out[...] = (dot(send, right[...], 1, 0) * scale).reshape(out.shape)


def product_kernel(here_ref, left, right, recv, *refs, scale):
    outs, product = refs[:-1], refs[-1]
    plane = here_ref[0] // PLANE
    product[...] = (dot(left[...], right[...], 1, 0) * scale).reshape(product.shape)
    for out, d in zip(outs, [0] + line_order(len(outs))):
        out[...] = product[plane ^ d] + recv[plane ^ d]


def sum_kernel(*refs):
    total = refs[0][...]
    for x in refs[1:-1]:
        total = total + x[...]
    refs[-1][...] = total


def outputs_kernel(here_ref, rates, lens, q_in, k_in, v_in, g_in, mine, recv, q_out, k_out, v_out, *scratch):
    q, k, v, g, q_grad, k_grad, v_grad, sems = scratch
    copies = fetch((q_in, k_in, v_in, g_in), (q, k, v, g), sems)
    here = here_ref[0]
    block, features = q.shape
    half, _, width, _ = mine.shape
    reached, away = causal(here, block, lens)
    for copy in copies:
        copy.wait()
    for row, *pair in half_heads(here, half):
        for head, states in zip(pair, (mine, recv)):
            lanes = head_lanes(head, width)
            rate = rates[head]
            qh, kh, vh, gh = q[:, lanes], k[:, lanes], v[:, lanes], g[:, lanes]
            decay = jnp.where(reached, jnp.exp(-rate * away), 0.0)
            scores = dot(kh, qh, 1, 1) * decay
            grads = dot(vh, gh, 1, 1) * decay
            into, past = entry_exit(here, rate, block, lens, 0, (block, width))
            before, after = states[row, 0], states[row, 1]
            q_grad[:, lanes] = (dot2(grads, kh, 0, 0) + into * dot2(gh, before, 1, 0)).astype(bf16)
            k_grad[:, lanes] = (dot2(grads, qh, 1, 0) + past * dot2(vh, after, 1, 1)).astype(bf16)
            v_grad[:, lanes] = (dot2(scores, gh, 1, 0) + past * dot2(kh, after, 1, 0)).astype(bf16)
    outs = [pltpu.make_async_copy(x, y, sems.at[i]) for i, (x, y) in enumerate(((q_grad, q_out), (k_grad, k_out), (v_grad, v_out)))]
    for copy in outs:
        copy.start()
    for copy in outs:
        copy.wait()


def for_all_dp(outs, here, planes, dps):
    order = jnp.stack(in_order(here))
    whole = jnp.zeros((CHIPS,) + outs[0].shape, f32).at[order].set(jnp.stack(outs))
    rows = whole.shape[1] // (CORES * planes)
    whole = whole.reshape(CHIPS, CORES, planes, rows, -1).transpose(2, 0, 1, 3, 4)
    whole = whole.reshape(dps, planes, CHIPS, CORES, rows // dps, -1).transpose(2, 3, 1, 0, 4, 5)
    whole = whole.reshape((CHIPS,) + outs[0].shape)[order]
    return [whole[d] for d in range(CHIPS)]


def call(kernel, specs, outs, name, scratch=(), flops=0, moved=0, out_specs=None, after=(), **named):
    reads = len(specs)

    def body(*refs):
        kernel(*refs[:reads], *refs[reads + len(after) :], **named)

    def run(*operands):
        operands = [
            pltpu.with_memory_space_constraint(x, pltpu.HBM) if spec is HBM else x for x, spec in zip(operands, specs)
        ]
        return pl.pallas_call(
            body,
            out_shape=[jax.ShapeDtypeStruct(shape, dtype) for shape, dtype in outs],
            in_specs=list(specs) + [pl.BlockSpec(memory_space=pl.ANY)] * len(after),
            out_specs=out_specs or [VMEM] * len(outs),
            scratch_shapes=list(scratch),
            cost_estimate=pl.CostEstimate(flops=flops, bytes_accessed=moved, transcendentals=0),
            compiler_params=pltpu.CompilerParams(vmem_limit_bytes=16 * 1024 * 1024),
            name=name,
        )(*operands, *after)

    return run


def on_device(queries, keys, values, out_grad, layer_grad, norm_gain, decay_rates, doc_lengths):
    seqs, block, features = queries.shape
    assert seqs == 1
    heads = decay_rates.shape[0]
    width = features // heads
    columns = layer_grad.shape[2]
    half = heads // CORES
    part = half // CHIPS
    count = lax.axis_size("ctx")
    planes = count // PLANE
    dps = lax.axis_size("dp")
    scale = 1.0 / math.sqrt(seqs * block * dps * count)
    here = lax.axis_index("ctx").astype(jnp.int32).reshape(1)
    facts = (here, decay_rates, doc_lengths)
    q, k, v, g = (x.reshape(block, features) for x in (queries, keys, values, out_grad))
    layer = layer_grad.reshape(block, columns)

    def swap(x, bit, near=count):
        pairs = [(i, i ^ bit) for i in range(count) if abs(i // PLANE - (i ^ bit) // PLANE) <= near]
        return lax.ppermute(x, "ctx", pairs)

    def first_of_plane(x):
        return lax.ppermute(x, "ctx", [(i, i ^ (1 + i % CORES) * CORES) for i in range(count)])

    def second_of_plane(x):
        return lax.ppermute(x, "ctx", [(i, i ^ (2 - i % CORES) * CORES) for i in range(count)])

    def in_plane(pieces):
        own, first, second, diagonal = pieces
        return [own, first_of_plane(first), second_of_plane(second), swap(diagonal, 3 * CORES)]

    def in_line(pieces, order, near=count):
        return [swap(x, d * PLANE, near) for x, d in zip(pieces, order)]

    pair = ((half, 2, width, width), f32)
    small = ((part, 2, width, width), f32)
    one = ((part, width, width), f32)
    rows_in = pltpu.VMEM((block, features), bf16)
    half_layer = ((block // 2, columns), f32)
    keep, send, chip_w = call(
        summary_kernel,
        [SMEM] + [HBM] * 6,
        [pair] * 2 + [((half, 4, 128), f32)],
        "summary",
        scratch=[rows_in] * 4
        + [
            pltpu.SMEM((heads,), f32),
            pltpu.SMEM(doc_lengths.shape, jnp.int32),
            pltpu.SemaphoreType.DMA((6,)),
        ],
        flops=1 << 26,
        moved=1 << 21,
    )(*facts, q, k, v, g)
    recv = swap(send, 1)
    totals = call(
        chip_kernel, [VMEM] * 3, [small] * CHIPS, "chip_total", moved=1 << 20
    )(chip_w, keep, recv)
    attn, gain_col, into_rows = call(
        within_kernel,
        [SMEM] * 3 + [VMEM] * 4,
        [((features, block), f32)] * 2 + [((heads, block), f32)],
        "within",
        flops=1 << 28,
        moved=1 << 22,
        after=totals[:1],
    )(*facts, norm_gain.reshape(1, features), q, k, v)
    totals = in_plane(totals)
    (layer_wide,) = call(
        widen_kernel, [VMEM], [((block, columns), f32)], "widen", moved=1 << 19, after=[attn, totals[1]]
    )(layer)
    plane_w, line_w, entry_w, state_w = call(
        weights_kernel,
        [SMEM] * 3,
        [
            ((part, CHIPS, 2, 128), f32),
            ((part, planes - 1, 4, 128), f32),
            ((part, CHIPS, CHIPS + 1, 2, 128), f32),
            ((half, 8, 128), f32),
        ],
        "weights",
        flops=1 << 34,
        moved=1 << 18,
        after=[layer_wide],
        block=block,
    )(*facts)
    layer_first, layer_second = first_of_plane(layer_wide), second_of_plane(layer_wide)
    near = -(-LONGEST // (PLANE * block))
    onward = call(
        plane_kernel,
        [VMEM] * (2 + CHIPS),
        [one] * (planes - 1),
        "plane_total",
        moved=1 << 19,
        after=[attn],
    )(plane_w, line_w, *totals)
    others = in_line(onward, scan_order(planes), near)
    entries = call(
        entry_kernel,
        [VMEM] * (2 + CHIPS + len(others)),
        [small] * CHIPS,
        "entries",
        moved=1 << 20,
        lines=len(others),
    )(entry_w, line_w, *totals, *others)
    entries = in_plane(entries)
    top, bottom = call(forward_kernel, [VMEM] * 2, [half_layer] * 2, "forward", moved=1 << 20)(layer_first, layer_second)
    far_top, far_bottom = second_of_plane(top), first_of_plane(bottom)
    narrow = ((block // 2, columns), bf16)
    (far_top,) = call(narrow_kernel, [VMEM], [narrow], "far_top", flops=5 << 30, moved=1 << 18)(far_top)
    (far_bottom,) = call(narrow_kernel, [VMEM], [narrow], "far_bottom", flops=1 << 18, moved=1 << 18)(far_bottom)
    mine, send = call(
        states_kernel, [VMEM] * (3 + CHIPS), [pair] * 2, "states", moved=1 << 21
    )(state_w, keep, recv, *entries)
    theirs = swap(send, 1)

    rows = features // count
    normed = call(
        norm_kernel,
        [SMEM] + [VMEM] * 6,
        [((features // CHIPS, block), f32)] * CHIPS,
        "norm",
        scratch=[pltpu.VMEM((features, block), f32)],
        flops=1 << 26,
        moved=1 << 21,
        after=[far_top],
        rows=rows,
    )(here, q, attn, gain_col, into_rows, mine, theirs)
    if dps > 1:
        normed = for_all_dp(normed, here[0], planes, dps)
    normed = in_plane(normed)
    layers = [layer_first, layer_second, far_top, far_bottom]
    by_plane = ((planes, rows, columns), f32)
    product, left, right = call(
        product_send_kernel,
        [SMEM] + [VMEM] * (CHIPS + len(layers) + 1),
        [by_plane, ((planes * rows, CHIPS * block), bf16), ((CHIPS * block, columns), bf16)],
        "product_send",
        flops=1 << 27,
        moved=1 << 22,
        scale=scale,
    )(here, *normed, *layers, layer)
    parts = call(
        product_kernel,
        [SMEM] + [VMEM] * 3,
        [((rows, columns), f32)] * planes,
        "product",
        scratch=[pltpu.VMEM(*by_plane)],
        flops=1 << 27,
        moved=1 << 21,
        scale=scale,
    )(here, left, right, swap(product, 1))
    parts = [parts[0]] + in_line(parts[1:], line_order(planes))
    q_grad, k_grad, v_grad = call(
        outputs_kernel,
        [SMEM] * 3 + [HBM] * 4 + [VMEM] * 2,
        [((block, features), bf16)] * 3,
        "outputs",
        scratch=[rows_in] * 7 + [pltpu.SemaphoreType.DMA((4,))],
        out_specs=[HBM] * 3,
        flops=1 << 29,
        moved=1 << 22,
    )(*facts, q, k, v, g, mine, theirs)
    (proj_grad,) = call(sum_kernel, [VMEM] * planes, [((rows, columns), f32)], "sum", moved=1 << 19)(*parts)
    if dps > 1:
        proj_grad = lax.psum_scatter(proj_grad, "dp", scatter_dimension=0, tiled=True)
    shape_out = (seqs, block, features)
    return (q_grad.reshape(shape_out), k_grad.reshape(shape_out), v_grad.reshape(shape_out), proj_grad)


def solution(mesh):
    rows = P("dp", "ctx", None)
    return jax.shard_map(
        on_device,
        mesh=mesh,
        in_specs=(rows, rows, rows, rows, rows, P(), P(), P("dp", None)),
        out_specs=(rows, rows, rows, P(("dp", "ctx"), None)),
        check_vma=False,
    )
```
